32 devices in a mesh: batch: 8 (over z, x), blk: 4 (over y, core).
Axes of the slice: x: 2, y: 2, z: 4, core: 2. Of those that a mesh axis runs over, the one named last changes fastest.
Arguments:
- obs_tokens: int32 [16, 40, 36], P('batch', 'blk'), may hold values from 0 to 330
- returns: int32 [16, 40], P('batch', 'blk'), may hold values from 0 to 119
- actions: int32 [16, 40], P('batch', 'blk'), may hold values from 0 to 17
- rewards: int32 [16, 40], P('batch', 'blk'), may hold values from 0 to 3
- game_ids: int32 [16, 40], P('batch', 'blk'), may hold values from 0 to 40
- segments: int32 [16, 40], P('batch', 'blk'), may hold values from 0 to 1, never falling along the last dimension, each value on 1 to 39 neighbouring positions
- embed_table: float32 [512, 1280], P(('batch', 'blk')), may hold values from -4 to 4
- qkv_weight: float32 [1280, 3840], P(('batch', 'blk')), may hold values from -0.15625 to 0.15625
- proj_weight: float32 [1280, 1280], P(('batch', 'blk')), may hold values from -1 to 1
- up_weight: float32 [1280, 5120], P(('batch', 'blk')), may hold values from -0.15625 to 0.15625
- down_weight: float32 [5120, 1280], P(('batch', 'blk')), may hold values from -0.078125 to 0.078125
- head_weight: float32 [1280, 142], P(('batch', 'blk')), may hold values from -0.15625 to 0.15625
- norm_gains: float32 [3, 1280], P(None, ('batch', 'blk')), may hold values from 0.5 to 1.5
- first_embed: float32 [512, 1280], P(('batch', 'blk')), may hold values from -1.9073486e-05 to 1.9073486e-05
- first_qkv: float32 [1280, 3840], P(('batch', 'blk')), may hold values from -1.9073486e-05 to 1.9073486e-05
- first_proj: float32 [1280, 1280], P(('batch', 'blk')), may hold values from -1.9073486e-05 to 1.9073486e-05
- first_up: float32 [1280, 5120], P(('batch', 'blk')), may hold values from -1.9073486e-05 to 1.9073486e-05
- first_down: float32 [5120, 1280], P(('batch', 'blk')), may hold values from -1.9073486e-05 to 1.9073486e-05
- first_head: float32 [1280, 142], P(('batch', 'blk')), may hold values from -1.9073486e-05 to 1.9073486e-05
- first_gains: float32 [3, 1280], P(None, ('batch', 'blk')), may hold values from -9.1552734e-05 to 9.1552734e-05
- second_embed: float32 [512, 1280], P(('batch', 'blk')), may hold values from 1.2194075e-12 to 4.87763e-12
- second_qkv: float32 [1280, 3840], P(('batch', 'blk')), may hold values from 1.2194075e-12 to 4.87763e-12
- second_proj: float32 [1280, 1280], P(('batch', 'blk')), may hold values from 1.2194075e-12 to 4.87763e-12
- second_up: float32 [1280, 5120], P(('batch', 'blk')), may hold values from 1.2194075e-12 to 4.87763e-12
- second_down: float32 [5120, 1280], P(('batch', 'blk')), may hold values from 1.2194075e-12 to 4.87763e-12
- second_head: float32 [1280, 142], P(('batch', 'blk')), may hold values from 1.2194075e-12 to 4.87763e-12
- second_gains: float32 [3, 1280], P(None, ('batch', 'blk')), may hold values from 3.0485187e-11 to 1.2194075e-10
Outputs:
- new_embed: float32 [512, 1280], P(('batch', 'blk'))
- new_qkv: float32 [1280, 3840], P(('batch', 'blk'))
- new_proj: float32 [1280, 1280], P(('batch', 'blk'))
- new_up: float32 [1280, 5120], P(('batch', 'blk'))
- new_down: float32 [5120, 1280], P(('batch', 'blk'))
- new_head: float32 [1280, 142], P(('batch', 'blk'))
- new_gains: float32 [3, 1280], P(None, ('batch', 'blk'))
- mean_embed: float32 [512, 1280], P(('batch', 'blk'))
- mean_qkv: float32 [1280, 3840], P(('batch', 'blk'))
- mean_proj: float32 [1280, 1280], P(('batch', 'blk'))
- mean_up: float32 [1280, 5120], P(('batch', 'blk'))
- mean_down: float32 [5120, 1280], P(('batch', 'blk'))
- mean_head: float32 [1280, 142], P(('batch', 'blk'))
- mean_gains: float32 [3, 1280], P(None, ('batch', 'blk'))
- square_embed: float32 [512, 1280], P(('batch', 'blk'))
- square_qkv: float32 [1280, 3840], P(('batch', 'blk'))
- square_proj: float32 [1280, 1280], P(('batch', 'blk'))
- square_up: float32 [1280, 5120], P(('batch', 'blk'))
- square_down: float32 [5120, 1280], P(('batch', 'blk'))
- square_head: float32 [1280, 142], P(('batch', 'blk'))
- square_gains: float32 [3, 1280], P(None, ('batch', 'blk'))
- copy_embed: bfloat16 [512, 1280], P(('batch', 'blk'))
- copy_qkv: bfloat16 [1280, 3840], P(('batch', 'blk'))
- copy_proj: bfloat16 [1280, 1280], P(('batch', 'blk'))
- copy_up: bfloat16 [1280, 5120], P(('batch', 'blk'))
- copy_down: bfloat16 [5120, 1280], P(('batch', 'blk'))
- copy_head: bfloat16 [1280, 142], P(('batch', 'blk'))
- grad_norm: float32 [], replicated
- loss_terms: float32 [3], replicated
- group_norms: float32 [2, 9], replicated
The draws below stay inside these ranges and needn't reach their ends.
Inputs may be any that keep to these rules, and one draw needn't show every extreme that they name: `segments`: segment numbers never fall along a sequence's 4 * 10 timesteps.
All inputs are finite; a program needn't handle non-finite values.
Results may differ from the reference program's by a relative error of at most 0.012.
Values may be sent and summed in bfloat16 or wider, within the bound.
A program may use at most 320 MiB of HBM per device.

```python
import math
import jax
import jax.numpy as jnp
import numpy as np
from jax import lax

D = 1280
HEADS = 20
HEAD_DIM = 64
FF = 5120
RET_BINS = 120
ACTIONS = 18
REWARDS = 4
GAMES = 41
TSTEP = 39
OBS = 36
PATCH = 331
STEP = 10
SEQ_DEV = 2
TPD = 10
HEAD_COLS = 142
TABLE = 512
PARAMS = 20501760
SEQS = 16
N_BATCH = 8
N_BLK = 4


def plant(entries, key, smallest, largest):
    longest = entries.shape.index(max(entries.shape))
    spots = []
    for shift in (0, 1):
        where = [jax.random.randint(jax.random.fold_in(key, axis), (), 0, length) for axis, length in enumerate(entries.shape)]
        where[longest] = (where[longest] + shift) % entries.shape[longest]
        spots.append(tuple(where))
    return entries.at[spots[0]].set(smallest).at[spots[1]].set(largest)


def steps_of(rng, dims, cuts, low, high):
    level = 1.0
    for position, shards_of in cuts:
        steps = jax.random.uniform(jax.random.fold_in(jax.random.fold_in(rng, 6), position), (shards_of,), jnp.float32, low / len(cuts), high / len(cuts))
        level = level * jnp.repeat(jnp.exp(steps), dims[position] // shards_of).reshape((-1,) + (1,) * (len(dims) - 1 - position))
    return level


def rank_bounds(amount, skew):
    portions = [(1 << 20) // math.isqrt(standing ** skew) + 1 for standing in range(1, amount + 1)]
    width = 1 + sum(portions) // (1 << 30)
    return np.cumsum(np.array([max(1, weight // width) for weight in portions]))


def ranked(key, extent, amount, skew):
    table = rank_bounds(amount, skew)
    pick = jax.random.randint(jax.random.fold_in(key, 1), extent, 0, int(table[amount - 1]))
    standing = jnp.searchsorted(jnp.asarray(table, jnp.int32), pick, side="right")
    return jax.random.permutation(jax.random.fold_in(key, 2), amount)[standing].astype(jnp.int32)


def split_up(count, total, most, skew):
    portions = [(1 << 20) // math.isqrt(rank ** skew) + 1 for rank in range(2, count + 1)]
    surplus, given = total - most - (count - 1), [1] * (count - 1)
    while surplus > 0:
        free = [i for i in range(count - 1) if given[i] < most]
        whole, left = sum([portions[i] for i in free]), surplus
        for i in free:
            more = min(most - given[i], max(1, left * portions[i] // whole), surplus)
            given[i] = given[i] + more
            surplus = surplus - more
    return np.array([most] + given)


def ragged(key, number_of, total, limit, skew):
    if number_of == 2:
        one = jax.random.randint(key, (), max(1, total - limit), min(limit, total - 1) + 1)
        return jnp.stack([one, total - one])
    lengths = jnp.asarray(split_up(number_of, total, limit, skew), jnp.int32)
    pairs = (number_of - 1) // 2
    giver, taker = lengths[1:1 + 2 * pairs:2], lengths[2:2 + 2 * pairs:2]
    room = jnp.minimum(giver - 1, limit - taker)
    passed = jax.random.randint(jax.random.fold_in(key, 1), (pairs,), 0, 1 << 20) % (room + 1)
    lengths = lengths.at[1:1 + 2 * pairs:2].set(giver - passed).at[2:2 + 2 * pairs:2].set(taker + passed)
    return lengths[jax.random.permutation(jax.random.fold_in(key, 2), number_of)]


def noise(own_key, extent, spread, most, shards=(), held_as=jnp.bfloat16):
    factor_of = steps_of(own_key, extent, shards, -0.22, 0.18) if shards else 1.0
    values = jax.random.normal(own_key, extent, jnp.float32) * spread * factor_of
    return jnp.minimum(jnp.maximum(values, -most), most).astype(held_as)


def setup_inputs(seed: int = 0) -> dict:
    keys = jax.random.split(jax.random.key(seed), 28)
    obs_tokens = plant(jax.random.randint(keys[0], (SEQS, N_BLK * TPD, OBS), 0, PATCH), jax.random.fold_in(keys[0], 1), 0, PATCH - 1).astype(jnp.int32)
    returns = plant(jax.random.randint(keys[1], (SEQS, N_BLK * TPD), 0, RET_BINS), jax.random.fold_in(keys[1], 1), 0, RET_BINS - 1).astype(jnp.int32)
    actions = plant(jax.random.randint(keys[2], (SEQS, N_BLK * TPD), 0, ACTIONS), jax.random.fold_in(keys[2], 1), 0, ACTIONS - 1).astype(jnp.int32)
    rewards = plant(jax.random.randint(keys[3], (SEQS, N_BLK * TPD), 0, REWARDS), jax.random.fold_in(keys[3], 1), 0, REWARDS - 1).astype(jnp.int32)
    game_ids = plant(ranked(keys[4], (SEQS, N_BLK * TPD), GAMES, 2), jax.random.fold_in(keys[4], 3), 0, GAMES - 1).astype(jnp.int32)
    segments = jax.vmap(lambda own: jnp.searchsorted(jnp.cumsum(ragged(own, 2, N_BLK * TPD, N_BLK * TPD - 1, 1)), jnp.arange(N_BLK * TPD), side="right"))(jax.random.split(keys[5], SEQS)).reshape((SEQS, N_BLK * TPD)).astype(jnp.int32)
    embed_table = noise(keys[6], (TABLE, D), 0.7, 4.0, ((0, 32),), jnp.float32)
    qkv_weight = noise(keys[7], (D, 3 * D), D ** -0.5, 0.15625, ((0, 32),), jnp.float32)
    proj_weight = noise(keys[8], (D, D), (D // 32) ** -0.5, 1.0, ((0, 32),), jnp.float32)
    up_weight = noise(keys[9], (D, FF), D ** -0.5, 0.15625, ((0, 32),), jnp.float32)
    down_weight = noise(keys[10], (FF, D), FF ** -0.5, 0.078125, ((0, 32),), jnp.float32)
    head_weight = noise(keys[11], (D, HEAD_COLS), D ** -0.5, 0.15625, ((0, 32),), jnp.float32)
    norm_gains = jnp.clip(1.0 + 0.1 * jax.random.normal(keys[12], (3, D), jnp.float32), 0.5, 1.5)
    first_embed = noise(keys[13], (TABLE, D), (0.0056 * PARAMS ** -0.5), 1.9073486328125e-05, ((0, 32),), jnp.float32)
    first_qkv = noise(keys[14], (D, 3 * D), (0.0056 * PARAMS ** -0.5), 1.9073486328125e-05, ((0, 32),), jnp.float32)
    first_proj = noise(keys[15], (D, D), (0.0056 * PARAMS ** -0.5), 1.9073486328125e-05, ((0, 32),), jnp.float32)
    first_up = noise(keys[16], (D, FF), (0.0056 * PARAMS ** -0.5), 1.9073486328125e-05, ((0, 32),), jnp.float32)
    first_down = noise(keys[17], (FF, D), (0.0056 * PARAMS ** -0.5), 1.9073486328125e-05, ((0, 32),), jnp.float32)
    first_head = noise(keys[18], (D, HEAD_COLS), (0.0056 * PARAMS ** -0.5), 1.9073486328125e-05, ((0, 32),), jnp.float32)
    first_gains = noise(keys[19], (3, D), (0.028 * PARAMS ** -0.5), 9.1552734375e-05, ((1, 32),), jnp.float32)
    second_embed = jnp.clip(jnp.exp(math.log(4.877629983940368e-12) - 1.3862944 * jax.random.uniform(keys[20], (TABLE, D), jnp.float32) ** steps_of(keys[20], (TABLE, D), ((0, 32),), -0.2, 0.2)), 1.219407495985092e-12, 4.877629983940368e-12)
    second_qkv = jnp.clip(jnp.exp(math.log(4.877629983940368e-12) - 1.3862944 * jax.random.uniform(keys[21], (D, 3 * D), jnp.float32) ** steps_of(keys[21], (D, 3 * D), ((0, 32),), -0.2, 0.2)), 1.219407495985092e-12, 4.877629983940368e-12)
    second_proj = jnp.clip(jnp.exp(math.log(4.877629983940368e-12) - 1.3862944 * jax.random.uniform(keys[22], (D, D), jnp.float32) ** steps_of(keys[22], (D, D), ((0, 32),), -0.2, 0.2)), 1.219407495985092e-12, 4.877629983940368e-12)
    second_up = jnp.clip(jnp.exp(math.log(4.877629983940368e-12) - 1.3862944 * jax.random.uniform(keys[23], (D, FF), jnp.float32) ** steps_of(keys[23], (D, FF), ((0, 32),), -0.2, 0.2)), 1.219407495985092e-12, 4.877629983940368e-12)
    second_down = jnp.clip(jnp.exp(math.log(4.877629983940368e-12) - 1.3862944 * jax.random.uniform(keys[24], (FF, D), jnp.float32) ** steps_of(keys[24], (FF, D), ((0, 32),), -0.2, 0.2)), 1.219407495985092e-12, 4.877629983940368e-12)
    second_head = jnp.clip(jnp.exp(math.log(4.877629983940368e-12) - 1.3862944 * jax.random.uniform(keys[25], (D, HEAD_COLS), jnp.float32) ** steps_of(keys[25], (D, HEAD_COLS), ((0, 32),), -0.2, 0.2)), 1.219407495985092e-12, 4.877629983940368e-12)
    second_gains = jnp.clip(jnp.exp(math.log(1.2194074916482833e-10) - 1.3862944 * jax.random.uniform(keys[26], (3, D), jnp.float32) ** steps_of(keys[26], (3, D), ((1, 32),), -0.2, 0.2)), 3.048518729120708e-11, 1.2194074916482833e-10)
    return {"obs_tokens": obs_tokens, "returns": returns, "actions": actions, "rewards": rewards, "game_ids": game_ids, "segments": segments, "embed_table": embed_table, "qkv_weight": qkv_weight, "proj_weight": proj_weight, "up_weight": up_weight, "down_weight": down_weight, "head_weight": head_weight, "norm_gains": norm_gains, "first_embed": first_embed, "first_qkv": first_qkv, "first_proj": first_proj, "first_up": first_up, "first_down": first_down, "first_head": first_head, "first_gains": first_gains, "second_embed": second_embed, "second_qkv": second_qkv, "second_proj": second_proj, "second_up": second_up, "second_down": second_down, "second_head": second_head, "second_gains": second_gains}


@jax.custom_vjp
def low(v):
    return lax.optimization_barrier(v.astype(jnp.bfloat16)).astype(jnp.float32)

@jax.custom_vjp
def low_back(v):
    return v

def low_keep(v):
    return (low(v), None)

def low_pass(kept, grad):
    return (grad,)

def back_keep(v):
    return (v, None)

def back_low(kept, grad):
    return (low(grad),)
low.defvjp(low_keep, low_pass)
low_back.defvjp(back_keep, back_low)
HIGH = lax.Precision.HIGHEST

def mat(left, right):
    return jnp.dot(left, right, precision=HIGH, preferred_element_type=jnp.float32)

def layer_norm(v, gain):
    center = v - lax.optimization_barrier(jnp.mean(v, -1, keepdims=True))
    return center * lax.rsqrt(lax.optimization_barrier(jnp.mean(center * center, -1, keepdims=True)) + 1e-05) * gain

def head_losses(logits, ret, act, rew, weight):
    parts = ((logits[:, 0, :RET_BINS], ret), (logits[:, 1, RET_BINS:RET_BINS + ACTIONS], act), (logits[:, 2, RET_BINS + ACTIONS:], rew))
    result = []
    for part, target in parts:
        top = lax.optimization_barrier(jnp.max(part, -1, keepdims=True))
        lse = jnp.log(lax.optimization_barrier(jnp.sum(jnp.exp(part - top), -1))) + top[:, 0]
        picked = lax.optimization_barrier(jnp.sum(jnp.where(target[:, None] == jnp.arange(part.shape[1]), part, 0.0), -1))
        result.append(jnp.sum((lse - picked) * weight))
    return jnp.stack(result)

def forward(params, obs, ret, act, rew, seg, weight):
    table, w_qkv, w_proj, w_up, w_down, w_head = [low(w) for w in params[:6]]
    gains = low(params[6])
    seqs = obs.shape[0]
    steps_all = N_BLK * TPD
    length = steps_all * TSTEP
    codes = jnp.concatenate([obs, PATCH + ret[..., None], PATCH + RET_BINS + act[..., None], PATCH + RET_BINS + ACTIONS + rew[..., None]], -1)
    places = PATCH + HEAD_COLS + jnp.arange(TSTEP)
    columns = jnp.arange(TABLE)
    hot = ((codes[..., None] == columns) | (places[:, None] == columns)).astype(jnp.float32)
    x = mat(hot.reshape(-1, TABLE), table)
    a = low(layer_norm(x, gains[0]))
    qkv = low(low_back(mat(a, w_qkv)))
    q = jnp.moveaxis(qkv[:, :D].reshape(seqs, length, HEADS, HEAD_DIM), 2, 0)
    k = jnp.moveaxis(qkv[:, D:2 * D].reshape(seqs, length, HEADS, HEAD_DIM), 2, 0)
    v = jnp.moveaxis(qkv[:, 2 * D:].reshape(seqs, length, HEADS, HEAD_DIM), 2, 0)
    token_seg = jnp.repeat(seg, TSTEP, axis=1)
    index = jnp.arange(length)
    allowed = (index[None, :] <= index[:, None])[None] & (token_seg[:, :, None] == token_seg[:, None, :])

    def head_attend(item):
        query, key, value = item
        scores = low_back(jnp.einsum('sqd,skd->sqk', query, key, precision=HIGH) * HEAD_DIM ** (-0.5))
        scores = jnp.where(allowed, scores, -1e+30)
        top = lax.optimization_barrier(jnp.max(scores, -1, keepdims=True))
        expo = jnp.exp(scores - top)
        probs = low(expo / lax.optimization_barrier(jnp.sum(expo, -1, keepdims=True)))
        return jnp.einsum('sqk,skd->sqd', probs, value, precision=HIGH)
    att = lax.map(jax.checkpoint(head_attend), (q, k, v))
    att = jnp.moveaxis(att, 0, 2).reshape(-1, D)
    att = low(low_back(att))
    x2 = x + low_back(mat(att, w_proj))
    b = low(layer_norm(x2, gains[1]))
    u = low_back(mat(b, w_up))
    hidden = low(jax.nn.gelu(u, approximate=True))
    x3 = x2 + low_back(mat(hidden, w_down))
    picked = x3.reshape(seqs, steps_all, TSTEP, D)[:, :, OBS - 1:OBS + 2]
    c = low(layer_norm(picked, gains[2])).reshape(-1, D)
    logits = low_back(mat(c, w_head)).reshape(seqs * steps_all, 3, HEAD_COLS)
    return head_losses(logits, ret.reshape(-1), act.reshape(-1), rew.reshape(-1), weight.reshape(-1))

def group_squares(arrays):
    mats = jnp.stack([jnp.sum(w * w) for w in arrays[:6]])
    return jnp.concatenate([mats, lax.optimization_barrier(jnp.sum(arrays[6] * arrays[6], 1))])

def per_group(ratio, index, array):
    return ratio[index] if index < 6 else ratio[6:9][:, None]

def reference(obs_tokens, returns, actions, rewards, game_ids, segments, embed_table, qkv_weight, proj_weight, up_weight, down_weight, head_weight, norm_gains, first_embed, first_qkv, first_proj, first_up, first_down, first_head, first_gains, second_embed, second_qkv, second_proj, second_up, second_down, second_head, second_gains):
    masters = (embed_table, qkv_weight, proj_weight, up_weight, down_weight, head_weight, norm_gains)
    firsts = (first_embed, first_qkv, first_proj, first_up, first_down, first_head, first_gains)
    seconds = (second_embed, second_qkv, second_proj, second_up, second_down, second_head, second_gains)
    game_hot = (game_ids[..., None] == jnp.arange(GAMES)).astype(jnp.float32)
    counts = lax.optimization_barrier(jnp.sum(game_hot, (0, 1)))
    per_game = 1.0 / (GAMES * jnp.maximum(counts, 1.0))
    row_weight = lax.optimization_barrier(jnp.sum(game_hot * per_game, -1))

    def split(v):
        return v.reshape((N_BATCH, SEQ_DEV) + v.shape[1:])
    items = (split(obs_tokens), split(returns), split(actions), split(rewards), split(segments), split(row_weight))

    def block(carry, item):
        obs, ret, act, rew, seg, weight = item
        losses, pull = jax.vjp(lambda *p: forward(p, obs, ret, act, rew, seg, weight), *masters)
        grads = pull(jnp.ones((3,), jnp.float32))
        return ((tuple((s + g for s, g in zip(carry[0], grads))), carry[1] + losses), None)
    start = (tuple((jnp.zeros_like(w) for w in masters)), jnp.zeros((3,), jnp.float32))
    (grads, loss_terms), unused = lax.scan(block, start, items)
    grad_norm = jnp.sqrt(jnp.sum(group_squares(grads)))
    factor = jnp.minimum(1.0, 0.05 / grad_norm)
    means = tuple((0.9 * m + 0.1 * (factor * g) for m, g in zip(firsts, grads)))
    squares = tuple((0.99 * s + 0.01 * (factor * g) * (factor * g) for s, g in zip(seconds, grads)))
    updates = tuple((m / (1.0 - 0.9 ** STEP) / (jnp.sqrt(s / (1.0 - 0.99 ** STEP)) + 1e-08) + 0.01 * w for m, s, w in zip(means, squares, masters)))
    weight_norm = jnp.sqrt(group_squares(masters))
    update_norm = jnp.sqrt(group_squares(updates))
    ratio = weight_norm / update_norm
    news = tuple((w - 0.3 * per_group(ratio, i, w) * d for i, (w, d) in enumerate(zip(masters, updates))))
    copies = tuple((w.astype(jnp.bfloat16) for w in news[:6]))
    norms = jnp.stack([weight_norm, update_norm])
    return (news[0], news[1], news[2], news[3], news[4], news[5], news[6], means[0], means[1], means[2], means[3], means[4], means[5], means[6], squares[0], squares[1], squares[2], squares[3], squares[4], squares[5], squares[6], copies[0], copies[1], copies[2], copies[3], copies[4], copies[5], grad_norm, loss_terms, norms)
```

```python
import functools
import math

import jax
import jax.numpy as jnp
from jax import lax
from jax.experimental import pallas as pl
from jax.experimental.pallas import tpu as pltpu
from jax.sharding import Mesh
from jax.sharding import PartitionSpec as P

HEADS = 20
RET_BINS = 120
ACTIONS = 18
GAMES = 41
TSTEP = 39
OBS = 36
PATCH = 331
STEP = 10
HEAD_COLS = 142
TABLE = 512
PICKS = 3
BF = jnp.bfloat16
F32 = jnp.float32
HIGH = lax.Precision.HIGHEST
GROUP = ("bl", "blk")
BATCH = ("bh", "bl")
ALL = ("bh", "bl", "blk")


def exchange_kernel(axes, kinds, *refs):
    count = len(kinds)
    srcs, dsts = refs[:count], refs[count : 2 * count]
    local_sem, send_sem, recv_sem = refs[2 * count :]
    sizes = [lax.axis_size(a) for a in axes]
    total = math.prod(sizes)
    me = 0
    for a, s in zip(axes, sizes):
        me = me * s + lax.axis_index(a)

    def device(j):
        where = {}
        for a, s in reversed(list(zip(axes, sizes))):
            where[a] = lax.rem(j, s)
            j = j // s
        return where

    def block(i, j):
        return srcs[i] if kinds[i] == "gather" else srcs[i].at[j]

    barrier = pltpu.get_barrier_semaphore()
    for k in range(1, total):
        pl.semaphore_signal(
            barrier,
            inc=1,
            device_id=device(lax.rem(me + k, total)),
            device_id_type=pl.DeviceIdType.MESH,
        )
    local = [
        pltpu.make_async_copy(block(i, me), dsts[i].at[me], local_sem.at[i]) for i in range(count)
    ]
    for c in local:
        c.start()
    pl.semaphore_wait(barrier, total - 1)
    sent = []
    for i in range(count):
        for k in range(1, total):
            to = lax.rem(me + k, total)
            c = pltpu.make_async_remote_copy(
                src_ref=block(i, to),
                dst_ref=dsts[i].at[me],
                send_sem=send_sem.at[i, k],
                recv_sem=recv_sem.at[i, k],
                device_id=device(to),
                device_id_type=pl.DeviceIdType.MESH,
            )
            c.start()
            sent.append(c)
    for c in local:
        c.wait()
    for c in sent:
        c.wait()


def exchange(arrays, kinds, axes, ident):
    total = math.prod(lax.axis_size(a) for a in axes)
    shapes = [
        jax.ShapeDtypeStruct((total,) + x.shape if k == "gather" else x.shape, x.dtype)
        for x, k in zip(arrays, kinds)
    ]
    n = len(arrays)
    return pl.pallas_call(
        functools.partial(exchange_kernel, axes, kinds),
        out_shape=shapes,
        in_specs=[pl.BlockSpec(memory_space=pl.ANY)] * n,
        out_specs=[pl.BlockSpec(memory_space=pl.ANY)] * n,
        scratch_shapes=[
            pltpu.SemaphoreType.DMA((n,)),
            pltpu.SemaphoreType.DMA((n, total)),
            pltpu.SemaphoreType.DMA((n, total)),
        ],
        compiler_params=pltpu.CompilerParams(collective_id=ident, has_side_effects=True),
    )(*arrays)


def pad_to(x, rows, cols):
    widths = [(0, 0)] * (x.ndim - 2) + [(0, rows - x.shape[-2]), (0, cols - x.shape[-1])]
    return jnp.pad(x, widths)


def up_to(n, m):
    return -(-n // m) * m


def dot(left, right, ca=1, cb=0, precision=None):
    return lax.dot_general(
        left,
        right,
        (((ca,), (cb,)), ((), ())),
        precision=precision,
        preferred_element_type=F32,
    )


def layer_norm(v, gain):
    center = v - jnp.mean(v, -1, keepdims=True)
    return center * lax.rsqrt(jnp.mean(center * center, -1, keepdims=True) + 1e-05) * gain


def head_losses(logits, ret, act, rew, weight):
    parts = (
        (logits[:, 0, :RET_BINS], ret),
        (logits[:, 1, RET_BINS : RET_BINS + ACTIONS], act),
        (logits[:, 2, RET_BINS + ACTIONS :], rew),
    )
    result = []
    for part, target in parts:
        top = jnp.max(part, -1, keepdims=True)
        lse = jnp.log(jnp.sum(jnp.exp(part - top), -1)) + top[:, 0]
        picked = jnp.sum(jnp.where(target[:, None] == jnp.arange(part.shape[1]), part, 0.0), -1)
        result.append(jnp.sum((lse - picked) * weight))
    return jnp.stack(result)


def group_squares(arrays):
    mats = jnp.stack([jnp.sum(w * w) for w in arrays[:6]])
    return jnp.concatenate([mats, jnp.sum(arrays[6] * arrays[6], 1)])


def per_group(ratio, index):
    return ratio[index] if index < 6 else ratio[6:9][:, None]


def gradients(obs_tokens, returns, actions, rewards, game_ids, segments, masters):
    table, w_qkv, w_proj, w_up, w_down, w_head, gains = masters
    nbh, nk = lax.axis_size("bh"), lax.axis_size("blk")
    nb, members = nbh * 2, 2 * nk
    total = nb * nk
    bh, bl, k = lax.axis_index("bh"), lax.axis_index("bl"), lax.axis_index("blk")
    b, g = bh * 2 + bl, bl * nk + k
    seqs, steps_here = obs_tokens.shape[:2]
    width = table.shape[1]
    rows, table_rows = w_qkv.shape[0], table.shape[0]
    steps = steps_here * nk
    heads = HEADS // nk
    head_dim = width // HEADS
    wide = heads * head_dim
    cols = 3 * wide // nb
    ff_rows = w_down.shape[0]
    padded_rows = up_to(rows, 16)

    info = jnp.concatenate(
        [obs_tokens]
        + [v[..., None] for v in (returns, actions, rewards, game_ids, segments)],
        -1,
    ).reshape(seqs * steps_here, -1)
    info = pad_to(info, up_to(seqs * steps_here, 8), 128)
    table_bf = pad_to(table.astype(BF), up_to(table_rows, 16), width)
    misc = pad_to(
        jnp.concatenate([w_head.astype(BF), gains.astype(BF).T], 1), padded_rows, 256
    )
    qkv_blocks = w_qkv.astype(BF).reshape(rows, 3, nk, wide).transpose(2, 0, 1, 3)
    qkv_blocks = qkv_blocks.reshape(nk, rows, nb, cols).transpose(2, 0, 1, 3)
    qkv_blocks = pad_to(qkv_blocks.reshape(total, rows, cols), padded_rows, 128)
    info_all, table_all, misc_all, qkv_mine = exchange(
        (info, table_bf, misc, qkv_blocks), ("gather", "gather", "gather", "scatter"), ALL, 0
    )
    up_blocks = w_up.astype(BF).reshape(rows, nbh, members, ff_rows).transpose(2, 0, 1, 3)
    up_blocks = pad_to(up_blocks.reshape(members, rows, nbh * ff_rows), padded_rows, nbh * ff_rows)
    (up_mine,) = exchange((up_blocks,), ("scatter",), GROUP, 1)
    up_full = lax.all_gather(
        up_mine[:, :rows].reshape(members * rows, nbh * ff_rows), "bh", axis=0, tiled=True
    )
    down_full = lax.all_gather(w_down.astype(BF), "bh", axis=0, tiled=True)
    proj_full = lax.all_gather(w_proj.astype(BF), ALL, axis=0, tiled=True)

    table_all = table_all[:, :table_rows].reshape(TABLE, width)
    misc_all = misc_all[:, :rows].reshape(width, 256)
    head_full = misc_all[:, :HEAD_COLS]
    gain = misc_all[:, HEAD_COLS : HEAD_COLS + 3].T.astype(F32)
    w_mine = qkv_mine[:, :rows, :cols].reshape(width, cols)
    info_all = info_all[:, : seqs * steps_here].reshape(nb, nk, seqs, steps_here, 128)
    info_all = info_all.transpose(0, 2, 1, 3, 4).reshape(nb, seqs, steps, 128)
    games = info_all[..., OBS + 3]
    counts = jnp.sum((games.reshape(-1, 1) == jnp.arange(GAMES)).astype(F32), 0)
    per_game = 1.0 / (GAMES * jnp.maximum(counts, 1.0))
    info_group = lax.dynamic_slice_in_dim(info_all, bh * 2, 2, 0)
    info_here = lax.dynamic_index_in_dim(info_all, b, 0, False)

    table_f = table_all.astype(F32)
    center = table_f - jnp.mean(table_f, 1, keepdims=True)
    center_gain = (center * gain[0]).astype(BF)
    center_bf = center.astype(BF)
    qkv_cols = dot(center_gain, w_mine)
    (qkv_table,) = exchange(
        (pad_to(qkv_cols.astype(BF), TABLE, 128),), ("gather",), BATCH, 2
    )
    qkv_table = qkv_table[:, :, :cols].transpose(1, 0, 2).reshape(TABLE, 3 * wide)
    first_place = PATCH + HEAD_COLS
    gram = dot(center, center[first_place:], 1, 1, HIGH)
    own_square = jnp.sum(center * center, 1)
    scale_table = lax.rsqrt(
        (own_square[:, None] + own_square[None, first_place:] + 2.0 * gram) / width + 1e-05
    )
    scale_high = scale_table.astype(BF)
    scale_low = (scale_table - scale_high.astype(F32)).astype(BF)
    scale_both = jnp.concatenate([scale_high, scale_low], 1)

    offsets = jnp.array([0] * OBS + [PATCH, PATCH + RET_BINS, PATCH + RET_BINS + ACTIONS])
    columns = jnp.arange(TABLE)
    codes = info_here[..., :TSTEP] + offsets
    code_hot = codes[..., None] == columns
    place_hot = (first_place + jnp.arange(TSTEP))[:, None] == columns
    hot = (code_hot | place_hot).astype(BF).reshape(seqs * steps * TSTEP, TABLE)
    scales = dot(code_hot.astype(BF).reshape(-1, TABLE), scale_both)
    scales = scales.reshape(seqs * steps, TSTEP, 2, TSTEP)
    eye = jnp.eye(TSTEP, dtype=F32)
    scales = jnp.sum(scales * eye[:, None, :], (2, 3)).reshape(-1, 1)

    picks = slice(OBS - 1, OBS + 2)

    def pick(x):
        return x.reshape(seqs * steps, TSTEP, -1)[:, picks].reshape(seqs * steps * PICKS, -1)

    hot_pick, scale_pick = pick(hot), pick(scales)
    queries = (scale_pick * dot(hot_pick, qkv_table[:, :wide])).astype(BF)
    keys_values = (scales * dot(hot, qkv_table[:, wide:])).astype(BF)

    def split_heads(x):
        return x.reshape(seqs, -1, heads, head_dim).transpose(0, 2, 1, 3)

    q, kk, v = (
        split_heads(queries),
        split_heads(keys_values[:, :wide]),
        split_heads(keys_values[:, wide:]),
    )
    seg = info_here[..., OBS + 4]
    place = jnp.arange(steps * TSTEP)
    query_place = place.reshape(steps, TSTEP)[:, picks].reshape(-1)
    allowed = (place[None, :] <= query_place[:, None])[None] & (
        jnp.repeat(seg, PICKS, 1)[:, :, None] == jnp.repeat(seg, TSTEP, 1)[:, None, :]
    )
    factor = head_dim**-0.5
    scores = jnp.einsum("shqd,shkd->shqk", q, kk, preferred_element_type=F32) * factor
    scores = jnp.where(allowed[:, None], scores, -1e30)
    expo = jnp.exp(scores - jnp.max(scores, -1, keepdims=True))
    probs = expo / jnp.sum(expo, -1, keepdims=True)
    probs_bf = probs.astype(BF)
    att = jnp.einsum("shqk,shkd->shqd", probs_bf, v, preferred_element_type=F32).astype(BF)
    att = att.transpose(0, 2, 1, 3).reshape(-1, wide)

    (att_all,) = exchange((att,), ("gather",), GROUP, 3)
    queries_here = att.shape[0]
    att_all = att_all.reshape(2, nk, queries_here, wide).transpose(0, 2, 1, 3)
    att_all = att_all.reshape(2 * queries_here, width)
    group_codes = (info_group[..., :TSTEP] + offsets)[..., picks]
    group_hot = (
        (group_codes[..., None] == columns) | (place_hot[picks])
    ).astype(BF).reshape(-1, TABLE)
    picked_x = dot(group_hot, table_all)
    x2 = picked_x + dot(att_all, proj_full)
    low = layer_norm(x2, gain[1]).astype(BF)
    u = dot(low, up_full)
    hid_full, gelu_back = jax.vjp(lambda t: jax.nn.gelu(t, approximate=True), u)
    hid = hid_full.astype(BF)
    own = x2.shape[0] // members
    part = dot(hid, down_full).astype(BF).reshape(members, own, width)
    (parts,) = exchange((part,), ("scatter",), GROUP, 4)
    x2_own = lax.dynamic_slice_in_dim(x2, g * own, own, 0)
    x3 = x2_own + jnp.sum(parts.astype(F32), 0)
    c_full, norm_last = jax.vjp(layer_norm, x3, gain[2])
    c = c_full.astype(BF)
    logits = dot(c, head_full)
    own_steps = own // PICKS
    info_own = lax.dynamic_slice_in_dim(
        info_group.reshape(-1, 128), g * own_steps, own_steps, 0
    )
    game_hot = (info_own[:, OBS + 3, None] == jnp.arange(GAMES)).astype(F32)
    row_weight = jnp.sum(game_hot * per_game, -1)
    losses, loss_back = jax.vjp(
        lambda l: head_losses(
            l.reshape(own_steps, PICKS, -1),
            info_own[:, OBS],
            info_own[:, OBS + 1],
            info_own[:, OBS + 2],
            row_weight,
        ),
        logits,
    )
    dlogits = loss_back(jnp.ones((3,), F32))[0].astype(BF)
    d_head = dot(c, dlogits, 0, 0)
    dx3, d_gain_last = norm_last(dot(dlogits, head_full, 1, 1))
    (dz,) = exchange((dx3.astype(BF),), ("gather",), GROUP, 5)
    dz = dz.reshape(-1, width)
    d_down = dot(hid, dz, 0, 0)
    du = gelu_back(dot(dz, down_full, 1, 1))[0].astype(BF)
    d_up = dot(low, du, 0, 0)
    d_low = dot(du, up_full, 1, 1).astype(BF).reshape(members, own, width)
    (d_lows,) = exchange((d_low,), ("scatter",), GROUP, 6)
    norm_mid = jax.vjp(layer_norm, x2_own, gain[1])[1]
    dx2_norm, d_gain_mid = norm_mid(jnp.sum(d_lows.astype(F32), 0))
    dx2 = dx3 + dx2_norm
    dy_own = dx2.astype(BF)
    (dy,) = exchange((dy_own,), ("gather",), GROUP, 7)
    dy = dy.reshape(-1, width)
    att_rows = lax.dynamic_index_in_dim(
        att_all.reshape(-1, nbh, members, rows), g, 2, False
    ).reshape(-1, nbh * rows)
    d_proj = dot(att_rows, dy, 0, 0)
    sum_up = lax.psum_scatter(d_up.astype(BF), "bh", scatter_dimension=0, tiled=True)
    sum_down = lax.psum_scatter(d_down.astype(BF), "bh", scatter_dimension=0, tiled=True)
    sum_proj = lax.psum_scatter(d_proj.astype(BF), "bh", scatter_dimension=0, tiled=True)

    dy_here = lax.dynamic_slice_in_dim(dy, bl * queries_here, queries_here, 0)
    proj_here = lax.dynamic_slice_in_dim(proj_full, k * wide, wide, 0)
    datt = split_heads(dot(dy_here, proj_here, 1, 1).astype(BF))
    dprob = jnp.einsum("shqd,shkd->shqk", datt, v, preferred_element_type=F32)
    dscore = (probs * (dprob - jnp.sum(probs * dprob, -1, keepdims=True))).astype(BF)
    dq = jnp.einsum("shqk,shkd->shqd", dscore, kk, preferred_element_type=F32) * factor
    dk = jnp.einsum("shqk,shqd->shkd", dscore, q, preferred_element_type=F32) * factor
    dv = jnp.einsum("shqk,shqd->shkd", probs_bf, datt, preferred_element_type=F32)

    def join_heads(x):
        return x.transpose(0, 2, 1, 3).reshape(-1, wide)

    dq = join_heads(dq)
    dkv = jnp.concatenate([join_heads(dk), join_heads(dv)], 1)
    d_table_q = dot(hot_pick, (scale_pick * dq).astype(BF), 0, 0)
    d_table_kv = dot(hot, (scales * dkv).astype(BF), 0, 0)
    d_table = jnp.concatenate([d_table_q, d_table_kv], 1)
    kappa = jnp.sum(dkv * keys_values.astype(F32), 1, keepdims=True)
    kappa_pick = jnp.sum(dq * queries.astype(F32), 1, keepdims=True)
    kappa = kappa.reshape(seqs * steps, TSTEP, 1)
    kappa = kappa.at[:, picks].add(kappa_pick.reshape(seqs * steps, PICKS, 1)).reshape(-1, 1)
    weighted = hot * (scales * scales * kappa / width).astype(BF)
    pairs = dot(hot, weighted, 0, 0)

    d_table = d_table.astype(BF).reshape(TABLE, nb, cols).transpose(1, 0, 2)
    (d_tables,) = exchange((pad_to(d_table, TABLE, 128),), ("scatter",), BATCH, 8)
    d_table_mine = jnp.sum(d_tables[:, :, :cols].astype(F32), 0).astype(BF)
    d_w = dot(center_gain, d_table_mine, 0, 0)
    d_norm = dot(d_table_mine, w_mine, 1, 1)
    d_gain_first = jnp.sum(center * d_norm, 0)
    d_scaled = d_norm * gain[0]
    own_hot = lax.dynamic_slice_in_dim(group_hot, g * own, own, 0)
    d_embed = (
        d_scaled
        - jnp.mean(d_scaled, 1, keepdims=True)
        - dot(pairs.astype(BF), center_bf)
        + dot(own_hot, dy_own, 0, 0)
    )
    d_misc = jnp.concatenate(
        [d_head, jnp.stack([d_gain_first, d_gain_mid, d_gain_last], 1)], 1
    )
    d_misc = pad_to(d_misc.astype(BF).reshape(total, rows, -1), padded_rows, 256)
    d_w = pad_to(d_w.astype(BF).reshape(total, rows, cols), padded_rows, 128)
    d_embed = d_embed.astype(BF).reshape(total, table_rows, width)
    d_embed = pad_to(d_embed, up_to(table_rows, 16), width)
    d_embeds, d_miscs, d_ws = exchange(
        (d_embed, d_misc, d_w), ("scatter", "scatter", "scatter"), ALL, 9
    )
    d_embed = jnp.sum(d_embeds.astype(F32), 0)[:table_rows]
    d_misc = jnp.sum(d_miscs.astype(F32), 0)[:rows]
    d_ws = d_ws[:, :rows, :cols].reshape(nb, nk, rows, cols).transpose(2, 1, 0, 3)
    d_ws = d_ws.reshape(rows, nk, 3, wide).transpose(0, 2, 1, 3).reshape(rows, 3 * width)
    sum_up = pad_to(sum_up.reshape(members, rows, -1), padded_rows, nbh * ff_rows)
    (ups,) = exchange((sum_up,), ("scatter",), GROUP, 10)
    ups = ups[:, :rows].reshape(members, rows, nbh, ff_rows).transpose(1, 2, 0, 3)
    ups = ups.reshape(rows, nbh * members * ff_rows)
    grads = (
        d_embed,
        d_ws.astype(F32),
        sum_proj.astype(F32),
        ups.astype(F32),
        sum_down.astype(F32),
        d_misc[:, :HEAD_COLS],
        d_misc[:, HEAD_COLS : HEAD_COLS + 3].T,
    )
    return grads, losses


def all_sum(values, ident):
    block = jnp.zeros((8, 128), F32).at[0, : values.shape[0]].set(values)
    (blocks,) = exchange((block,), ("gather",), ALL, ident)
    return jnp.sum(blocks[:, 0], 0)[: values.shape[0]]


def shards(*args):
    obs_tokens, returns, actions, rewards, game_ids, segments = args[:6]
    masters, firsts, seconds = args[6:13], args[13:20], args[20:27]
    grads, losses = gradients(
        obs_tokens, returns, actions, rewards, game_ids, segments, masters
    )
    sums = all_sum(
        jnp.concatenate([group_squares(grads), group_squares(masters), losses]), 11
    )
    grad_sq, weight_sq, loss_terms = sums[:9], sums[9:18], sums[18:21]
    grad_norm = jnp.sqrt(jnp.sum(grad_sq))
    factor = jnp.minimum(1.0, 0.05 / grad_norm)
    means = tuple((0.9 * m + 0.1 * (factor * g) for m, g in zip(firsts, grads)))
    squares = tuple(
        (0.99 * s + 0.01 * (factor * g) * (factor * g) for s, g in zip(seconds, grads))
    )
    updates = tuple(
        (
            m / (1.0 - 0.9**STEP) / (jnp.sqrt(s / (1.0 - 0.99**STEP)) + 1e-08) + 0.01 * w
            for m, s, w in zip(means, squares, masters)
        )
    )
    update_sq = all_sum(group_squares(updates), 12)
    weight_norm = jnp.sqrt(weight_sq)
    update_norm = jnp.sqrt(update_sq)
    ratio = weight_norm / update_norm
    news = tuple(
        (w - 0.3 * per_group(ratio, i) * d for i, (w, d) in enumerate(zip(masters, updates)))
    )
    copies = tuple((w.astype(BF) for w in news[:6]))
    norms = jnp.stack([weight_norm, update_norm])
    return news + means + squares + copies + (grad_norm, loss_terms, norms)


def solution(mesh):
    nb, nk = mesh.shape["batch"], mesh.shape["blk"]
    split = Mesh(mesh.devices.reshape(nb // 2, 2, nk), ALL)
    rows, gains = P(ALL, None), P(None, ALL)
    weights = (rows,) * 6 + (gains,)
    in_specs = (P(BATCH, "blk", None),) + (P(BATCH, "blk"),) * 5 + weights * 3
    out_specs = weights * 3 + (rows,) * 6 + (P(), P(), P())
    return jax.shard_map(
        shards, mesh=split, in_specs=in_specs, out_specs=out_specs, check_vma=False
    )
```

```python
import functools
import math

import jax
import jax.numpy as jnp
import numpy as np
from jax import lax
from jax.experimental import pallas as pl
from jax.experimental.pallas import tpu as pltpu
from jax.sharding import Mesh
from jax.sharding import PartitionSpec as P

HEADS = 20
RET_BINS = 120
ACTIONS = 18
GAMES = 41
TSTEP = 39
OBS = 36
PATCH = 331
STEP = 10
HEAD_COLS = 142
TABLE = 512
PICKS = 3
LANES = 128
FIRST_PLACE = PATCH + HEAD_COLS
BF = jnp.bfloat16
F32 = jnp.float32
HIGH = lax.Precision.HIGHEST
BLK = ("kh", "kl")
GROUP = ("bl", "kh", "kl")
BATCH = ("ba", "bl", "bc")
COPIES = ("ba", "bc")
ALL = ("ba", "bl", "bc", "kh", "kl")
VMEM_LIMIT = 56 * 2**20
PLACES = list(range(OBS - 1, OBS + 2)) + [p for p in range(TSTEP) if not OBS - 1 <= p < OBS + 2]


def up_to(n, m):
    return -(-n // m) * m


def pad_to(x, rows, cols):
    if x.shape[-2:] == (rows, cols):
        return x
    widths = [(0, 0)] * (x.ndim - 2) + [(0, rows - x.shape[-2]), (0, cols - x.shape[-1])]
    return jnp.pad(x, widths)


def dot(left, right, ca=1, cb=0, precision=None):
    return lax.dot_general(
        left,
        right,
        (((ca,), (cb,)), ((), ())),
        precision=precision,
        preferred_element_type=F32,
    )


class Links:
    def __init__(self, sends, recvs):
        self.sends, self.recvs, self.open = sends, recvs, []
        self.size = {a: lax.axis_size(a) for a in ALL}
        self.here = {a: lax.axis_index(a) for a in ALL}

    def at(self, axis, step):
        return lax.rem(self.here[axis] + step, self.size[axis])

    def number(self, axes, steps):
        n = 0
        for a in axes:
            n = n * self.size[a] + self.at(a, steps.get(a, 0))
        return n

    def moves(self, axes):
        result = [{}]
        for a in axes:
            result = [dict(m, **{a: r}) for m in result for r in range(self.size[a])]
        return [{a: r for a, r in m.items() if r} for m in result if any(m.values())]

    def greet(self, axes, everyone=False):
        barrier = pltpu.get_barrier_semaphore()
        if everyone:
            moves = self.moves(axes)
        else:
            moves = [{a: r} for a in axes for r in range(1, self.size[a])]
        for move in moves:
            pl.semaphore_signal(
                barrier,
                inc=1,
                device_id={a: self.at(a, r) for a, r in move.items()},
                device_id_type=pl.DeviceIdType.MESH,
            )
        pl.semaphore_wait(barrier, len(moves))

    def send(self, src, dst, move):
        n = len(self.open)
        c = pltpu.make_async_remote_copy(
            src_ref=src,
            dst_ref=dst,
            send_sem=self.sends.at[n],
            recv_sem=self.recvs.at[n],
            device_id={a: self.at(a, r) for a, r in move.items()},
            device_id_type=pl.DeviceIdType.MESH,
        )
        c.start()
        self.open.append(c)
        return c

    def finish(self):
        for c in self.open:
            c.wait_send()


class Gather:
    def __init__(self, links, src, dst, route, local):
        self.links, self.src, self.dst = links, src, dst
        self.route, self.local, self.waits, self.stage = list(route), local, [], 0

    def step(self):
        links = self.links
        for c in self.waits:
            c.wait_recv()
        self.waits = []
        if self.stage == len(self.route):
            return False
        if self.stage == 1:
            self.local.wait()
            self.local = None
        count = math.prod(links.size[a] for a in self.route[: self.stage])
        start = links.number(self.route[self.stage :][::-1], {}) * count
        here = self.dst.at[pl.ds(start, count)]
        block = self.src if self.stage == 0 else here
        there = self.dst.at[start] if self.stage == 0 else here
        axis = self.route[self.stage]
        for r in range(1, links.size[axis]):
            self.waits.append(links.send(block, there, {axis: r}))
        self.stage += 1
        return True

    def close(self):
        if self.local is not None:
            self.local.wait()


class Reduce:
    def __init__(self, links, src, out, route, arrived, totals):
        self.links, self.now, self.out = links, src, out
        self.route, self.arrived, self.totals = list(route), arrived, totals
        self.waits, self.stage = [], 0

    def part(self, axis, step):
        count = self.now.shape[0] // self.links.size[axis]
        return pl.ds(self.links.at(axis, step) * count, count)

    def step(self):
        if self.stage:
            axis = self.route[self.stage - 1]
            for c in self.waits:
                c.wait_recv()
            total = self.now[self.part(axis, 0)].astype(F32)
            for n in range(len(self.waits)):
                total = total + self.arrived[self.stage - 1][n].astype(F32)
            if self.stage == len(self.route):
                self.out[...] = total[0]
                return False
            self.now = self.totals[self.stage - 1]
            self.now[...] = total.astype(self.now.dtype)
        axis = self.route[self.stage]
        self.waits = []
        for r in range(1, self.links.size[axis]):
            dst = self.arrived[self.stage].at[r - 1]
            self.waits.append(self.links.send(self.now.at[self.part(axis, r)], dst, {axis: r}))
        self.stage += 1
        return True


def start_scatters(links, jobs):
    copies = []
    for src, dst, axes, kind in jobs:
        me = links.number(axes, {})
        for move in links.moves(axes):
            block = src.at[links.number(axes, move)] if kind == "scatter" else src
            copies.append(links.send(block, dst.at[me], move))
    return copies


def run(jobs):
    jobs = list(jobs)
    while jobs:
        jobs = [j for j in jobs if j.step()]


def sizes_of(axes):
    return tuple(lax.axis_size(a) for a in axes)


def exchange_kernel(kinds, routes, *refs):
    count = len(kinds)
    srcs, dsts = refs[:count], refs[count : 2 * count]
    local_sem, send_sem, recv_sem = refs[2 * count :]
    links = Links(send_sem, recv_sem)
    local = []
    for i, route in enumerate(routes):
        me = links.number(route[::-1] if kinds[i] == "gather" else route, {})
        block = srcs[i].at[me] if kinds[i] == "scatter" else srcs[i]
        local.append(pltpu.make_async_copy(block, dsts[i].at[me], local_sem.at[i]))
        local[-1].start()
    everyone = any(k != "gather" for k in kinds)
    links.greet([a for a in ALL if any(a in x for x in routes)], everyone)
    gathers = [
        Gather(links, srcs[i], dsts[i], routes[i], local[i])
        for i in range(count)
        if kinds[i] == "gather"
    ]
    for j in gathers:
        j.step()
    copies = []
    for i in range(count):
        if kinds[i] != "gather":
            copies += start_scatters(links, [(srcs[i], dsts[i], routes[i], kinds[i])])
    run(gathers)
    for j in gathers:
        j.close()
    for c in copies:
        c.wait_recv()
    for i in range(count):
        if kinds[i] != "gather":
            local[i].wait()
    links.finish()


def natural(x, axes, route):
    back = route[::-1]
    x = x.reshape(sizes_of(back) + x.shape[1:])
    order = [back.index(a) for a in axes] + list(range(len(axes), x.ndim))
    return x.transpose(order).reshape((-1,) + x.shape[len(axes) :])


def for_route(x, axes, route):
    x = x.reshape(sizes_of(axes) + x.shape[1:])
    order = [axes.index(a) for a in route] + list(range(len(axes), x.ndim))
    return x.transpose(order).reshape((-1,) + x.shape[len(axes) :])


def exchange(items, ident):
    arrays, kinds, routes = zip(*items)
    shapes, copies = [], 0
    for x, kind, route in zip(arrays, kinds, routes):
        sizes = sizes_of(route)
        shape = x.shape if kind == "scatter" else (math.prod(sizes),) + x.shape
        shapes.append(jax.ShapeDtypeStruct(shape, x.dtype))
        copies += sum(sizes) - len(sizes) if kind == "gather" else math.prod(sizes) - 1
    n = len(arrays)
    return pl.pallas_call(
        functools.partial(exchange_kernel, kinds, routes),
        out_shape=shapes,
        in_specs=[pl.BlockSpec(memory_space=pl.ANY)] * n,
        out_specs=[pl.BlockSpec(memory_space=pl.ANY)] * n,
        scratch_shapes=[
            pltpu.SemaphoreType.DMA((n,)),
            pltpu.SemaphoreType.DMA((copies,)),
            pltpu.SemaphoreType.DMA((copies,)),
        ],
        compiler_params=pltpu.CompilerParams(collective_id=ident, has_side_effects=True),
    )(*arrays)


def reduce_buffers(shape, dtype, route):
    arrived, totals = [], []
    for i, axis in enumerate(route):
        rest = (math.prod(sizes_of(route[i + 1 :])),) + shape
        arrived.append(pltpu.VMEM((lax.axis_size(axis) - 1,) + rest, dtype))
        totals.append(pltpu.VMEM(rest, dtype))
    return arrived + totals[:-1]


def reduce_kernel(routes, other_axes, *refs):
    refs = list(refs)

    def take(n):
        got = refs[:n]
        del refs[:n]
        return got

    sums, stages = len(routes), len(routes[0])
    srcs, other_srcs = take(sums), take(len(other_axes))
    outs, other_dsts = take(sums), take(len(other_axes))
    buffers = [(take(stages), take(stages - 1)) for _ in range(sums)]
    local_sem, send_sem, recv_sem = refs
    links = Links(send_sem, recv_sem)
    local = []
    for i, axes in enumerate(other_axes):
        me = links.number(axes, {})
        local.append(
            pltpu.make_async_copy(other_srcs[i].at[me], other_dsts[i].at[me], local_sem.at[i])
        )
        local[-1].start()
    seen = [a for a in ALL if a in routes[0] or any(a in x for x in other_axes)]
    links.greet(seen, bool(other_axes))
    jobs = [
        Reduce(links, srcs[i], outs[i], routes[i], *buffers[i]) for i in range(sums)
    ]
    for j in jobs:
        j.step()
    copies = start_scatters(
        links, [(s, d, a, "scatter") for s, d, a in zip(other_srcs, other_dsts, other_axes)]
    )
    run(jobs)
    for c in copies:
        c.wait_recv()
    for c in local:
        c.wait()
    links.finish()


def reduce(arrays, routes, others, ident):
    outs = [jax.ShapeDtypeStruct(x.shape[1:], F32) for x in arrays]
    outs += [jax.ShapeDtypeStruct(x.shape, x.dtype) for x, _ in others]
    scratch = []
    for x, route in zip(arrays, routes):
        scratch += reduce_buffers(x.shape[1:], x.dtype, route)
    sizes = sizes_of(routes[0])
    copies = len(arrays) * (sum(sizes) - len(sizes))
    copies += sum(math.prod(sizes_of(axes)) - 1 for _, axes in others)
    scratch += [
        pltpu.SemaphoreType.DMA((max(len(others), 1),)),
        pltpu.SemaphoreType.DMA((copies,)),
        pltpu.SemaphoreType.DMA((copies,)),
    ]
    vmem, hbm = pl.BlockSpec(memory_space=pltpu.VMEM), pl.BlockSpec(memory_space=pl.ANY)
    specs = [vmem] * len(arrays) + [hbm] * len(others)
    return pl.pallas_call(
        functools.partial(reduce_kernel, tuple(routes), tuple(axes for _, axes in others)),
        out_shape=outs,
        in_specs=specs,
        out_specs=specs,
        scratch_shapes=scratch,
        compiler_params=pltpu.CompilerParams(
            collective_id=ident, has_side_effects=True, vmem_limit_bytes=VMEM_LIMIT
        ),
    )(*arrays, *[x for x, _ in others])


def sum_everywhere(links, value, mine, slots):
    mine[...] = value
    moves = links.moves(ALL)
    waits = [links.send(mine, slots.at[n], move) for n, move in enumerate(moves)]
    for c in waits:
        c.wait_recv()
    return value + jnp.sum(slots[...], 0)


def all_sum_kernel(value, out, mine, slots, send_sem, recv_sem):
    links = Links(send_sem, recv_sem)
    links.greet(ALL, True)
    out[...] = sum_everywhere(links, value[...], mine, slots)
    links.finish()


def summed_call(body, arrays, ident):
    vmem = pl.BlockSpec(memory_space=pltpu.VMEM)
    copies = math.prod(sizes_of(ALL)) - 1
    return pl.pallas_call(
        body,
        out_shape=jax.ShapeDtypeStruct((8, LANES), F32),
        in_specs=[vmem] * len(arrays),
        out_specs=vmem,
        scratch_shapes=[
            pltpu.VMEM((8, LANES), F32),
            pltpu.VMEM((copies, 8, LANES), F32),
            pltpu.SemaphoreType.DMA((copies,)),
            pltpu.SemaphoreType.DMA((copies,)),
        ],
        compiler_params=pltpu.CompilerParams(
            collective_id=ident, has_side_effects=True, vmem_limit_bytes=VMEM_LIMIT
        ),
    )(*arrays)


def local_call(body, outs, arrays, scratch=(), **kw):
    return pl.pallas_call(
        body,
        out_shape=outs,
        scratch_shapes=list(scratch),
        compiler_params=pltpu.CompilerParams(vmem_limit_bytes=VMEM_LIMIT),
        **kw,
    )(*arrays)


def table_kernel(table, gains, w, cols_ref, scale_ref, center_ref, center_gain_ref, center):
    rows, width = table.shape
    gain = gains[0:1]
    for i in range(0, rows, 64):
        part = table[i : i + 64].astype(F32)
        part = part - jnp.mean(part, 1, keepdims=True)
        center[i : i + 64] = part
        center_ref[i : i + 64] = part.astype(BF)
        center_gain_ref[i : i + 64] = (part * gain).astype(BF)
    cols_ref[...] = dot(center_gain_ref[...], w[...]).T.astype(BF)
    first = FIRST_PLACE - 1
    places = center[first:rows]
    gram = dot(places, center[...], 1, 1, HIGH)
    own = jnp.sum(places * places, 1, keepdims=True)
    every = center[...]
    every = dot(jnp.ones((8, width), F32), every * every, 1, 1, HIGH)[0:1]
    scale = lax.rsqrt((2.0 * gram + own + every) / width + 1e-05)
    lane = lax.broadcasted_iota(jnp.int32, scale.shape, 1)
    scale = jnp.where(lane < FIRST_PLACE, scale, 0.0)
    high = scale.astype(BF)
    scale_ref[0 : rows - first] = high
    scale_ref[rows - first :] = (scale - high.astype(F32)).astype(BF)


def fill_hot(hot, code, place):
    rows, length = hot.shape
    for i in range(0, rows, 64):
        index = lax.broadcasted_iota(jnp.int32, (64, length), 0) + i
        hit = (index == code) | (index == place + FIRST_PLACE)
        hot[i : i + 64] = jnp.where(hit, 1.0, 0.0).astype(BF)


def attend_kernel(heads, rows, cols, table, scales, att, q_ref, kv_ref, prob_ref, scale_ref, hot, bias):
    wide = att.shape[1]
    dim = wide // heads
    code, pos, seg, place = (rows[0, i : i + 1] for i in range(4))
    fill_hot(hot, code, place)
    length = hot.shape[1]
    both = dot(scales[...], hot[...])
    half = both.shape[0] // 2
    both = both[:half] + both[half:]
    index = lax.broadcasted_iota(jnp.int32, both.shape, 0)
    scale = jnp.sum(jnp.where(index == place + 1, both, 0.0), 0, keepdims=True)
    scale_ref[0] = jnp.broadcast_to(scale, (8, length))
    q = dot(table[0:wide], hot[:, 0:LANES]) * scale[:, 0:LANES]
    q_low = q.astype(BF)
    q_ref[0] = q_low
    for i in (0, wide):
        part = dot(table[wide + i : 2 * wide + i], hot[...])
        kv_ref[0, i : i + wide] = (part * scale).astype(BF)
    seen = (pos <= cols[0, :, 0:1]) & (seg == cols[0, :, 1:2])
    bias[...] = jnp.where(seen, 0.0, -1e30)
    factor = dim**-0.5
    for h in range(heads):
        part = slice(h * dim, (h + 1) * dim)
        query = (q_low[part].astype(F32) * factor).T.astype(BF)
        scores = dot(query, kv_ref[0, part]) + bias[...]
        expo = jnp.exp(scores - jnp.max(scores, 1, keepdims=True))
        probs = (expo * (1.0 / jnp.sum(expo, 1, keepdims=True))).astype(BF)
        prob_ref[0, h] = probs
        value = kv_ref[0, wide + h * dim : wide + (h + 1) * dim]
        att[0, part] = dot(value, probs, 1, 1).astype(BF)


def attend_back_kernel(heads, width, rows, q_ref, kv_ref, prob_ref, scale_ref, datt, d_table, pairs, hot, grad, grad_q):
    wide = q_ref.shape[1]
    dim = wide // heads
    code, place = rows[0, 0:1], rows[0, 3:4]
    scale = scale_ref[0, 0:1]
    fill_hot(hot, code, place)
    length = hot.shape[1]
    factor = dim**-0.5
    kappa = jnp.zeros((1, length), F32)
    kappa_q = jnp.zeros((1, LANES), F32)
    for h in range(heads):
        part = slice(h * dim, (h + 1) * dim)
        part_v = slice(wide + h * dim, wide + (h + 1) * dim)
        key, value = kv_ref[0, part], kv_ref[0, part_v]
        query = q_ref[0, part]
        d_out = datt[part]
        d_rows = d_out.astype(F32).T.astype(BF)
        probs_low = prob_ref[0, h]
        probs = probs_low.astype(F32)
        d_prob = dot(d_rows, value)
        weighted = probs * d_prob
        d_score = (weighted - probs * jnp.sum(weighted, 1, keepdims=True)).astype(BF)
        dv = dot(d_out, probs_low)
        dk = dot(query, d_score) * factor
        dq = dot(key, d_score, 1, 1) * factor
        kappa += jnp.sum(dk * key.astype(F32) + dv * value.astype(F32), 0, keepdims=True)
        kappa_q += jnp.sum(dq * query.astype(F32), 0, keepdims=True)
        grad[part] = (dk * scale).astype(BF)
        grad[part_v] = (dv * scale).astype(BF)
        grad_q[part] = (dq * scale[:, 0:LANES]).astype(BF)

    @pl.when(pl.program_id(0) == 0)
    def _():
        d_table[...] = jnp.zeros_like(d_table)
        pairs[...] = jnp.zeros_like(pairs)

    d_table[0:wide] += dot(grad_q[...], hot[:, 0:LANES], 1, 1)
    d_table[wide:] += dot(grad[...], hot[...], 1, 1)
    kappa = jnp.concatenate([kappa[:, 0:LANES] + kappa_q, kappa[:, LANES:]], 1)
    weight = scale * scale * kappa * (1.0 / width)
    for i in range(0, hot.shape[0], 128):
        left = (hot[i : i + 128].astype(F32) * weight).astype(BF)
        pairs[i : i + 128] += dot(left, hot[...], 1, 1)


def attend(rows, cols, table, scales, heads):
    seqs, _, length = rows.shape
    wide = table.shape[0] // 3

    def spec(*shape):
        return pl.BlockSpec((1,) + shape, lambda s: (s,) + (0,) * len(shape))

    def whole(x):
        return pl.BlockSpec(x.shape, lambda s: (0,) * x.ndim)

    outs = [
        ((wide, LANES), BF),
        ((wide, LANES), BF),
        ((2 * wide, length), BF),
        ((heads, LANES, length), BF),
        ((8, length), F32),
    ]
    return local_call(
        functools.partial(attend_kernel, heads),
        [jax.ShapeDtypeStruct((seqs,) + s, t) for s, t in outs],
        (rows, cols, table, scales),
        [pltpu.VMEM((TABLE, length), BF), pltpu.VMEM((LANES, length), F32)],
        grid=(seqs,),
        in_specs=[spec(8, length), spec(LANES, LANES), whole(table), whole(scales)],
        out_specs=[spec(*s) for s, _ in outs],
    )


def attend_back(rows, q, kv, probs, scale, datt, width):
    seqs, _, length = rows.shape
    heads, wide = probs.shape[1], q.shape[1]

    def spec(x):
        return pl.BlockSpec((1,) + x.shape[1:], lambda s: (s,) + (0,) * (x.ndim - 1))

    outs = [(3 * wide, TABLE), (TABLE, TABLE)]
    return local_call(
        functools.partial(attend_back_kernel, heads, width),
        [jax.ShapeDtypeStruct(s, F32) for s in outs],
        (rows, q, kv, probs, scale, datt),
        [
            pltpu.VMEM((TABLE, length), BF),
            pltpu.VMEM((2 * wide, length), BF),
            pltpu.VMEM((wide, LANES), BF),
        ],
        grid=(seqs,),
        in_specs=[spec(x) for x in (rows, q, kv, probs, scale)]
        + [pl.BlockSpec((wide, LANES), lambda s: (0, s))],
        out_specs=[pl.BlockSpec(s, lambda i: (0, 0)) for s in outs],
    )


def over_rows(ref, body, start):
    rows = ref.shape[0]
    if rows % 8:
        return body(slice(0, rows), start)

    def step(i, carry):
        return body(pl.ds(pl.multiple_of(i * 8, 8), 8), carry)

    return lax.fori_loop(0, rows // 8, step, start)


def lane_sums(values, offset):
    lane = lax.broadcasted_iota(jnp.int32, (8, LANES), 1)
    block = jnp.zeros((8, LANES), F32)
    for i, v in enumerate(values):
        block = jnp.where(lane == i + offset, v, block)
    return block


def sum_squares(ref):
    rows, cols = ref.shape
    height = 8 if rows % 8 == 0 else rows

    def add(part, acc):
        v = ref[part, :]
        return acc + v * v

    return over_rows(ref, add, jnp.zeros((height, cols), F32))


def group_sums(refs):
    sums = [jnp.sum(sum_squares(r)) for r in refs[:6]]
    square = refs[6][...] * refs[6][...]
    return sums + [jnp.sum(square[i : i + 1]) for i in range(3)]


def squares_kernel(*refs):
    grads, masters = refs[:7], refs[7:14]
    losses, out, mine, slots, send_sem, recv_sem = refs[14:]
    links = Links(send_sem, recv_sem)
    block = lane_sums(group_sums(grads), 0) + lane_sums(group_sums(masters), 9)
    links.greet(ALL, True)
    out[...] = sum_everywhere(links, block + losses[...], mine, slots)
    links.finish()


def at_first(body):
    pl.when(pl.program_id(0) == 0)(body)


def moments_kernel(*refs):
    sums = refs[0]
    grads, masters, firsts, seconds = (refs[1 + 7 * i : 8 + 7 * i] for i in range(4))
    means, squares, updates = (refs[29 + 7 * i : 36 + 7 * i] for i in range(3))
    out = refs[50]
    total = sums[...]
    lane = lax.broadcasted_iota(jnp.int32, (8, LANES), 1)
    norm = jnp.sqrt(jnp.sum(jnp.where(lane < 9, total, 0.0)[0:1], 1, keepdims=True))
    factor = jnp.minimum(1.0, 0.05 / norm)

    def one(i):
        def step(part, acc):
            g = factor * grads[i][part, :]
            mean = 0.9 * firsts[i][part, :] + 0.1 * g
            square = 0.99 * seconds[i][part, :] + 0.01 * g * g
            update = (mean / (1.0 - 0.9**STEP)) / (
                jnp.sqrt(square / (1.0 - 0.99**STEP)) + 1e-08
            ) + 0.01 * masters[i][part, :]
            means[i][part, :] = mean
            squares[i][part, :] = square
            updates[i][part, :] = update
            return acc + update * update

        rows, cols = grads[i].shape
        height = 8 if rows % 8 == 0 else rows
        return over_rows(grads[i], step, jnp.zeros((height, cols), F32))

    @at_first
    def _():
        table, gains = one(0), one(6)
        values = [jnp.sum(table)] + [0.0] * 5 + [jnp.sum(gains[j : j + 1]) for j in range(3)]
        out[...] = lane_sums(values, 0)

    out[...] += lane_sums([jnp.sum(one(i)) for i in range(1, 6)], 1)


def weights_kernel(*refs):
    update_sums, sums = refs[:2]
    masters, updates = refs[2:9], refs[9:16]
    news, copies = refs[16:23], refs[23:29]
    norms_ref = refs[29]
    update_norm = jnp.sqrt(update_sums[0:1, 0:9])
    weight_norm = jnp.sqrt(sums[0:1, 9:18])
    ratio = weight_norm / update_norm

    def one(i):
        def step(part, acc):
            new = masters[i][part, :] - 0.3 * ratio[0:1, i : i + 1] * updates[i][part, :]
            news[i][part, :] = new
            copies[i][part, :] = new.astype(BF)
            return 0

        over_rows(masters[i], step, 0)

    @at_first
    def _():
        norms_ref[0:1, 0:9] = weight_norm
        norms_ref[1:2, 0:9] = update_norm
        one(0)
        for j in range(3):
            row = slice(j, j + 1)
            news[6][row] = masters[6][row] - 0.3 * ratio[0:1, 6 + j : 7 + j] * updates[6][row]

    for i in range(1, 6):
        one(i)


def by_rows(body, heads, groups, outs, tails):
    shapes = [x.shape for x in groups[0]]
    parts = 5 if all(shapes[i][0] % 80 == 0 or shapes[i][0] == 40 for i in range(1, 6)) else 1

    def spec(i, shape):
        if i in (0, 6):
            return pl.BlockSpec(shape, lambda n: (0, 0))
        return pl.BlockSpec((shape[0] // parts, shape[1]), lambda n: (n, 0))

    def whole(x):
        return pl.BlockSpec(x.shape, lambda n: (0,) * len(x.shape))

    in_specs = [whole(x) for x in heads]
    in_specs += [spec(i, s) for _ in groups for i, s in enumerate(shapes)]
    out_specs = [spec(i, x.shape) for group in outs for i, x in enumerate(group)]
    out_specs += [whole(x) for x in tails]
    return local_call(
        body,
        [x for group in outs for x in group] + tails,
        list(heads) + [x for group in groups for x in group],
        grid=(parts,),
        in_specs=in_specs,
        out_specs=out_specs,
    )


def layer_norm(v, gain):
    center = v - jnp.mean(v, -1, keepdims=True)
    return center * lax.rsqrt(jnp.mean(center * center, -1, keepdims=True) + 1e-05) * gain


def gradients(obs_tokens, returns, actions, rewards, game_ids, segments, masters):
    table, w_qkv, w_proj, w_up, w_down, w_head, gains = masters
    na, nk = lax.axis_size("ba"), 4
    nb, members = na * 4, 2 * nk
    total = nb * nk
    bl = lax.axis_index("bl")
    k = lax.axis_index("kh") * 2 + lax.axis_index("kl")
    g = bl * nk + k
    seqs, steps_here = obs_tokens.shape[:2]
    width = table.shape[1]
    rows, table_rows = w_qkv.shape[0], table.shape[0]
    steps = steps_here * nk
    heads = HEADS // nk
    wide = width // nk
    cols = 3 * wide // nb
    ff_rows = w_down.shape[0]
    padded_rows = up_to(rows, 16)
    padded_table = up_to(table_rows, 16)
    half = width // 2

    info = [obs_tokens] + [v[..., None] for v in (returns, actions, rewards, game_ids, segments)]
    info = jnp.concatenate(info, -1).reshape(seqs * steps_here, -1)
    info = pad_to(info, up_to(seqs * steps_here, 8), LANES)
    counts_here = jnp.sum((game_ids[..., None] == jnp.arange(GAMES)).astype(F32), (0, 1))
    table_bf = pad_to(table.astype(BF), padded_table, width)
    small = jnp.concatenate(
        [
            pad_to(w_head.astype(BF), rows, 256),
            pad_to(gains.astype(BF), 3, 256),
            pad_to(counts_here.astype(BF)[None], 1, 256),
            jnp.zeros((padded_rows - rows - 4, 256), BF),
        ]
    )
    qkv_blocks = w_qkv.astype(BF).reshape(rows, 3, nk, wide).transpose(2, 0, 1, 3)
    qkv_blocks = qkv_blocks.reshape(nk, rows, nb, cols).transpose(2, 0, 1, 3)
    qkv_blocks = pad_to(qkv_blocks.reshape(total, rows, cols), padded_rows, LANES)
    ff_cols = na * 2 * ff_rows
    up_blocks = w_up.astype(BF).reshape(rows, na, 2, 2, nk, ff_rows).transpose(2, 4, 0, 1, 3, 5)
    up_blocks = pad_to(up_blocks.reshape(members, rows, ff_cols), padded_rows, ff_cols)
    one_way = ("ba", "bl", "bc", "kh", "kl")
    other_way = ("ba", "bl", "kh", "bc", "kl")
    table_left, table_right, small_all, qkv_mine, info_here, up_mine = exchange(
        (
            (table_bf[:, :half], "gather", one_way),
            (table_bf[:, half:], "gather", other_way),
            (small, "gather", other_way),
            (qkv_blocks, "scatter", ALL),
            (info, "direct", BLK),
            (up_blocks, "scatter", GROUP),
        ),
        0,
    )
    to_heads = [(i, i % nb * nk + i // nb) for i in range(total)]
    proj_here = lax.ppermute(w_proj.astype(BF), ALL, to_heads)
    proj_here = lax.all_gather(proj_here, BATCH, axis=0, tiled=True)
    down_full = lax.all_gather(w_down.astype(BF), COPIES, axis=0, tiled=True)
    up_full = lax.all_gather(up_mine[:, :rows], COPIES, axis=0, tiled=False)
    up_full = up_full.reshape(na, 2, 2, nk, rows, ff_cols).transpose(0, 2, 1, 3, 4, 5)
    up_full = up_full.reshape(width, ff_cols)

    table_all = jnp.concatenate(
        [
            natural(table_left, ALL, one_way)[:, :table_rows],
            natural(table_right, ALL, other_way)[:, :table_rows],
        ],
        2,
    ).reshape(TABLE, width)
    small_all = natural(small_all, ALL, other_way)
    gain = small_all[:, rows : rows + 3, :rows].transpose(1, 0, 2).reshape(3, width).astype(F32)
    w_mine = qkv_mine[:, :rows].reshape(width, LANES)
    scale_rows = TABLE - FIRST_PLACE + 1
    cols_mine, scale_table, center_bf, center_gain = local_call(
        table_kernel,
        [
            jax.ShapeDtypeStruct((LANES, TABLE), BF),
            jax.ShapeDtypeStruct((2 * scale_rows, TABLE), BF),
            jax.ShapeDtypeStruct((TABLE, width), BF),
            jax.ShapeDtypeStruct((TABLE, width), BF),
        ],
        (table_all, pad_to(gain, 8, width), w_mine),
        [pltpu.VMEM((TABLE, width), F32)],
    )
    upper, lower = exchange(
        (
            (cols_mine[: LANES // 2], "gather", ("ba", "bl", "bc")),
            (cols_mine[LANES // 2 :], "gather", ("bc", "bl", "ba")),
        ),
        1,
    )
    qkv_table = jnp.concatenate(
        [natural(upper, BATCH, ("ba", "bl", "bc")), natural(lower, BATCH, ("bc", "bl", "ba"))], 1
    )
    qkv_table = qkv_table[:, :cols].reshape(3 * wide, TABLE)

    info_here = info_here[:, : seqs * steps_here].reshape(nk, seqs, steps_here, LANES)
    info_here = info_here.transpose(1, 0, 2, 3).reshape(seqs, steps, LANES)
    length = up_to(TSTEP * steps, LANES)
    place_of = np.repeat(np.array(PLACES), steps)
    time_of = np.tile(np.arange(steps), TSTEP)
    tail = length - TSTEP * steps
    pos = np.pad(time_of * TSTEP + place_of, (0, tail), constant_values=1 << 20)
    place_of = np.pad(place_of, (0, tail), constant_values=-1000)
    starts = np.array([0] * OBS + [PATCH, PATCH + RET_BINS, PATCH + RET_BINS + ACTIONS])
    codes = info_here[..., :TSTEP] + starts.astype(np.int32)
    codes = jnp.concatenate(
        [codes[..., OBS - 1 : OBS + 2], codes[..., : OBS - 1], codes[..., OBS + 2 :]], -1
    )
    codes = codes.transpose(0, 2, 1).reshape(seqs, TSTEP * steps)
    codes = jnp.pad(codes, ((0, 0), (0, tail)), constant_values=-1)
    seg = jnp.tile(info_here[..., OBS + 4], (1, TSTEP))
    seg = jnp.pad(seg, ((0, 0), (0, tail)), constant_values=-1)
    zero = jnp.zeros((seqs, length), jnp.int32)
    token_rows = jnp.stack(
        [codes, zero + jnp.asarray(pos, jnp.int32), seg, zero + jnp.asarray(place_of, jnp.int32)]
        + [zero] * 4,
        1,
    )
    token_cols = jnp.stack([zero[:, :LANES] + pos[:LANES].astype(np.int32), seg[:, :LANES]], -1)
    token_cols = jnp.pad(token_cols, ((0, 0), (0, 0), (0, LANES - 2)))
    att, q, kv, probs, scale = attend(token_rows, token_cols, qkv_table, scale_table, heads)

    own = seqs * LANES // nk

    def halves(x, axes, routes):
        x = x.astype(BF).reshape(-1, own, width)
        return [
            for_route(part, axes, route)
            for part, route in zip((x[..., :half], x[..., half:]), routes)
        ]

    def summed(x, axes, routes, ident):
        return jnp.concatenate(reduce(halves(x, axes, routes), routes, [], ident), 1)

    def spread(x, routes, ident):
        parts = zip((x[:, :half], x[:, half:]), ("gather",) * 2, routes)
        axes = tuple(a for a in ALL if a in routes[0])
        parts = exchange(tuple(parts), ident)
        parts = [natural(p, axes, r) for p, r in zip(parts, routes)]
        return jnp.concatenate(parts, 2).reshape(-1, width)

    blk_routes = (("kl", "kh"), ("kl", "kh"))
    sum_routes = (("kl", "kh", "bl"), ("kl", "bl", "kh"))
    spread_routes = (("bl", "kh", "kl"), ("kh", "bl", "kl"))
    att_proj = jnp.einsum("scq,cd->sqd", att, proj_here, preferred_element_type=F32)
    att_proj = summed(att_proj, BLK, blk_routes, 2)
    slots = lax.rem(k, nk // seqs) * own + jnp.arange(own)
    seq_own = k * own // LANES
    codes_own = lax.dynamic_slice(codes, (seq_own, lax.rem(k, nk // seqs) * own), (1, own))[0]
    place_own = jnp.asarray(place_of[:LANES], jnp.int32)
    place_own = lax.dynamic_slice(place_own, (lax.rem(k, nk // seqs) * own,), (own,))
    columns = jnp.arange(TABLE)
    own_hot = (codes_own[:, None] == columns) | (place_own[:, None] + FIRST_PLACE == columns)
    own_hot = own_hot.astype(BF)
    x2 = dot(own_hot, table_all) + att_proj
    low_own = layer_norm(x2, gain[1]).astype(BF)
    low = spread(low_own, spread_routes, 3)
    u = dot(low, up_full)
    hid_full, gelu_back = jax.vjp(lambda t: jax.nn.gelu(t, approximate=True), u)
    hid = hid_full.astype(BF)
    x3 = x2 + summed(dot(hid, down_full), GROUP, sum_routes, 4)
    c_full, norm_last = jax.vjp(layer_norm, x3, gain[2])
    c = c_full.astype(BF)
    head_full = small_all[:, :rows].reshape(width, 256)
    logits = dot(c, head_full)
    kind = slots // steps
    info_seq = lax.dynamic_index_in_dim(info_here, seq_own, 0, False)
    info_own = jnp.take(info_seq, lax.rem(slots, steps), axis=0)
    counts = jnp.sum(small_all[:, rows + 3, :GAMES].astype(F32), 0)
    per_game = 1.0 / (GAMES * jnp.maximum(counts, 1.0))
    game_own = (info_own[:, OBS + 3, None] == jnp.arange(GAMES)).astype(F32)
    weight = jnp.where(kind < PICKS, jnp.sum(game_own * per_game, -1), 0.0)
    lane = jnp.arange(256)
    low_end = jnp.where(kind == 0, 0, jnp.where(kind == 1, RET_BINS, RET_BINS + ACTIONS))
    high_end = jnp.where(kind == 0, RET_BINS, jnp.where(kind == 1, RET_BINS + ACTIONS, HEAD_COLS))
    target = low_end + jnp.where(
        kind == 0,
        info_own[:, OBS],
        jnp.where(kind == 1, info_own[:, OBS + 1], info_own[:, OBS + 2]),
    )
    mine = (lane >= low_end[:, None]) & (lane < high_end[:, None])
    masked = jnp.where(mine, logits, -1e30)
    top = jnp.max(masked, -1, keepdims=True)
    expo = jnp.exp(masked - top)
    expo_sum = jnp.sum(expo, -1, keepdims=True)
    hit = lane == target[:, None]
    picked = jnp.sum(jnp.where(hit, logits, 0.0), -1)
    row_loss = (jnp.log(expo_sum[:, 0]) + top[:, 0] - picked) * weight
    losses = [jnp.sum(jnp.where(kind == j, row_loss, 0.0)) for j in range(PICKS)]
    dlogits = (weight[:, None] * (expo / expo_sum - hit)).astype(BF)
    d_head = dot(c, dlogits, 0, 0)
    dx3, d_gain_last = norm_last(dot(dlogits, head_full, 1, 1))
    dz = spread(dx3.astype(BF), spread_routes, 5)
    d_down = dot(hid, dz, 0, 0)
    sum_down = lax.psum_scatter(d_down.astype(BF), COPIES, scatter_dimension=0, tiled=True)
    du = gelu_back(dot(dz, down_full, 1, 1))[0].astype(BF)
    d_up = dot(low, du, 0, 0).astype(BF)
    d_up = d_up.reshape(na, 2, 2, nk, rows, ff_cols).transpose(0, 2, 1, 3, 4, 5)
    d_up = d_up.reshape(width, ff_cols)
    sum_up = lax.psum_scatter(d_up, COPIES, scatter_dimension=0, tiled=True)
    d_low = summed(dot(du, up_full, 1, 1), GROUP, sum_routes, 6)
    dx2_norm, d_gain_mid = jax.vjp(layer_norm, x2, gain[1])[1](d_low)
    dx2 = dx3 + dx2_norm
    dy_own = dx2.astype(BF)
    dy = spread(dy_own, (("kh", "kl"), ("kh", "kl")), 7).reshape(seqs, LANES, width)
    d_proj = jnp.einsum("scq,sqd->cd", att, dy, preferred_element_type=F32).astype(BF)
    sum_proj = lax.psum_scatter(d_proj, BATCH, scatter_dimension=0, tiled=True)
    sum_proj = lax.ppermute(sum_proj, ALL, [(j, i) for i, j in to_heads])

    datt = dot(proj_here, dy.reshape(-1, width), 1, 1).astype(BF)
    d_table, pairs = attend_back(token_rows, q, kv, probs, scale, datt, width)
    d_table = pad_to(d_table.astype(BF).reshape(nb, cols, TABLE), LANES, TABLE)
    table_routes = (("bc", "bl", "ba"), ("bl", "bc", "ba"))
    d_table_mine = reduce(
        [
            for_route(part, BATCH, route)
            for part, route in zip((d_table[..., : TABLE // 2], d_table[..., TABLE // 2 :]), table_routes)
        ],
        table_routes,
        [],
        8,
    )
    d_table_mine = jnp.concatenate(d_table_mine, 1).astype(BF)
    d_w = dot(center_gain, d_table_mine, 0, 1)
    d_norm = dot(d_table_mine, w_mine, 0, 1)
    d_gain_first = jnp.sum(center_bf.astype(F32) * d_norm, 0)
    d_scaled = d_norm * gain[0]
    d_embed = (
        d_scaled
        - jnp.mean(d_scaled, 1, keepdims=True)
        - dot(pairs.astype(BF), center_bf)
        + dot(own_hot, dy_own, 0, 0)
    )
    d_gains = jnp.stack([d_gain_first, d_gain_mid, d_gain_last]).astype(BF)
    d_misc = jnp.concatenate(
        [
            d_head.astype(BF).reshape(total, rows, 256),
            pad_to(d_gains.reshape(3, total, rows).transpose(1, 0, 2), 3, 256),
            jnp.zeros((total, padded_rows - rows - 3, 256), BF),
        ],
        1,
    )
    d_w = pad_to(d_w.astype(BF).reshape(total, rows, LANES), padded_rows, LANES)
    d_embed = pad_to(d_embed.astype(BF).reshape(total, table_rows, width), padded_table, width)
    sum_up = pad_to(sum_up.reshape(members, rows, -1), padded_rows, ff_cols)
    one_way = ("kl", "kh", "bc", "bl", "ba")
    other_way = ("kl", "bc", "kh", "bl", "ba")
    d_left, d_right, d_misc, d_ws, ups = reduce(
        [
            for_route(d_embed[..., :half], ALL, one_way),
            for_route(d_embed[..., half:], ALL, other_way),
            for_route(d_misc, ALL, other_way),
        ],
        (one_way, other_way, other_way),
        [(d_w, ALL), (sum_up, GROUP)],
        9,
    )
    d_embed = jnp.concatenate([d_left, d_right], 1)
    d_ws = d_ws[:, :rows, :cols].reshape(nb, nk, rows, cols).transpose(2, 1, 0, 3)
    d_ws = d_ws.reshape(rows, nk, 3, wide).transpose(0, 2, 1, 3).reshape(rows, 3 * width)
    ups = ups[:, :rows].reshape(2, nk, rows, na, 2, ff_rows).transpose(2, 3, 0, 4, 1, 5)
    ups = ups.reshape(rows, nb * nk * ff_rows)
    grads = (
        d_embed[:table_rows],
        d_ws.astype(F32),
        sum_proj.astype(F32),
        ups.astype(F32),
        sum_down.astype(F32),
        d_misc[:rows, :HEAD_COLS],
        d_misc[rows : rows + 3, :rows],
    )
    return grads, losses


def shards(*args):
    masters, firsts, seconds = args[6:13], args[13:20], args[20:27]
    grads, losses = gradients(*args[:6], masters)
    like = [jax.ShapeDtypeStruct(w.shape, F32) for w in masters]
    low = [jax.ShapeDtypeStruct(w.shape, BF) for w in masters[:6]]
    tile = jax.ShapeDtypeStruct((8, LANES), F32)
    loss_tile = jnp.zeros((8, LANES), F32).at[:, 18:21].set(jnp.stack(losses))
    sums = summed_call(squares_kernel, grads + masters + (loss_tile,), 10)
    result = by_rows(
        moments_kernel, (sums,), (grads, masters, firsts, seconds), [like] * 3, [tile]
    )
    means, squares, updates = result[:7], result[7:14], result[14:21]
    update_sums = summed_call(all_sum_kernel, (result[21],), 11)
    result = by_rows(
        weights_kernel, (update_sums, sums), (masters, updates), [like, low], [tile]
    )
    news, copies, norms = result[:7], result[7:13], result[13][:2, :9]
    grad_norm = jnp.sqrt(jnp.sum(sums[0, :9]))
    return tuple(news) + tuple(means) + tuple(squares) + tuple(copies) + (
        grad_norm,
        sums[0, 18:21],
        norms,
    )


def solution(mesh):
    nb, nk = mesh.shape["batch"], mesh.shape["blk"]
    split = Mesh(mesh.devices.reshape(nb // 4, 2, 2, nk // 2, 2), ALL)
    rows, gains = P(ALL, None), P(None, ALL)
    weights = (rows,) * 6 + (gains,)
    in_specs = (P(BATCH, BLK, None),) + (P(BATCH, BLK),) * 5 + weights * 3
    out_specs = weights * 3 + (rows,) * 6 + (P(), P(), P())
    return jax.shard_map(
        shards, mesh=split, in_specs=in_specs, out_specs=out_specs, check_vma=False
    )
```

```python
import functools
import math

import jax
import jax.numpy as jnp
import numpy as np
from jax import lax
from jax.experimental import pallas as pl
from jax.experimental.pallas import tpu as pltpu
from jax.sharding import Mesh
from jax.sharding import PartitionSpec as P

HEADS = 20
RET_BINS = 120
ACTIONS = 18
GAMES = 41
TSTEP = 39
OBS = 36
PATCH = 331
STEP = 10
HEAD_COLS = 142
TABLE = 512
PICKS = 3
LANES = 128
FIRST_PLACE = PATCH + HEAD_COLS
BF = jnp.bfloat16
F32 = jnp.float32
HIGH = lax.Precision.HIGHEST
BLK = ("kh", "kl")
GROUP = ("bl", "kh", "kl")
BATCH = ("ba", "bl", "bc")
COPIES = ("ba", "bc")
ALL = ("ba", "bl", "bc", "kh", "kl")
VMEM_LIMIT = 56 * 2**20
PLACES = list(range(OBS - 1, OBS + 2)) + [p for p in range(TSTEP) if not OBS - 1 <= p < OBS + 2]


def up_to(n, m):
    return -(-n // m) * m


def pad_to(x, rows, cols):
    if x.shape[-2:] == (rows, cols):
        return x
    widths = [(0, 0)] * (x.ndim - 2) + [(0, rows - x.shape[-2]), (0, cols - x.shape[-1])]
    return jnp.pad(x, widths)


def dot(left, right, ca=1, cb=0, precision=None):
    return lax.dot_general(
        left,
        right,
        (((ca,), (cb,)), ((), ())),
        precision=precision,
        preferred_element_type=F32,
    )


class Links:
    def __init__(self, sends, recvs):
        self.sends, self.recvs, self.open = sends, recvs, []
        self.size = {a: lax.axis_size(a) for a in ALL}
        self.here = {a: lax.axis_index(a) for a in ALL}

    def at(self, axis, step):
        return lax.rem(self.here[axis] + step, self.size[axis])

    def number(self, axes, steps):
        n = 0
        for a in axes:
            n = n * self.size[a] + self.at(a, steps.get(a, 0))
        return n

    def moves(self, axes):
        result = [{}]
        for a in axes:
            result = [dict(m, **{a: r}) for m in result for r in range(self.size[a])]
        return [{a: r for a, r in m.items() if r} for m in result if any(m.values())]

    def greet(self, axes, everyone=False):
        barrier = pltpu.get_barrier_semaphore()
        if everyone:
            moves = self.moves(axes)
        else:
            moves = [{a: r} for a in axes for r in range(1, self.size[a])]
        for move in moves:
            pl.semaphore_signal(
                barrier,
                inc=1,
                device_id={a: self.at(a, r) for a, r in move.items()},
                device_id_type=pl.DeviceIdType.MESH,
            )
        pl.semaphore_wait(barrier, len(moves))

    def send(self, src, dst, move):
        n = len(self.open)
        c = pltpu.make_async_remote_copy(
            src_ref=src,
            dst_ref=dst,
            send_sem=self.sends.at[n],
            recv_sem=self.recvs.at[n],
            device_id={a: self.at(a, r) for a, r in move.items()},
            device_id_type=pl.DeviceIdType.MESH,
        )
        c.start()
        self.open.append(c)
        return c

    def finish(self):
        for c in self.open:
            c.wait_send()


class Gather:
    def __init__(self, links, src, dst, route, local):
        self.links, self.src, self.dst = links, src, dst
        self.route, self.local, self.waits, self.stage = list(route), local, [], 0

    def step(self):
        links = self.links
        for c in self.waits:
            c.wait_recv()
        self.waits = []
        if self.stage == len(self.route):
            return False
        if self.stage == 1 and self.local is not None:
            self.local.wait()
            self.local = None
        count = math.prod(links.size[a] for a in self.route[: self.stage])
        start = links.number(self.route[self.stage :][::-1], {}) * count
        here = self.dst.at[pl.ds(start, count)]
        block = self.src if self.stage == 0 else here
        there = self.dst.at[start] if self.stage == 0 else here
        axis = self.route[self.stage]
        for r in range(1, links.size[axis]):
            self.waits.append(links.send(block, there, {axis: r}))
        self.stage += 1
        return True

    def close(self):
        if self.local is not None:
            self.local.wait()


class Reduce:
    def __init__(self, links, src, out, route, arrived, totals):
        self.links, self.now, self.out = links, src, out
        self.route, self.arrived, self.totals = list(route), arrived, totals
        self.waits, self.stage = [], 0

    def part(self, axis, step):
        count = self.now.shape[0] // self.links.size[axis]
        return pl.ds(self.links.at(axis, step) * count, count)

    def step(self):
        if self.stage:
            axis = self.route[self.stage - 1]
            for c in self.waits:
                c.wait_recv()
            total = self.now[self.part(axis, 0)].astype(F32)
            for n in range(len(self.waits)):
                total = total + self.arrived[self.stage - 1][n].astype(F32)
            if self.stage == len(self.route):
                self.out[...] = total[0]
                return False
            self.now = self.totals[self.stage - 1]
            self.now[...] = total.astype(self.now.dtype)
        axis = self.route[self.stage]
        self.waits = []
        for r in range(1, self.links.size[axis]):
            dst = self.arrived[self.stage].at[r - 1]
            self.waits.append(self.links.send(self.now.at[self.part(axis, r)], dst, {axis: r}))
        self.stage += 1
        return True


def start_scatters(links, jobs):
    copies = []
    for src, dst, axes, kind in jobs:
        me = links.number(axes, {})
        for move in links.moves(axes):
            block = src.at[links.number(axes, move)] if kind == "scatter" else src
            copies.append(links.send(block, dst.at[me], move))
    return copies


def run(jobs):
    jobs = list(jobs)
    while jobs:
        jobs = [j for j in jobs if j.step()]


def sizes_of(axes):
    return tuple(lax.axis_size(a) for a in axes)


def exchange_kernel(kinds, routes, *refs):
    count = len(kinds)
    srcs, dsts = refs[:count], refs[count : 2 * count]
    local_sem, send_sem, recv_sem = refs[2 * count :]
    links = Links(send_sem, recv_sem)
    local = []
    for i, route in enumerate(routes):
        me = links.number(route[::-1] if kinds[i] == "gather" else route, {})
        block = srcs[i].at[me] if kinds[i] == "scatter" else srcs[i]
        local.append(pltpu.make_async_copy(block, dsts[i].at[me], local_sem.at[i]))
        local[-1].start()
    everyone = any(k != "gather" for k in kinds)
    links.greet([a for a in ALL if any(a in x for x in routes)], everyone)
    gathers = [
        Gather(links, srcs[i], dsts[i], routes[i], local[i])
        for i in range(count)
        if kinds[i] == "gather"
    ]
    for j in gathers:
        j.step()
    copies = []
    for i in range(count):
        if kinds[i] != "gather":
            copies += start_scatters(links, [(srcs[i], dsts[i], routes[i], kinds[i])])
    run(gathers)
    for j in gathers:
        j.close()
    for c in copies:
        c.wait_recv()
    for i in range(count):
        if kinds[i] != "gather":
            local[i].wait()
    links.finish()


def natural(x, axes, route):
    back = route[::-1]
    x = x.reshape(sizes_of(back) + x.shape[1:])
    order = [back.index(a) for a in axes] + list(range(len(axes), x.ndim))
    return x.transpose(order).reshape((-1,) + x.shape[len(axes) :])


def for_route(x, axes, route):
    x = x.reshape(sizes_of(axes) + x.shape[1:])
    order = [axes.index(a) for a in route] + list(range(len(axes), x.ndim))
    return x.transpose(order).reshape((-1,) + x.shape[len(axes) :])


def exchange(items, ident):
    arrays, kinds, routes = zip(*items)
    shapes, copies = [], 0
    for x, kind, route in zip(arrays, kinds, routes):
        sizes = sizes_of(route)
        shape = x.shape if kind == "scatter" else (math.prod(sizes),) + x.shape
        shapes.append(jax.ShapeDtypeStruct(shape, x.dtype))
        copies += sum(sizes) - len(sizes) if kind == "gather" else math.prod(sizes) - 1
    n = len(arrays)
    return pl.pallas_call(
        functools.partial(exchange_kernel, kinds, routes),
        out_shape=shapes,
        in_specs=[pl.BlockSpec(memory_space=pl.ANY)] * n,
        out_specs=[pl.BlockSpec(memory_space=pl.ANY)] * n,
        scratch_shapes=[
            pltpu.SemaphoreType.DMA((n,)),
            pltpu.SemaphoreType.DMA((copies,)),
            pltpu.SemaphoreType.DMA((copies,)),
        ],
        compiler_params=pltpu.CompilerParams(collective_id=ident, has_side_effects=True),
    )(*arrays)


def reduce_buffers(shape, dtype, route):
    arrived, totals = [], []
    for i, axis in enumerate(route):
        rest = (math.prod(sizes_of(route[i + 1 :])),) + shape
        arrived.append(pltpu.VMEM((lax.axis_size(axis) - 1,) + rest, dtype))
        totals.append(pltpu.VMEM(rest, dtype))
    return arrived + totals[:-1]


def reduce_kernel(routes, other_axes, *refs):
    refs = list(refs)

    def take(n):
        got = refs[:n]
        del refs[:n]
        return got

    sums = len(routes)
    srcs, other_srcs = take(sums), take(len(other_axes))
    outs, other_dsts = take(sums), take(len(other_axes))
    buffers = [(take(len(r)), take(len(r) - 1)) for r in routes]
    local_sem, send_sem, recv_sem = refs
    links = Links(send_sem, recv_sem)
    local = []
    for i, axes in enumerate(other_axes):
        me = links.number(axes, {})
        local.append(
            pltpu.make_async_copy(other_srcs[i].at[me], other_dsts[i].at[me], local_sem.at[i])
        )
        local[-1].start()
    seen = [a for a in ALL if any(a in x for x in tuple(routes) + other_axes)]
    links.greet(seen, bool(other_axes))
    jobs = [
        Reduce(links, srcs[i], outs[i], routes[i], *buffers[i]) for i in range(sums)
    ]
    for j in jobs:
        j.step()
    copies = start_scatters(
        links, [(s, d, a, "scatter") for s, d, a in zip(other_srcs, other_dsts, other_axes)]
    )
    run(jobs)
    for c in copies:
        c.wait_recv()
    for c in local:
        c.wait()
    links.finish()


def reduce(arrays, routes, others, ident):
    outs = [jax.ShapeDtypeStruct(x.shape[1:], F32) for x in arrays]
    outs += [jax.ShapeDtypeStruct(x.shape, x.dtype) for x, _ in others]
    scratch = []
    for x, route in zip(arrays, routes):
        scratch += reduce_buffers(x.shape[1:], x.dtype, route)
    copies = sum(sum(sizes_of(r)) - len(r) for r in routes)
    copies += sum(math.prod(sizes_of(axes)) - 1 for _, axes in others)
    scratch += [
        pltpu.SemaphoreType.DMA((max(len(others), 1),)),
        pltpu.SemaphoreType.DMA((copies,)),
        pltpu.SemaphoreType.DMA((copies,)),
    ]
    vmem, hbm = pl.BlockSpec(memory_space=pltpu.VMEM), pl.BlockSpec(memory_space=pl.ANY)
    specs = [vmem] * len(arrays) + [hbm] * len(others)
    return pl.pallas_call(
        functools.partial(reduce_kernel, tuple(routes), tuple(axes for _, axes in others)),
        out_shape=outs,
        in_specs=specs,
        out_specs=specs,
        scratch_shapes=scratch,
        compiler_params=pltpu.CompilerParams(
            collective_id=ident, has_side_effects=True, vmem_limit_bytes=VMEM_LIMIT
        ),
    )(*arrays, *[x for x, _ in others])


def sum_everywhere(links, value, mine, slots):
    mine[...] = value
    moves = links.moves(ALL)
    waits = [links.send(mine, slots.at[n], move) for n, move in enumerate(moves)]
    for c in waits:
        c.wait_recv()
    return value + jnp.sum(slots[...], 0)


def all_sum_kernel(value, out, mine, slots, send_sem, recv_sem):
    links = Links(send_sem, recv_sem)
    links.greet(ALL, True)
    out[...] = sum_everywhere(links, value[...], mine, slots)
    links.finish()


def summed_call(body, arrays, ident):
    vmem = pl.BlockSpec(memory_space=pltpu.VMEM)
    copies = math.prod(sizes_of(ALL)) - 1
    return pl.pallas_call(
        body,
        out_shape=jax.ShapeDtypeStruct((8, LANES), F32),
        in_specs=[vmem] * len(arrays),
        out_specs=vmem,
        scratch_shapes=[
            pltpu.VMEM((8, LANES), F32),
            pltpu.VMEM((copies, 8, LANES), F32),
            pltpu.SemaphoreType.DMA((copies,)),
            pltpu.SemaphoreType.DMA((copies,)),
        ],
        compiler_params=pltpu.CompilerParams(
            collective_id=ident, has_side_effects=True, vmem_limit_bytes=VMEM_LIMIT
        ),
    )(*arrays)


def local_call(body, outs, arrays, scratch=(), **kw):
    return pl.pallas_call(
        body,
        out_shape=outs,
        scratch_shapes=list(scratch),
        compiler_params=pltpu.CompilerParams(vmem_limit_bytes=VMEM_LIMIT),
        **kw,
    )(*arrays)


def table_kernel(table, gains, w, cols_ref, scale_ref, center_ref, center_gain_ref, center):
    rows, width = table.shape
    gain = gains[0:1]
    for i in range(0, rows, 64):
        part = table[i : i + 64].astype(F32)
        part = part - jnp.mean(part, 1, keepdims=True)
        center[i : i + 64] = part
        center_ref[i : i + 64] = part.astype(BF)
        center_gain_ref[i : i + 64] = (part * gain).astype(BF)
    cols_ref[...] = dot(center_gain_ref[...], w[...]).T.astype(BF)
    first = FIRST_PLACE - 1
    places = center[first:rows]
    gram = dot(places, center[...], 1, 1, HIGH)
    own = jnp.sum(places * places, 1, keepdims=True)
    every = center[...]
    every = dot(jnp.ones((8, width), F32), every * every, 1, 1, HIGH)[0:1]
    scale = lax.rsqrt((2.0 * gram + own + every) / width + 1e-05)
    lane = lax.broadcasted_iota(jnp.int32, scale.shape, 1)
    scale = jnp.where(lane < FIRST_PLACE, scale, 0.0)
    high = scale.astype(BF)
    scale_ref[0 : rows - first] = high
    scale_ref[rows - first :] = (scale - high.astype(F32)).astype(BF)


def fill_hot(hot, code, place):
    rows, length = hot.shape
    for i in range(0, rows, 64):
        index = lax.broadcasted_iota(jnp.int32, (64, length), 0) + i
        hit = (index == code) | (index == place + FIRST_PLACE)
        hot[i : i + 64] = jnp.where(hit, 1.0, 0.0).astype(BF)


def attend_seq(s, heads, rows, cols, table, scales, keep):
    att, q_ref, kv_ref, prob_ref, scale_ref, hot, bias = keep
    wide = att.shape[1]
    dim = wide // heads
    code, pos, seg, place = (rows[s, i : i + 1] for i in range(4))
    fill_hot(hot, code, place)
    length = hot.shape[1]
    both = dot(scales[...], hot[...])
    half = both.shape[0] // 2
    both = both[:half] + both[half:]
    index = lax.broadcasted_iota(jnp.int32, both.shape, 0)
    scale = jnp.sum(jnp.where(index == place + 1, both, 0.0), 0, keepdims=True)
    scale_ref[s] = jnp.broadcast_to(scale, (8, length))
    q = dot(table[0:wide], hot[:, 0:LANES]) * scale[:, 0:LANES]
    q_low = q.astype(BF)
    q_ref[s] = q_low
    for i in (0, wide):
        part = dot(table[wide + i : 2 * wide + i], hot[...])
        kv_ref[s, i : i + wide] = (part * scale).astype(BF)
    seen = (pos <= cols[s, :, 0:1]) & (seg == cols[s, :, 1:2])
    bias[...] = jnp.where(seen, 0.0, -1e30)
    factor = dim**-0.5
    for h in range(heads):
        part = slice(h * dim, (h + 1) * dim)
        query = (q_low[part].astype(F32) * factor).T.astype(BF)
        scores = dot(query, kv_ref[s, part]) + bias[...]
        expo = jnp.exp(scores - jnp.max(scores, 1, keepdims=True))
        probs = (expo * (1.0 / jnp.sum(expo, 1, keepdims=True))).astype(BF)
        prob_ref[s, h] = probs
        value = kv_ref[s, wide + h * dim : wide + (h + 1) * dim]
        att[s, part] = dot(value, probs, 1, 1).astype(BF)


def attend_back_seq(s, heads, width, rows, keep, datt, d_table, pairs, grad, grad_q):
    att, q_ref, kv_ref, prob_ref, scale_ref, hot, bias = keep
    wide = att.shape[1]
    dim = wide // heads
    code, place = rows[s, 0:1], rows[s, 3:4]
    scale = scale_ref[s, 0:1]
    fill_hot(hot, code, place)
    length = hot.shape[1]
    factor = dim**-0.5
    kappa = jnp.zeros((1, length), F32)
    kappa_q = jnp.zeros((1, LANES), F32)
    for h in range(heads):
        part = slice(h * dim, (h + 1) * dim)
        part_v = slice(wide + h * dim, wide + (h + 1) * dim)
        key, value = kv_ref[s, part], kv_ref[s, part_v]
        query = q_ref[s, part]
        d_out = datt[s, part]
        d_rows = d_out.astype(F32).T.astype(BF)
        probs_low = prob_ref[s, h]
        probs = probs_low.astype(F32)
        d_prob = dot(d_rows, value)
        weighted = probs * d_prob
        d_score = (weighted - probs * jnp.sum(weighted, 1, keepdims=True)).astype(BF)
        dv = dot(d_out, probs_low)
        dk = dot(query, d_score) * factor
        dq = dot(key, d_score, 1, 1) * factor
        kappa += jnp.sum(dk * key.astype(F32) + dv * value.astype(F32), 0, keepdims=True)
        kappa_q += jnp.sum(dq * query.astype(F32), 0, keepdims=True)
        grad[part] = (dk * scale).astype(BF)
        grad[part_v] = (dv * scale).astype(BF)
        grad_q[part] = (dq * scale[:, 0:LANES]).astype(BF)
    d_table[0:wide] += dot(grad_q[...], hot[:, 0:LANES], 1, 1)
    d_table[wide:] += dot(grad[...], hot[...], 1, 1)
    kappa = jnp.concatenate([kappa[:, 0:LANES] + kappa_q, kappa[:, LANES:]], 1)
    weight = scale * scale * kappa * (1.0 / width)
    for i in range(0, hot.shape[0], 128):
        left = (hot[i : i + 128].astype(F32) * weight).astype(BF)
        pairs[i : i + 128] += dot(left, hot[...], 1, 1)


def norm_parts(v):
    center = v - jnp.mean(v, -1, keepdims=True)
    scale = lax.rsqrt(jnp.mean(center * center, -1, keepdims=True) + 1e-05)
    return center * scale, scale


def norm_back(unit, scale, gain, d_out):
    d_unit = d_out * gain
    inner = jnp.mean(d_unit * unit, -1, keepdims=True)
    d_in = scale * (d_unit - jnp.mean(d_unit, -1, keepdims=True) - unit * inner)
    return d_in, jnp.sum(d_out * unit, 0, keepdims=True)


GELU_SCALE = 0.7978845608028654
GELU_CUBE = 0.044715
HOP_ONE = ("bl", "kh", "kl")
HOP_TWO = ("kh", "bl", "kl")


def core_kernel(heads, parted, *refs):
    refs = list(refs)

    def take(n):
        got = refs[:n]
        del refs[:n]
        return got

    rows, cols, table_t, scales, table, gains, proj, head, own, up_own = take(10)
    down_a, down_b = take(2)
    d_table, pairs, up_out, down_out, proj_out, head_out, dy_out, small_out = take(8)
    att, q_ref, kv_ref, prob_ref, scale_ref, hot, bias = keep = take(7)
    up, down, u_ref, hid, low, wide_in = take(6)
    datt, grad, grad_q, d_up, d_down = take(5)
    up_got, up_sum, up_got2, down_got, down_sum = take(5)
    blk_src, blk_buffers = take(2), [take(3), take(3)]
    low_parts, z_src = take(2), take(2)
    z_buffers, low_buffers = [take(5), take(5)], [take(5), take(5)]
    dz_parts, d_src, dy_parts, results = take(2), take(2), take(1), take(2)
    local_sem, send_sem, recv_sem = refs
    links = Links(send_sem, recv_sem)
    size, here = links.size, links.here
    seqs, width = att.shape[0], table.shape[1]
    half, own_rows = width // 2, own.shape[0]
    wide = att.shape[1]
    blocks = width // (size["ba"] * 2 * size["bc"])
    ff_rows = u_ref.shape[1] // (size["ba"] * size["bc"])

    def up_at(ba, bl, bc):
        start = ((ba * 2 + bl) * size["bc"] + bc) * blocks
        return pl.ds(pl.multiple_of(start, 16), blocks)

    def down_at(ba, bc, part):
        start = (ba * size["bc"] + bc) * ff_rows + part * (ff_rows // 2)
        return pl.ds(pl.multiple_of(start, 8), ff_rows // 2)

    local = []

    def copy_here(src, dst):
        local.append(pltpu.make_async_copy(src, dst, local_sem.at[len(local)]))
        local[-1].start()

    up_first, late = [], []
    if parted:
        for bl in range(2):
            copy_here(up_own.at[bl], up.at[up_at(here["ba"], bl, here["bc"])])
        for part, ref in enumerate((down_a, down_b)):
            for n in range(size["ba"]):
                copy_here(ref.at[n], down.at[down_at(n, here["bc"], part)])
    else:
        up, down, d_up, d_down = up_own, down_a, up_out, down_out
    links.greet(ALL)
    if parted:
        for bl in range(2):
            for r in range(1, size["ba"]):
                place = up.at[up_at(here["ba"], bl, here["bc"])]
                up_first.append(links.send(up_own.at[bl], place, {"ba": r}))
        for part, ref in enumerate((down_a, down_b)):
            for n in range(size["ba"]):
                place = down.at[down_at(n, here["bc"], part)]
                late.append(links.send(ref.at[n], place, {"bc": 1}))

    def forward(s, carry):
        attend_seq(s, heads, rows, cols, table_t, scales, keep)
        return carry

    lax.fori_loop(0, seqs, forward, 0)
    for c in local:
        c.wait()
    for c in up_first:
        c.wait_recv()
    for n in range(size["ba"] if parted else 0):
        for bl in range(2):
            place = up.at[up_at(n, bl, here["bc"])]
            late.append(links.send(place, place, {"bc": 1}))

    def blk_index(k):
        return (k % 2) * 2 + k // 2

    for s in range(seqs):
        part = dot(att[s], proj[...], 0, 0).astype(BF)
        for j in range(LANES // own_rows):
            block = part[j * own_rows : (j + 1) * own_rows]
            at = blk_index(s * (LANES // own_rows) + j)
            blk_src[0][at], blk_src[1][at] = block[:, :half], block[:, half:]
    jobs = [
        Reduce(links, blk_src[i], results[i], ("kl", "kh"), blk_buffers[i][:2], blk_buffers[i][2:])
        for i in range(2)
    ]
    for j in jobs:
        j.step()
    columns = lax.broadcasted_iota(jnp.int32, (own_rows, table.shape[0]), 1)
    info = own[...]
    code, place = info[:, 5:6].astype(jnp.int32), info[:, 6:7].astype(jnp.int32)
    own_hot = jnp.where((columns == code) | (columns == place), 1.0, 0.0).astype(BF)
    x = dot(own_hot, table[...])
    run(jobs)
    x2 = x + jnp.concatenate([results[0][...], results[1][...]], 1)
    unit_mid, scale_mid = norm_parts(x2)
    low_own = (unit_mid * gains[1:2]).astype(BF)

    def start_spread(value, parts):
        gathers = []
        for i, route in enumerate((HOP_ONE, HOP_TWO)):
            me = links.number(route[::-1], {})
            parts[i][me] = value[:, i * half : (i + 1) * half]
            gathers.append(Gather(links, parts[i].at[me], parts[i], route, None))
        for j in gathers:
            j.step()
        return gathers

    def swapped(j):
        kl, kh, bl = j // 4, j // 2 % 2, j % 2
        return (kl * 2 + bl) * 2 + kh

    def end_spread(gathers, parts, whole):
        run(gathers)
        for j in range(8):
            span = slice(j * own_rows, (j + 1) * own_rows)
            whole[span, 0:half] = parts[0][j]
            whole[span, half:] = parts[1][swapped(j)]

    def start_sum(parts, buffers):
        routes = (HOP_ONE[::-1], HOP_TWO[::-1])
        jobs = [
            Reduce(links, parts[i], results[i], routes[i], buffers[i][:3], buffers[i][3:])
            for i in range(2)
        ]
        for j in jobs:
            j.step()
        return jobs

    end_spread(start_spread(low_own, low_parts), low_parts, low)
    for c in late:
        c.wait_recv()
    group = 8 * own_rows
    step = 2 * own_rows

    def hidden(i, carry):
        span = pl.ds(pl.multiple_of(i * step, step), step)
        u = dot(low[span, :], up[...])
        u_ref[span, :] = u
        t = jnp.tanh(GELU_SCALE * (u + GELU_CUBE * u * u * u))
        hid[span, :] = (0.5 * u * (1.0 + t)).astype(BF)
        return carry

    lax.fori_loop(0, group // step, hidden, 0)
    for i in range(group // step):
        part = dot(hid[i * step : (i + 1) * step], down[...]).astype(BF)
        for n in range(2):
            block = part[n * own_rows : (n + 1) * own_rows]
            j = 2 * i + n
            z_src[0][j], z_src[1][swapped(j)] = block[:, :half], block[:, half:]
    run(start_sum(z_src, z_buffers))
    x3 = x2 + jnp.concatenate([results[0][...], results[1][...]], 1)

    unit_last, scale_last = norm_parts(x3)
    c_low = (unit_last * gains[2:3]).astype(BF)
    logits = dot(c_low, head[...])
    lane = lax.broadcasted_iota(jnp.int32, logits.shape, 1).astype(F32)
    weight, kind = info[:, 3:4], info[:, 4:5]
    masked = jnp.where((lane >= info[:, 0:1]) & (lane < info[:, 1:2]), logits, -1e30)
    top = jnp.max(masked, 1, keepdims=True)
    expo = jnp.exp(masked - top)
    expo_sum = jnp.sum(expo, 1, keepdims=True)
    hit = jnp.where(lane == info[:, 2:3], 1.0, 0.0)
    picked = jnp.sum(hit * logits, 1, keepdims=True)
    row_loss = (jnp.log(expo_sum) + top - picked) * weight
    losses = [jnp.sum(jnp.where(kind == j, row_loss, 0.0)) for j in range(PICKS)]
    d_logits = (weight * (expo / expo_sum - hit)).astype(BF)
    dx3, gain_last = norm_back(unit_last, scale_last, gains[2:3], dot(d_logits, head[...], 1, 1))
    gathers = start_spread(dx3.astype(BF), dz_parts)
    head_out[...] = dot(c_low, d_logits, 0, 0).astype(BF)
    end_spread(gathers, dz_parts, wide_in)

    def hidden_back(i, carry):
        span = pl.ds(pl.multiple_of(i * step, step), step)
        d_hid = dot(wide_in[span, :], down[...], 1, 1)
        u = u_ref[span, :]
        t = jnp.tanh(GELU_SCALE * (u + GELU_CUBE * u * u * u))
        slope = GELU_SCALE * (1.0 + 3.0 * GELU_CUBE * u * u)
        u_ref[span, :] = d_hid * (0.5 * (1.0 + t) + 0.5 * u * (1.0 - t * t) * slope)
        return carry

    lax.fori_loop(0, group // step, hidden_back, 0)
    for i in range(group // step):
        du = u_ref[i * step : (i + 1) * step].astype(BF)
        part = dot(du, up[...], 1, 1).astype(BF)
        for n in range(2):
            block = part[n * own_rows : (n + 1) * own_rows]
            j = 2 * i + n
            d_src[0][j], d_src[1][swapped(j)] = block[:, :half], block[:, half:]
    jobs = start_sum(d_src, low_buffers)
    du = u_ref[...].astype(BF)
    for i in range(0, width, LANES):
        d_up[i : i + LANES] = dot(low[:, i : i + LANES], du, 0, 0).astype(BF)
    sent_up, sent_down = [], []
    for n in range(size["ba"] if parted else 0):
        for bl in range(2):
            part = d_up.at[up_at(n, bl, links.at("bc", 1))]
            sent_up.append(links.send(part, up_got.at[n, bl], {"bc": 1}))
    for i in range(0, hid.shape[1], LANES):
        d_down[i : i + LANES] = dot(hid[:, i : i + LANES], wide_in[...], 0, 0).astype(BF)
    for n in range(size["ba"] if parted else 0):
        for part in range(2):
            block = d_down.at[down_at(n, links.at("bc", 1), part)]
            sent_down.append(links.send(block, down_got.at[n, part], {"bc": 1}))
    run(jobs)
    d_low = jnp.concatenate([results[0][...], results[1][...]], 1)
    d_mid, gain_mid = norm_back(unit_mid, scale_mid, gains[1:2], d_low)
    dy = (dx3 + d_mid).astype(BF)
    dy_out[...] = dy
    small_out[...] = jnp.zeros_like(small_out)
    small_out[0:1] = gain_mid
    small_out[1:2] = gain_last
    lane = lax.broadcasted_iota(jnp.int32, (1, width), 1)
    for j in range(PICKS):
        small_out[2:3] += jnp.where(lane == j, losses[j], 0.0)
    me = links.number(("kl", "kh"), {})
    dy_parts[0][me] = dy
    run([Gather(links, dy_parts[0].at[me], dy_parts[0], ("kh", "kl"), None)])

    for c in sent_up:
        c.wait_recv()
    for n in range(size["ba"] if parted else 0):
        for bl in range(2):
            total = d_up[up_at(n, bl, here["bc"]), :].astype(F32) + up_got[n, bl].astype(F32)
            up_sum[n, bl] = total.astype(BF)
    sent_up = []
    for r in range(1, size["ba"] if parted else 1):
        part = up_sum.at[links.at("ba", r)]
        sent_up.append(links.send(part, up_got2.at[r - 1], {"ba": r}))
    for s in range(seqs):
        first = dy_parts[0][blk_index(2 * s)]
        second = dy_parts[0][blk_index(2 * s + 1)]
        d_rows = jnp.concatenate([first, second], 0)
        datt[s] = dot(proj[...], d_rows, 1, 1).astype(BF)
        part = dot(att[s], d_rows)
        if s:
            part = part + proj_out[...]
        proj_out[...] = part
    d_table[...] = jnp.zeros_like(d_table)
    pairs[...] = jnp.zeros_like(pairs)

    def backward(s, carry):
        attend_back_seq(s, heads, width, rows, keep, datt, d_table, pairs, grad, grad_q)
        return carry

    lax.fori_loop(0, seqs, backward, 0)
    for c in sent_down:
        c.wait_recv()
    for n in range(size["ba"] if parted else 0):
        for part in range(2):
            mine = d_down[down_at(n, here["bc"], part), :].astype(F32)
            span = slice(part * (ff_rows // 2), (part + 1) * (ff_rows // 2))
            down_out[n, span] = (mine + down_got[n, part].astype(F32)).astype(BF)
    if parted:
        total = up_sum[here["ba"]].astype(F32)
        for n, c in enumerate(sent_up):
            c.wait_recv()
            total = total + up_got2[n].astype(F32)
        up_out[...] = total.astype(BF)
    links.finish()


def core(rows, cols, table_t, scales, table, gains, proj, head, own, up_own, down_a, down_b, heads, ident):
    seqs, _, length = rows.shape
    wide, width = proj.shape
    na = lax.axis_size("ba")
    ff_cols, own_rows = up_own.shape[-1], own.shape[0]
    up_rows, ff_rows = width // (na * 4), ff_cols // (na * 2)
    parted = up_own.ndim == 3
    half, group = width // 2, 8 * own_rows
    outs = [
        ((3 * wide, TABLE), F32),
        ((TABLE, TABLE), F32),
        ((2, up_rows, ff_cols) if parted else (width, ff_cols), BF),
        ((na, ff_rows, width) if parted else (ff_cols, width), BF),
        ((wide, width), F32),
        ((width, 256), BF),
        ((own_rows, width), BF),
        ((8, width), F32),
    ]
    scratch = [
        ((seqs, wide, LANES), BF),
        ((seqs, wide, LANES), BF),
        ((seqs, 2 * wide, length), BF),
        ((seqs, heads, LANES, length), BF),
        ((seqs, 8, length), F32),
        ((TABLE, length), BF),
        ((LANES, length), F32),
        ((width, ff_cols), BF),
        ((ff_cols, width), BF),
        ((group, ff_cols), F32),
        ((group, ff_cols), BF),
        ((group, width), BF),
        ((group, width), BF),
        ((seqs, wide, LANES), BF),
        ((2 * wide, length), BF),
        ((wide, LANES), BF),
        ((width, ff_cols), BF),
        ((ff_cols, width), BF),
        ((na, 2, up_rows, ff_cols), BF),
        ((na, 2, up_rows, ff_cols), BF),
        ((max(na - 1, 1), 2, up_rows, ff_cols), BF),
        ((na, 2, ff_rows // 2, width), BF),
        ((8, LANES), BF),
    ]
    scratch = [pltpu.VMEM(*x) for x in scratch]
    block = (own_rows, half)
    four, eight = pltpu.VMEM((4,) + block, BF), pltpu.VMEM((8,) + block, BF)
    scratch += [four] * 2
    for _ in range(2):
        scratch += reduce_buffers(block, BF, ("kl", "kh"))
    scratch += [eight] * 4
    for _ in range(2):
        scratch += reduce_buffers(block, BF, HOP_ONE[::-1])
        scratch += reduce_buffers(block, BF, HOP_TWO[::-1])
    scratch += [eight] * 4 + [pltpu.VMEM((4, own_rows, width), BF)]
    scratch += [pltpu.VMEM(block, F32)] * 2
    copies = 2 * (na - 1) + 4 * na + 4 + 4 * 6 + 2 + 4 * na + na
    scratch += [
        pltpu.SemaphoreType.DMA((2 + 2 * na,)),
        pltpu.SemaphoreType.DMA((copies,)),
        pltpu.SemaphoreType.DMA((copies,)),
    ]
    vmem = pl.BlockSpec(memory_space=pltpu.VMEM)
    return pl.pallas_call(
        functools.partial(core_kernel, heads, parted),
        out_shape=[jax.ShapeDtypeStruct(*x) for x in outs],
        in_specs=[vmem] * 12,
        out_specs=[vmem] * len(outs),
        scratch_shapes=scratch,
        compiler_params=pltpu.CompilerParams(
            collective_id=ident, has_side_effects=True, vmem_limit_bytes=62 * 2**20
        ),
    )(rows, cols, table_t, scales, table, gains, proj, head, own, up_own, down_a, down_b)


def over_rows(ref, body, start):
    rows = ref.shape[0]
    if rows % 8:
        return body(slice(0, rows), start)

    def step(i, carry):
        return body(pl.ds(pl.multiple_of(i * 8, 8), 8), carry)

    return lax.fori_loop(0, rows // 8, step, start)


def lane_sums(values, offset):
    lane = lax.broadcasted_iota(jnp.int32, (8, LANES), 1)
    block = jnp.zeros((8, LANES), F32)
    for i, v in enumerate(values):
        block = jnp.where(lane == i + offset, v, block)
    return block


def sum_squares(ref):
    rows, cols = ref.shape
    height = 8 if rows % 8 == 0 else rows

    def add(part, acc):
        v = ref[part, :]
        return acc + v * v

    return over_rows(ref, add, jnp.zeros((height, cols), F32))


def group_sums(refs):
    sums = [jnp.sum(sum_squares(r)) for r in refs[:6]]
    square = refs[6][...] * refs[6][...]
    return sums + [jnp.sum(square[i : i + 1]) for i in range(3)]


def squares_kernel(*refs):
    grads, masters = refs[:7], refs[7:14]
    losses, out, mine, slots, send_sem, recv_sem = refs[14:]
    links = Links(send_sem, recv_sem)
    block = lane_sums(group_sums(grads), 0) + lane_sums(group_sums(masters), 9)
    links.greet(ALL, True)
    out[...] = sum_everywhere(links, block + losses[...], mine, slots)
    links.finish()


def at_first(body):
    pl.when(pl.program_id(0) == 0)(body)


def moments_kernel(*refs):
    sums = refs[0]
    grads, masters, firsts, seconds = (refs[1 + 7 * i : 8 + 7 * i] for i in range(4))
    means, squares, updates = (refs[29 + 7 * i : 36 + 7 * i] for i in range(3))
    out = refs[50]
    total = sums[...]
    lane = lax.broadcasted_iota(jnp.int32, (8, LANES), 1)
    norm = jnp.sqrt(jnp.sum(jnp.where(lane < 9, total, 0.0)[0:1], 1, keepdims=True))
    factor = jnp.minimum(1.0, 0.05 / norm)

    def one(i):
        def step(part, acc):
            g = factor * grads[i][part, :]
            mean = 0.9 * firsts[i][part, :] + 0.1 * g
            square = 0.99 * seconds[i][part, :] + 0.01 * g * g
            update = (mean / (1.0 - 0.9**STEP)) / (
                jnp.sqrt(square / (1.0 - 0.99**STEP)) + 1e-08
            ) + 0.01 * masters[i][part, :]
            means[i][part, :] = mean
            squares[i][part, :] = square
            updates[i][part, :] = update
            return acc + update * update

        rows, cols = grads[i].shape
        height = 8 if rows % 8 == 0 else rows
        return over_rows(grads[i], step, jnp.zeros((height, cols), F32))

    @at_first
    def _():
        table, gains = one(0), one(6)
        values = [jnp.sum(table)] + [0.0] * 5 + [jnp.sum(gains[j : j + 1]) for j in range(3)]
        out[...] = lane_sums(values, 0)

    out[...] += lane_sums([jnp.sum(one(i)) for i in range(1, 6)], 1)


def weights_kernel(*refs):
    update_sums, sums = refs[:2]
    masters, updates = refs[2:9], refs[9:16]
    news, copies = refs[16:23], refs[23:29]
    norms_ref = refs[29]
    update_norm = jnp.sqrt(update_sums[0:1, 0:9])
    weight_norm = jnp.sqrt(sums[0:1, 9:18])
    ratio = weight_norm / update_norm

    def one(i):
        def step(part, acc):
            new = masters[i][part, :] - 0.3 * ratio[0:1, i : i + 1] * updates[i][part, :]
            news[i][part, :] = new
            copies[i][part, :] = new.astype(BF)
            return 0

        over_rows(masters[i], step, 0)

    @at_first
    def _():
        norms_ref[0:1, 0:9] = weight_norm
        norms_ref[1:2, 0:9] = update_norm
        one(0)
        for j in range(3):
            row = slice(j, j + 1)
            news[6][row] = masters[6][row] - 0.3 * ratio[0:1, 6 + j : 7 + j] * updates[6][row]

    for i in range(1, 6):
        one(i)


def by_rows(body, heads, groups, outs, tails):
    shapes = [x.shape for x in groups[0]]
    parts = 5 if all(shapes[i][0] % 80 == 0 or shapes[i][0] == 40 for i in range(1, 6)) else 1

    def spec(i, shape):
        if i in (0, 6):
            return pl.BlockSpec(shape, lambda n: (0, 0))
        return pl.BlockSpec((shape[0] // parts, shape[1]), lambda n: (n, 0))

    def whole(x):
        return pl.BlockSpec(x.shape, lambda n: (0,) * len(x.shape))

    in_specs = [whole(x) for x in heads]
    in_specs += [spec(i, s) for _ in groups for i, s in enumerate(shapes)]
    out_specs = [spec(i, x.shape) for group in outs for i, x in enumerate(group)]
    out_specs += [whole(x) for x in tails]
    return local_call(
        body,
        [x for group in outs for x in group] + tails,
        list(heads) + [x for group in groups for x in group],
        grid=(parts,),
        in_specs=in_specs,
        out_specs=out_specs,
    )


def layer_norm(v, gain):
    center = v - jnp.mean(v, -1, keepdims=True)
    return center * lax.rsqrt(jnp.mean(center * center, -1, keepdims=True) + 1e-05) * gain


def gradients(obs_tokens, returns, actions, rewards, game_ids, segments, masters):
    table, w_qkv, w_proj, w_up, w_down, w_head, gains = masters
    na, nk = lax.axis_size("ba"), 4
    nb, members = na * 4, 2 * nk
    total = nb * nk
    bl = lax.axis_index("bl")
    k = lax.axis_index("kh") * 2 + lax.axis_index("kl")
    g = bl * nk + k
    seqs, steps_here = obs_tokens.shape[:2]
    width = table.shape[1]
    rows, table_rows = w_qkv.shape[0], table.shape[0]
    steps = steps_here * nk
    heads = HEADS // nk
    wide = width // nk
    cols = 3 * wide // nb
    ff_rows = w_down.shape[0]
    padded_rows = up_to(rows, 16)
    padded_table = up_to(table_rows, 16)
    half = width // 2

    info = [obs_tokens] + [v[..., None] for v in (returns, actions, rewards, game_ids, segments)]
    info = jnp.concatenate(info, -1).reshape(seqs * steps_here, -1)
    info = pad_to(info, up_to(seqs * steps_here, 8), LANES)
    counts_here = jnp.sum((game_ids[..., None] == jnp.arange(GAMES)).astype(F32), (0, 1))
    table_bf = pad_to(table.astype(BF), padded_table, width)
    small = jnp.concatenate(
        [
            pad_to(w_head.astype(BF), rows, 256),
            pad_to(gains.astype(BF), 3, 256),
            pad_to(counts_here.astype(BF)[None], 1, 256),
            jnp.zeros((padded_rows - rows - 4, 256), BF),
        ]
    )
    qkv_blocks = w_qkv.astype(BF).reshape(rows, 3, nk, wide).transpose(2, 0, 1, 3)
    qkv_blocks = qkv_blocks.reshape(nk, rows, nb, cols).transpose(2, 0, 1, 3)
    qkv_blocks = pad_to(qkv_blocks.reshape(total, rows, cols), padded_rows, LANES)
    ff_cols = na * 2 * ff_rows
    up_blocks = w_up.astype(BF).reshape(rows, na, 2, 2, nk, ff_rows).transpose(2, 4, 0, 1, 3, 5)
    up_blocks = pad_to(up_blocks.reshape(members, rows, ff_cols), padded_rows, ff_cols)
    to_heads = [(i, i % nb * nk + i // nb) for i in range(total)]
    proj_rows = pad_to(lax.ppermute(w_proj.astype(BF), ALL, to_heads), padded_rows, width)
    parted = ff_rows % 32 == 0 and nk * rows % 16 == 0
    down_low = w_down.astype(BF)
    one_way = ("ba", "bl", "bc", "kh", "kl")
    other_way = ("ba", "bl", "kh", "bc", "kl")
    items = [
        (table_bf[:, :half], "gather", one_way),
        (table_bf[:, half:], "gather", other_way),
        (small, "gather", other_way),
        (qkv_blocks, "scatter", ALL),
        (info, "direct", BLK),
        (up_blocks, "scatter", GROUP),
    ]
    if parted:
        items.append((down_low[: ff_rows // 2], "gather", ("ba",)))
    got = exchange(items, 0)
    table_left, table_right, small_all, qkv_mine, info_here, up_mine = got[:6]
    if parted:
        up_mine = up_mine[:, :rows].reshape(2, nk * rows, ff_cols)
        down_first = got[6]
    else:
        up_mine = lax.all_gather(up_mine[:, :rows], COPIES, axis=0, tiled=False)
        up_mine = up_mine.reshape(na, 2, 2, nk, rows, ff_cols).transpose(0, 2, 1, 3, 4, 5)
        up_mine = up_mine.reshape(width, ff_cols)
        down_first = lax.all_gather(down_low, COPIES, axis=0, tiled=True)

    table_all = jnp.concatenate(
        [
            natural(table_left, ALL, one_way)[:, :table_rows],
            natural(table_right, ALL, other_way)[:, :table_rows],
        ],
        2,
    ).reshape(TABLE, width)
    small_all = natural(small_all, ALL, other_way)
    gain = small_all[:, rows : rows + 3, :rows].transpose(1, 0, 2).reshape(3, width).astype(F32)
    w_mine = qkv_mine[:, :rows].reshape(width, LANES)
    scale_rows = TABLE - FIRST_PLACE + 1
    cols_mine, scale_table, center_bf, center_gain = local_call(
        table_kernel,
        [
            jax.ShapeDtypeStruct((LANES, TABLE), BF),
            jax.ShapeDtypeStruct((2 * scale_rows, TABLE), BF),
            jax.ShapeDtypeStruct((TABLE, width), BF),
            jax.ShapeDtypeStruct((TABLE, width), BF),
        ],
        (table_all, pad_to(gain, 8, width), w_mine),
        [pltpu.VMEM((TABLE, width), F32)],
    )
    table_ways = (("ba", "bl", "bc"), ("bc", "bl", "ba"))
    items = [
        (cols_mine[: LANES // 2], "gather", table_ways[0]),
        (cols_mine[LANES // 2 :], "gather", table_ways[1]),
        (proj_rows, "gather", ("ba", "bc", "bl")),
    ]
    if parted:
        items.append((down_low[ff_rows // 2 :], "gather", ("ba",)))
    got = exchange(items, 1)
    down_second = got[3] if parted else jnp.zeros((16, LANES), BF)
    qkv_table = jnp.concatenate(
        [natural(got[0], BATCH, table_ways[0]), natural(got[1], BATCH, table_ways[1])], 1
    )
    qkv_table = qkv_table[:, :cols].reshape(3 * wide, TABLE)
    proj_here = natural(got[2], BATCH, ("ba", "bc", "bl"))[:, :rows].reshape(wide, width)

    info_here = info_here[:, : seqs * steps_here].reshape(nk, seqs, steps_here, LANES)
    info_here = info_here.transpose(1, 0, 2, 3).reshape(seqs, steps, LANES)
    length = up_to(TSTEP * steps, LANES)
    place_of = np.repeat(np.array(PLACES), steps)
    time_of = np.tile(np.arange(steps), TSTEP)
    tail = length - TSTEP * steps
    pos = np.pad(time_of * TSTEP + place_of, (0, tail), constant_values=1 << 20)
    place_of = np.pad(place_of, (0, tail), constant_values=-1000)
    starts = np.array([0] * OBS + [PATCH, PATCH + RET_BINS, PATCH + RET_BINS + ACTIONS])
    codes = info_here[..., :TSTEP] + starts.astype(np.int32)
    codes = jnp.concatenate(
        [codes[..., OBS - 1 : OBS + 2], codes[..., : OBS - 1], codes[..., OBS + 2 :]], -1
    )
    codes = codes.transpose(0, 2, 1).reshape(seqs, TSTEP * steps)
    codes = jnp.pad(codes, ((0, 0), (0, tail)), constant_values=-1)
    seg = jnp.tile(info_here[..., OBS + 4], (1, TSTEP))
    seg = jnp.pad(seg, ((0, 0), (0, tail)), constant_values=-1)
    zero = jnp.zeros((seqs, length), jnp.int32)
    token_rows = jnp.stack(
        [codes, zero + jnp.asarray(pos, jnp.int32), seg, zero + jnp.asarray(place_of, jnp.int32)]
        + [zero] * 4,
        1,
    )
    token_cols = jnp.stack([zero[:, :LANES] + pos[:LANES].astype(np.int32), seg[:, :LANES]], -1)
    token_cols = jnp.pad(token_cols, ((0, 0), (0, 0), (0, LANES - 2)))

    own = seqs * LANES // nk
    slots = lax.rem(k, nk // seqs) * own + jnp.arange(own)
    seq_own = k * own // LANES
    codes_own = lax.dynamic_slice(codes, (seq_own, lax.rem(k, nk // seqs) * own), (1, own))[0]
    place_own = jnp.asarray(place_of[:LANES], jnp.int32)
    place_own = lax.dynamic_slice(place_own, (lax.rem(k, nk // seqs) * own,), (own,))
    kind = slots // steps
    info_seq = lax.dynamic_index_in_dim(info_here, seq_own, 0, False)
    info_own = info_seq.at[lax.rem(slots, steps)].get(mode="promise_in_bounds")
    counts = jnp.sum(small_all[:, rows + 3, :GAMES].astype(F32), 0)
    per_game = 1.0 / (GAMES * jnp.maximum(counts, 1.0))
    game_own = (info_own[:, OBS + 3, None] == jnp.arange(GAMES)).astype(F32)
    weight = jnp.where(kind < PICKS, jnp.sum(game_own * per_game, -1), 0.0)
    low_end = jnp.where(kind == 0, 0, jnp.where(kind == 1, RET_BINS, RET_BINS + ACTIONS))
    high_end = jnp.where(kind == 0, RET_BINS, jnp.where(kind == 1, RET_BINS + ACTIONS, HEAD_COLS))
    target = low_end + jnp.where(
        kind == 0,
        info_own[:, OBS],
        jnp.where(kind == 1, info_own[:, OBS + 1], info_own[:, OBS + 2]),
    )
    own_info = [low_end, high_end, target, weight, kind, codes_own, place_own + FIRST_PLACE]
    own_info = pad_to(jnp.stack([v.astype(F32) for v in own_info], 1), own, LANES)
    head_full = small_all[:, :rows].reshape(width, 256)
    d_table, pairs, sum_up, sum_down, d_proj, d_head, dy_own, d_small = core(
        token_rows,
        token_cols,
        qkv_table,
        scale_table,
        table_all,
        pad_to(gain, 8, width),
        proj_here,
        head_full,
        own_info,
        up_mine,
        down_first,
        down_second,
        heads,
        2,
    )
    d_gain_mid, d_gain_last = d_small[0], d_small[1]
    losses = [d_small[2, j] for j in range(PICKS)]
    columns = jnp.arange(TABLE)
    own_hot = (codes_own[:, None] == columns) | (place_own[:, None] + FIRST_PLACE == columns)
    own_hot = own_hot.astype(BF)
    if not parted:
        sum_up = sum_up.reshape(na, 2, 2, nk, rows, ff_cols).transpose(0, 2, 1, 3, 4, 5)
        sum_up = sum_up.reshape(width, ff_cols)
        sum_up = lax.psum_scatter(sum_up, COPIES, scatter_dimension=0, tiled=True)
        sum_down = lax.psum_scatter(sum_down, COPIES, scatter_dimension=0, tiled=True)

    d_table = pad_to(d_table.astype(BF).reshape(nb, cols, TABLE), LANES, TABLE)
    d_proj = pad_to(d_proj.astype(BF).reshape(nb, rows, width), padded_rows, width)
    proj_route = ("bl", "bc", "ba")
    table_routes = (("bc", "bl", "ba"), ("bl", "bc", "ba"))
    left, right, sum_proj = reduce(
        [
            for_route(d_table[..., : TABLE // 2], BATCH, table_routes[0]),
            for_route(d_table[..., TABLE // 2 :], BATCH, table_routes[1]),
            for_route(d_proj, BATCH, proj_route),
        ],
        table_routes + (proj_route,),
        [],
        3,
    )
    sum_proj = lax.ppermute(sum_proj[:rows], ALL, [(j, i) for i, j in to_heads])
    d_table_mine = jnp.concatenate([left, right], 1).astype(BF)
    d_w = dot(center_gain, d_table_mine, 0, 1)
    d_norm = dot(d_table_mine, w_mine, 0, 1)
    d_gain_first = jnp.sum(center_bf.astype(F32) * d_norm, 0)
    d_scaled = d_norm * gain[0]
    d_embed = (
        d_scaled
        - jnp.mean(d_scaled, 1, keepdims=True)
        - dot(pairs.astype(BF), center_bf)
        + dot(own_hot, dy_own, 0, 0)
    )
    d_gains = jnp.stack([d_gain_first, d_gain_mid, d_gain_last]).astype(BF)
    d_misc = jnp.concatenate(
        [
            d_head.reshape(total, rows, 256),
            pad_to(d_gains.reshape(3, total, rows).transpose(1, 0, 2), 3, 256),
            jnp.zeros((total, padded_rows - rows - 3, 256), BF),
        ],
        1,
    )
    d_w = pad_to(d_w.astype(BF).reshape(total, rows, LANES), padded_rows, LANES)
    d_embed = pad_to(d_embed.astype(BF).reshape(total, table_rows, width), padded_table, width)
    sum_up = pad_to(sum_up.reshape(members, rows, -1), padded_rows, ff_cols)
    one_way = ("kl", "kh", "bc", "bl", "ba")
    other_way = ("kl", "bc", "kh", "bl", "ba")
    arrays = [
        for_route(d_embed[..., :half], ALL, one_way),
        for_route(d_embed[..., half:], ALL, other_way),
        for_route(d_misc, ALL, other_way),
    ]
    routes = (one_way, other_way, other_way)
    if parted:
        arrays.append(sum_down)
        routes += (("ba",),)
    got = reduce(arrays, routes, [(d_w, ALL), (sum_up, GROUP)], 4)
    d_left, d_right, d_misc = got[:3]
    d_ws, ups = got[-2:]
    if parted:
        sum_down = got[3]
    d_embed = jnp.concatenate([d_left, d_right], 1)
    d_ws = d_ws[:, :rows, :cols].reshape(nb, nk, rows, cols).transpose(2, 1, 0, 3)
    d_ws = d_ws.reshape(rows, nk, 3, wide).transpose(0, 2, 1, 3).reshape(rows, 3 * width)
    ups = ups[:, :rows].reshape(2, nk, rows, na, 2, ff_rows).transpose(2, 3, 0, 4, 1, 5)
    ups = ups.reshape(rows, nb * nk * ff_rows)
    grads = (
        d_embed[:table_rows],
        d_ws.astype(F32),
        sum_proj,
        ups.astype(F32),
        sum_down.astype(F32),
        d_misc[:rows, :HEAD_COLS],
        d_misc[rows : rows + 3, :rows],
    )
    return grads, losses


def shards(*args):
    masters, firsts, seconds = args[6:13], args[13:20], args[20:27]
    grads, losses = gradients(*args[:6], masters)
    like = [jax.ShapeDtypeStruct(w.shape, F32) for w in masters]
    low = [jax.ShapeDtypeStruct(w.shape, BF) for w in masters[:6]]
    tile = jax.ShapeDtypeStruct((8, LANES), F32)
    loss_tile = jnp.zeros((8, LANES), F32).at[:, 18:21].set(jnp.stack(losses))
    sums = summed_call(squares_kernel, grads + masters + (loss_tile,), 5)
    result = by_rows(
        moments_kernel, (sums,), (grads, masters, firsts, seconds), [like] * 3, [tile]
    )
    means, squares, updates = result[:7], result[7:14], result[14:21]
    update_sums = summed_call(all_sum_kernel, (result[21],), 6)
    result = by_rows(
        weights_kernel, (update_sums, sums), (masters, updates), [like, low], [tile]
    )
    news, copies, norms = result[:7], result[7:13], result[13][:2, :9]
    grad_norm = jnp.sqrt(jnp.sum(sums[0, :9]))
    return tuple(news) + tuple(means) + tuple(squares) + tuple(copies) + (
        grad_norm,
        sums[0, 18:21],
        norms,
    )


def solution(mesh):
    nb, nk = mesh.shape["batch"], mesh.shape["blk"]
    split = Mesh(mesh.devices.reshape(nb // 4, 2, 2, nk // 2, 2), ALL)
    rows, gains = P(ALL, None), P(None, ALL)
    weights = (rows,) * 6 + (gains,)
    in_specs = (P(BATCH, BLK, None),) + (P(BATCH, BLK),) * 5 + weights * 3
    out_specs = weights * 3 + (rows,) * 6 + (P(), P(), P())
    return jax.shard_map(
        shards, mesh=split, in_specs=in_specs, out_specs=out_specs, check_vma=False
    )
```

```python
import functools
import math
import types

import jax
import jax.numpy as jnp
import numpy as np
from jax import lax
from jax.experimental import pallas as pl
from jax.experimental.pallas import tpu as pltpu
from jax.sharding import Mesh
from jax.sharding import PartitionSpec as P

HEADS = 20
RET_BINS = 120
ACTIONS = 18
GAMES = 41
TSTEP = 39
OBS = 36
PATCH = 331
STEP = 10
HEAD_COLS = 142
TABLE = 512
PICKS = 3
LANES = 128
FIRST_PLACE = PATCH + HEAD_COLS
BF = jnp.bfloat16
F32 = jnp.float32
HIGH = lax.Precision.HIGHEST
BLK = ("kh", "kl")
GROUP = ("bl", "kh", "kl")
BATCH = ("ba", "bl", "bc")
COPIES = ("ba", "bc")
ALL = ("ba", "bl", "bc", "kh", "kl")
VMEM_LIMIT = 56 * 2**20
PLACES = list(range(OBS - 1, OBS + 2)) + [p for p in range(TSTEP) if not OBS - 1 <= p < OBS + 2]


def up_to(n, m):
    return -(-n // m) * m


def pad_to(x, rows, cols):
    if x.shape[-2:] == (rows, cols):
        return x
    widths = [(0, 0)] * (x.ndim - 2) + [(0, rows - x.shape[-2]), (0, cols - x.shape[-1])]
    return jnp.pad(x, widths)


def dot(left, right, ca=1, cb=0, precision=None):
    return lax.dot_general(
        left,
        right,
        (((ca,), (cb,)), ((), ())),
        precision=precision,
        preferred_element_type=F32,
    )


class Links:
    def __init__(self, sends, recvs):
        self.sends, self.recvs, self.open, self.used = sends, recvs, [], 0
        self.size = {a: lax.axis_size(a) for a in ALL}
        self.here = {a: lax.axis_index(a) for a in ALL}

    def at(self, axis, step):
        return lax.rem(self.here[axis] + step, self.size[axis])

    def number(self, axes, steps):
        n = 0
        for a in axes:
            n = n * self.size[a] + self.at(a, steps.get(a, 0))
        return n

    def moves(self, axes):
        result = [{}]
        for a in axes:
            result = [dict(m, **{a: r}) for m in result for r in range(self.size[a])]
        return [{a: r for a, r in m.items() if r} for m in result if any(m.values())]

    def greet(self, axes, everyone=False):
        barrier = pltpu.get_barrier_semaphore()
        if everyone:
            moves = self.moves(axes)
        else:
            moves = [{a: r} for a in axes for r in range(1, self.size[a])]
        for move in moves:
            pl.semaphore_signal(
                barrier,
                inc=1,
                device_id={a: self.at(a, r) for a, r in move.items()},
                device_id_type=pl.DeviceIdType.MESH,
            )
        pl.semaphore_wait(barrier, len(moves))

    def send(self, src, dst, move):
        n, self.used = self.used, self.used + 1
        c = pltpu.make_async_remote_copy(
            src_ref=src,
            dst_ref=dst,
            send_sem=self.sends.at[n],
            recv_sem=self.recvs.at[n],
            device_id={a: self.at(a, r) for a, r in move.items()},
            device_id_type=pl.DeviceIdType.MESH,
        )
        c.start()
        self.open.append(c)
        return c

    def finish(self, copies=None):
        copies = list(self.open if copies is None else copies)
        for c in copies:
            c.wait_send()
        self.open = [c for c in self.open if not any(c is d for d in copies)]


class Gather:
    def __init__(self, links, src, dst, route, local):
        self.links, self.src, self.dst = links, src, dst
        self.route, self.local, self.waits, self.stage = list(route), local, [], 0

    def step(self):
        links = self.links
        for c in self.waits:
            c.wait_recv()
        self.waits = []
        if self.stage == len(self.route):
            return False
        if self.stage == 1 and self.local is not None:
            self.local.wait()
            self.local = None
        count = math.prod(links.size[a] for a in self.route[: self.stage])
        start = links.number(self.route[self.stage :][::-1], {}) * count
        here = self.dst.at[pl.ds(start, count)]
        block = self.src if self.stage == 0 else here
        there = self.dst.at[start] if self.stage == 0 else here
        axis = self.route[self.stage]
        for r in range(1, links.size[axis]):
            self.waits.append(links.send(block, there, {axis: r}))
        self.stage += 1
        return True

    def close(self):
        if self.local is not None:
            self.local.wait()


class Reduce:
    def __init__(self, links, src, out, route, arrived, totals):
        self.links, self.now, self.out = links, src, out
        self.route, self.arrived, self.totals = list(route), arrived, totals
        self.waits, self.stage = [], 0

    def part(self, axis, step):
        count = self.now.shape[0] // self.links.size[axis]
        return pl.ds(self.links.at(axis, step) * count, count)

    def step(self):
        if self.stage:
            axis = self.route[self.stage - 1]
            for c in self.waits:
                c.wait_recv()
            total = self.now[self.part(axis, 0)].astype(F32)
            for n in range(len(self.waits)):
                total = total + self.arrived[self.stage - 1][n].astype(F32)
            if self.stage == len(self.route):
                self.out[...] = total[0]
                return False
            self.now = self.totals[self.stage - 1]
            self.now[...] = total.astype(self.now.dtype)
        axis = self.route[self.stage]
        self.waits = []
        for r in range(1, self.links.size[axis]):
            dst = self.arrived[self.stage].at[r - 1]
            self.waits.append(self.links.send(self.now.at[self.part(axis, r)], dst, {axis: r}))
        self.stage += 1
        return True


def start_scatters(links, jobs):
    copies = []
    for src, dst, axes, kind in jobs:
        me = links.number(axes, {})
        for move in links.moves(axes):
            block = src.at[links.number(axes, move)] if kind == "scatter" else src
            copies.append(links.send(block, dst.at[me], move))
    return copies


def run(jobs):
    jobs = list(jobs)
    while jobs:
        jobs = [j for j in jobs if j.step()]


def sizes_of(axes):
    return tuple(lax.axis_size(a) for a in axes)


def exchange_kernel(kinds, routes, *refs):
    count = len(kinds)
    srcs, dsts = refs[:count], refs[count : 2 * count]
    local_sem, send_sem, recv_sem = refs[2 * count :]
    links = Links(send_sem, recv_sem)
    local = []
    for i, route in enumerate(routes):
        me = links.number(route[::-1] if kinds[i] == "gather" else route, {})
        block = srcs[i].at[me] if kinds[i] == "scatter" else srcs[i]
        local.append(pltpu.make_async_copy(block, dsts[i].at[me], local_sem.at[i]))
        local[-1].start()
    everyone = any(k != "gather" for k in kinds)
    links.greet([a for a in ALL if any(a in x for x in routes)], everyone)
    gathers = [
        Gather(links, srcs[i], dsts[i], routes[i], local[i])
        for i in range(count)
        if kinds[i] == "gather"
    ]
    for j in gathers:
        j.step()
    copies = []
    for i in range(count):
        if kinds[i] != "gather":
            copies += start_scatters(links, [(srcs[i], dsts[i], routes[i], kinds[i])])
    run(gathers)
    for j in gathers:
        j.close()
    for c in copies:
        c.wait_recv()
    for i in range(count):
        if kinds[i] != "gather":
            local[i].wait()
    links.finish()


def natural(x, axes, route):
    back = route[::-1]
    x = x.reshape(sizes_of(back) + x.shape[1:])
    order = [back.index(a) for a in axes] + list(range(len(axes), x.ndim))
    return x.transpose(order).reshape((-1,) + x.shape[len(axes) :])


def for_route(x, axes, route):
    x = x.reshape(sizes_of(axes) + x.shape[1:])
    order = [axes.index(a) for a in route] + list(range(len(axes), x.ndim))
    return x.transpose(order).reshape((-1,) + x.shape[len(axes) :])


def exchange(items, ident):
    arrays, kinds, routes = zip(*items)
    shapes, copies = [], 0
    for x, kind, route in zip(arrays, kinds, routes):
        sizes = sizes_of(route)
        shape = x.shape if kind == "scatter" else (math.prod(sizes),) + x.shape
        shapes.append(jax.ShapeDtypeStruct(shape, x.dtype))
        copies += sum(sizes) - len(sizes) if kind == "gather" else math.prod(sizes) - 1
    n = len(arrays)
    return pl.pallas_call(
        functools.partial(exchange_kernel, kinds, routes),
        out_shape=shapes,
        in_specs=[pl.BlockSpec(memory_space=pl.ANY)] * n,
        out_specs=[pl.BlockSpec(memory_space=pl.ANY)] * n,
        scratch_shapes=[
            pltpu.SemaphoreType.DMA((n,)),
            pltpu.SemaphoreType.DMA((copies,)),
            pltpu.SemaphoreType.DMA((copies,)),
        ],
        compiler_params=pltpu.CompilerParams(collective_id=ident, has_side_effects=True),
    )(*arrays)


def reduce_buffers(shape, dtype, route):
    arrived, totals = [], []
    for i, axis in enumerate(route):
        rest = (math.prod(sizes_of(route[i + 1 :])),) + shape
        arrived.append(pltpu.VMEM((lax.axis_size(axis) - 1,) + rest, dtype))
        totals.append(pltpu.VMEM(rest, dtype))
    return arrived + totals[:-1]


def reduce_kernel(routes, other_axes, *refs):
    refs = list(refs)

    def take(n):
        got = refs[:n]
        del refs[:n]
        return got

    sums = len(routes)
    srcs, other_srcs = take(sums), take(len(other_axes))
    outs, other_dsts = take(sums), take(len(other_axes))
    buffers = [(take(len(r)), take(len(r) - 1)) for r in routes]
    local_sem, send_sem, recv_sem = refs
    links = Links(send_sem, recv_sem)
    local = []
    for i, axes in enumerate(other_axes):
        me = links.number(axes, {})
        local.append(
            pltpu.make_async_copy(other_srcs[i].at[me], other_dsts[i].at[me], local_sem.at[i])
        )
        local[-1].start()
    seen = [a for a in ALL if any(a in x for x in tuple(routes) + other_axes)]
    links.greet(seen, bool(other_axes))
    jobs = [
        Reduce(links, srcs[i], outs[i], routes[i], *buffers[i]) for i in range(sums)
    ]
    for j in jobs:
        j.step()
    copies = start_scatters(
        links, [(s, d, a, "scatter") for s, d, a in zip(other_srcs, other_dsts, other_axes)]
    )
    run(jobs)
    for c in copies:
        c.wait_recv()
    for c in local:
        c.wait()
    links.finish()


def reduce(arrays, routes, others, ident):
    outs = [jax.ShapeDtypeStruct(x.shape[1:], F32) for x in arrays]
    outs += [jax.ShapeDtypeStruct(x.shape, x.dtype) for x, _ in others]
    scratch = []
    for x, route in zip(arrays, routes):
        scratch += reduce_buffers(x.shape[1:], x.dtype, route)
    copies = sum(sum(sizes_of(r)) - len(r) for r in routes)
    copies += sum(math.prod(sizes_of(axes)) - 1 for _, axes in others)
    scratch += [
        pltpu.SemaphoreType.DMA((max(len(others), 1),)),
        pltpu.SemaphoreType.DMA((copies,)),
        pltpu.SemaphoreType.DMA((copies,)),
    ]
    vmem, hbm = pl.BlockSpec(memory_space=pltpu.VMEM), pl.BlockSpec(memory_space=pl.ANY)
    specs = [vmem] * len(arrays) + [hbm] * len(others)
    return pl.pallas_call(
        functools.partial(reduce_kernel, tuple(routes), tuple(axes for _, axes in others)),
        out_shape=outs,
        in_specs=specs,
        out_specs=specs,
        scratch_shapes=scratch,
        compiler_params=pltpu.CompilerParams(
            collective_id=ident, has_side_effects=True, vmem_limit_bytes=VMEM_LIMIT
        ),
    )(*arrays, *[x for x, _ in others])


def sum_everywhere(links, value, mine, slots):
    mine[...] = value
    moves = links.moves(ALL)
    waits = [links.send(mine, slots.at[n], move) for n, move in enumerate(moves)]
    for c in waits:
        c.wait_recv()
    return value + jnp.sum(slots[...], 0)


def all_sum_kernel(value, out, mine, slots, send_sem, recv_sem):
    links = Links(send_sem, recv_sem)
    links.greet(ALL, True)
    out[...] = sum_everywhere(links, value[...], mine, slots)
    links.finish()


def summed_call(body, arrays, ident):
    vmem = pl.BlockSpec(memory_space=pltpu.VMEM)
    copies = math.prod(sizes_of(ALL)) - 1
    return pl.pallas_call(
        body,
        out_shape=jax.ShapeDtypeStruct((8, LANES), F32),
        in_specs=[vmem] * len(arrays),
        out_specs=vmem,
        scratch_shapes=[
            pltpu.VMEM((8, LANES), F32),
            pltpu.VMEM((copies, 8, LANES), F32),
            pltpu.SemaphoreType.DMA((copies,)),
            pltpu.SemaphoreType.DMA((copies,)),
        ],
        compiler_params=pltpu.CompilerParams(
            collective_id=ident, has_side_effects=True, vmem_limit_bytes=VMEM_LIMIT
        ),
    )(*arrays)


def local_call(body, outs, arrays, scratch=(), **kw):
    return pl.pallas_call(
        body,
        out_shape=outs,
        scratch_shapes=list(scratch),
        compiler_params=pltpu.CompilerParams(vmem_limit_bytes=VMEM_LIMIT),
        **kw,
    )(*arrays)


def table_kernel(table, gains, w, cols_ref, scale_ref, center_ref, center_gain_ref, center):
    rows, width = table.shape
    gain = gains[0:1]
    for i in range(0, rows, 64):
        part = table[i : i + 64].astype(F32)
        part = part - jnp.mean(part, 1, keepdims=True)
        center[i : i + 64] = part
        center_ref[i : i + 64] = part.astype(BF)
        center_gain_ref[i : i + 64] = (part * gain).astype(BF)
    cols_ref[...] = dot(center_gain_ref[...], w[...]).T.astype(BF)
    first = FIRST_PLACE - 1
    places = center[first:rows]
    gram = dot(places, center[...], 1, 1, HIGH)
    own = jnp.sum(places * places, 1, keepdims=True)
    every = center[...]
    every = dot(jnp.ones((8, width), F32), every * every, 1, 1, HIGH)[0:1]
    scale = lax.rsqrt((2.0 * gram + own + every) / width + 1e-05)
    lane = lax.broadcasted_iota(jnp.int32, scale.shape, 1)
    scale = jnp.where(lane < FIRST_PLACE, scale, 0.0)
    high = scale.astype(BF)
    scale_ref[0 : rows - first] = high
    scale_ref[rows - first :] = (scale - high.astype(F32)).astype(BF)


def fill_hot(hot, code, place):
    rows, length = hot.shape
    for i in range(0, rows, 64):
        index = lax.broadcasted_iota(jnp.int32, (64, length), 0) + i
        hit = (index == code) | (index == place + FIRST_PLACE)
        hot[i : i + 64] = jnp.where(hit, 1.0, 0.0).astype(BF)


def attend_seq(s, heads, tokens, pos_col, seg_col, table, parts, scales, keep):
    att, q_ref, kv_ref, prob_ref, scale_ref, hot, bias = keep
    wide = att.shape[1]
    dim = wide // heads
    code, pos, seg, place = tokens
    fill_hot(hot, code, place)
    length = hot.shape[1]
    both = dot(scales[...], hot[...])
    half = both.shape[0] // 2
    both = both[:half] + both[half:]
    index = lax.broadcasted_iota(jnp.int32, both.shape, 0)
    scale = jnp.sum(jnp.where(index == place + 1, both, 0.0), 0, keepdims=True)
    scale_ref[s] = jnp.broadcast_to(scale, (8, length))
    q = dot(table[parts[0], :], hot[:, 0:LANES]) * scale[:, 0:LANES]
    q_low = q.astype(BF)
    q_ref[s] = q_low
    for i in range(2):
        part = dot(table[parts[1 + i], :], hot[...])
        kv_ref[s, i * wide : (i + 1) * wide] = (part * scale).astype(BF)
    seen = (pos <= pos_col) & (seg == seg_col)
    bias[...] = jnp.where(seen, 0.0, -1e30)
    factor = dim**-0.5
    for h in range(heads):
        part = slice(h * dim, (h + 1) * dim)
        query = (q_low[part].astype(F32) * factor).T.astype(BF)
        scores = dot(query, kv_ref[s, part]) + bias[...]
        expo = jnp.exp(scores - jnp.max(scores, 1, keepdims=True))
        probs = (expo * (1.0 / jnp.sum(expo, 1, keepdims=True))).astype(BF)
        prob_ref[s, h] = probs
        value = kv_ref[s, wide + h * dim : wide + (h + 1) * dim]
        att[s, part] = dot(value, probs, 1, 1).astype(BF)


def attend_back_seq(s, heads, width, code, place, keep, datt, d_table, pairs, grad, grad_q):
    att, q_ref, kv_ref, prob_ref, scale_ref, hot, bias = keep
    wide = att.shape[1]
    dim = wide // heads
    scale = scale_ref[s, 0:1]
    fill_hot(hot, code, place)
    length = hot.shape[1]
    factor = dim**-0.5
    kappa = jnp.zeros((1, length), F32)
    kappa_q = jnp.zeros((1, LANES), F32)
    for h in range(heads):
        part = slice(h * dim, (h + 1) * dim)
        part_v = slice(wide + h * dim, wide + (h + 1) * dim)
        key, value = kv_ref[s, part], kv_ref[s, part_v]
        query = q_ref[s, part]
        d_out = datt[s, part]
        d_rows = d_out.astype(F32).T.astype(BF)
        probs_low = prob_ref[s, h]
        probs = probs_low.astype(F32)
        d_prob = dot(d_rows, value)
        weighted = probs * d_prob
        d_score = (weighted - probs * jnp.sum(weighted, 1, keepdims=True)).astype(BF)
        dv = dot(d_out, probs_low)
        dk = dot(query, d_score) * factor
        dq = dot(key, d_score, 1, 1) * factor
        kappa += jnp.sum(dk * key.astype(F32) + dv * value.astype(F32), 0, keepdims=True)
        kappa_q += jnp.sum(dq * query.astype(F32), 0, keepdims=True)
        grad[part] = (dk * scale).astype(BF)
        grad[part_v] = (dv * scale).astype(BF)
        grad_q[part] = (dq * scale[:, 0:LANES]).astype(BF)
    d_table[0:wide] += dot(grad_q[...], hot[:, 0:LANES], 1, 1)
    d_table[wide:] += dot(grad[...], hot[...], 1, 1)
    kappa = jnp.concatenate([kappa[:, 0:LANES] + kappa_q, kappa[:, LANES:]], 1)
    weight = scale * scale * kappa * (1.0 / width)
    for i in range(0, hot.shape[0], 128):
        left = (hot[i : i + 128].astype(F32) * weight).astype(BF)
        pairs[i : i + 128] += dot(left, hot[...], 1, 1)


def norm_parts(v):
    center = v - jnp.mean(v, -1, keepdims=True)
    scale = lax.rsqrt(jnp.mean(center * center, -1, keepdims=True) + 1e-05)
    return center * scale, scale


def norm_back(unit, scale, gain, d_out):
    d_unit = d_out * gain
    inner = jnp.mean(d_unit * unit, -1, keepdims=True)
    d_in = scale * (d_unit - jnp.mean(d_unit, -1, keepdims=True) - unit * inner)
    return d_in, jnp.sum(d_out * unit, 0, keepdims=True)


GELU_SCALE = 0.7978845608028654
GELU_CUBE = 0.044715
HOP_ONE = ("bl", "kh", "kl")
HOP_TWO = ("kh", "bl", "kl")


def core_kernel(heads, parted, *refs):
    refs = list(refs)

    def take(n):
        got = refs[:n]
        del refs[:n]
        return got

    r = types.SimpleNamespace(heads=heads, parted=parted)
    r.chunks, r.near, r.hops = 2, "bc", (HOP_ONE, HOP_TWO)
    rows, cols, table_t, scales, r.table, r.gains, r.proj, r.head, own, up_own = take(10)
    down_a, down_b = take(2)
    r.d_table, r.pairs, r.up_out, r.down_out, r.proj_out, r.head_out = take(6)
    r.dy_out, r.small_out = take(2)
    r.keep = take(7)
    r.up, r.down, r.u, r.hid, r.low, r.wide_in = take(6)
    r.datt, r.grad, r.grad_q, r.d_up, r.d_down = take(5)
    take_middle(r, take)
    local_sem, send_sem, recv_sem = refs
    links = r.links = Links(send_sem, recv_sem)
    size, here = links.size, links.here
    seqs, width = r.keep[0].shape[0], r.table.shape[1]
    set_places(r)
    if not parted:
        r.up, r.down, r.d_up, r.d_down = up_own, down_a, r.up_out, r.down_out

    local, up_first, late = [], [], []

    def copy_here(src, dst):
        local.append(pltpu.make_async_copy(src, dst, local_sem.at[len(local)]))
        local[-1].start()

    def send_down(ref, part):
        half = r.ff_rows // 2
        for n in range(size["ba"]):
            start = (n * size["bc"] + here["bc"]) * r.ff_rows + part * half
            place = r.down.at[pl.ds(pl.multiple_of(start, 8), half)]
            copy_here(ref.at[n], place)
            waiting.append((ref.at[n], place))

    waiting = []
    if parted:
        for bl in range(2):
            copy_here(up_own.at[bl], r.up.at[r.up_at(here["ba"], bl, here["bc"])])
        for part, ref in enumerate((down_a, down_b)):
            send_down(ref, part)
    links.greet(ALL)
    if parted:
        for bl in range(2):
            for n in range(1, size["ba"]):
                place = r.up.at[r.up_at(here["ba"], bl, here["bc"])]
                up_first.append(links.send(up_own.at[bl], place, {"ba": n}))
        for src, place in waiting:
            late.append(links.send(src, place, {"bc": 1}))

    parts = [slice(i * r.wide, (i + 1) * r.wide) for i in range(3)]

    def forward(s, carry):
        tokens = [rows[s, i : i + 1] for i in range(4)]
        attend_seq(
            s, heads, tokens, cols[s, :, 0:1], cols[s, :, 1:2], table_t, parts, scales, r.keep
        )
        return carry

    lax.fori_loop(0, seqs, forward, 0)
    for c in local:
        c.wait()
    for c in up_first:
        c.wait_recv()
    for n in range(size["ba"] if parted else 0):
        for bl in range(2):
            place = r.up.at[r.up_at(n, bl, here["bc"])]
            late.append(links.send(place, place, {"bc": 1}))
    info = own[...]
    r.low_end, r.high_end, r.target, r.weight, r.kind, code, place = (
        info[:, i : i + 1] for i in range(7)
    )
    columns = lax.broadcasted_iota(jnp.int32, (r.own, r.table.shape[0]), 1).astype(F32)
    r.own_hot = jnp.where((columns == code) | (columns == place), 1.0, 0.0).astype(BF)

    def weights_here():
        for c in late:
            c.wait_recv()

    r.weights_here, r.tick, r.free_weights = weights_here, lambda: None, lambda: None

    def backward(s, carry):
        attend_back_seq(
            s,
            heads,
            width,
            rows[s, 0:1],
            rows[s, 3:4],
            r.keep,
            r.datt,
            r.d_table,
            r.pairs,
            r.grad,
            r.grad_q,
        )
        return carry

    r.backward = backward
    middle(r)
    links.finish()


def take_middle(r, take):
    r.up_got, r.up_sum, r.up_got2, r.down_got = take(4)
    r.blk_src, r.blk_buffers = take(2), [take(3), take(3)]
    r.low_parts, r.z_src = take(2), take(2)
    r.z_buffers, r.low_buffers = [take(5), take(5)], [take(5), take(5)]
    r.dz_parts, r.d_src, r.dy_parts, r.results = take(2), take(2), take(1), take(2)


def middle_scratch(na, own, width, ff_cols, chunks, hops):
    up_rows, ff_rows = width // (na * 2 * chunks), ff_cols // (na * 2)
    shapes = [
        (na, chunks, up_rows, ff_cols),
        (na, chunks, up_rows, ff_cols),
        (max(na - 1, 1), chunks, up_rows, ff_cols),
        (na, ff_rows, width),
    ]
    scratch = [pltpu.VMEM(x, BF) for x in shapes]
    block = (own, width // 2)
    four, eight = pltpu.VMEM((4,) + block, BF), pltpu.VMEM((8,) + block, BF)
    scratch += [four] * 2
    for _ in range(2):
        scratch += reduce_buffers(block, BF, ("kl", "kh"))
    scratch += [eight] * 4
    for _ in range(2):
        for hop in hops:
            scratch += reduce_buffers(block, BF, hop[::-1])
    scratch += [eight] * 4 + [pltpu.VMEM((4, own, width), BF)]
    return scratch + [pltpu.VMEM(block, F32)] * 2


def set_places(r):
    size = r.links.size
    r.seqs, r.wide = r.keep[0].shape[:2]
    r.width = r.table.shape[1]
    r.own = r.dy_out.shape[0]
    copies = size["ba"] * 2
    r.blocks, r.ff_rows = r.width // (copies * r.chunks), r.u.shape[1] // copies

    def up_at(ba, chunk, near):
        start = ((ba * r.chunks + chunk) * 2 + near) * r.blocks
        return pl.ds(pl.multiple_of(start, 8), r.blocks)

    def down_at(ba, near):
        return pl.ds(pl.multiple_of((ba * 2 + near) * r.ff_rows, 8), r.ff_rows)

    r.up_at, r.down_at = up_at, down_at


def middle(r):
    links, size, here, parted = r.links, r.links.size, r.links.here, r.parted
    att, proj, gains, results = r.keep[0], r.proj, r.gains, r.results
    seqs, width, own_rows, half = r.seqs, r.width, r.own, r.width // 2
    up, down, u_ref, hid, low, wide_in = r.up, r.down, r.u, r.hid, r.low, r.wide_in
    d_up, d_down, up_at, down_at = r.d_up, r.d_down, r.up_at, r.down_at

    def blk_index(k):
        return (k % 2) * 2 + k // 2

    for s in range(seqs):
        part = dot(att[s], proj[...], 0, 0).astype(BF)
        for j in range(LANES // own_rows):
            block = part[j * own_rows : (j + 1) * own_rows]
            at = blk_index(s * (LANES // own_rows) + j)
            r.blk_src[0][at], r.blk_src[1][at] = block[:, :half], block[:, half:]
    bufs = r.blk_buffers
    jobs = [
        Reduce(links, r.blk_src[i], results[i], ("kl", "kh"), bufs[i][:2], bufs[i][2:])
        for i in range(2)
    ]
    for j in jobs:
        j.step()
    x = dot(r.own_hot, r.table[...])
    r.tick()
    run(jobs)
    x2 = x + jnp.concatenate([results[0][...], results[1][...]], 1)
    unit_mid, scale_mid = norm_parts(x2)
    low_own = (unit_mid * gains[1:2]).astype(BF)

    def start_spread(value, parts):
        gathers = []
        for i, route in enumerate(r.hops):
            me = links.number(route[::-1], {})
            parts[i][me] = value[:, i * half : (i + 1) * half]
            gathers.append(Gather(links, parts[i].at[me], parts[i], route, None))
        for j in gathers:
            j.step()
        return gathers

    def swapped(j):
        kl, kh, bl = j // 4, j // 2 % 2, j % 2
        return (kl * 2 + bl) * 2 + kh

    def end_spread(gathers, parts, whole):
        run(gathers)
        for j in range(8):
            span = slice(j * own_rows, (j + 1) * own_rows)
            whole[span, 0:half] = parts[0][j]
            whole[span, half:] = parts[1][swapped(j)]

    def start_sum(parts, buffers):
        routes = [h[::-1] for h in r.hops]
        jobs = [
            Reduce(links, parts[i], results[i], routes[i], buffers[i][:3], buffers[i][3:])
            for i in range(2)
        ]
        for j in jobs:
            j.step()
        return jobs

    gathers = start_spread(low_own, r.low_parts)
    r.tick()
    end_spread(gathers, r.low_parts, low)
    r.weights_here()
    group = 8 * own_rows
    step = 2 * own_rows

    def hidden(i, carry):
        span = pl.ds(pl.multiple_of(i * step, step), step)
        u = dot(low[span, :], up[...])
        u_ref[span, :] = u
        t = jnp.tanh(GELU_SCALE * (u + GELU_CUBE * u * u * u))
        hid[span, :] = (0.5 * u * (1.0 + t)).astype(BF)
        return carry

    lax.fori_loop(0, group // step, hidden, 0)
    for i in range(group // step):
        part = dot(hid[i * step : (i + 1) * step], down[...]).astype(BF)
        for n in range(2):
            block = part[n * own_rows : (n + 1) * own_rows]
            j = 2 * i + n
            r.z_src[0][j], r.z_src[1][swapped(j)] = block[:, :half], block[:, half:]
    jobs = start_sum(r.z_src, r.z_buffers)
    r.tick()
    run(jobs)
    r.tick()
    x3 = x2 + jnp.concatenate([results[0][...], results[1][...]], 1)

    unit_last, scale_last = norm_parts(x3)
    c_low = (unit_last * gains[2:3]).astype(BF)
    logits = dot(c_low, r.head[...])
    lane = lax.broadcasted_iota(jnp.int32, logits.shape, 1).astype(F32)
    weight, kind = r.weight, r.kind
    masked = jnp.where((lane >= r.low_end) & (lane < r.high_end), logits, -1e30)
    top = jnp.max(masked, 1, keepdims=True)
    expo = jnp.exp(masked - top)
    expo_sum = jnp.sum(expo, 1, keepdims=True)
    hit = jnp.where(lane == r.target, 1.0, 0.0)
    picked = jnp.sum(hit * logits, 1, keepdims=True)
    row_loss = (jnp.log(expo_sum) + top - picked) * weight
    losses = [jnp.sum(jnp.where(kind == j, row_loss, 0.0)) for j in range(PICKS)]
    d_logits = (weight * (expo / expo_sum - hit)).astype(BF)
    dx3, gain_last = norm_back(unit_last, scale_last, gains[2:3], dot(d_logits, r.head[...], 1, 1))
    gathers = start_spread(dx3.astype(BF), r.dz_parts)
    r.head_out[...] = dot(c_low, d_logits, 0, 0).astype(BF)
    end_spread(gathers, r.dz_parts, wide_in)

    def hidden_back(i, carry):
        span = pl.ds(pl.multiple_of(i * step, step), step)
        d_hid = dot(wide_in[span, :], down[...], 1, 1)
        u = u_ref[span, :]
        t = jnp.tanh(GELU_SCALE * (u + GELU_CUBE * u * u * u))
        slope = GELU_SCALE * (1.0 + 3.0 * GELU_CUBE * u * u)
        u_ref[span, :] = d_hid * (0.5 * (1.0 + t) + 0.5 * u * (1.0 - t * t) * slope)
        return carry

    lax.fori_loop(0, group // step, hidden_back, 0)
    for i in range(group // step):
        du = u_ref[i * step : (i + 1) * step].astype(BF)
        part = dot(du, up[...], 1, 1).astype(BF)
        for n in range(2):
            block = part[n * own_rows : (n + 1) * own_rows]
            j = 2 * i + n
            r.d_src[0][j], r.d_src[1][swapped(j)] = block[:, :half], block[:, half:]
    jobs = start_sum(r.d_src, r.low_buffers)
    r.free_weights()
    du = u_ref[...].astype(BF)
    for i in range(0, width, LANES):
        d_up[i : i + LANES] = dot(low[:, i : i + LANES], du, 0, 0).astype(BF)
    sent_up, sent_down = [], []
    for n in range(size["ba"] if parted else 0):
        for chunk in range(r.chunks):
            part = d_up.at[up_at(n, chunk, links.at(r.near, 1))]
            sent_up.append(links.send(part, r.up_got.at[n, chunk], {r.near: 1}))
    for i in range(0, hid.shape[1], LANES):
        d_down[i : i + LANES] = dot(hid[:, i : i + LANES], wide_in[...], 0, 0).astype(BF)
    run(jobs)
    d_low = jnp.concatenate([results[0][...], results[1][...]], 1)
    d_mid, gain_mid = norm_back(unit_mid, scale_mid, gains[1:2], d_low)
    dy = (dx3 + d_mid).astype(BF)
    r.dy_out[...] = dy
    small_out = r.small_out
    small_out[...] = jnp.zeros_like(small_out)
    small_out[0:1] = gain_mid
    small_out[1:2] = gain_last
    lane = lax.broadcasted_iota(jnp.int32, (1, width), 1)
    for j in range(PICKS):
        small_out[2:3] += jnp.where(lane == j, losses[j], 0.0)
    me = links.number(("kl", "kh"), {})
    r.dy_parts[0][me] = dy
    run([Gather(links, r.dy_parts[0].at[me], r.dy_parts[0], ("kh", "kl"), None)])

    for s in range(seqs):
        first = r.dy_parts[0][blk_index(2 * s)]
        second = r.dy_parts[0][blk_index(2 * s + 1)]
        d_rows = jnp.concatenate([first, second], 0)
        r.datt[s] = dot(proj[...], d_rows, 1, 1).astype(BF)
        part = dot(att[s], d_rows)
        if s:
            part = part + r.proj_out[...]
        r.proj_out[...] = part
    r.d_table[...] = jnp.zeros_like(r.d_table)
    r.pairs[...] = jnp.zeros_like(r.pairs)
    for n in range(size["ba"] if parted else 0):
        block = d_down.at[down_at(n, links.at(r.near, 1))]
        sent_down.append(links.send(block, r.down_got.at[n], {r.near: 1}))
    r.backward(0, 0)
    for c in sent_up:
        c.wait_recv()
    for n in range(size["ba"] if parted else 0):
        for chunk in range(r.chunks):
            mine = d_up[up_at(n, chunk, here[r.near]), :].astype(F32)
            r.up_sum[n, chunk] = (mine + r.up_got[n, chunk].astype(F32)).astype(BF)
    sent_up = []
    for n in range(1, size["ba"] if parted else 1):
        part = r.up_sum.at[links.at("ba", n)]
        sent_up.append(links.send(part, r.up_got2.at[n - 1], {"ba": n}))
    for s in range(1, seqs):
        r.backward(s, 0)
    for c in sent_down:
        c.wait_recv()
    for n in range(size["ba"] if parted else 0):
        mine = d_down[down_at(n, here[r.near]), :].astype(F32)
        r.down_out[n] = (mine + r.down_got[n].astype(F32)).astype(BF)
    if parted:
        total = r.up_sum[here["ba"]].astype(F32)
        for n, c in enumerate(sent_up):
            c.wait_recv()
            total = total + r.up_got2[n].astype(F32)
        r.up_out[...] = total.astype(BF)


def core(rows, cols, table_t, scales, table, gains, proj, head, own, up_own, down_a, down_b, heads, ident):
    seqs, _, length = rows.shape
    wide, width = proj.shape
    na = lax.axis_size("ba")
    ff_cols, own_rows = up_own.shape[-1], own.shape[0]
    up_rows, ff_rows = width // (na * 4), ff_cols // (na * 2)
    parted = up_own.ndim == 3
    group = 8 * own_rows
    outs = [
        ((3 * wide, TABLE), F32),
        ((TABLE, TABLE), F32),
        ((2, up_rows, ff_cols) if parted else (width, ff_cols), BF),
        ((na, ff_rows, width) if parted else (ff_cols, width), BF),
        ((wide, width), F32),
        ((width, 256), BF),
        ((own_rows, width), BF),
        ((8, width), F32),
    ]
    scratch = [
        ((seqs, wide, LANES), BF),
        ((seqs, wide, LANES), BF),
        ((seqs, 2 * wide, length), BF),
        ((seqs, heads, LANES, length), BF),
        ((seqs, 8, length), F32),
        ((TABLE, length), BF),
        ((LANES, length), F32),
        ((width, ff_cols), BF),
        ((ff_cols, width), BF),
        ((group, ff_cols), F32),
        ((group, ff_cols), BF),
        ((group, width), BF),
        ((group, width), BF),
        ((seqs, wide, LANES), BF),
        ((2 * wide, length), BF),
        ((wide, LANES), BF),
        ((width, ff_cols), BF),
        ((ff_cols, width), BF),
    ]
    scratch = [pltpu.VMEM(*x) for x in scratch]
    scratch += middle_scratch(na, own_rows, width, ff_cols, 2, (HOP_ONE, HOP_TWO))
    copies = 2 * (na - 1) + 4 * na + 4 + 4 * 6 + 2 + 4 * na + na
    scratch += [
        pltpu.SemaphoreType.DMA((2 + 2 * na,)),
        pltpu.SemaphoreType.DMA((copies,)),
        pltpu.SemaphoreType.DMA((copies,)),
    ]
    vmem = pl.BlockSpec(memory_space=pltpu.VMEM)
    return pl.pallas_call(
        functools.partial(core_kernel, heads, parted),
        out_shape=[jax.ShapeDtypeStruct(*x) for x in outs],
        in_specs=[vmem] * 12,
        out_specs=[vmem] * len(outs),
        scratch_shapes=scratch,
        compiler_params=pltpu.CompilerParams(
            collective_id=ident, has_side_effects=True, vmem_limit_bytes=62 * 2**20
        ),
    )(rows, cols, table_t, scales, table, gains, proj, head, own, up_own, down_a, down_b)


EARLY = ("ba", "bl", "kh", "bc", "kl")
TABLE_WAYS = (("ba", "bl", "bc"), ("ba", "bc", "bl"))
PROJ_WAY = ("ba", "bl", "bc")
TEAM = ("bl", "bc", "kl")
TEAM_HOPS = (("bl", "bc", "kl"), ("bc", "bl", "kl"))
EMBED_WAYS = (("ba", "bl", "bc", "kh", "kl"), EARLY)


def slots(axes, route):
    back, result = route[::-1], []
    for i in range(2 ** len(axes)):
        bits = {a: i >> (len(axes) - 1 - n) & 1 for n, a in enumerate(axes)}
        result.append(sum(bits[a] << (len(back) - 1 - n) for n, a in enumerate(back)))
    return result


def tile_column(kh, t):
    per = HEADS // 4
    t = jnp.minimum(t, 3 * per - 1) if not isinstance(t, int) else min(t, 3 * per - 1)
    return t // per * 2 * per + per * kh + t % per


def grow(x, rows):
    return jnp.concatenate([x, jnp.zeros((rows - x.shape[0],) + x.shape[1:], x.dtype)], 0)


def front_kernel(heads, steps, *refs):
    refs = list(refs)

    def take(n):
        got = refs[:n]
        del refs[:n]
        return got

    r = types.SimpleNamespace(heads=heads, parted=True, steps=steps)
    r.chunks, r.near, r.hops = 4, "kh", TEAM_HOPS
    embed, w_qkv, w_up, w_down, proj_in, tiny, head_in, info, lanes, units, places = take(11)
    r.d_table, r.pairs, r.up_out, r.down_out, r.proj_out, r.head_out = take(6)
    r.dy_out, r.small_out, r.table, w_own, r.gains, hot_out = take(6)
    r.keep = take(7)
    r.up, r.down, r.u, r.hid, r.low, r.wide_in = take(6)
    r.datt, r.grad, r.grad_q = take(3)
    r.d_up, r.d_down = r.up, r.down
    e_parts = take(2)
    tiny_got, w_low, w_got, info_got, up_src, up_got, proj_got, r.proj = take(8)
    head_got, r.head = take(2)
    t_parts = take(2)
    table_t, center, center_gain, scales, token_info, own_info = take(6)
    take_middle(r, take)
    local_sem, send_sem, recv_sem = refs
    links = r.links = Links(send_sem, recv_sem)
    size, here = links.size, links.here
    width = r.table.shape[1]
    half, rows = width // 2, w_qkv.shape[0]
    set_places(r)
    wide, seqs = r.wide, r.seqs
    padded = w_low.shape[0]
    table_rows = embed.shape[0]
    total, nb = 32, 8
    kl = here["kl"]
    b_here = links.number(BATCH, {})
    me = links.number(ALL, {})

    low = embed[...].astype(BF)
    for i in range(2):
        slot = links.number(EMBED_WAYS[i][::-1], {})
        e_parts[i][slot] = low[:, i * half : (i + 1) * half]
    early = links.number(EARLY[::-1], {})
    tiny_got[early] = tiny[...]
    for i in range(0, w_low.shape[1], 640):
        w_low[:, i : i + 640] = grow(w_qkv[:, i : i + 640], padded).astype(BF)
    links.greet(ALL, True)
    jobs = []
    for i in range(2):
        slot = links.number(EMBED_WAYS[i][::-1], {})
        jobs.append(Gather(links, e_parts[i].at[slot], e_parts[i], EMBED_WAYS[i], None))
    jobs.append(Gather(links, tiny_got.at[early], tiny_got, EARLY, None))
    for j in jobs:
        j.step()

    def columns_of(move):
        at = {a: links.at(a, move.get(a, 0)) for a in ALL}
        t = at["kl"] * nb + (at["ba"] * 2 + at["bl"]) * 2 + at["bc"]
        return pl.ds(pl.multiple_of(tile_column(at["kh"], t) * LANES, LANES), LANES)

    w_sent = []
    for move in links.moves(ALL):
        w_sent.append(links.send(w_low.at[:, columns_of(move)], w_got.at[me], move))
    own_tile = pltpu.make_async_copy(w_low.at[:, columns_of({})], w_got.at[me], local_sem.at[0])
    own_tile.start()
    blk_here = links.number(BLK, {})
    info_got[blk_here] = info[...]
    info_sent = start_scatters(links, [(info_got.at[blk_here], info_got, BLK, "direct")])

    place = r.down.at[r.down_at(here["ba"], here["kh"])]
    place[...] = w_down[...].astype(BF)
    down_first = [links.send(place, place, {"ba": 1})]

    for g in range(8):
        pieces = []
        for c in range(4):
            i = ((c // 2 * 4 + g // 2) * 2 + c % 2) * 2 + g % 2
            pieces.append(w_up[:, i * r.ff_rows : (i + 1) * r.ff_rows])
        up_src[g] = grow(jnp.concatenate(pieces, 1), padded).astype(BF)
    for j in jobs:
        j.step()
    member = links.number(TEAM, {})
    up_sent = start_scatters(links, [(up_src, up_got, TEAM, "scatter")])
    up_got[member] = up_src[member]
    proj_slot = links.number(PROJ_WAY[::-1], {})
    proj_got[proj_slot] = proj_in[...]
    head_got[early] = head_in[...]
    run(jobs)
    for c in up_sent:
        c.wait_recv()
    up_first = []
    for c in range(4):
        parts = [up_got[c * 2 + n].astype(F32)[:rows] for n in range(2)]
        place = r.up.at[r.up_at(here["ba"], c, here["kh"])]
        place[...] = jnp.concatenate(parts, 0).astype(BF)
        up_first.append(links.send(place, place, {"ba": 1}))

    where = [slots(ALL, way) for way in EMBED_WAYS]
    for i in range(total):
        span = slice(i * table_rows, (i + 1) * table_rows)
        r.table[span, 0:half] = e_parts[0][where[0][i]]
        r.table[span, half:] = e_parts[1][where[1][i]]
    flat = tiny_got[...].reshape(total * 16, LANES)
    row = lax.broadcasted_iota(jnp.int32, (total * 16, width), 0)
    local_row = lax.broadcasted_iota(jnp.int32, (LANES, width), 0)
    r.gains[...] = jnp.zeros_like(r.gains)

    def gain_row(j):
        pick = jnp.where(row == units[0:1] + j, 1.0, 0.0).astype(BF)
        spread = dot(flat, pick, 0, 0)
        r.gains[j : j + 1] = jnp.sum(
            jnp.where(local_row == units[1:2], spread, 0.0), 0, keepdims=True
        )

    gain_row(0)
    for i in range(0, TABLE, 64):
        part = r.table[i : i + 64].astype(F32)
        part = part - jnp.mean(part, 1, keepdims=True)
        center[i : i + 64] = part
        center_gain[i : i + 64] = (part * r.gains[0:1]).astype(BF)
    own_tile.wait()
    for c in w_sent:
        c.wait_recv()
    for i in range(0, total, 2):
        pair = [w_got[i + n].astype(F32)[:rows] for n in range(2)]
        w_own[i * rows : (i + 2) * rows] = jnp.concatenate(pair, 0).astype(BF)
    tile = dot(center_gain[...], w_own[...]).T.astype(BF)
    tables = []
    for i in range(2):
        slot = links.number(TABLE_WAYS[i][::-1], {})
        mine = t_parts[i].at[kl]
        mine[slot] = tile[i * LANES // 2 : (i + 1) * LANES // 2]
        tables.append(Gather(links, mine.at[slot], mine, TABLE_WAYS[i], None))
        tables[i].step()

    late = []
    proj_job = Gather(links, proj_got.at[proj_slot], proj_got, PROJ_WAY, None)
    proj_job.step()
    head_job = Gather(links, head_got.at[early], head_got, EARLY, None)

    first = FIRST_PLACE - 1
    n_places = TABLE - first
    spots = center[first:TABLE]
    gram = dot(spots, center[...], 1, 1, HIGH)
    own_square = jnp.sum(spots * spots, 1, keepdims=True)
    every = center[...]
    every = dot(jnp.ones((8, width), F32), every * every, 1, 1, HIGH)[0:1]
    scale = lax.rsqrt((2.0 * gram + own_square + every) / width + 1e-05)
    lane = lax.broadcasted_iota(jnp.int32, scale.shape, 1)
    scale = jnp.where(lane < FIRST_PLACE, scale, 0.0)
    high = scale.astype(BF)
    scales[0:n_places] = high
    scales[n_places:] = (scale - high.astype(F32)).astype(BF)
    for j in tables:
        j.step()
    for c in down_first:
        c.wait_recv()
    for n in range(2):
        place = r.down.at[r.down_at(n, here["kh"])]
        late.append(links.send(place, place, {"kh": 1}))

    for c in info_sent:
        c.wait_recv()
    fields = info_got[...].reshape(4 * info.shape[0], LANES)
    length = lanes.shape[1]
    lane_time, lane_place, lane_pos = (lanes[i : i + 1] for i in range(3))
    sub = lax.broadcasted_iota(jnp.int32, (LANES, length), 0).astype(F32)
    for s in range(seqs):
        pick = jnp.where(places[0 : fields.shape[0], s : s + 1] == lane_time, 1.0, 0.0)
        by_lane = dot(fields, pick, 0, 0, HIGH)
        code = jnp.sum(jnp.where(sub == lane_place, by_lane, 0.0), 0, keepdims=True)
        code = code + jnp.where(lane_place == OBS, float(PATCH), 0.0)
        code = code + jnp.where(lane_place == OBS + 1, float(PATCH + RET_BINS), 0.0)
        code = code + jnp.where(lane_place == OBS + 2, float(PATCH + RET_BINS + ACTIONS), 0.0)
        token_info[s, 0:1] = jnp.where(lane_place < 0.0, -1.0, code)
        token_info[s, 1:2] = by_lane[OBS + 4 : OBS + 5]
        own_info[s] = dot(pick[:, 0:LANES], fields, 0, 0, HIGH)
        for j in tables:
            if j.stage < 3:
                j.step()
    run(tables)
    other = []
    for i in range(2):
        mine = t_parts[i].at[kl]
        other.append(links.send(mine, mine, {"kl": 1}))
    proj_job.step()
    gain_row(1)
    gain_row(2)
    for c in other:
        c.wait_recv()
    for i in range(2):
        order = slots(BATCH, TABLE_WAYS[i])
        for n in range(2):
            for b in range(nb):
                start = (n * nb + b) * LANES + i * LANES // 2
                table_t[start : start + LANES // 2] = t_parts[i][n, order[b]]

    parts = [
        pl.ds(pl.multiple_of(i * 2 * wide + kl * wide, 64), wide) for i in range(3)
    ]
    query_pos = places[0:LANES, 2:3]

    def forward(s, carry):
        code = token_info[s, 0:1].astype(jnp.int32)
        tokens = (code, lane_pos, token_info[s, 1:2], lane_place.astype(jnp.int32))
        seg_col = own_info[s, :, OBS + 4 : OBS + 5]
        attend_seq(s, heads, tokens, query_pos, seg_col, table_t, parts, scales, r.keep)
        return carry

    for c in up_first:
        c.wait_recv()
    for n in range(2):
        for chunk in range(4):
            place = r.up.at[r.up_at(n, chunk, here["kh"])]
            late.append(links.send(place, place, {"kh": 1}))
    head_job.step()
    forward(0, 0)
    proj_job.step()
    head_job.step()
    forward(1, 0)
    run([proj_job])
    order = slots(BATCH, PROJ_WAY)
    for b in range(0, nb, 2):
        pair = [proj_got[order[b + n]].astype(F32)[:rows] for n in range(2)]
        r.proj[b * rows : (b + 2) * rows] = jnp.concatenate(pair, 0).astype(BF)
    head_job.step()

    own = r.own
    mine = own_info[here["kh"], pl.ds(pl.multiple_of(kl * own, 8), own), :]
    slot = lax.broadcasted_iota(jnp.int32, (own, 1), 0) + kl * own
    steps = r.steps
    kind = jnp.where(slot >= 3 * steps, 3.0, jnp.where(slot >= 2 * steps, 2.0, jnp.where(slot >= steps, 1.0, 0.0)))

    def by_kind(*options):
        value = options[3]
        for j in range(3):
            value = jnp.where(kind == j, options[j], value)
        return value

    ret, act, rew = (mine[:, OBS + i : OBS + i + 1] for i in range(3))
    code = by_kind(
        mine[:, OBS - 1 : OBS], ret + PATCH, act + (PATCH + RET_BINS), mine[:, 0:1]
    )
    place = by_kind(OBS - 1.0, float(OBS), OBS + 1.0, 0.0) + FIRST_PLACE
    r.kind = kind
    r.low_end = by_kind(0.0, float(RET_BINS), float(RET_BINS + ACTIONS), 0.0)
    r.high_end = by_kind(
        float(RET_BINS), float(RET_BINS + ACTIONS), float(HEAD_COLS), float(RET_BINS)
    )
    r.target = by_kind(ret, act + RET_BINS, rew + (RET_BINS + ACTIONS), 0.0 * ret)
    counts = jnp.sum(tiny_got[...].astype(F32), 0)[3:4]
    per_game = 1.0 / (GAMES * jnp.maximum(counts, 1.0))
    lane = lax.broadcasted_iota(jnp.int32, (own, LANES), 1).astype(F32)
    game = jnp.where(lane == mine[:, OBS + 3 : OBS + 4], per_game, 0.0)
    r.weight = jnp.where(kind < 3.0, jnp.sum(game, 1, keepdims=True), 0.0)
    columns = lax.broadcasted_iota(jnp.int32, (own, TABLE), 1).astype(F32)
    r.own_hot = jnp.where((columns == code) | (columns == place), 1.0, 0.0).astype(BF)
    hot_out[...] = r.own_hot

    def tick():
        if head_job.stage < len(head_job.route):
            head_job.step()

    def weights_here():
        run([head_job])
        order = slots(ALL, EARLY)
        for i in range(0, total, 2):
            pair = [head_got[order[i + n]].astype(F32)[:rows] for n in range(2)]
            r.head[i * rows : (i + 2) * rows] = jnp.concatenate(pair, 0).astype(BF)
        for c in late:
            c.wait_recv()

    def free_weights():
        links.finish(late + down_first + up_first)

    r.tick, r.weights_here, r.free_weights = tick, weights_here, free_weights

    def backward(s, carry):
        attend_back_seq(
            s,
            heads,
            width,
            token_info[s, 0:1].astype(jnp.int32),
            lane_place.astype(jnp.int32),
            r.keep,
            r.datt,
            r.d_table,
            r.pairs,
            r.grad,
            r.grad_q,
        )
        return carry

    r.backward = backward
    middle(r)
    links.finish()


def front(embed, w_qkv, w_up, w_down, proj_rows, tiny, head, info, steps, ident):
    rows, width = w_qkv.shape[0], embed.shape[1]
    ff_rows = w_down.shape[0]
    ff_cols, na, seqs, padded = 4 * ff_rows, 2, 2, proj_rows.shape[0]
    wide, heads = width // 4, HEADS // 4
    own = seqs * LANES // 4
    group = 8 * own
    length = up_to(TSTEP * steps, LANES)
    tail = length - TSTEP * steps
    place_of = np.repeat(np.array(PLACES), steps)
    time_of = np.tile(np.arange(steps), TSTEP)
    lanes = np.zeros((8, length), np.float32)
    lanes[0] = np.pad(time_of, (0, tail), constant_values=-5)
    lanes[1] = np.pad(place_of, (0, tail), constant_values=-1000)
    lanes[2] = np.pad(time_of * TSTEP + place_of, (0, tail), constant_values=1 << 20)
    units = np.zeros((8, width), np.int32)
    units[0] = np.array(slots(ALL, EARLY))[np.arange(width) // rows] * 16
    units[1] = np.arange(width) % rows
    count = info.shape[0]
    at = np.arange(4 * count)
    place, local = at % count, steps // 4
    places = np.full((max(4 * count, LANES), 8), -9, np.float32)
    for s in range(seqs):
        fits = place // local == s
        places[: 4 * count, s] = np.where(fits, at // count * local + place % local, -9)
    places[:LANES, 2] = lanes[2, :LANES]
    outs = [
        ((3 * wide, TABLE), F32),
        ((TABLE, TABLE), F32),
        ((4, width // 16, ff_cols), BF),
        ((na, ff_rows, width), BF),
        ((wide, width), F32),
        ((width, 256), BF),
        ((own, width), BF),
        ((8, width), F32),
        ((TABLE, width), BF),
        ((width, LANES), BF),
        ((8, width), F32),
        ((own, TABLE), BF),
    ]
    n_places = TABLE - FIRST_PLACE + 1
    scratch = [
        ((seqs, wide, LANES), BF),
        ((seqs, wide, LANES), BF),
        ((seqs, 2 * wide, length), BF),
        ((seqs, heads, LANES, length), BF),
        ((seqs, 8, length), F32),
        ((TABLE, length), BF),
        ((LANES, length), F32),
        ((width, ff_cols), BF),
        ((ff_cols, width), BF),
        ((group, ff_cols), F32),
        ((group, ff_cols), BF),
        ((group, width), BF),
        ((group, width), BF),
        ((seqs, wide, LANES), BF),
        ((2 * wide, length), BF),
        ((wide, LANES), BF),
        ((32, TABLE // 32, width // 2), BF),
        ((32, TABLE // 32, width // 2), BF),
        ((32, 16, LANES), BF),
        ((padded, 3 * width), BF),
        ((32, padded, LANES), BF),
        ((4, count, LANES), F32),
        ((8, padded, ff_cols), BF),
        ((8, padded, ff_cols), BF),
        ((8, padded, width), BF),
        ((wide, width), BF),
        ((32, padded, 256), BF),
        ((width, 256), BF),
        ((2, 8, LANES // 2, TABLE), BF),
        ((2, 8, LANES // 2, TABLE), BF),
        ((16 * LANES, TABLE), BF),
        ((TABLE, width), F32),
        ((TABLE, width), BF),
        ((2 * n_places, TABLE), BF),
        ((seqs, 8, length), F32),
        ((seqs, LANES, LANES), F32),
    ]
    scratch = [pltpu.VMEM(*x) for x in scratch]
    scratch += middle_scratch(na, own, width, ff_cols, 4, TEAM_HOPS)
    copies = 15 + 31 + 3 + 7 + 6 + 2 + 1 + 3 + 5 + 4 + 10 + 4 + 24 + 2 + 10 + 4
    scratch += [
        pltpu.SemaphoreType.DMA((1,)),
        pltpu.SemaphoreType.DMA((copies,)),
        pltpu.SemaphoreType.DMA((copies,)),
    ]
    vmem = pl.BlockSpec(memory_space=pltpu.VMEM)
    arrays = (embed, w_qkv, w_up, w_down, proj_rows, tiny, head, info)
    arrays += (jnp.asarray(lanes), jnp.asarray(units), jnp.asarray(places))
    return pl.pallas_call(
        functools.partial(front_kernel, heads, steps),
        out_shape=[jax.ShapeDtypeStruct(*x) for x in outs],
        in_specs=[vmem] * len(arrays),
        out_specs=[vmem] * len(outs),
        scratch_shapes=scratch,
        compiler_params=pltpu.CompilerParams(
            collective_id=ident, has_side_effects=True, vmem_limit_bytes=63 * 2**20
        ),
    )(*arrays)


def over_rows(ref, body, start):
    rows = ref.shape[0]
    if rows % 8:
        return body(slice(0, rows), start)

    def step(i, carry):
        return body(pl.ds(pl.multiple_of(i * 8, 8), 8), carry)

    return lax.fori_loop(0, rows // 8, step, start)


def lane_sums(values, offset):
    lane = lax.broadcasted_iota(jnp.int32, (8, LANES), 1)
    block = jnp.zeros((8, LANES), F32)
    for i, v in enumerate(values):
        block = jnp.where(lane == i + offset, v, block)
    return block


def sum_squares(ref):
    rows, cols = ref.shape
    height = 8 if rows % 8 == 0 else rows

    def add(part, acc):
        v = ref[part, :]
        return acc + v * v

    return over_rows(ref, add, jnp.zeros((height, cols), F32))


def group_sums(refs):
    sums = [jnp.sum(sum_squares(r)) for r in refs[:6]]
    square = refs[6][...] * refs[6][...]
    return sums + [jnp.sum(square[i : i + 1]) for i in range(3)]


def squares_kernel(*refs):
    grads, masters = refs[:7], refs[7:14]
    losses, out, mine, slots, send_sem, recv_sem = refs[14:]
    links = Links(send_sem, recv_sem)
    block = lane_sums(group_sums(grads), 0) + lane_sums(group_sums(masters), 9)
    links.greet(ALL, True)
    out[...] = sum_everywhere(links, block + losses[...], mine, slots)
    links.finish()


TILE_WAYS = (("kl", "bc", "bl", "ba"), ("kl", "bl", "bc", "ba"))
PROJ_BACK = ("bc", "bl", "ba")
BACK_WAYS = (("kl", "kh", "bc", "bl", "ba"), ("kl", "bc", "kh", "bl", "ba"))
MISC_BACK = BACK_WAYS[1]


def slots_for(axes, route):
    return slots(axes, route[::-1])


def back_kernel(*refs):
    refs = list(refs)

    def take(n):
        got = refs[:n]
        del refs[:n]
        return got

    d_table, pairs, up_in, down_in, proj_in, head_in, dy, small, table, w_own = take(10)
    gains, own_hot, units, losses = take(4)
    masters = take(7)
    grads, sums = take(7), take(1)[0]
    t_src, e_src, t_out, e_out = take(2), take(2), take(2), take(2)
    proj_src, misc_src, gain_src, proj_out, misc_out, gain_out = take(6)
    center, center_gain, base, dw_src, dw_got, up_src, up_got = take(7)
    t_bufs = [take(7), take(7)]
    e_bufs = [take(9), take(9)]
    proj_bufs, misc_bufs, gain_bufs, down_bufs = take(5), take(9), take(9), take(1)
    mine, slots_got, local_sem, send_sem, recv_sem = refs
    links = Links(send_sem, recv_sem)
    size, here = links.size, links.here
    width = table.shape[1]
    half, rows, padded = width // 2, grads[1].shape[0], dw_src.shape[1]
    wide, total, nb = proj_in.shape[0], 32, 8
    me = links.number(ALL, {})

    for ref in t_src:
        ref[...] = jnp.zeros_like(ref)
    order = [slots_for(("kl",) + BATCH, way) for way in TILE_WAYS]
    for v in range(2):

        @pl.when(here["kl"] == v)
        def _(v=v):
            for p in range(3):
                for n in range(wide // 64):
                    unit = (p * 2 + v) * (wide // 64) + n
                    start = p * wide + n * 64
                    value = d_table[start : start + 64].astype(BF)
                    t_src[unit % 2][order[unit % 2][unit // 2]] = value

    place = slots_for(BATCH, PROJ_BACK)
    for b in range(nb):
        proj_src[place[b]] = grow(proj_in[b * rows : (b + 1) * rows], padded).astype(BF)
    links.greet(ALL, True)

    def reduction(src, out, way, bufs):
        n = len(way)
        return Reduce(links, src, out, way, bufs[:n], bufs[n:])

    tiles = [reduction(t_src[i], t_out[i], TILE_WAYS[i], t_bufs[i]) for i in range(2)]
    for j in tiles:
        j.step()
    for c in range(4):
        for n in range(2):
            part = up_in[c].astype(F32)[n * rows : (n + 1) * rows]
            up_src[c * 2 + n] = grow(part, padded).astype(BF)
    up_sent = start_scatters(links, [(up_src, up_got, TEAM, "scatter")])
    member = links.number(TEAM, {})
    up_got[member] = up_src[member]
    jobs = [
        reduction(proj_src, proj_out, PROJ_BACK, proj_bufs),
        reduction(down_in, grads[4], ("ba",), down_bufs),
    ]
    for j in jobs:
        j.step()

    owner = lax.broadcasted_iota(jnp.int32, (total, width), 0)
    inner = lax.broadcasted_iota(jnp.int32, (LANES, width), 0)
    inner = jnp.where(inner == units[1:2], 1.0, 0.0)

    def by_owner(row):
        return dot(jnp.where(owner == units[0:1], row, 0.0), inner, 1, 1, HIGH)

    mid, last = by_owner(small[0:1]), by_owner(small[1:2])
    sub = lax.broadcasted_iota(jnp.int32, (padded - rows, 256), 0)
    place = slots_for(ALL, MISC_BACK)
    for i in range(total):
        first, second = (
            jnp.concatenate([v[i : i + 1], v[i : i + 1]], 1) for v in (mid, last)
        )
        tail = jnp.where(sub == 0, first, jnp.where(sub == 1, second, 0.0))
        if i % 2 == 0:
            pair = head_in[i * rows : (i + 2) * rows].astype(F32)
        block = pair[i % 2 * rows : (i % 2 + 1) * rows]
        misc_src[place[i]] = jnp.concatenate([block, tail], 0).astype(BF)
    misc_job = reduction(misc_src, misc_out, MISC_BACK, misc_bufs)
    misc_job.step()
    for j in tiles:
        j.step()

    for i in range(0, TABLE, 64):
        part = table[i : i + 64].astype(F32)
        part = part - jnp.mean(part, 1, keepdims=True)
        center[i : i + 64] = part
        center_gain[i : i + 64] = (part * gains[0:1]).astype(BF)
    for j in tiles:
        j.step()
    for i in range(0, TABLE, LANES):
        low = center[...].astype(BF)
        part = dot(own_hot[:, i : i + LANES], dy[...], 0, 0)
        base[i : i + LANES] = part - dot(pairs[i : i + LANES].astype(BF), low)
    run(tiles)
    d_tile = jnp.concatenate([t_out[0][...], t_out[1][...]], 0).astype(BF)
    d_w = dot(center_gain[...], d_tile, 0, 1)
    for i in range(total):
        dw_src[i] = grow(d_w[i * rows : (i + 1) * rows], padded).astype(BF)

    def tile_of(move):
        at = {a: links.at(a, move.get(a, 0)) for a in ALL}
        t = at["kl"] * nb + (at["ba"] * 2 + at["bl"]) * 2 + at["bc"]
        return pl.ds(pl.multiple_of((at["kh"] * 16 + t) * LANES, LANES), LANES)

    spot = dw_got.at[:, tile_of({})]
    dw_sent = []
    for move in links.moves(ALL):
        dw_sent.append(links.send(dw_src.at[links.number(ALL, move)], spot, move))
    own_tile = pltpu.make_async_copy(dw_src.at[me], spot, local_sem.at[0])
    own_tile.start()
    order = [slots_for(ALL, way) for way in BACK_WAYS]
    gain = jnp.zeros((1, width), F32)
    for i in range(0, TABLE, LANES):
        d_norm = dot(d_tile[:, i : i + LANES], w_own[...], 0, 1)
        gain += jnp.sum(center[i : i + LANES] * d_norm, 0, keepdims=True)
        scaled = d_norm * gains[0:1]
        value = base[i : i + LANES] + scaled - jnp.mean(scaled, 1, keepdims=True)
        value = value.astype(BF)
        for n in range(0, LANES, 16):
            block = (i + n) // 16
            for side in range(2):
                part = value[n : n + 16, side * half : (side + 1) * half]
                e_src[side][order[side][block]] = part
    embeds = [reduction(e_src[i], e_out[i], BACK_WAYS[i], e_bufs[i]) for i in range(2)]
    for j in embeds:
        j.step()
    gain = by_owner(gain)
    sub = lax.broadcasted_iota(jnp.int32, (16, LANES), 0)
    place = slots_for(ALL, MISC_BACK)
    for i in range(total):
        gain_src[place[i]] = jnp.where(sub == 0, gain[i : i + 1], 0.0).astype(BF)
    gain_job = reduction(gain_src, gain_out, MISC_BACK, gain_bufs)
    gain_job.step()
    block = lane_sums(group_sums(masters), 9)
    run(jobs)

    home = 8 * links.number(BLK, {}) + links.number(BATCH, {})
    stays = home == me
    count = links.used
    links.used += 1
    left, there = home, {}
    for axis in ALL[::-1]:
        there[axis] = lax.rem(left, 2)
        left = left // 2

    def proj_copy():
        return pltpu.make_async_remote_copy(
            src_ref=proj_out.at[0:rows],
            dst_ref=grads[2],
            send_sem=send_sem.at[count],
            recv_sem=recv_sem.at[count],
            device_id=there,
            device_id_type=pl.DeviceIdType.MESH,
        )

    @pl.when(jnp.logical_not(stays))
    def _():
        proj_copy().start()

    @pl.when(stays)
    def _():
        grads[2][...] = proj_out[0:rows]

    run(embeds + [gain_job, misc_job])
    for side in range(2):
        grads[0][:, side * half : (side + 1) * half] = e_out[side][...]
    n_head = grads[5].shape[1]
    grads[5][...] = misc_out[0:rows, 0:n_head]
    grads[6][0:1] = gain_out[0:1, 0:rows]
    grads[6][1:3] = misc_out[rows : rows + 2, 0:rows]
    for c in up_sent:
        c.wait_recv()
    ff = grads[3].shape[1] // total
    for j in range(8):
        pieces = []
        for n in range(4):
            member, c = j % 4 * 2 + n % 2, j // 4 * 2 + n // 2
            pieces.append(up_got[member].astype(F32)[:rows, c * ff : (c + 1) * ff])
        grads[3][:, j * 4 * ff : (j + 1) * 4 * ff] = jnp.concatenate(pieces, 1)
    own_tile.wait()
    for c in dw_sent:
        c.wait_recv()
    per = HEADS // 4
    for c in range(6 * per):
        t = c % (2 * per) // per * 16 + c // (2 * per) * per + c % per
        value = dw_got[:, t * LANES : (t + 1) * LANES].astype(F32)[:rows]
        grads[1][:, c * LANES : (c + 1) * LANES] = value

    @pl.when(jnp.logical_not(stays))
    def _():
        proj_copy().wait_recv()
        proj_copy().wait_send()

    block = block + lane_sums(group_sums(grads), 0)
    sums[...] = sum_everywhere(links, block + losses[...], mine, slots_got)
    links.finish()


def back(got, masters, loss_tile, ident):
    rows, width = masters[1].shape[0], masters[0].shape[1]
    padded, table_rows, half = up_to(rows, 16), masters[0].shape[0], width // 2
    ff_cols = got[2].shape[2]
    units = np.zeros((8, width), np.int32)
    units[0], units[1] = np.arange(width) // rows, np.arange(width) % rows
    wide = got[4].shape[0]
    f32_tile = (8, LANES)
    outs = [(w.shape, F32) for w in masters] + [(f32_tile, F32)]
    t_block, e_block = (LANES // 2, TABLE), (table_rows, half)
    scratch = [((16,) + t_block, BF)] * 2 + [((32,) + e_block, BF)] * 2
    scratch += [(t_block, F32)] * 2 + [(e_block, F32)] * 2
    scratch += [
        ((8, padded, width), BF),
        ((32, padded, 256), BF),
        ((32, 16, LANES), BF),
        ((padded, width), F32),
        ((padded, 256), F32),
        ((16, LANES), F32),
        ((TABLE, width), F32),
        ((TABLE, width), BF),
        ((TABLE, width), F32),
        ((32, padded, LANES), BF),
        ((padded, 32 * LANES), BF),
        ((8, padded, ff_cols), BF),
        ((8, padded, ff_cols), BF),
    ]
    scratch = [pltpu.VMEM(*x) for x in scratch]
    for way in TILE_WAYS:
        scratch += reduce_buffers(t_block, BF, way)
    for way in BACK_WAYS:
        scratch += reduce_buffers(e_block, BF, way)
    scratch += reduce_buffers((padded, width), BF, PROJ_BACK)
    scratch += reduce_buffers((padded, 256), BF, MISC_BACK)
    scratch += reduce_buffers((16, LANES), BF, MISC_BACK)
    scratch += reduce_buffers(got[3].shape[1:], BF, ("ba",))
    copies = 8 + 10 + 3 + 5 + 5 + 1 + 7 + 31 + 1 + 31
    scratch += [
        pltpu.VMEM(f32_tile, F32),
        pltpu.VMEM((31,) + f32_tile, F32),
        pltpu.SemaphoreType.DMA((1,)),
        pltpu.SemaphoreType.DMA((copies,)),
        pltpu.SemaphoreType.DMA((copies,)),
    ]
    vmem = pl.BlockSpec(memory_space=pltpu.VMEM)
    arrays = tuple(got) + (jnp.asarray(units), loss_tile) + tuple(masters)
    result = pl.pallas_call(
        back_kernel,
        out_shape=[jax.ShapeDtypeStruct(*x) for x in outs],
        in_specs=[vmem] * len(arrays),
        out_specs=[vmem] * len(outs),
        scratch_shapes=scratch,
        compiler_params=pltpu.CompilerParams(
            collective_id=ident, has_side_effects=True, vmem_limit_bytes=63 * 2**20
        ),
    )(*arrays)
    return tuple(result[:7]), result[7]


def at_first(body):
    pl.when(pl.program_id(0) == 0)(body)


def moments_kernel(*refs):
    sums = refs[0]
    grads, masters, firsts, seconds = (refs[1 + 7 * i : 8 + 7 * i] for i in range(4))
    means, squares, updates = (refs[29 + 7 * i : 36 + 7 * i] for i in range(3))
    out = refs[50]
    total = sums[...]
    lane = lax.broadcasted_iota(jnp.int32, (8, LANES), 1)
    norm = jnp.sqrt(jnp.sum(jnp.where(lane < 9, total, 0.0)[0:1], 1, keepdims=True))
    factor = jnp.minimum(1.0, 0.05 / norm)

    def one(i):
        def step(part, acc):
            g = factor * grads[i][part, :]
            mean = 0.9 * firsts[i][part, :] + 0.1 * g
            square = 0.99 * seconds[i][part, :] + 0.01 * g * g
            update = (mean / (1.0 - 0.9**STEP)) / (
                jnp.sqrt(square / (1.0 - 0.99**STEP)) + 1e-08
            ) + 0.01 * masters[i][part, :]
            means[i][part, :] = mean
            squares[i][part, :] = square
            updates[i][part, :] = update
            return acc + update * update

        rows, cols = grads[i].shape
        height = 8 if rows % 8 == 0 else rows
        return over_rows(grads[i], step, jnp.zeros((height, cols), F32))

    @at_first
    def _():
        table, gains = one(0), one(6)
        values = [jnp.sum(table)] + [0.0] * 5 + [jnp.sum(gains[j : j + 1]) for j in range(3)]
        out[...] = lane_sums(values, 0)

    out[...] += lane_sums([jnp.sum(one(i)) for i in range(1, 6)], 1)


def weights_kernel(*refs):
    update_sums, sums = refs[:2]
    masters, updates = refs[2:9], refs[9:16]
    news, copies = refs[16:23], refs[23:29]
    norms_ref = refs[29]
    update_norm = jnp.sqrt(update_sums[0:1, 0:9])
    weight_norm = jnp.sqrt(sums[0:1, 9:18])
    ratio = weight_norm / update_norm

    def one(i):
        def step(part, acc):
            new = masters[i][part, :] - 0.3 * ratio[0:1, i : i + 1] * updates[i][part, :]
            news[i][part, :] = new
            copies[i][part, :] = new.astype(BF)
            return 0

        over_rows(masters[i], step, 0)

    @at_first
    def _():
        norms_ref[0:1, 0:9] = weight_norm
        norms_ref[1:2, 0:9] = update_norm
        one(0)
        for j in range(3):
            row = slice(j, j + 1)
            news[6][row] = masters[6][row] - 0.3 * ratio[0:1, 6 + j : 7 + j] * updates[6][row]

    for i in range(1, 6):
        one(i)


def by_rows(body, heads, groups, outs, tails):
    shapes = [x.shape for x in groups[0]]
    parts = 5 if all(shapes[i][0] % 80 == 0 or shapes[i][0] == 40 for i in range(1, 6)) else 1

    def spec(i, shape):
        if i in (0, 6):
            return pl.BlockSpec(shape, lambda n: (0, 0))
        return pl.BlockSpec((shape[0] // parts, shape[1]), lambda n: (n, 0))

    def whole(x):
        return pl.BlockSpec(x.shape, lambda n: (0,) * len(x.shape))

    in_specs = [whole(x) for x in heads]
    in_specs += [spec(i, s) for _ in groups for i, s in enumerate(shapes)]
    out_specs = [spec(i, x.shape) for group in outs for i, x in enumerate(group)]
    out_specs += [whole(x) for x in tails]
    return local_call(
        body,
        [x for group in outs for x in group] + tails,
        list(heads) + [x for group in groups for x in group],
        grid=(parts,),
        in_specs=in_specs,
        out_specs=out_specs,
    )


def layer_norm(v, gain):
    center = v - jnp.mean(v, -1, keepdims=True)
    return center * lax.rsqrt(jnp.mean(center * center, -1, keepdims=True) + 1e-05) * gain


def gradients(obs_tokens, returns, actions, rewards, game_ids, segments, masters):
    table, w_qkv, w_proj, w_up, w_down, w_head, gains = masters
    na, nk = lax.axis_size("ba"), 4
    nb, members = na * 4, 2 * nk
    total = nb * nk
    bl = lax.axis_index("bl")
    k = lax.axis_index("kh") * 2 + lax.axis_index("kl")
    g = bl * nk + k
    seqs, steps_here = obs_tokens.shape[:2]
    width = table.shape[1]
    rows, table_rows = w_qkv.shape[0], table.shape[0]
    steps = steps_here * nk
    heads = HEADS // nk
    wide = width // nk
    cols = 3 * wide // nb
    ff_rows = w_down.shape[0]
    padded_rows = up_to(rows, 16)
    padded_table = up_to(table_rows, 16)
    half = width // 2

    info = [obs_tokens] + [v[..., None] for v in (returns, actions, rewards, game_ids, segments)]
    info = jnp.concatenate(info, -1).reshape(seqs * steps_here, -1)
    info = pad_to(info, up_to(seqs * steps_here, 8), LANES)
    counts_here = jnp.sum((game_ids[..., None] == jnp.arange(GAMES)).astype(F32), (0, 1))
    to_heads = [(i, i % nb * nk + i // nb) for i in range(total)]
    proj_rows = pad_to(lax.ppermute(w_proj.astype(BF), ALL, to_heads), padded_rows, width)
    if total == 32 and table_rows == 16 and rows == 40 and seqs == 2 and ff_rows == 160:
        tiny = jnp.concatenate(
            [
                pad_to(gains.astype(BF), 3, LANES),
                pad_to(counts_here.astype(BF)[None], 1, LANES),
                jnp.zeros((12, LANES), BF),
            ]
        )
        got = front(
            table,
            w_qkv,
            w_up,
            w_down,
            proj_rows,
            tiny,
            pad_to(w_head.astype(BF), padded_rows, 256),
            info.astype(F32),
            steps,
            0,
        )
        losses = jnp.pad(got[7][2:3, :PICKS], ((0, 7), (18, LANES - 18 - PICKS)))
        return back(got, masters, losses, 1)
    table_bf = pad_to(table.astype(BF), padded_table, width)
    small = jnp.concatenate(
        [
            pad_to(w_head.astype(BF), rows, 256),
            pad_to(gains.astype(BF), 3, 256),
            pad_to(counts_here.astype(BF)[None], 1, 256),
            jnp.zeros((padded_rows - rows - 4, 256), BF),
        ]
    )
    qkv_blocks = w_qkv.astype(BF).reshape(rows, 3, nk, wide).transpose(2, 0, 1, 3)
    qkv_blocks = qkv_blocks.reshape(nk, rows, nb, cols).transpose(2, 0, 1, 3)
    qkv_blocks = pad_to(qkv_blocks.reshape(total, rows, cols), padded_rows, LANES)
    ff_cols = na * 2 * ff_rows
    up_blocks = w_up.astype(BF).reshape(rows, na, 2, 2, nk, ff_rows).transpose(2, 4, 0, 1, 3, 5)
    up_blocks = pad_to(up_blocks.reshape(members, rows, ff_cols), padded_rows, ff_cols)
    parted = ff_rows % 32 == 0 and nk * rows % 16 == 0
    down_low = w_down.astype(BF)
    one_way = ("ba", "bl", "bc", "kh", "kl")
    other_way = ("ba", "bl", "kh", "bc", "kl")
    items = [
        (table_bf[:, :half], "gather", one_way),
        (table_bf[:, half:], "gather", other_way),
        (small, "gather", other_way),
        (qkv_blocks, "scatter", ALL),
        (info, "direct", BLK),
        (up_blocks, "scatter", GROUP),
    ]
    if parted:
        items.append((down_low[: ff_rows // 2], "gather", ("ba",)))
    got = exchange(items, 0)
    table_left, table_right, small_all, qkv_mine, info_here, up_mine = got[:6]
    if parted:
        up_mine = up_mine[:, :rows].reshape(2, nk * rows, ff_cols)
        down_first = got[6]
    else:
        up_mine = lax.all_gather(up_mine[:, :rows], COPIES, axis=0, tiled=False)
        up_mine = up_mine.reshape(na, 2, 2, nk, rows, ff_cols).transpose(0, 2, 1, 3, 4, 5)
        up_mine = up_mine.reshape(width, ff_cols)
        down_first = lax.all_gather(down_low, COPIES, axis=0, tiled=True)

    table_all = jnp.concatenate(
        [
            natural(table_left, ALL, one_way)[:, :table_rows],
            natural(table_right, ALL, other_way)[:, :table_rows],
        ],
        2,
    ).reshape(TABLE, width)
    small_all = natural(small_all, ALL, other_way)
    gain = small_all[:, rows : rows + 3, :rows].transpose(1, 0, 2).reshape(3, width).astype(F32)
    w_mine = qkv_mine[:, :rows].reshape(width, LANES)
    scale_rows = TABLE - FIRST_PLACE + 1
    cols_mine, scale_table, center_bf, center_gain = local_call(
        table_kernel,
        [
            jax.ShapeDtypeStruct((LANES, TABLE), BF),
            jax.ShapeDtypeStruct((2 * scale_rows, TABLE), BF),
            jax.ShapeDtypeStruct((TABLE, width), BF),
            jax.ShapeDtypeStruct((TABLE, width), BF),
        ],
        (table_all, pad_to(gain, 8, width), w_mine),
        [pltpu.VMEM((TABLE, width), F32)],
    )
    table_ways = (("ba", "bl", "bc"), ("bc", "bl", "ba"))
    items = [
        (cols_mine[: LANES // 2], "gather", table_ways[0]),
        (cols_mine[LANES // 2 :], "gather", table_ways[1]),
        (proj_rows, "gather", ("ba", "bc", "bl")),
    ]
    if parted:
        items.append((down_low[ff_rows // 2 :], "gather", ("ba",)))
    got = exchange(items, 1)
    down_second = got[3] if parted else jnp.zeros((16, LANES), BF)
    qkv_table = jnp.concatenate(
        [natural(got[0], BATCH, table_ways[0]), natural(got[1], BATCH, table_ways[1])], 1
    )
    qkv_table = qkv_table[:, :cols].reshape(3 * wide, TABLE)
    proj_here = natural(got[2], BATCH, ("ba", "bc", "bl"))[:, :rows].reshape(wide, width)

    info_here = info_here[:, : seqs * steps_here].reshape(nk, seqs, steps_here, LANES)
    info_here = info_here.transpose(1, 0, 2, 3).reshape(seqs, steps, LANES)
    length = up_to(TSTEP * steps, LANES)
    place_of = np.repeat(np.array(PLACES), steps)
    time_of = np.tile(np.arange(steps), TSTEP)
    tail = length - TSTEP * steps
    pos = np.pad(time_of * TSTEP + place_of, (0, tail), constant_values=1 << 20)
    place_of = np.pad(place_of, (0, tail), constant_values=-1000)
    starts = np.array([0] * OBS + [PATCH, PATCH + RET_BINS, PATCH + RET_BINS + ACTIONS])
    codes = info_here[..., :TSTEP] + starts.astype(np.int32)
    codes = jnp.concatenate(
        [codes[..., OBS - 1 : OBS + 2], codes[..., : OBS - 1], codes[..., OBS + 2 :]], -1
    )
    codes = codes.transpose(0, 2, 1).reshape(seqs, TSTEP * steps)
    codes = jnp.pad(codes, ((0, 0), (0, tail)), constant_values=-1)
    seg = jnp.tile(info_here[..., OBS + 4], (1, TSTEP))
    seg = jnp.pad(seg, ((0, 0), (0, tail)), constant_values=-1)
    zero = jnp.zeros((seqs, length), jnp.int32)
    token_rows = jnp.stack(
        [codes, zero + jnp.asarray(pos, jnp.int32), seg, zero + jnp.asarray(place_of, jnp.int32)]
        + [zero] * 4,
        1,
    )
    token_cols = jnp.stack([zero[:, :LANES] + pos[:LANES].astype(np.int32), seg[:, :LANES]], -1)
    token_cols = jnp.pad(token_cols, ((0, 0), (0, 0), (0, LANES - 2)))

    own = seqs * LANES // nk
    slots = lax.rem(k, nk // seqs) * own + jnp.arange(own)
    seq_own = k * own // LANES
    codes_own = lax.dynamic_slice(codes, (seq_own, lax.rem(k, nk // seqs) * own), (1, own))[0]
    place_own = jnp.asarray(place_of[:LANES], jnp.int32)
    place_own = lax.dynamic_slice(place_own, (lax.rem(k, nk // seqs) * own,), (own,))
    kind = slots // steps
    info_seq = lax.dynamic_index_in_dim(info_here, seq_own, 0, False)
    info_own = info_seq.at[lax.rem(slots, steps)].get(mode="promise_in_bounds")
    counts = jnp.sum(small_all[:, rows + 3, :GAMES].astype(F32), 0)
    per_game = 1.0 / (GAMES * jnp.maximum(counts, 1.0))
    game_own = (info_own[:, OBS + 3, None] == jnp.arange(GAMES)).astype(F32)
    weight = jnp.where(kind < PICKS, jnp.sum(game_own * per_game, -1), 0.0)
    low_end = jnp.where(kind == 0, 0, jnp.where(kind == 1, RET_BINS, RET_BINS + ACTIONS))
    high_end = jnp.where(kind == 0, RET_BINS, jnp.where(kind == 1, RET_BINS + ACTIONS, HEAD_COLS))
    target = low_end + jnp.where(
        kind == 0,
        info_own[:, OBS],
        jnp.where(kind == 1, info_own[:, OBS + 1], info_own[:, OBS + 2]),
    )
    own_info = [low_end, high_end, target, weight, kind, codes_own, place_own + FIRST_PLACE]
    own_info = pad_to(jnp.stack([v.astype(F32) for v in own_info], 1), own, LANES)
    head_full = small_all[:, :rows].reshape(width, 256)
    d_table, pairs, sum_up, sum_down, d_proj, d_head, dy_own, d_small = core(
        token_rows,
        token_cols,
        qkv_table,
        scale_table,
        table_all,
        pad_to(gain, 8, width),
        proj_here,
        head_full,
        own_info,
        up_mine,
        down_first,
        down_second,
        heads,
        2,
    )
    d_gain_mid, d_gain_last = d_small[0], d_small[1]
    losses = [d_small[2, j] for j in range(PICKS)]
    columns = jnp.arange(TABLE)
    own_hot = (codes_own[:, None] == columns) | (place_own[:, None] + FIRST_PLACE == columns)
    own_hot = own_hot.astype(BF)
    if not parted:
        sum_up = sum_up.reshape(na, 2, 2, nk, rows, ff_cols).transpose(0, 2, 1, 3, 4, 5)
        sum_up = sum_up.reshape(width, ff_cols)
        sum_up = lax.psum_scatter(sum_up, COPIES, scatter_dimension=0, tiled=True)
        sum_down = lax.psum_scatter(sum_down, COPIES, scatter_dimension=0, tiled=True)

    d_table = pad_to(d_table.astype(BF).reshape(nb, cols, TABLE), LANES, TABLE)
    d_proj = pad_to(d_proj.astype(BF).reshape(nb, rows, width), padded_rows, width)
    proj_route = ("bl", "bc", "ba")
    table_routes = (("bc", "bl", "ba"), ("bl", "bc", "ba"))
    left, right, sum_proj = reduce(
        [
            for_route(d_table[..., : TABLE // 2], BATCH, table_routes[0]),
            for_route(d_table[..., TABLE // 2 :], BATCH, table_routes[1]),
            for_route(d_proj, BATCH, proj_route),
        ],
        table_routes + (proj_route,),
        [],
        3,
    )
    sum_proj = lax.ppermute(sum_proj[:rows], ALL, [(j, i) for i, j in to_heads])
    d_table_mine = jnp.concatenate([left, right], 1).astype(BF)
    d_w = dot(center_gain, d_table_mine, 0, 1)
    d_norm = dot(d_table_mine, w_mine, 0, 1)
    d_gain_first = jnp.sum(center_bf.astype(F32) * d_norm, 0)
    d_scaled = d_norm * gain[0]
    d_embed = (
        d_scaled
        - jnp.mean(d_scaled, 1, keepdims=True)
        - dot(pairs.astype(BF), center_bf)
        + dot(own_hot, dy_own, 0, 0)
    )
    d_gains = jnp.stack([d_gain_first, d_gain_mid, d_gain_last]).astype(BF)
    d_misc = jnp.concatenate(
        [
            d_head.reshape(total, rows, 256),
            pad_to(d_gains.reshape(3, total, rows).transpose(1, 0, 2), 3, 256),
            jnp.zeros((total, padded_rows - rows - 3, 256), BF),
        ],
        1,
    )
    d_w = pad_to(d_w.astype(BF).reshape(total, rows, LANES), padded_rows, LANES)
    d_embed = pad_to(d_embed.astype(BF).reshape(total, table_rows, width), padded_table, width)
    sum_up = pad_to(sum_up.reshape(members, rows, -1), padded_rows, ff_cols)
    one_way = ("kl", "kh", "bc", "bl", "ba")
    other_way = ("kl", "bc", "kh", "bl", "ba")
    arrays = [
        for_route(d_embed[..., :half], ALL, one_way),
        for_route(d_embed[..., half:], ALL, other_way),
        for_route(d_misc, ALL, other_way),
    ]
    routes = (one_way, other_way, other_way)
    if parted:
        arrays.append(sum_down)
        routes += (("ba",),)
    got = reduce(arrays, routes, [(d_w, ALL), (sum_up, GROUP)], 4)
    d_left, d_right, d_misc = got[:3]
    d_ws, ups = got[-2:]
    if parted:
        sum_down = got[3]
    d_embed = jnp.concatenate([d_left, d_right], 1)
    d_ws = d_ws[:, :rows, :cols].reshape(nb, nk, rows, cols).transpose(2, 1, 0, 3)
    d_ws = d_ws.reshape(rows, nk, 3, wide).transpose(0, 2, 1, 3).reshape(rows, 3 * width)
    ups = ups[:, :rows].reshape(2, nk, rows, na, 2, ff_rows).transpose(2, 3, 0, 4, 1, 5)
    ups = ups.reshape(rows, nb * nk * ff_rows)
    grads = (
        d_embed[:table_rows],
        d_ws.astype(F32),
        sum_proj,
        ups.astype(F32),
        sum_down.astype(F32),
        d_misc[:rows, :HEAD_COLS],
        d_misc[rows : rows + 3, :rows],
    )
    loss_tile = jnp.zeros((8, LANES), F32).at[:, 18:21].set(jnp.stack(losses))
    return grads, summed_call(squares_kernel, grads + masters + (loss_tile,), 5)


def shards(*args):
    masters, firsts, seconds = args[6:13], args[13:20], args[20:27]
    grads, sums = gradients(*args[:6], masters)
    like = [jax.ShapeDtypeStruct(w.shape, F32) for w in masters]
    low = [jax.ShapeDtypeStruct(w.shape, BF) for w in masters[:6]]
    tile = jax.ShapeDtypeStruct((8, LANES), F32)
    result = by_rows(
        moments_kernel, (sums,), (grads, masters, firsts, seconds), [like] * 3, [tile]
    )
    means, squares, updates = result[:7], result[7:14], result[14:21]
    update_sums = summed_call(all_sum_kernel, (result[21],), 6)
    result = by_rows(
        weights_kernel, (update_sums, sums), (masters, updates), [like, low], [tile]
    )
    news, copies, norms = result[:7], result[7:13], result[13][:2, :9]
    grad_norm = jnp.sqrt(jnp.sum(sums[0, :9]))
    return tuple(news) + tuple(means) + tuple(squares) + tuple(copies) + (
        grad_norm,
        sums[0, 18:21],
        norms,
    )


def solution(mesh):
    nb, nk = mesh.shape["batch"], mesh.shape["blk"]
    split = Mesh(mesh.devices.reshape(nb // 4, 2, 2, nk // 2, 2), ALL)
    rows, gains = P(ALL, None), P(None, ALL)
    weights = (rows,) * 6 + (gains,)
    in_specs = (P(BATCH, BLK, None),) + (P(BATCH, BLK),) * 5 + weights * 3
    out_specs = weights * 3 + (rows,) * 6 + (P(), P(), P())
    return jax.shard_map(
        shards, mesh=split, in_specs=in_specs, out_specs=out_specs, check_vma=False
    )
```

```python
import functools
import math
import types

import jax
import jax.numpy as jnp
import numpy as np
from jax import lax
from jax.experimental import pallas as pl
from jax.experimental.pallas import tpu as pltpu
from jax.sharding import Mesh
from jax.sharding import PartitionSpec as P

HEADS = 20
RET_BINS = 120
ACTIONS = 18
GAMES = 41
TSTEP = 39
OBS = 36
PATCH = 331
STEP = 10
HEAD_COLS = 142
TABLE = 512
PICKS = 3
LANES = 128
FIRST_PLACE = PATCH + HEAD_COLS
BF = jnp.bfloat16
F32 = jnp.float32
HIGH = lax.Precision.HIGHEST
BLK = ("kh", "kl")
GROUP = ("bl", "kh", "kl")
BATCH = ("ba", "bl", "bc")
COPIES = ("ba", "bc")
ALL = ("ba", "bl", "bc", "kh", "kl")
VMEM_LIMIT = 56 * 2**20
PLACES = list(range(OBS - 1, OBS + 2)) + [p for p in range(TSTEP) if not OBS - 1 <= p < OBS + 2]


def up_to(n, m):
    return -(-n // m) * m


def pad_to(x, rows, cols):
    if x.shape[-2:] == (rows, cols):
        return x
    widths = [(0, 0)] * (x.ndim - 2) + [(0, rows - x.shape[-2]), (0, cols - x.shape[-1])]
    return jnp.pad(x, widths)


def dot(left, right, ca=1, cb=0, precision=None):
    return lax.dot_general(
        left,
        right,
        (((ca,), (cb,)), ((), ())),
        precision=precision,
        preferred_element_type=F32,
    )


class Links:
    def __init__(self, sends, recvs):
        self.sends, self.recvs, self.open, self.used = sends, recvs, [], 0
        self.size = {a: lax.axis_size(a) for a in ALL}
        self.here = {a: lax.axis_index(a) for a in ALL}

    def at(self, axis, step):
        return lax.rem(self.here[axis] + step, self.size[axis])

    def number(self, axes, steps):
        n = 0
        for a in axes:
            n = n * self.size[a] + self.at(a, steps.get(a, 0))
        return n

    def moves(self, axes):
        result = [{}]
        for a in axes:
            result = [dict(m, **{a: r}) for m in result for r in range(self.size[a])]
        return [{a: r for a, r in m.items() if r} for m in result if any(m.values())]

    def greet(self, axes, everyone=False):
        self.hail(axes, everyone)
        self.met()

    def met(self):
        pl.semaphore_wait(pltpu.get_barrier_semaphore(), self.hailed)

    def hail(self, axes, everyone=False):
        barrier = pltpu.get_barrier_semaphore()
        if everyone:
            moves = self.moves(axes)
        else:
            moves = [{a: r} for a in axes for r in range(1, self.size[a])]
        for move in moves:
            pl.semaphore_signal(
                barrier,
                inc=1,
                device_id={a: self.at(a, r) for a, r in move.items()},
                device_id_type=pl.DeviceIdType.MESH,
            )
        self.hailed = len(moves)

    def send(self, src, dst, move):
        n, self.used = self.used, self.used + 1
        c = pltpu.make_async_remote_copy(
            src_ref=src,
            dst_ref=dst,
            send_sem=self.sends.at[n],
            recv_sem=self.recvs.at[n],
            device_id={a: self.at(a, r) for a, r in move.items()},
            device_id_type=pl.DeviceIdType.MESH,
        )
        c.start()
        self.open.append(c)
        return c

    def finish(self, copies=None):
        copies = list(self.open if copies is None else copies)
        for c in copies:
            c.wait_send()
        self.open = [c for c in self.open if not any(c is d for d in copies)]


class Gather:
    def __init__(self, links, src, dst, route, local):
        self.links, self.src, self.dst = links, src, dst
        self.route, self.local, self.waits, self.stage = list(route), local, [], 0
        self.sent = []

    def step(self):
        links = self.links
        for c in self.waits:
            c.wait_recv()
        self.waits = []
        if self.stage == len(self.route):
            return False
        if self.stage == 1 and self.local is not None:
            self.local.wait()
            self.local = None
        count = math.prod(links.size[a] for a in self.route[: self.stage])
        start = links.number(self.route[self.stage :][::-1], {}) * count
        here = self.dst.at[pl.ds(start, count)]
        block = self.src if self.stage == 0 else here
        there = self.dst.at[start] if self.stage == 0 else here
        axis = self.route[self.stage]
        for r in range(1, links.size[axis]):
            self.waits.append(links.send(block, there, {axis: r}))
        self.sent += self.waits
        self.stage += 1
        return True

    def close(self):
        if self.local is not None:
            self.local.wait()


class Reduce:
    def __init__(self, links, src, out, route, arrived, totals):
        self.links, self.now, self.out = links, src, out
        self.route, self.arrived, self.totals = list(route), arrived, totals
        self.waits, self.stage, self.done = [], 0, False

    def part(self, axis, step):
        count = self.now.shape[0] // self.links.size[axis]
        return pl.ds(self.links.at(axis, step) * count, count)

    def step(self):
        if self.done:
            return False
        if self.stage:
            axis = self.route[self.stage - 1]
            for c in self.waits:
                c.wait_recv()
            total = self.now[self.part(axis, 0)].astype(F32)
            for n in range(len(self.waits)):
                total = total + self.arrived[self.stage - 1][n].astype(F32)
            if self.stage == len(self.route):
                self.out[...] = total[0]
                self.done = True
                return False
            self.now = self.totals[self.stage - 1]
            self.now[...] = total.astype(self.now.dtype)
        axis = self.route[self.stage]
        self.waits = []
        for r in range(1, self.links.size[axis]):
            dst = self.arrived[self.stage].at[r - 1]
            self.waits.append(self.links.send(self.now.at[self.part(axis, r)], dst, {axis: r}))
        self.stage += 1
        return True


def start_scatters(links, jobs):
    copies = []
    for src, dst, axes, kind in jobs:
        me = links.number(axes, {})
        for move in links.moves(axes):
            block = src.at[links.number(axes, move)] if kind == "scatter" else src
            copies.append(links.send(block, dst.at[me], move))
    return copies


def run(jobs):
    jobs = list(jobs)
    while jobs:
        jobs = [j for j in jobs if j.step()]


def sizes_of(axes):
    return tuple(lax.axis_size(a) for a in axes)


def exchange_kernel(kinds, routes, *refs):
    count = len(kinds)
    srcs, dsts = refs[:count], refs[count : 2 * count]
    local_sem, send_sem, recv_sem = refs[2 * count :]
    links = Links(send_sem, recv_sem)
    local = []
    for i, route in enumerate(routes):
        me = links.number(route[::-1] if kinds[i] == "gather" else route, {})
        block = srcs[i].at[me] if kinds[i] == "scatter" else srcs[i]
        local.append(pltpu.make_async_copy(block, dsts[i].at[me], local_sem.at[i]))
        local[-1].start()
    everyone = any(k != "gather" for k in kinds)
    links.greet([a for a in ALL if any(a in x for x in routes)], everyone)
    gathers = [
        Gather(links, srcs[i], dsts[i], routes[i], local[i])
        for i in range(count)
        if kinds[i] == "gather"
    ]
    for j in gathers:
        j.step()
    copies = []
    for i in range(count):
        if kinds[i] != "gather":
            copies += start_scatters(links, [(srcs[i], dsts[i], routes[i], kinds[i])])
    run(gathers)
    for j in gathers:
        j.close()
    for c in copies:
        c.wait_recv()
    for i in range(count):
        if kinds[i] != "gather":
            local[i].wait()
    links.finish()


def natural(x, axes, route):
    back = route[::-1]
    x = x.reshape(sizes_of(back) + x.shape[1:])
    order = [back.index(a) for a in axes] + list(range(len(axes), x.ndim))
    return x.transpose(order).reshape((-1,) + x.shape[len(axes) :])


def for_route(x, axes, route):
    x = x.reshape(sizes_of(axes) + x.shape[1:])
    order = [axes.index(a) for a in route] + list(range(len(axes), x.ndim))
    return x.transpose(order).reshape((-1,) + x.shape[len(axes) :])


def exchange(items, ident):
    arrays, kinds, routes = zip(*items)
    shapes, copies = [], 0
    for x, kind, route in zip(arrays, kinds, routes):
        sizes = sizes_of(route)
        shape = x.shape if kind == "scatter" else (math.prod(sizes),) + x.shape
        shapes.append(jax.ShapeDtypeStruct(shape, x.dtype))
        copies += sum(sizes) - len(sizes) if kind == "gather" else math.prod(sizes) - 1
    n = len(arrays)
    return pl.pallas_call(
        functools.partial(exchange_kernel, kinds, routes),
        out_shape=shapes,
        in_specs=[pl.BlockSpec(memory_space=pl.ANY)] * n,
        out_specs=[pl.BlockSpec(memory_space=pl.ANY)] * n,
        scratch_shapes=[
            pltpu.SemaphoreType.DMA((n,)),
            pltpu.SemaphoreType.DMA((copies,)),
            pltpu.SemaphoreType.DMA((copies,)),
        ],
        compiler_params=pltpu.CompilerParams(collective_id=ident, has_side_effects=True),
    )(*arrays)


def reduce_buffers(shape, dtype, route):
    arrived, totals = [], []
    for i, axis in enumerate(route):
        rest = (math.prod(sizes_of(route[i + 1 :])),) + shape
        arrived.append(pltpu.VMEM((lax.axis_size(axis) - 1,) + rest, dtype))
        totals.append(pltpu.VMEM(rest, dtype))
    return arrived + totals[:-1]


def reduce_kernel(routes, other_axes, *refs):
    refs = list(refs)

    def take(n):
        got = refs[:n]
        del refs[:n]
        return got

    sums = len(routes)
    srcs, other_srcs = take(sums), take(len(other_axes))
    outs, other_dsts = take(sums), take(len(other_axes))
    buffers = [(take(len(r)), take(len(r) - 1)) for r in routes]
    local_sem, send_sem, recv_sem = refs
    links = Links(send_sem, recv_sem)
    local = []
    for i, axes in enumerate(other_axes):
        me = links.number(axes, {})
        local.append(
            pltpu.make_async_copy(other_srcs[i].at[me], other_dsts[i].at[me], local_sem.at[i])
        )
        local[-1].start()
    seen = [a for a in ALL if any(a in x for x in tuple(routes) + other_axes)]
    links.greet(seen, bool(other_axes))
    jobs = [
        Reduce(links, srcs[i], outs[i], routes[i], *buffers[i]) for i in range(sums)
    ]
    for j in jobs:
        j.step()
    copies = start_scatters(
        links, [(s, d, a, "scatter") for s, d, a in zip(other_srcs, other_dsts, other_axes)]
    )
    run(jobs)
    for c in copies:
        c.wait_recv()
    for c in local:
        c.wait()
    links.finish()


def reduce(arrays, routes, others, ident):
    outs = [jax.ShapeDtypeStruct(x.shape[1:], F32) for x in arrays]
    outs += [jax.ShapeDtypeStruct(x.shape, x.dtype) for x, _ in others]
    scratch = []
    for x, route in zip(arrays, routes):
        scratch += reduce_buffers(x.shape[1:], x.dtype, route)
    copies = sum(sum(sizes_of(r)) - len(r) for r in routes)
    copies += sum(math.prod(sizes_of(axes)) - 1 for _, axes in others)
    scratch += [
        pltpu.SemaphoreType.DMA((max(len(others), 1),)),
        pltpu.SemaphoreType.DMA((copies,)),
        pltpu.SemaphoreType.DMA((copies,)),
    ]
    vmem, hbm = pl.BlockSpec(memory_space=pltpu.VMEM), pl.BlockSpec(memory_space=pl.ANY)
    specs = [vmem] * len(arrays) + [hbm] * len(others)
    return pl.pallas_call(
        functools.partial(reduce_kernel, tuple(routes), tuple(axes for _, axes in others)),
        out_shape=outs,
        in_specs=specs,
        out_specs=specs,
        scratch_shapes=scratch,
        compiler_params=pltpu.CompilerParams(
            collective_id=ident, has_side_effects=True, vmem_limit_bytes=VMEM_LIMIT
        ),
    )(*arrays, *[x for x, _ in others])


def sum_everywhere(links, value, mine, slots):
    mine[...] = value
    moves = links.moves(ALL)
    waits = [links.send(mine, slots.at[n], move) for n, move in enumerate(moves)]
    for c in waits:
        c.wait_recv()
    return value + jnp.sum(slots[...], 0)


def all_sum_kernel(value, out, mine, slots, send_sem, recv_sem):
    links = Links(send_sem, recv_sem)
    links.greet(ALL, True)
    out[...] = sum_everywhere(links, value[...], mine, slots)
    links.finish()


def summed_call(body, arrays, ident):
    vmem = pl.BlockSpec(memory_space=pltpu.VMEM)
    copies = math.prod(sizes_of(ALL)) - 1
    return pl.pallas_call(
        body,
        out_shape=jax.ShapeDtypeStruct((8, LANES), F32),
        in_specs=[vmem] * len(arrays),
        out_specs=vmem,
        scratch_shapes=[
            pltpu.VMEM((8, LANES), F32),
            pltpu.VMEM((copies, 8, LANES), F32),
            pltpu.SemaphoreType.DMA((copies,)),
            pltpu.SemaphoreType.DMA((copies,)),
        ],
        compiler_params=pltpu.CompilerParams(
            collective_id=ident, has_side_effects=True, vmem_limit_bytes=VMEM_LIMIT
        ),
    )(*arrays)


def local_call(body, outs, arrays, scratch=(), **kw):
    return pl.pallas_call(
        body,
        out_shape=outs,
        scratch_shapes=list(scratch),
        compiler_params=pltpu.CompilerParams(vmem_limit_bytes=VMEM_LIMIT),
        **kw,
    )(*arrays)


def table_kernel(table, gains, w, cols_ref, scale_ref, center_ref, center_gain_ref, center):
    rows, width = table.shape
    gain = gains[0:1]
    for i in range(0, rows, 64):
        part = table[i : i + 64].astype(F32)
        part = part - jnp.mean(part, 1, keepdims=True)
        center[i : i + 64] = part
        center_ref[i : i + 64] = part.astype(BF)
        center_gain_ref[i : i + 64] = (part * gain).astype(BF)
    cols_ref[...] = dot(center_gain_ref[...], w[...]).T.astype(BF)
    first = FIRST_PLACE - 1
    places = center[first:rows]
    gram = dot(places, center[...], 1, 1, HIGH)
    own = jnp.sum(places * places, 1, keepdims=True)
    every = center[...]
    every = dot(jnp.ones((8, width), F32), every * every, 1, 1, HIGH)[0:1]
    scale = lax.rsqrt((2.0 * gram + own + every) / width + 1e-05)
    lane = lax.broadcasted_iota(jnp.int32, scale.shape, 1)
    scale = jnp.where(lane < FIRST_PLACE, scale, 0.0)
    high = scale.astype(BF)
    scale_ref[0 : rows - first] = high
    scale_ref[rows - first :] = (scale - high.astype(F32)).astype(BF)


def fill_hot(hot, code, place):
    rows, length = hot.shape
    for i in range(0, rows, 64):
        index = lax.broadcasted_iota(jnp.int32, (64, length), 0) + i
        hit = (index == code) | (index == place + FIRST_PLACE)
        hot[i : i + 64] = jnp.where(hit, 1.0, 0.0).astype(BF)


def attend_seq(s, heads, tokens, pos_col, seg_col, table, parts, scales, keep):
    att, q_ref, kv_ref, prob_ref, scale_ref, hot, bias = keep
    wide = att.shape[1]
    dim = wide // heads
    code, pos, seg, place = tokens
    fill_hot(hot, code, place)
    length = hot.shape[1]
    both = dot(scales[...], hot[...])
    half = both.shape[0] // 2
    both = both[:half] + both[half:]
    index = lax.broadcasted_iota(jnp.int32, both.shape, 0)
    scale = jnp.sum(jnp.where(index == place + 1, both, 0.0), 0, keepdims=True)
    scale_ref[s] = jnp.broadcast_to(scale, (8, length))
    q = dot(table[parts[0], :], hot[:, 0:LANES]) * scale[:, 0:LANES]
    q_low = q.astype(BF)
    q_ref[s] = q_low
    for i in range(2):
        part = dot(table[parts[1 + i], :], hot[...])
        kv_ref[s, i * wide : (i + 1) * wide] = (part * scale).astype(BF)
    seen = (pos <= pos_col) & (seg == seg_col)
    bias[...] = jnp.where(seen, 0.0, -1e30)
    factor = dim**-0.5
    for h in range(heads):
        part = slice(h * dim, (h + 1) * dim)
        query = (q_low[part].astype(F32) * factor).T.astype(BF)
        scores = dot(query, kv_ref[s, part]) + bias[...]
        expo = jnp.exp(scores - jnp.max(scores, 1, keepdims=True))
        probs = (expo * (1.0 / jnp.sum(expo, 1, keepdims=True))).astype(BF)
        prob_ref[s, h] = probs
        value = kv_ref[s, wide + h * dim : wide + (h + 1) * dim]
        att[s, part] = dot(value, probs, 1, 1).astype(BF)


def attend_back_seq(s, heads, width, code, place, keep, datt, d_table, pairs, grad, grad_q):
    att, q_ref, kv_ref, prob_ref, scale_ref, hot, bias = keep
    wide = att.shape[1]
    dim = wide // heads
    scale = scale_ref[s, 0:1]
    fill_hot(hot, code, place)
    length = hot.shape[1]
    factor = dim**-0.5
    kappa = jnp.zeros((1, length), F32)
    kappa_q = jnp.zeros((1, LANES), F32)
    for h in range(heads):
        part = slice(h * dim, (h + 1) * dim)
        part_v = slice(wide + h * dim, wide + (h + 1) * dim)
        key, value = kv_ref[s, part], kv_ref[s, part_v]
        query = q_ref[s, part]
        d_out = datt[s, part]
        d_rows = d_out.astype(F32).T.astype(BF)
        probs_low = prob_ref[s, h]
        probs = probs_low.astype(F32)
        d_prob = dot(d_rows, value)
        weighted = probs * d_prob
        d_score = (weighted - probs * jnp.sum(weighted, 1, keepdims=True)).astype(BF)
        dv = dot(d_out, probs_low)
        dk = dot(query, d_score) * factor
        dq = dot(key, d_score, 1, 1) * factor
        kappa += jnp.sum(dk * key.astype(F32) + dv * value.astype(F32), 0, keepdims=True)
        kappa_q += jnp.sum(dq * query.astype(F32), 0, keepdims=True)
        grad[part] = (dk * scale).astype(BF)
        grad[part_v] = (dv * scale).astype(BF)
        grad_q[part] = (dq * scale[:, 0:LANES]).astype(BF)
    d_table[0:wide] += dot(grad_q[...], hot[:, 0:LANES], 1, 1)
    d_table[wide:] += dot(grad[...], hot[...], 1, 1)
    kappa = jnp.concatenate([kappa[:, 0:LANES] + kappa_q, kappa[:, LANES:]], 1)
    weight = scale * scale * kappa * (1.0 / width)
    for i in range(0, hot.shape[0], 128):
        left = (hot[i : i + 128].astype(F32) * weight).astype(BF)
        pairs[i : i + 128] += dot(left, hot[...], 1, 1)


def norm_parts(v):
    center = v - jnp.mean(v, -1, keepdims=True)
    scale = lax.rsqrt(jnp.mean(center * center, -1, keepdims=True) + 1e-05)
    return center * scale, scale


def norm_back(unit, scale, gain, d_out):
    d_unit = d_out * gain
    inner = jnp.mean(d_unit * unit, -1, keepdims=True)
    d_in = scale * (d_unit - jnp.mean(d_unit, -1, keepdims=True) - unit * inner)
    return d_in, jnp.sum(d_out * unit, 0, keepdims=True)


GELU_SCALE = 0.7978845608028654
GELU_CUBE = 0.044715
HOP_ONE = ("bl", "kh", "kl")
HOP_TWO = ("kh", "bl", "kl")


def core_kernel(heads, parted, *refs):
    refs = list(refs)

    def take(n):
        got = refs[:n]
        del refs[:n]
        return got

    r = types.SimpleNamespace(heads=heads, parted=parted)
    r.chunks, r.near, r.hops = 2, "bc", (HOP_ONE, HOP_TWO)
    rows, cols, table_t, scales, r.table, r.gains, r.proj, r.head, own, up_own = take(10)
    down_a, down_b = take(2)
    r.d_table, r.pairs, r.up_out, r.down_out, r.proj_out, r.head_out = take(6)
    r.dy_out, r.small_out = take(2)
    r.keep = take(7)
    r.up, r.down, r.u, r.hid, r.low, r.wide_in = take(6)
    r.datt, r.grad, r.grad_q, r.d_up, r.d_down = take(5)
    take_middle(r, take)
    local_sem, send_sem, recv_sem = refs
    links = r.links = Links(send_sem, recv_sem)
    size, here = links.size, links.here
    seqs, width = r.keep[0].shape[0], r.table.shape[1]
    set_places(r)
    if not parted:
        r.up, r.down, r.d_up, r.d_down = up_own, down_a, r.up_out, r.down_out

    local, up_first, late = [], [], []

    def copy_here(src, dst):
        local.append(pltpu.make_async_copy(src, dst, local_sem.at[len(local)]))
        local[-1].start()

    def send_down(ref, part):
        half = r.ff_rows // 2
        for n in range(size["ba"]):
            start = (n * size["bc"] + here["bc"]) * r.ff_rows + part * half
            place = r.down.at[pl.ds(pl.multiple_of(start, 8), half)]
            copy_here(ref.at[n], place)
            waiting.append((ref.at[n], place))

    waiting = []
    if parted:
        for bl in range(2):
            copy_here(up_own.at[bl], r.up.at[r.up_at(here["ba"], bl, here["bc"])])
        for part, ref in enumerate((down_a, down_b)):
            send_down(ref, part)
    links.greet(ALL)
    if parted:
        for bl in range(2):
            for n in range(1, size["ba"]):
                place = r.up.at[r.up_at(here["ba"], bl, here["bc"])]
                up_first.append(links.send(up_own.at[bl], place, {"ba": n}))
        for src, place in waiting:
            late.append(links.send(src, place, {"bc": 1}))

    parts = [slice(i * r.wide, (i + 1) * r.wide) for i in range(3)]

    def forward(s, carry):
        tokens = [rows[s, i : i + 1] for i in range(4)]
        attend_seq(
            s, heads, tokens, cols[s, :, 0:1], cols[s, :, 1:2], table_t, parts, scales, r.keep
        )
        return carry

    lax.fori_loop(0, seqs, forward, 0)
    for c in local:
        c.wait()
    for c in up_first:
        c.wait_recv()
    for n in range(size["ba"] if parted else 0):
        for bl in range(2):
            place = r.up.at[r.up_at(n, bl, here["bc"])]
            late.append(links.send(place, place, {"bc": 1}))
    info = own[...]
    r.low_end, r.high_end, r.target, r.weight, r.kind, code, place = (
        info[:, i : i + 1] for i in range(7)
    )
    columns = lax.broadcasted_iota(jnp.int32, (r.own, r.table.shape[0]), 1).astype(F32)
    r.own_hot = jnp.where((columns == code) | (columns == place), 1.0, 0.0).astype(BF)

    def weights_here():
        for c in late:
            c.wait_recv()

    r.weights_here, r.tick, r.free_weights = weights_here, lambda: None, lambda: None
    r.proj_on = lambda: None

    def backward(s, carry):
        attend_back_seq(
            s,
            heads,
            width,
            rows[s, 0:1],
            rows[s, 3:4],
            r.keep,
            r.datt,
            r.d_table,
            r.pairs,
            r.grad,
            r.grad_q,
        )
        return carry

    r.backward = backward
    middle(r)
    links.finish()


def take_middle(r, take):
    r.up_got, r.up_sum, r.up_got2, r.down_got = take(4)
    r.blk_src, r.blk_buffers = take(2), [take(3), take(3)]
    r.low_parts, r.z_src = take(2), take(2)
    r.z_buffers, r.low_buffers = [take(5), take(5)], [take(5), take(5)]
    r.dz_parts, r.d_src, r.dy_parts, r.results = take(2), take(2), take(1), take(2)


def middle_scratch(na, own, width, ff_cols, chunks, hops):
    up_rows, ff_rows = width // (na * 2 * chunks), ff_cols // (na * 2)
    shapes = [
        (na, chunks, up_rows, ff_cols),
        (na, chunks, up_rows, ff_cols),
        (max(na - 1, 1), chunks, up_rows, ff_cols),
        (na, ff_rows, width),
    ]
    scratch = [pltpu.VMEM(x, BF) for x in shapes]
    block = (own, width // 2)
    four, eight = pltpu.VMEM((4,) + block, BF), pltpu.VMEM((8,) + block, BF)
    scratch += [four] * 2
    for _ in range(2):
        scratch += reduce_buffers(block, BF, ("kl", "kh"))
    scratch += [eight] * 4
    for _ in range(2):
        for hop in hops:
            scratch += reduce_buffers(block, BF, hop[::-1])
    scratch += [eight] * 4 + [pltpu.VMEM((4, own, width), BF)]
    return scratch + [pltpu.VMEM(block, F32)] * 2


def set_places(r):
    size = r.links.size
    r.seqs, r.wide = r.keep[0].shape[:2]
    r.width = r.table.shape[1]
    r.own = r.dy_out.shape[0]
    copies = size["ba"] * 2
    r.blocks, r.ff_rows = r.width // (copies * r.chunks), r.u.shape[1] // copies

    def up_at(ba, chunk, near):
        start = ((ba * r.chunks + chunk) * 2 + near) * r.blocks
        return pl.ds(pl.multiple_of(start, 8), r.blocks)

    def down_at(ba, near):
        return pl.ds(pl.multiple_of((ba * 2 + near) * r.ff_rows, 8), r.ff_rows)

    r.up_at, r.down_at = up_at, down_at


def middle(r):
    links, size, here, parted = r.links, r.links.size, r.links.here, r.parted
    att, proj, gains, results = r.keep[0], r.proj, r.gains, r.results
    seqs, width, own_rows, half = r.seqs, r.width, r.own, r.width // 2
    up, down, u_ref, hid, low, wide_in = r.up, r.down, r.u, r.hid, r.low, r.wide_in
    d_up, d_down, up_at, down_at = r.d_up, r.d_down, r.up_at, r.down_at

    def blk_index(k):
        return (k % 2) * 2 + k // 2

    for s in range(seqs):
        part = dot(att[s], proj[...], 0, 0).astype(BF)
        for j in range(LANES // own_rows):
            block = part[j * own_rows : (j + 1) * own_rows]
            at = blk_index(s * (LANES // own_rows) + j)
            r.blk_src[0][at], r.blk_src[1][at] = block[:, :half], block[:, half:]
    bufs = r.blk_buffers
    jobs = [
        Reduce(links, r.blk_src[i], results[i], ("kl", "kh"), bufs[i][:2], bufs[i][2:])
        for i in range(2)
    ]
    for j in jobs:
        j.step()
    x = dot(r.own_hot, r.table[...])
    r.tick()
    run(jobs)
    x2 = x + jnp.concatenate([results[0][...], results[1][...]], 1)
    unit_mid, scale_mid = norm_parts(x2)
    low_own = (unit_mid * gains[1:2]).astype(BF)

    def start_spread(value, parts):
        gathers = []
        for i, route in enumerate(r.hops):
            me = links.number(route[::-1], {})
            parts[i][me] = value[:, i * half : (i + 1) * half]
            gathers.append(Gather(links, parts[i].at[me], parts[i], route, None))
        for j in gathers:
            j.step()
        return gathers

    def swapped(j):
        kl, kh, bl = j // 4, j // 2 % 2, j % 2
        return (kl * 2 + bl) * 2 + kh

    def end_spread(gathers, parts, whole):
        run(gathers)
        for j in range(8):
            span = slice(j * own_rows, (j + 1) * own_rows)
            whole[span, 0:half] = parts[0][j]
            whole[span, half:] = parts[1][swapped(j)]

    def start_sum(parts, buffers):
        routes = [h[::-1] for h in r.hops]
        jobs = [
            Reduce(links, parts[i], results[i], routes[i], buffers[i][:3], buffers[i][3:])
            for i in range(2)
        ]
        for j in jobs:
            j.step()
        return jobs

    gathers = start_spread(low_own, r.low_parts)
    r.tick()
    end_spread(gathers, r.low_parts, low)
    r.weights_here()
    group = 8 * own_rows
    step = 2 * own_rows

    def hidden(i, carry):
        span = pl.ds(pl.multiple_of(i * step, step), step)
        u = dot(low[span, :], up[...])
        u_ref[span, :] = u
        t = jnp.tanh(GELU_SCALE * (u + GELU_CUBE * u * u * u))
        hid[span, :] = (0.5 * u * (1.0 + t)).astype(BF)
        return carry

    lax.fori_loop(0, group // step, hidden, 0)
    for i in range(group // step):
        part = dot(hid[i * step : (i + 1) * step], down[...]).astype(BF)
        for n in range(2):
            block = part[n * own_rows : (n + 1) * own_rows]
            j = 2 * i + n
            r.z_src[0][j], r.z_src[1][swapped(j)] = block[:, :half], block[:, half:]
    jobs = start_sum(r.z_src, r.z_buffers)
    r.tick()
    run(jobs)
    r.tick()
    x3 = x2 + jnp.concatenate([results[0][...], results[1][...]], 1)

    unit_last, scale_last = norm_parts(x3)
    c_low = (unit_last * gains[2:3]).astype(BF)
    logits = dot(c_low, r.head[...])
    lane = lax.broadcasted_iota(jnp.int32, logits.shape, 1).astype(F32)
    weight, kind = r.weight, r.kind
    masked = jnp.where((lane >= r.low_end) & (lane < r.high_end), logits, -1e30)
    top = jnp.max(masked, 1, keepdims=True)
    expo = jnp.exp(masked - top)
    expo_sum = jnp.sum(expo, 1, keepdims=True)
    hit = jnp.where(lane == r.target, 1.0, 0.0)
    picked = jnp.sum(hit * logits, 1, keepdims=True)
    row_loss = (jnp.log(expo_sum) + top - picked) * weight
    losses = [jnp.sum(jnp.where(kind == j, row_loss, 0.0)) for j in range(PICKS)]
    d_logits = (weight * (expo / expo_sum - hit)).astype(BF)
    dx3, gain_last = norm_back(unit_last, scale_last, gains[2:3], dot(d_logits, r.head[...], 1, 1))
    gathers = start_spread(dx3.astype(BF), r.dz_parts)
    r.head_out[...] = dot(c_low, d_logits, 0, 0).astype(BF)
    end_spread(gathers, r.dz_parts, wide_in)

    def hidden_back(i, carry):
        span = pl.ds(pl.multiple_of(i * step, step), step)
        d_hid = dot(wide_in[span, :], down[...], 1, 1)
        u = u_ref[span, :]
        t = jnp.tanh(GELU_SCALE * (u + GELU_CUBE * u * u * u))
        slope = GELU_SCALE * (1.0 + 3.0 * GELU_CUBE * u * u)
        u_ref[span, :] = d_hid * (0.5 * (1.0 + t) + 0.5 * u * (1.0 - t * t) * slope)
        return carry

    lax.fori_loop(0, group // step, hidden_back, 0)
    for i in range(group // step):
        du = u_ref[i * step : (i + 1) * step].astype(BF)
        part = dot(du, up[...], 1, 1).astype(BF)
        for n in range(2):
            block = part[n * own_rows : (n + 1) * own_rows]
            j = 2 * i + n
            r.d_src[0][j], r.d_src[1][swapped(j)] = block[:, :half], block[:, half:]
    jobs = start_sum(r.d_src, r.low_buffers)
    r.free_weights()
    du = u_ref[...].astype(BF)
    for i in range(0, width, LANES):
        d_up[i : i + LANES] = dot(low[:, i : i + LANES], du, 0, 0).astype(BF)
    sent_up, sent_down = [], []
    for n in range(size["ba"] if parted else 0):
        for chunk in range(r.chunks):
            part = d_up.at[up_at(n, chunk, links.at(r.near, 1))]
            sent_up.append(links.send(part, r.up_got.at[n, chunk], {r.near: 1}))
    for i in range(0, hid.shape[1], LANES):
        d_down[i : i + LANES] = dot(hid[:, i : i + LANES], wide_in[...], 0, 0).astype(BF)
    run(jobs)
    d_low = jnp.concatenate([results[0][...], results[1][...]], 1)
    d_mid, gain_mid = norm_back(unit_mid, scale_mid, gains[1:2], d_low)
    dy = (dx3 + d_mid).astype(BF)
    r.dy_out[...] = dy
    small_out = r.small_out
    small_out[...] = jnp.zeros_like(small_out)
    small_out[0:1] = gain_mid
    small_out[1:2] = gain_last
    lane = lax.broadcasted_iota(jnp.int32, (1, width), 1)
    for j in range(PICKS):
        small_out[2:3] += jnp.where(lane == j, losses[j], 0.0)
    me = links.number(("kl", "kh"), {})
    r.dy_parts[0][me] = dy
    run([Gather(links, r.dy_parts[0].at[me], r.dy_parts[0], ("kh", "kl"), None)])

    for s in range(seqs):
        first = r.dy_parts[0][blk_index(2 * s)]
        second = r.dy_parts[0][blk_index(2 * s + 1)]
        d_rows = jnp.concatenate([first, second], 0)
        r.datt[s] = dot(proj[...], d_rows, 1, 1).astype(BF)
        part = dot(att[s], d_rows)
        if s:
            part = part + r.proj_out[...]
        r.proj_out[...] = part
    r.d_table[...] = jnp.zeros_like(r.d_table)
    r.pairs[...] = jnp.zeros_like(r.pairs)
    r.proj_on()
    for c in sent_up:
        c.wait_recv()
    for n in range(size["ba"] if parted else 0):
        for chunk in range(r.chunks):
            mine = d_up[up_at(n, chunk, here[r.near]), :].astype(F32)
            r.up_sum[n, chunk] = (mine + r.up_got[n, chunk].astype(F32)).astype(BF)
    sent_up = []
    for n in range(1, size["ba"] if parted else 1):
        part = r.up_sum.at[links.at("ba", n)]
        sent_up.append(links.send(part, r.up_got2.at[n - 1], {"ba": n}))
    for n in range(size["ba"] if parted else 0):
        block = d_down.at[down_at(n, links.at(r.near, 1))]
        sent_down.append(links.send(block, r.down_got.at[n], {r.near: 1}))
    r.backward(0, 0)
    for s in range(1, seqs):
        r.backward(s, 0)
    for c in sent_down:
        c.wait_recv()
    for n in range(size["ba"] if parted else 0):
        mine = d_down[down_at(n, here[r.near]), :].astype(F32)
        r.down_out[n] = (mine + r.down_got[n].astype(F32)).astype(BF)
    if parted:
        total = r.up_sum[here["ba"]].astype(F32)
        for n, c in enumerate(sent_up):
            c.wait_recv()
            total = total + r.up_got2[n].astype(F32)
        r.up_out[...] = total.astype(BF)


def core(rows, cols, table_t, scales, table, gains, proj, head, own, up_own, down_a, down_b, heads, ident):
    seqs, _, length = rows.shape
    wide, width = proj.shape
    na = lax.axis_size("ba")
    ff_cols, own_rows = up_own.shape[-1], own.shape[0]
    up_rows, ff_rows = width // (na * 4), ff_cols // (na * 2)
    parted = up_own.ndim == 3
    group = 8 * own_rows
    outs = [
        ((3 * wide, TABLE), F32),
        ((TABLE, TABLE), F32),
        ((2, up_rows, ff_cols) if parted else (width, ff_cols), BF),
        ((na, ff_rows, width) if parted else (ff_cols, width), BF),
        ((wide, width), F32),
        ((width, 256), BF),
        ((own_rows, width), BF),
        ((8, width), F32),
    ]
    scratch = [
        ((seqs, wide, LANES), BF),
        ((seqs, wide, LANES), BF),
        ((seqs, 2 * wide, length), BF),
        ((seqs, heads, LANES, length), BF),
        ((seqs, 8, length), F32),
        ((TABLE, length), BF),
        ((LANES, length), F32),
        ((width, ff_cols), BF),
        ((ff_cols, width), BF),
        ((group, ff_cols), F32),
        ((group, ff_cols), BF),
        ((group, width), BF),
        ((group, width), BF),
        ((seqs, wide, LANES), BF),
        ((2 * wide, length), BF),
        ((wide, LANES), BF),
        ((width, ff_cols), BF),
        ((ff_cols, width), BF),
    ]
    scratch = [pltpu.VMEM(*x) for x in scratch]
    scratch += middle_scratch(na, own_rows, width, ff_cols, 2, (HOP_ONE, HOP_TWO))
    copies = 2 * (na - 1) + 4 * na + 4 + 4 * 6 + 2 + 4 * na + na
    scratch += [
        pltpu.SemaphoreType.DMA((2 + 2 * na,)),
        pltpu.SemaphoreType.DMA((copies,)),
        pltpu.SemaphoreType.DMA((copies,)),
    ]
    vmem = pl.BlockSpec(memory_space=pltpu.VMEM)
    return pl.pallas_call(
        functools.partial(core_kernel, heads, parted),
        out_shape=[jax.ShapeDtypeStruct(*x) for x in outs],
        in_specs=[vmem] * 12,
        out_specs=[vmem] * len(outs),
        scratch_shapes=scratch,
        compiler_params=pltpu.CompilerParams(
            collective_id=ident, has_side_effects=True, vmem_limit_bytes=62 * 2**20
        ),
    )(rows, cols, table_t, scales, table, gains, proj, head, own, up_own, down_a, down_b)


EARLY = ("ba", "bl", "kh", "bc", "kl")
TABLE_WAYS = (("ba", "bl", "bc"), ("ba", "bc", "bl"))
PROJ_WAY = ("ba", "bl", "bc")
TEAM = ("bl", "bc", "kl")
TEAM_HOPS = (("bl", "bc", "kl"), ("bc", "bl", "kl"))
EMBED_WAYS = (("ba", "bl", "bc", "kh", "kl"), EARLY)


def slots(axes, route):
    back, result = route[::-1], []
    for i in range(2 ** len(axes)):
        bits = {a: i >> (len(axes) - 1 - n) & 1 for n, a in enumerate(axes)}
        result.append(sum(bits[a] << (len(back) - 1 - n) for n, a in enumerate(back)))
    return result


def tile_column(kh, t):
    per = HEADS // 4
    t = jnp.minimum(t, 3 * per - 1) if not isinstance(t, int) else min(t, 3 * per - 1)
    return t // per * 2 * per + per * kh + t % per


def grow(x, rows):
    return jnp.concatenate([x, jnp.zeros((rows - x.shape[0],) + x.shape[1:], x.dtype)], 0)


def front_kernel(heads, steps, *refs):
    refs = list(refs)

    def take(n):
        got = refs[:n]
        del refs[:n]
        return got

    r = types.SimpleNamespace(heads=heads, parted=True, steps=steps)
    r.chunks, r.near, r.hops = 4, "kh", TEAM_HOPS
    embed, w_qkv, w_up, w_down, proj_in, tiny, head_in, info, lanes, units, places = take(11)
    r.d_table, r.pairs, r.up_out, r.down_out, proj_part, r.head_out = take(6)
    r.dy_out, r.small_out, r.table, w_own, r.gains, hot_out = take(6)
    r.keep = take(7)
    r.up, r.down, r.u, r.hid, r.low, r.wide_in = take(6)
    r.datt, r.grad, r.grad_q = take(3)
    r.d_up, r.d_down = r.up, r.down
    e_parts = take(2)
    tiny_got, w_low, w_got, info_got, up_src, up_got, proj_got, r.proj = take(8)
    head_got, r.head = take(2)
    t_parts = take(2)
    table_t, center, center_gain, scales, token_info, own_info = take(6)
    proj_new, r.proj_out = take(2)
    take_middle(r, take)
    local_sem, send_sem, recv_sem = refs
    links = r.links = Links(send_sem, recv_sem)
    size, here = links.size, links.here
    width = r.table.shape[1]
    half, rows = width // 2, w_qkv.shape[0]
    set_places(r)
    wide, seqs = r.wide, r.seqs
    padded = w_low.shape[0]
    table_rows = embed.shape[0]
    total, nb = 32, 8
    kl = here["kl"]
    b_here = links.number(BATCH, {})
    me = links.number(ALL, {})

    links.hail(ALL, True)
    low = embed[...].astype(BF)
    for i in range(2):
        slot = links.number(EMBED_WAYS[i][::-1], {})
        e_parts[i][slot] = low[:, i * half : (i + 1) * half]
    early = links.number(EARLY[::-1], {})
    tiny_got[early] = tiny[...]
    for i in range(0, w_low.shape[1], 640):
        w_low[:, i : i + 640] = grow(w_qkv[:, i : i + 640], padded).astype(BF)
    down_place = r.down.at[r.down_at(here["ba"], here["kh"])]
    down_place[...] = w_down[...].astype(BF)
    links.met()
    jobs = []
    for i in range(2):
        slot = links.number(EMBED_WAYS[i][::-1], {})
        jobs.append(Gather(links, e_parts[i].at[slot], e_parts[i], EMBED_WAYS[i], None))
    jobs.append(Gather(links, tiny_got.at[early], tiny_got, EARLY, None))
    for j in jobs:
        j.step()

    def columns_of(move):
        at = {a: links.at(a, move.get(a, 0)) for a in ALL}
        t = at["kl"] * nb + (at["ba"] * 2 + at["bl"]) * 2 + at["bc"]
        return pl.ds(pl.multiple_of(tile_column(at["kh"], t) * LANES, LANES), LANES)

    w_sent = []
    for move in links.moves(ALL):
        w_sent.append(links.send(w_low.at[:, columns_of(move)], w_got.at[me], move))
    own_tile = pltpu.make_async_copy(w_low.at[:, columns_of({})], w_got.at[me], local_sem.at[0])
    own_tile.start()
    blk_here = links.number(BLK, {})
    info_got[blk_here] = info[...]
    info_sent = start_scatters(links, [(info_got.at[blk_here], info_got, BLK, "direct")])

    down_first = [links.send(down_place, down_place, {"ba": 1})]

    for g in range(8):
        pieces = []
        for c in range(4):
            i = ((c // 2 * 4 + g // 2) * 2 + c % 2) * 2 + g % 2
            pieces.append(w_up[:, i * r.ff_rows : (i + 1) * r.ff_rows])
        up_src[g] = grow(jnp.concatenate(pieces, 1), padded).astype(BF)
    for j in jobs:
        j.step()
    member = links.number(TEAM, {})
    up_sent = start_scatters(links, [(up_src, up_got, TEAM, "scatter")])
    up_got[member] = up_src[member]
    proj_slot = links.number(PROJ_WAY[::-1], {})
    proj_got[proj_slot] = proj_in[...]
    head_got[early] = head_in[...]
    run(jobs)
    for c in up_sent:
        c.wait_recv()
    up_first, up_places = [], []
    for c in range(4):
        parts = [up_got[c * 2 + n].astype(F32)[:rows] for n in range(2)]
        place = r.up.at[r.up_at(here["ba"], c, here["kh"])]
        place[...] = jnp.concatenate(parts, 0).astype(BF)
        up_places.append(place)

    where = [slots(ALL, way) for way in EMBED_WAYS]
    for i in range(total):
        span = slice(i * table_rows, (i + 1) * table_rows)
        r.table[span, 0:half] = e_parts[0][where[0][i]]
        r.table[span, half:] = e_parts[1][where[1][i]]
    flat = tiny_got[...].reshape(total * 16, LANES)
    row = lax.broadcasted_iota(jnp.int32, (total * 16, width), 0)
    local_row = lax.broadcasted_iota(jnp.int32, (LANES, width), 0)
    r.gains[...] = jnp.zeros_like(r.gains)

    def gain_row(j):
        pick = jnp.where(row == units[0:1] + j, 1.0, 0.0).astype(BF)
        spread = dot(flat, pick, 0, 0)
        r.gains[j : j + 1] = jnp.sum(
            jnp.where(local_row == units[1:2], spread, 0.0), 0, keepdims=True
        )

    gain_row(0)
    for i in range(0, TABLE, 64):
        part = r.table[i : i + 64].astype(F32)
        part = part - jnp.mean(part, 1, keepdims=True)
        center[i : i + 64] = part
        center_gain[i : i + 64] = (part * r.gains[0:1]).astype(BF)
    own_tile.wait()
    for c in w_sent:
        c.wait_recv()
    for i in range(0, total, 2):
        pair = [w_got[i + n].astype(F32)[:rows] for n in range(2)]
        w_own[i * rows : (i + 2) * rows] = jnp.concatenate(pair, 0).astype(BF)
    tile = dot(center_gain[...], w_own[...]).T.astype(BF)
    tables = []
    for i in range(2):
        slot = links.number(TABLE_WAYS[i][::-1], {})
        mine = t_parts[i].at[kl]
        mine[slot] = tile[i * LANES // 2 : (i + 1) * LANES // 2]
        tables.append(Gather(links, mine.at[slot], mine, TABLE_WAYS[i], None))
        tables[i].step()

    late = []
    for place in up_places:
        up_first.append(links.send(place, place, {"ba": 1}))
    proj_job = Gather(links, proj_got.at[proj_slot], proj_got, PROJ_WAY, None)
    proj_job.step()
    head_job = Gather(links, head_got.at[early], head_got, EARLY, None)

    first = FIRST_PLACE - 1
    n_places = TABLE - first
    spots = center[first:TABLE]
    gram = dot(spots, center[...], 1, 1, HIGH)
    own_square = jnp.sum(spots * spots, 1, keepdims=True)
    every = center[...]
    every = dot(jnp.ones((8, width), F32), every * every, 1, 1, HIGH)[0:1]
    scale = lax.rsqrt((2.0 * gram + own_square + every) / width + 1e-05)
    lane = lax.broadcasted_iota(jnp.int32, scale.shape, 1)
    scale = jnp.where(lane < FIRST_PLACE, scale, 0.0)
    high = scale.astype(BF)
    scales[0:n_places] = high
    scales[n_places:] = (scale - high.astype(F32)).astype(BF)
    for j in tables:
        j.step()
    for c in down_first:
        c.wait_recv()
    for n in range(2):
        place = r.down.at[r.down_at(n, here["kh"])]
        late.append(links.send(place, place, {"kh": 1}))

    for c in info_sent:
        c.wait_recv()
    fields = info_got[...].reshape(4 * info.shape[0], LANES)
    length = lanes.shape[1]
    lane_time, lane_place, lane_pos = (lanes[i : i + 1] for i in range(3))
    sub = lax.broadcasted_iota(jnp.int32, (LANES, length), 0).astype(F32)
    for s in range(seqs):
        pick = jnp.where(places[0 : fields.shape[0], s : s + 1] == lane_time, 1.0, 0.0)
        by_lane = dot(fields, pick, 0, 0, HIGH)
        code = jnp.sum(jnp.where(sub == lane_place, by_lane, 0.0), 0, keepdims=True)
        code = code + jnp.where(lane_place == OBS, float(PATCH), 0.0)
        code = code + jnp.where(lane_place == OBS + 1, float(PATCH + RET_BINS), 0.0)
        code = code + jnp.where(lane_place == OBS + 2, float(PATCH + RET_BINS + ACTIONS), 0.0)
        token_info[s, 0:1] = jnp.where(lane_place < 0.0, -1.0, code)
        token_info[s, 1:2] = by_lane[OBS + 4 : OBS + 5]
        own_info[s] = dot(pick[:, 0:LANES], fields, 0, 0, HIGH)
        for j in tables:
            if j.stage < 3:
                j.step()
    run(tables)
    other = []
    for i in range(2):
        mine = t_parts[i].at[kl]
        other.append(links.send(mine, mine, {"kl": 1}))
    proj_job.step()
    gain_row(1)
    gain_row(2)
    for c in other:
        c.wait_recv()
    for i in range(2):
        order = slots(BATCH, TABLE_WAYS[i])
        for n in range(2):
            for b in range(nb):
                start = (n * nb + b) * LANES + i * LANES // 2
                table_t[start : start + LANES // 2] = t_parts[i][n, order[b]]

    parts = [
        pl.ds(pl.multiple_of(i * 2 * wide + kl * wide, 64), wide) for i in range(3)
    ]
    query_pos = places[0:LANES, 2:3]

    def forward(s, carry):
        code = token_info[s, 0:1].astype(jnp.int32)
        tokens = (code, lane_pos, token_info[s, 1:2], lane_place.astype(jnp.int32))
        seg_col = own_info[s, :, OBS + 4 : OBS + 5]
        attend_seq(s, heads, tokens, query_pos, seg_col, table_t, parts, scales, r.keep)
        return carry

    for c in up_first:
        c.wait_recv()
    for n in range(2):
        for chunk in range(4):
            place = r.up.at[r.up_at(n, chunk, here["kh"])]
            late.append(links.send(place, place, {"kh": 1}))
    head_job.step()
    forward(0, 0)
    proj_job.step()
    head_job.step()
    forward(1, 0)
    run([proj_job])
    order = slots(BATCH, PROJ_WAY)
    for b in range(0, nb, 2):
        pair = [proj_got[order[b + n]].astype(F32)[:rows] for n in range(2)]
        r.proj[b * rows : (b + 2) * rows] = jnp.concatenate(pair, 0).astype(BF)
    head_job.step()

    own = r.own
    mine = own_info[here["kh"], pl.ds(pl.multiple_of(kl * own, 8), own), :]
    slot = lax.broadcasted_iota(jnp.int32, (own, 1), 0) + kl * own
    steps = r.steps
    kind = jnp.where(slot >= 3 * steps, 3.0, jnp.where(slot >= 2 * steps, 2.0, jnp.where(slot >= steps, 1.0, 0.0)))

    def by_kind(*options):
        value = options[3]
        for j in range(3):
            value = jnp.where(kind == j, options[j], value)
        return value

    ret, act, rew = (mine[:, OBS + i : OBS + i + 1] for i in range(3))
    code = by_kind(
        mine[:, OBS - 1 : OBS], ret + PATCH, act + (PATCH + RET_BINS), mine[:, 0:1]
    )
    place = by_kind(OBS - 1.0, float(OBS), OBS + 1.0, 0.0) + FIRST_PLACE
    r.kind = kind
    r.low_end = by_kind(0.0, float(RET_BINS), float(RET_BINS + ACTIONS), 0.0)
    r.high_end = by_kind(
        float(RET_BINS), float(RET_BINS + ACTIONS), float(HEAD_COLS), float(RET_BINS)
    )
    r.target = by_kind(ret, act + RET_BINS, rew + (RET_BINS + ACTIONS), 0.0 * ret)
    counts = jnp.sum(tiny_got[...].astype(F32), 0)[3:4]
    per_game = 1.0 / (GAMES * jnp.maximum(counts, 1.0))
    lane = lax.broadcasted_iota(jnp.int32, (own, LANES), 1).astype(F32)
    game = jnp.where(lane == mine[:, OBS + 3 : OBS + 4], per_game, 0.0)
    r.weight = jnp.where(kind < 3.0, jnp.sum(game, 1, keepdims=True), 0.0)
    columns = lax.broadcasted_iota(jnp.int32, (own, TABLE), 1).astype(F32)
    r.own_hot = jnp.where((columns == code) | (columns == place), 1.0, 0.0).astype(BF)
    hot_out[...] = r.own_hot

    def tick():
        if head_job.stage < len(head_job.route):
            head_job.step()

    def weights_here():
        run([head_job])
        order = slots(ALL, EARLY)
        for i in range(0, total, 2):
            pair = [head_got[order[i + n]].astype(F32)[:rows] for n in range(2)]
            r.head[i * rows : (i + 2) * rows] = jnp.concatenate(pair, 0).astype(BF)
        for c in late:
            c.wait_recv()

    def free_weights():
        links.finish(late + down_first + up_first)

    r.tick, r.weights_here, r.free_weights = tick, weights_here, free_weights
    proj_sent = []

    def proj_on():
        links.finish(proj_job.sent)
        place = slots_for(BATCH, PROJ_BACK)
        for b in range(nb):
            block = grow(r.proj_out[b * rows : (b + 1) * rows], padded)
            proj_got[place[b]] = block.astype(BF)
        there = proj_got.at[pl.ds(links.at("bc", 1) * 4, 4)]
        proj_sent.append(links.send(there, proj_new, {"bc": 1}))

    r.proj_on = proj_on

    def backward(s, carry):
        attend_back_seq(
            s,
            heads,
            width,
            token_info[s, 0:1].astype(jnp.int32),
            lane_place.astype(jnp.int32),
            r.keep,
            r.datt,
            r.d_table,
            r.pairs,
            r.grad,
            r.grad_q,
        )
        return carry

    r.backward = backward
    middle(r)
    proj_sent[0].wait_recv()
    mine = proj_got[pl.ds(here["bc"] * 4, 4)].astype(F32)
    proj_part[...] = (mine + proj_new[...].astype(F32)).astype(BF)
    links.finish()


def front(embed, w_qkv, w_up, w_down, proj_rows, tiny, head, info, steps, ident):
    rows, width = w_qkv.shape[0], embed.shape[1]
    ff_rows = w_down.shape[0]
    ff_cols, na, seqs, padded = 4 * ff_rows, 2, 2, proj_rows.shape[0]
    wide, heads = width // 4, HEADS // 4
    own = seqs * LANES // 4
    group = 8 * own
    length = up_to(TSTEP * steps, LANES)
    tail = length - TSTEP * steps
    place_of = np.repeat(np.array(PLACES), steps)
    time_of = np.tile(np.arange(steps), TSTEP)
    lanes = np.zeros((8, length), np.float32)
    lanes[0] = np.pad(time_of, (0, tail), constant_values=-5)
    lanes[1] = np.pad(place_of, (0, tail), constant_values=-1000)
    lanes[2] = np.pad(time_of * TSTEP + place_of, (0, tail), constant_values=1 << 20)
    units = np.zeros((8, width), np.int32)
    units[0] = np.array(slots(ALL, EARLY))[np.arange(width) // rows] * 16
    units[1] = np.arange(width) % rows
    count = info.shape[0]
    at = np.arange(4 * count)
    place, local = at % count, steps // 4
    places = np.full((max(4 * count, LANES), 8), -9, np.float32)
    for s in range(seqs):
        fits = place // local == s
        places[: 4 * count, s] = np.where(fits, at // count * local + place % local, -9)
    places[:LANES, 2] = lanes[2, :LANES]
    outs = [
        ((3 * wide, TABLE), F32),
        ((TABLE, TABLE), F32),
        ((4, width // 16, ff_cols), BF),
        ((na, ff_rows, width), BF),
        ((4, padded, width), BF),
        ((width, 256), BF),
        ((own, width), BF),
        ((8, width), F32),
        ((TABLE, width), BF),
        ((width, LANES), BF),
        ((8, width), F32),
        ((own, TABLE), BF),
    ]
    n_places = TABLE - FIRST_PLACE + 1
    scratch = [
        ((seqs, wide, LANES), BF),
        ((seqs, wide, LANES), BF),
        ((seqs, 2 * wide, length), BF),
        ((seqs, heads, LANES, length), BF),
        ((seqs, 8, length), F32),
        ((TABLE, length), BF),
        ((LANES, length), F32),
        ((width, ff_cols), BF),
        ((ff_cols, width), BF),
        ((group, ff_cols), F32),
        ((group, ff_cols), BF),
        ((group, width), BF),
        ((group, width), BF),
        ((seqs, wide, LANES), BF),
        ((2 * wide, length), BF),
        ((wide, LANES), BF),
        ((32, TABLE // 32, width // 2), BF),
        ((32, TABLE // 32, width // 2), BF),
        ((32, 16, LANES), BF),
        ((padded, 3 * width), BF),
        ((32, padded, LANES), BF),
        ((4, count, LANES), F32),
        ((8, padded, ff_cols), BF),
        ((8, padded, ff_cols), BF),
        ((8, padded, width), BF),
        ((wide, width), BF),
        ((32, padded, 256), BF),
        ((width, 256), BF),
        ((2, 8, LANES // 2, TABLE), BF),
        ((2, 8, LANES // 2, TABLE), BF),
        ((16 * LANES, TABLE), BF),
        ((TABLE, width), F32),
        ((TABLE, width), BF),
        ((2 * n_places, TABLE), BF),
        ((seqs, 8, length), F32),
        ((seqs, LANES, LANES), F32),
    ]
    scratch = [pltpu.VMEM(*x) for x in scratch]
    scratch += [pltpu.VMEM((4, padded, width), BF), pltpu.VMEM((wide, width), F32)]
    scratch += middle_scratch(na, own, width, ff_cols, 4, TEAM_HOPS)
    copies = 15 + 31 + 3 + 7 + 6 + 2 + 1 + 3 + 5 + 4 + 10 + 4 + 24 + 2 + 10 + 4 + 1
    scratch += [
        pltpu.SemaphoreType.DMA((1,)),
        pltpu.SemaphoreType.DMA((copies,)),
        pltpu.SemaphoreType.DMA((copies,)),
    ]
    vmem = pl.BlockSpec(memory_space=pltpu.VMEM)
    arrays = (embed, w_qkv, w_up, w_down, proj_rows, tiny, head, info)
    arrays += (jnp.asarray(lanes), jnp.asarray(units), jnp.asarray(places))
    return pl.pallas_call(
        functools.partial(front_kernel, heads, steps),
        out_shape=[jax.ShapeDtypeStruct(*x) for x in outs],
        in_specs=[vmem] * len(arrays),
        out_specs=[vmem] * len(outs),
        scratch_shapes=scratch,
        compiler_params=pltpu.CompilerParams(
            collective_id=ident, has_side_effects=True, vmem_limit_bytes=63 * 2**20
        ),
    )(*arrays)


def over_rows(ref, body):
    rows, cols = ref.shape
    wide = 640 if cols % 640 == 0 else cols

    def piece(part, acc):
        for i in range(0, cols, wide):
            acc = acc + body(part, slice(i, i + wide))
        return acc

    start = jnp.zeros((8, LANES), F32)
    if rows % 8:
        return piece(slice(0, rows), start)

    def step(i, acc):
        return piece(pl.ds(pl.multiple_of(i * 8, 8), 8), acc)

    return lax.fori_loop(0, rows // 8, step, start)


def fold(v):
    rows, cols = v.shape
    if rows == 8 and cols % LANES == 0:
        total = v[:, 0:LANES]
        for i in range(LANES, cols, LANES):
            total = total + v[:, i : i + LANES]
        return total
    lane = lax.broadcasted_iota(jnp.int32, (8, LANES), 1)
    row = lax.broadcasted_iota(jnp.int32, (8, LANES), 0)
    return jnp.where((lane == 0) & (row == 0), jnp.sum(v), 0.0)


def lane_sums(values, offset):
    lane = lax.broadcasted_iota(jnp.int32, (8, LANES), 1)
    block = jnp.zeros((8, LANES), F32)
    for i, v in enumerate(values):
        block = jnp.where(lane == i + offset, v, block)
    return block


def sum_squares(ref):
    def add(part, cols):
        v = ref[part, cols]
        return fold(v * v)

    return over_rows(ref, add)


def group_sums(refs):
    sums = [jnp.sum(sum_squares(r)) for r in refs[:6]]
    square = refs[6][...] * refs[6][...]
    return sums + [jnp.sum(square[i : i + 1]) for i in range(3)]


def squares_kernel(*refs):
    grads, masters = refs[:7], refs[7:14]
    losses, out, mine, slots, send_sem, recv_sem = refs[14:]
    links = Links(send_sem, recv_sem)
    block = lane_sums(group_sums(grads), 0) + lane_sums(group_sums(masters), 9)
    links.greet(ALL, True)
    out[...] = sum_everywhere(links, block + losses[...], mine, slots)
    links.finish()


TILE_WAYS = (("kl", "bc", "bl", "ba"), ("kl", "bl", "bc", "ba"))
PROJ_BACK = ("bc", "bl", "ba")
BACK_WAYS = (("kl", "kh", "bc", "bl", "ba"), ("kl", "bc", "kh", "bl", "ba"))
MISC_BACK = BACK_WAYS[1]


def slots_for(axes, route):
    return slots(axes, route[::-1])


def back_kernel(*refs):
    refs = list(refs)

    def take(n):
        got = refs[:n]
        del refs[:n]
        return got

    d_table, pairs, up_in, down_in, proj_in, head_in, dy, small, table, w_own = take(10)
    gains, own_hot, units, losses = take(4)
    masters = take(7)
    grads, sums = take(7), take(1)[0]
    t_src, e_src, t_out, e_out = take(2), take(2), take(2), take(2)
    misc_src, gain_src, proj_out, misc_out, gain_out = take(5)
    center, center_gain, base, dw_src, dw_got, up_src, up_got = take(7)
    t_bufs = [take(7), take(7)]
    e_bufs = [take(9), take(9)]
    proj_bufs, misc_bufs, gain_bufs, down_bufs = take(3), take(9), take(9), take(1)
    mine, slots_got, local_sem, send_sem, recv_sem = refs
    links = Links(send_sem, recv_sem)
    size, here = links.size, links.here
    width = table.shape[1]
    half, rows, padded = width // 2, grads[1].shape[0], dw_src.shape[1]
    wide, total, nb = width // 4, 32, 8
    me = links.number(ALL, {})

    links.hail(ALL, True)
    for ref in t_src:
        ref[...] = jnp.zeros_like(ref)
    order = [slots_for(("kl",) + BATCH, way) for way in TILE_WAYS]
    for v in range(2):

        @pl.when(here["kl"] == v)
        def _(v=v):
            for p in range(3):
                for n in range(wide // 64):
                    unit = (p * 2 + v) * (wide // 64) + n
                    start = p * wide + n * 64
                    value = d_table[start : start + 64].astype(BF)
                    t_src[unit % 2][order[unit % 2][unit // 2]] = value

    links.met()

    def reduction(src, out, way, bufs):
        n = len(way)
        return Reduce(links, src, out, way, bufs[:n], bufs[n:])

    tiles = [reduction(t_src[i], t_out[i], TILE_WAYS[i], t_bufs[i]) for i in range(2)]
    for j in tiles:
        j.step()
    for c in range(4):
        for n in range(2):
            part = up_in[c].astype(F32)[n * rows : (n + 1) * rows]
            up_src[c * 2 + n] = grow(part, padded).astype(BF)
    up_sent = start_scatters(links, [(up_src, up_got, TEAM, "scatter")])
    member = links.number(TEAM, {})
    up_got[member] = up_src[member]
    proj_job = reduction(proj_in, proj_out, PROJ_BACK[1:], proj_bufs)
    proj_job.step()

    owner = lax.broadcasted_iota(jnp.int32, (total, width), 0)
    inner = lax.broadcasted_iota(jnp.int32, (LANES, width), 0)
    inner = jnp.where(inner == units[1:2], 1.0, 0.0)

    def by_owner(row):
        return dot(jnp.where(owner == units[0:1], row, 0.0), inner, 1, 1, HIGH)

    mid, last = by_owner(small[0:1]), by_owner(small[1:2])
    sub = lax.broadcasted_iota(jnp.int32, (padded - rows, 256), 0)
    place = slots_for(ALL, MISC_BACK)
    for i in range(total):
        first, second = (
            jnp.concatenate([v[i : i + 1], v[i : i + 1]], 1) for v in (mid, last)
        )
        tail = jnp.where(sub == 0, first, jnp.where(sub == 1, second, 0.0))
        if i % 2 == 0:
            pair = head_in[i * rows : (i + 2) * rows].astype(F32)
        block = pair[i % 2 * rows : (i % 2 + 1) * rows]
        misc_src[place[i]] = jnp.concatenate([block, tail], 0).astype(BF)
    misc_job = reduction(misc_src, misc_out, MISC_BACK, misc_bufs)
    misc_job.step()
    for j in tiles:
        j.step()

    for i in range(0, TABLE, 64):
        part = table[i : i + 64].astype(F32)
        part = part - jnp.mean(part, 1, keepdims=True)
        center[i : i + 64] = part
        center_gain[i : i + 64] = (part * gains[0:1]).astype(BF)
    for j in tiles:
        j.step()
    proj_job.step()
    for i in range(0, TABLE, LANES):
        low = center[...].astype(BF)
        part = dot(own_hot[:, i : i + LANES], dy[...], 0, 0)
        base[i : i + LANES] = part - dot(pairs[i : i + LANES].astype(BF), low)
    for j in tiles:
        j.step()
    proj_job.step()
    run(tiles)
    down_job = reduction(down_in, grads[4], ("ba",), down_bufs)
    down_job.step()
    d_tile = jnp.concatenate([t_out[0][...], t_out[1][...]], 0).astype(BF)
    d_w = dot(center_gain[...], d_tile, 0, 1)
    for i in range(total):
        dw_src[i] = grow(d_w[i * rows : (i + 1) * rows], padded).astype(BF)

    def tile_of(move):
        at = {a: links.at(a, move.get(a, 0)) for a in ALL}
        t = at["kl"] * nb + (at["ba"] * 2 + at["bl"]) * 2 + at["bc"]
        return pl.ds(pl.multiple_of((at["kh"] * 16 + t) * LANES, LANES), LANES)

    spot = dw_got.at[:, tile_of({})]
    dw_sent = []
    for move in links.moves(ALL):
        dw_sent.append(links.send(dw_src.at[links.number(ALL, move)], spot, move))
    own_tile = pltpu.make_async_copy(dw_src.at[me], spot, local_sem.at[0])
    own_tile.start()
    order = [slots_for(ALL, way) for way in BACK_WAYS]
    gain = jnp.zeros((1, width), F32)
    for i in range(0, TABLE, LANES):
        d_norm = dot(d_tile[:, i : i + LANES], w_own[...], 0, 1)
        gain += jnp.sum(center[i : i + LANES] * d_norm, 0, keepdims=True)
        scaled = d_norm * gains[0:1]
        value = base[i : i + LANES] + scaled - jnp.mean(scaled, 1, keepdims=True)
        value = value.astype(BF)
        for n in range(0, LANES, 16):
            block = (i + n) // 16
            for side in range(2):
                part = value[n : n + 16, side * half : (side + 1) * half]
                e_src[side][order[side][block]] = part
    embeds = [reduction(e_src[i], e_out[i], BACK_WAYS[i], e_bufs[i]) for i in range(2)]
    for j in embeds:
        j.step()
    run([proj_job])

    home = 8 * links.number(BLK, {}) + links.number(BATCH, {})
    stays = home == me
    count = links.used
    links.used += 1
    left, there = home, {}
    for axis in ALL[::-1]:
        there[axis] = lax.rem(left, 2)
        left = left // 2

    def proj_copy():
        return pltpu.make_async_remote_copy(
            src_ref=proj_out.at[0:rows],
            dst_ref=grads[2],
            send_sem=send_sem.at[count],
            recv_sem=recv_sem.at[count],
            device_id=there,
            device_id_type=pl.DeviceIdType.MESH,
        )

    @pl.when(jnp.logical_not(stays))
    def _():
        proj_copy().start()

    @pl.when(stays)
    def _():
        grads[2][...] = proj_out[0:rows]

    gain = by_owner(gain)
    sub = lax.broadcasted_iota(jnp.int32, (16, LANES), 0)
    place = slots_for(ALL, MISC_BACK)
    for i in range(total):
        gain_src[place[i]] = jnp.where(sub == 0, gain[i : i + 1], 0.0).astype(BF)
    gain_job = reduction(gain_src, gain_out, MISC_BACK, gain_bufs)
    gain_job.step()

    misc_job.step()
    block = lane_sums(group_sums(masters), 9)

    def advance():
        for j in embeds + [gain_job, misc_job]:
            if j.stage < len(j.route):
                j.step()

    advance()
    for c in up_sent:
        c.wait_recv()
    ff = grads[3].shape[1] // total
    for j in range(8):
        pieces = []
        for n in range(4):
            member, c = j % 4 * 2 + n % 2, j // 4 * 2 + n // 2
            pieces.append(up_got[member].astype(F32)[:rows, c * ff : (c + 1) * ff])
        grads[3][:, j * 4 * ff : (j + 1) * 4 * ff] = jnp.concatenate(pieces, 1)
    advance()
    own_tile.wait()
    for c in dw_sent:
        c.wait_recv()
    per = HEADS // 4
    for c in range(6 * per):
        t = c % (2 * per) // per * 16 + c // (2 * per) * per + c % per
        value = dw_got[:, t * LANES : (t + 1) * LANES].astype(F32)[:rows]
        grads[1][:, c * LANES : (c + 1) * LANES] = value

    @pl.when(jnp.logical_not(stays))
    def _():
        proj_copy().wait_recv()
        proj_copy().wait_send()

    advance()
    early = [jnp.sum(sum_squares(grads[i])) for i in (1, 2, 3)]
    run(embeds + [gain_job, misc_job])
    run([down_job])
    for side in range(2):
        grads[0][:, side * half : (side + 1) * half] = e_out[side][...]
    n_head = grads[5].shape[1]
    grads[5][...] = misc_out[0:rows, 0:n_head]
    grads[6][0:1] = gain_out[0:1, 0:rows]
    grads[6][1:3] = misc_out[rows : rows + 2, 0:rows]
    late = group_sums([grads[0]] * 4 + [grads[4], grads[5], grads[6]])
    late[1:4] = early
    block = block + lane_sums(late, 0)
    sums[...] = sum_everywhere(links, block + losses[...], mine, slots_got)
    links.finish()


def back(got, masters, loss_tile, ident):
    rows, width = masters[1].shape[0], masters[0].shape[1]
    padded, table_rows, half = up_to(rows, 16), masters[0].shape[0], width // 2
    ff_cols = got[2].shape[2]
    units = np.zeros((8, width), np.int32)
    units[0], units[1] = np.arange(width) // rows, np.arange(width) % rows
    f32_tile = (8, LANES)
    outs = [(w.shape, F32) for w in masters] + [(f32_tile, F32)]
    t_block, e_block = (LANES // 2, TABLE), (table_rows, half)
    scratch = [((16,) + t_block, BF)] * 2 + [((32,) + e_block, BF)] * 2
    scratch += [(t_block, F32)] * 2 + [(e_block, F32)] * 2
    scratch += [
        ((32, padded, 256), BF),
        ((32, 16, LANES), BF),
        ((padded, width), F32),
        ((padded, 256), F32),
        ((16, LANES), F32),
        ((TABLE, width), F32),
        ((TABLE, width), BF),
        ((TABLE, width), F32),
        ((32, padded, LANES), BF),
        ((padded, 32 * LANES), BF),
        ((8, padded, ff_cols), BF),
        ((8, padded, ff_cols), BF),
    ]
    scratch = [pltpu.VMEM(*x) for x in scratch]
    for way in TILE_WAYS:
        scratch += reduce_buffers(t_block, BF, way)
    for way in BACK_WAYS:
        scratch += reduce_buffers(e_block, BF, way)
    scratch += reduce_buffers((padded, width), BF, PROJ_BACK[1:])
    scratch += reduce_buffers((padded, 256), BF, MISC_BACK)
    scratch += reduce_buffers((16, LANES), BF, MISC_BACK)
    scratch += reduce_buffers(got[3].shape[1:], BF, ("ba",))
    copies = 8 + 10 + 3 + 5 + 5 + 1 + 7 + 31 + 1 + 31
    scratch += [
        pltpu.VMEM(f32_tile, F32),
        pltpu.VMEM((31,) + f32_tile, F32),
        pltpu.SemaphoreType.DMA((1,)),
        pltpu.SemaphoreType.DMA((copies,)),
        pltpu.SemaphoreType.DMA((copies,)),
    ]
    vmem = pl.BlockSpec(memory_space=pltpu.VMEM)
    arrays = tuple(got) + (jnp.asarray(units), loss_tile) + tuple(masters)
    result = pl.pallas_call(
        back_kernel,
        out_shape=[jax.ShapeDtypeStruct(*x) for x in outs],
        in_specs=[vmem] * len(arrays),
        out_specs=[vmem] * len(outs),
        scratch_shapes=scratch,
        compiler_params=pltpu.CompilerParams(
            collective_id=ident, has_side_effects=True, vmem_limit_bytes=63 * 2**20
        ),
    )(*arrays)
    return tuple(result[:7]), result[7]


def at_first(body):
    pl.when(pl.program_id(0) == 0)(body)


def moments_kernel(*refs):
    sums = refs[0]
    grads, masters, firsts, seconds = (refs[1 + 7 * i : 8 + 7 * i] for i in range(4))
    means, squares, updates = (refs[29 + 7 * i : 36 + 7 * i] for i in range(3))
    out = refs[50]
    total = sums[...]
    lane = lax.broadcasted_iota(jnp.int32, (8, LANES), 1)
    norm = jnp.sqrt(jnp.sum(jnp.where(lane < 9, total, 0.0)[0:1], 1, keepdims=True))
    factor = jnp.minimum(1.0, 0.05 / norm)

    def one(i):
        def step(part, cols):
            g = factor * grads[i][part, cols]
            mean = 0.9 * firsts[i][part, cols] + 0.1 * g
            square = 0.99 * seconds[i][part, cols] + 0.01 * g * g
            update = (mean * (1.0 / (1.0 - 0.9**STEP))) / (
                jnp.sqrt(square * (1.0 / (1.0 - 0.99**STEP))) + 1e-08
            ) + 0.01 * masters[i][part, cols]
            means[i][part, cols] = mean
            squares[i][part, cols] = square
            updates[i][part, cols] = update
            return fold(update * update)

        return over_rows(grads[i], step)

    @at_first
    def _():
        table = one(0)
        one(6)
        gains = updates[6][...] * updates[6][...]
        values = [jnp.sum(table)] + [0.0] * 5 + [jnp.sum(gains[j : j + 1]) for j in range(3)]
        out[...] = lane_sums(values, 0)

    out[...] += lane_sums([jnp.sum(one(i)) for i in range(1, 6)], 1)


def weights_kernel(*refs):
    update_sums, sums = refs[:2]
    masters, updates = refs[2:9], refs[9:16]
    news, copies = refs[16:23], refs[23:29]
    norms_ref, loss_ref, norm_ref = refs[29:]
    update_norm = jnp.sqrt(update_sums[0:1, 0:9])
    weight_norm = jnp.sqrt(sums[0:1, 9:18])
    ratio = weight_norm / update_norm

    def one(i):
        def step(part, cols):
            new = masters[i][part, cols] - 0.3 * ratio[0:1, i : i + 1] * updates[i][part, cols]
            news[i][part, cols] = new
            copies[i][part, cols] = new.astype(BF)
            return jnp.zeros((8, LANES), F32)

        over_rows(masters[i], step)

    @at_first
    def _():
        norms_ref[0:1] = weight_norm
        norms_ref[1:2] = update_norm
        loss_ref[...] = sums[0:1, 18 : 18 + PICKS]
        lane = lax.broadcasted_iota(jnp.int32, (1, LANES), 1)
        grad_sq = jnp.where(lane < 9, sums[0:1], 0.0)
        norm_ref[...] = jnp.sqrt(jnp.sum(grad_sq, 1, keepdims=True))
        one(0)
        for j in range(3):
            row = slice(j, j + 1)
            news[6][row] = masters[6][row] - 0.3 * ratio[0:1, 6 + j : 7 + j] * updates[6][row]

    for i in range(1, 6):
        one(i)


def by_rows(body, heads, groups, outs, tails):
    shapes = [x.shape for x in groups[0]]
    parts = 5 if all(shapes[i][0] % 80 == 0 or shapes[i][0] == 40 for i in range(1, 6)) else 1

    def spec(i, shape):
        if i in (0, 6):
            return pl.BlockSpec(shape, lambda n: (0, 0))
        return pl.BlockSpec((shape[0] // parts, shape[1]), lambda n: (n, 0))

    def whole(x):
        return pl.BlockSpec(x.shape, lambda n: (0,) * len(x.shape))

    in_specs = [whole(x) for x in heads]
    in_specs += [spec(i, s) for _ in groups for i, s in enumerate(shapes)]
    out_specs = [spec(i, x.shape) for group in outs for i, x in enumerate(group)]
    out_specs += [whole(x) for x in tails]
    return local_call(
        body,
        [x for group in outs for x in group] + tails,
        list(heads) + [x for group in groups for x in group],
        grid=(parts,),
        in_specs=in_specs,
        out_specs=out_specs,
    )


def layer_norm(v, gain):
    center = v - jnp.mean(v, -1, keepdims=True)
    return center * lax.rsqrt(jnp.mean(center * center, -1, keepdims=True) + 1e-05) * gain


def gradients(obs_tokens, returns, actions, rewards, game_ids, segments, masters):
    table, w_qkv, w_proj, w_up, w_down, w_head, gains = masters
    na, nk = lax.axis_size("ba"), 4
    nb, members = na * 4, 2 * nk
    total = nb * nk
    bl = lax.axis_index("bl")
    k = lax.axis_index("kh") * 2 + lax.axis_index("kl")
    g = bl * nk + k
    seqs, steps_here = obs_tokens.shape[:2]
    width = table.shape[1]
    rows, table_rows = w_qkv.shape[0], table.shape[0]
    steps = steps_here * nk
    heads = HEADS // nk
    wide = width // nk
    cols = 3 * wide // nb
    ff_rows = w_down.shape[0]
    padded_rows = up_to(rows, 16)
    padded_table = up_to(table_rows, 16)
    half = width // 2

    info = jnp.pad(obs_tokens, ((0, 0), (0, 0), (0, LANES - OBS)))
    for i, v in enumerate((returns, actions, rewards, game_ids, segments)):
        info = info + jnp.where(jnp.arange(LANES) == OBS + i, v[..., None], 0)
    info = info.reshape(seqs * steps_here, LANES)
    info = pad_to(info, up_to(seqs * steps_here, 8), LANES)
    counts_here = jnp.sum((game_ids[..., None] == jnp.arange(GAMES)).astype(F32), (0, 1))
    to_heads = [(i, i % nb * nk + i // nb) for i in range(total)]
    proj_rows = pad_to(lax.ppermute(w_proj.astype(BF), ALL, to_heads), padded_rows, width)
    if total == 32 and table_rows == 16 and rows == 40 and seqs == 2 and ff_rows == 160:
        tiny = jnp.pad(gains, ((0, 13), (0, LANES - rows)))
        tiny = tiny + jnp.pad(counts_here[None], ((3, 12), (0, LANES - GAMES)))
        tiny = tiny.astype(BF)
        got = front(
            table,
            w_qkv,
            w_up,
            w_down,
            proj_rows,
            tiny,
            pad_to(w_head.astype(BF), padded_rows, 256),
            info.astype(F32),
            steps,
            0,
        )
        losses = jnp.pad(got[7][2:3, :PICKS], ((0, 7), (18, LANES - 18 - PICKS)))
        return back(got, masters, losses, 1)
    table_bf = pad_to(table.astype(BF), padded_table, width)
    small = jnp.concatenate(
        [
            pad_to(w_head.astype(BF), rows, 256),
            pad_to(gains.astype(BF), 3, 256),
            pad_to(counts_here.astype(BF)[None], 1, 256),
            jnp.zeros((padded_rows - rows - 4, 256), BF),
        ]
    )
    qkv_blocks = w_qkv.astype(BF).reshape(rows, 3, nk, wide).transpose(2, 0, 1, 3)
    qkv_blocks = qkv_blocks.reshape(nk, rows, nb, cols).transpose(2, 0, 1, 3)
    qkv_blocks = pad_to(qkv_blocks.reshape(total, rows, cols), padded_rows, LANES)
    ff_cols = na * 2 * ff_rows
    up_blocks = w_up.astype(BF).reshape(rows, na, 2, 2, nk, ff_rows).transpose(2, 4, 0, 1, 3, 5)
    up_blocks = pad_to(up_blocks.reshape(members, rows, ff_cols), padded_rows, ff_cols)
    parted = ff_rows % 32 == 0 and nk * rows % 16 == 0
    down_low = w_down.astype(BF)
    one_way = ("ba", "bl", "bc", "kh", "kl")
    other_way = ("ba", "bl", "kh", "bc", "kl")
    items = [
        (table_bf[:, :half], "gather", one_way),
        (table_bf[:, half:], "gather", other_way),
        (small, "gather", other_way),
        (qkv_blocks, "scatter", ALL),
        (info, "direct", BLK),
        (up_blocks, "scatter", GROUP),
    ]
    if parted:
        items.append((down_low[: ff_rows // 2], "gather", ("ba",)))
    got = exchange(items, 0)
    table_left, table_right, small_all, qkv_mine, info_here, up_mine = got[:6]
    if parted:
        up_mine = up_mine[:, :rows].reshape(2, nk * rows, ff_cols)
        down_first = got[6]
    else:
        up_mine = lax.all_gather(up_mine[:, :rows], COPIES, axis=0, tiled=False)
        up_mine = up_mine.reshape(na, 2, 2, nk, rows, ff_cols).transpose(0, 2, 1, 3, 4, 5)
        up_mine = up_mine.reshape(width, ff_cols)
        down_first = lax.all_gather(down_low, COPIES, axis=0, tiled=True)

    table_all = jnp.concatenate(
        [
            natural(table_left, ALL, one_way)[:, :table_rows],
            natural(table_right, ALL, other_way)[:, :table_rows],
        ],
        2,
    ).reshape(TABLE, width)
    small_all = natural(small_all, ALL, other_way)
    gain = small_all[:, rows : rows + 3, :rows].transpose(1, 0, 2).reshape(3, width).astype(F32)
    w_mine = qkv_mine[:, :rows].reshape(width, LANES)
    scale_rows = TABLE - FIRST_PLACE + 1
    cols_mine, scale_table, center_bf, center_gain = local_call(
        table_kernel,
        [
            jax.ShapeDtypeStruct((LANES, TABLE), BF),
            jax.ShapeDtypeStruct((2 * scale_rows, TABLE), BF),
            jax.ShapeDtypeStruct((TABLE, width), BF),
            jax.ShapeDtypeStruct((TABLE, width), BF),
        ],
        (table_all, pad_to(gain, 8, width), w_mine),
        [pltpu.VMEM((TABLE, width), F32)],
    )
    table_ways = (("ba", "bl", "bc"), ("bc", "bl", "ba"))
    items = [
        (cols_mine[: LANES // 2], "gather", table_ways[0]),
        (cols_mine[LANES // 2 :], "gather", table_ways[1]),
        (proj_rows, "gather", ("ba", "bc", "bl")),
    ]
    if parted:
        items.append((down_low[ff_rows // 2 :], "gather", ("ba",)))
    got = exchange(items, 1)
    down_second = got[3] if parted else jnp.zeros((16, LANES), BF)
    qkv_table = jnp.concatenate(
        [natural(got[0], BATCH, table_ways[0]), natural(got[1], BATCH, table_ways[1])], 1
    )
    qkv_table = qkv_table[:, :cols].reshape(3 * wide, TABLE)
    proj_here = natural(got[2], BATCH, ("ba", "bc", "bl"))[:, :rows].reshape(wide, width)

    info_here = info_here[:, : seqs * steps_here].reshape(nk, seqs, steps_here, LANES)
    info_here = info_here.transpose(1, 0, 2, 3).reshape(seqs, steps, LANES)
    length = up_to(TSTEP * steps, LANES)
    place_of = np.repeat(np.array(PLACES), steps)
    time_of = np.tile(np.arange(steps), TSTEP)
    tail = length - TSTEP * steps
    pos = np.pad(time_of * TSTEP + place_of, (0, tail), constant_values=1 << 20)
    place_of = np.pad(place_of, (0, tail), constant_values=-1000)
    starts = np.array([0] * OBS + [PATCH, PATCH + RET_BINS, PATCH + RET_BINS + ACTIONS])
    codes = info_here[..., :TSTEP] + starts.astype(np.int32)
    codes = jnp.concatenate(
        [codes[..., OBS - 1 : OBS + 2], codes[..., : OBS - 1], codes[..., OBS + 2 :]], -1
    )
    codes = codes.transpose(0, 2, 1).reshape(seqs, TSTEP * steps)
    codes = jnp.pad(codes, ((0, 0), (0, tail)), constant_values=-1)
    seg = jnp.tile(info_here[..., OBS + 4], (1, TSTEP))
    seg = jnp.pad(seg, ((0, 0), (0, tail)), constant_values=-1)
    zero = jnp.zeros((seqs, length), jnp.int32)
    token_rows = jnp.stack(
        [codes, zero + jnp.asarray(pos, jnp.int32), seg, zero + jnp.asarray(place_of, jnp.int32)]
        + [zero] * 4,
        1,
    )
    token_cols = jnp.stack([zero[:, :LANES] + pos[:LANES].astype(np.int32), seg[:, :LANES]], -1)
    token_cols = jnp.pad(token_cols, ((0, 0), (0, 0), (0, LANES - 2)))

    own = seqs * LANES // nk
    slots = lax.rem(k, nk // seqs) * own + jnp.arange(own)
    seq_own = k * own // LANES
    codes_own = lax.dynamic_slice(codes, (seq_own, lax.rem(k, nk // seqs) * own), (1, own))[0]
    place_own = jnp.asarray(place_of[:LANES], jnp.int32)
    place_own = lax.dynamic_slice(place_own, (lax.rem(k, nk // seqs) * own,), (own,))
    kind = slots // steps
    info_seq = lax.dynamic_index_in_dim(info_here, seq_own, 0, False)
    info_own = info_seq.at[lax.rem(slots, steps)].get(mode="promise_in_bounds")
    counts = jnp.sum(small_all[:, rows + 3, :GAMES].astype(F32), 0)
    per_game = 1.0 / (GAMES * jnp.maximum(counts, 1.0))
    game_own = (info_own[:, OBS + 3, None] == jnp.arange(GAMES)).astype(F32)
    weight = jnp.where(kind < PICKS, jnp.sum(game_own * per_game, -1), 0.0)
    low_end = jnp.where(kind == 0, 0, jnp.where(kind == 1, RET_BINS, RET_BINS + ACTIONS))
    high_end = jnp.where(kind == 0, RET_BINS, jnp.where(kind == 1, RET_BINS + ACTIONS, HEAD_COLS))
    target = low_end + jnp.where(
        kind == 0,
        info_own[:, OBS],
        jnp.where(kind == 1, info_own[:, OBS + 1], info_own[:, OBS + 2]),
    )
    own_info = [low_end, high_end, target, weight, kind, codes_own, place_own + FIRST_PLACE]
    own_info = pad_to(jnp.stack([v.astype(F32) for v in own_info], 1), own, LANES)
    head_full = small_all[:, :rows].reshape(width, 256)
    d_table, pairs, sum_up, sum_down, d_proj, d_head, dy_own, d_small = core(
        token_rows,
        token_cols,
        qkv_table,
        scale_table,
        table_all,
        pad_to(gain, 8, width),
        proj_here,
        head_full,
        own_info,
        up_mine,
        down_first,
        down_second,
        heads,
        2,
    )
    d_gain_mid, d_gain_last = d_small[0], d_small[1]
    losses = [d_small[2, j] for j in range(PICKS)]
    columns = jnp.arange(TABLE)
    own_hot = (codes_own[:, None] == columns) | (place_own[:, None] + FIRST_PLACE == columns)
    own_hot = own_hot.astype(BF)
    if not parted:
        sum_up = sum_up.reshape(na, 2, 2, nk, rows, ff_cols).transpose(0, 2, 1, 3, 4, 5)
        sum_up = sum_up.reshape(width, ff_cols)
        sum_up = lax.psum_scatter(sum_up, COPIES, scatter_dimension=0, tiled=True)
        sum_down = lax.psum_scatter(sum_down, COPIES, scatter_dimension=0, tiled=True)

    d_table = pad_to(d_table.astype(BF).reshape(nb, cols, TABLE), LANES, TABLE)
    d_proj = pad_to(d_proj.astype(BF).reshape(nb, rows, width), padded_rows, width)
    proj_route = ("bl", "bc", "ba")
    table_routes = (("bc", "bl", "ba"), ("bl", "bc", "ba"))
    left, right, sum_proj = reduce(
        [
            for_route(d_table[..., : TABLE // 2], BATCH, table_routes[0]),
            for_route(d_table[..., TABLE // 2 :], BATCH, table_routes[1]),
            for_route(d_proj, BATCH, proj_route),
        ],
        table_routes + (proj_route,),
        [],
        3,
    )
    sum_proj = lax.ppermute(sum_proj[:rows], ALL, [(j, i) for i, j in to_heads])
    d_table_mine = jnp.concatenate([left, right], 1).astype(BF)
    d_w = dot(center_gain, d_table_mine, 0, 1)
    d_norm = dot(d_table_mine, w_mine, 0, 1)
    d_gain_first = jnp.sum(center_bf.astype(F32) * d_norm, 0)
    d_scaled = d_norm * gain[0]
    d_embed = (
        d_scaled
        - jnp.mean(d_scaled, 1, keepdims=True)
        - dot(pairs.astype(BF), center_bf)
        + dot(own_hot, dy_own, 0, 0)
    )
    d_gains = jnp.stack([d_gain_first, d_gain_mid, d_gain_last]).astype(BF)
    d_misc = jnp.concatenate(
        [
            d_head.reshape(total, rows, 256),
            pad_to(d_gains.reshape(3, total, rows).transpose(1, 0, 2), 3, 256),
            jnp.zeros((total, padded_rows - rows - 3, 256), BF),
        ],
        1,
    )
    d_w = pad_to(d_w.astype(BF).reshape(total, rows, LANES), padded_rows, LANES)
    d_embed = pad_to(d_embed.astype(BF).reshape(total, table_rows, width), padded_table, width)
    sum_up = pad_to(sum_up.reshape(members, rows, -1), padded_rows, ff_cols)
    one_way = ("kl", "kh", "bc", "bl", "ba")
    other_way = ("kl", "bc", "kh", "bl", "ba")
    arrays = [
        for_route(d_embed[..., :half], ALL, one_way),
        for_route(d_embed[..., half:], ALL, other_way),
        for_route(d_misc, ALL, other_way),
    ]
    routes = (one_way, other_way, other_way)
    if parted:
        arrays.append(sum_down)
        routes += (("ba",),)
    got = reduce(arrays, routes, [(d_w, ALL), (sum_up, GROUP)], 4)
    d_left, d_right, d_misc = got[:3]
    d_ws, ups = got[-2:]
    if parted:
        sum_down = got[3]
    d_embed = jnp.concatenate([d_left, d_right], 1)
    d_ws = d_ws[:, :rows, :cols].reshape(nb, nk, rows, cols).transpose(2, 1, 0, 3)
    d_ws = d_ws.reshape(rows, nk, 3, wide).transpose(0, 2, 1, 3).reshape(rows, 3 * width)
    ups = ups[:, :rows].reshape(2, nk, rows, na, 2, ff_rows).transpose(2, 3, 0, 4, 1, 5)
    ups = ups.reshape(rows, nb * nk * ff_rows)
    grads = (
        d_embed[:table_rows],
        d_ws.astype(F32),
        sum_proj,
        ups.astype(F32),
        sum_down.astype(F32),
        d_misc[:rows, :HEAD_COLS],
        d_misc[rows : rows + 3, :rows],
    )
    loss_tile = jnp.zeros((8, LANES), F32).at[:, 18:21].set(jnp.stack(losses))
    return grads, summed_call(squares_kernel, grads + masters + (loss_tile,), 5)


def shards(*args):
    masters, firsts, seconds = args[6:13], args[13:20], args[20:27]
    grads, sums = gradients(*args[:6], masters)
    like = [jax.ShapeDtypeStruct(w.shape, F32) for w in masters]
    low = [jax.ShapeDtypeStruct(w.shape, BF) for w in masters[:6]]
    tile = jax.ShapeDtypeStruct((8, LANES), F32)
    result = by_rows(
        moments_kernel, (sums,), (grads, masters, firsts, seconds), [like] * 3, [tile]
    )
    means, squares, updates = result[:7], result[7:14], result[14:21]
    update_sums = summed_call(all_sum_kernel, (result[21],), 6)
    last = [jax.ShapeDtypeStruct(x, F32) for x in ((2, 9), (1, PICKS), (1, 1))]
    result = by_rows(
        weights_kernel, (update_sums, sums), (masters, updates), [like, low], last
    )
    news, copies, norms = result[:7], result[7:13], result[13]
    loss_terms, grad_norm = result[14].reshape(PICKS), result[15].reshape(())
    return tuple(news) + tuple(means) + tuple(squares) + tuple(copies) + (
        grad_norm,
        loss_terms,
        norms,
    )


def solution(mesh):
    nb, nk = mesh.shape["batch"], mesh.shape["blk"]
    split = Mesh(mesh.devices.reshape(nb // 4, 2, 2, nk // 2, 2), ALL)
    rows, gains = P(ALL, None), P(None, ALL)
    weights = (rows,) * 6 + (gains,)
    in_specs = (P(BATCH, BLK, None),) + (P(BATCH, BLK),) * 5 + weights * 3
    out_specs = weights * 3 + (rows,) * 6 + (P(), P(), P())
    return jax.shard_map(
        shards, mesh=split, in_specs=in_specs, out_specs=out_specs, check_vma=False
    )
```

```python
import functools
import math
import types

import jax
import jax.numpy as jnp
import numpy as np
from jax import lax
from jax.experimental import pallas as pl
from jax.experimental.pallas import tpu as pltpu
from jax.sharding import Mesh
from jax.sharding import PartitionSpec as P

HEADS = 20
RET_BINS = 120
ACTIONS = 18
GAMES = 41
TSTEP = 39
OBS = 36
PATCH = 331
STEP = 10
HEAD_COLS = 142
TABLE = 512
PICKS = 3
LANES = 128
FIRST_PLACE = PATCH + HEAD_COLS
BF = jnp.bfloat16
F32 = jnp.float32
HIGH = lax.Precision.HIGHEST
BLK = ("kh", "kl")
GROUP = ("bl", "kh", "kl")
BATCH = ("ba", "bl", "bc")
COPIES = ("ba", "bc")
ALL = ("ba", "bl", "bc", "kh", "kl")
VMEM_LIMIT = 56 * 2**20
PLACES = list(range(OBS - 1, OBS + 2)) + [p for p in range(TSTEP) if not OBS - 1 <= p < OBS + 2]


def up_to(n, m):
    return -(-n // m) * m


def pad_to(x, rows, cols):
    if x.shape[-2:] == (rows, cols):
        return x
    widths = [(0, 0)] * (x.ndim - 2) + [(0, rows - x.shape[-2]), (0, cols - x.shape[-1])]
    return jnp.pad(x, widths)


def dot(left, right, ca=1, cb=0, precision=None):
    return lax.dot_general(
        left,
        right,
        (((ca,), (cb,)), ((), ())),
        precision=precision,
        preferred_element_type=F32,
    )


class Links:
    def __init__(self, sends, recvs):
        self.sends, self.recvs, self.open, self.used = sends, recvs, [], 0
        self.size = {a: lax.axis_size(a) for a in ALL}
        self.here = {a: lax.axis_index(a) for a in ALL}

    def at(self, axis, step):
        return lax.rem(self.here[axis] + step, self.size[axis])

    def number(self, axes, steps):
        n = 0
        for a in axes:
            n = n * self.size[a] + self.at(a, steps.get(a, 0))
        return n

    def moves(self, axes):
        result = [{}]
        for a in axes:
            result = [dict(m, **{a: r}) for m in result for r in range(self.size[a])]
        return [{a: r for a, r in m.items() if r} for m in result if any(m.values())]

    def greet(self, axes, everyone=False):
        self.hail(axes, everyone)
        self.met()

    def met(self):
        pl.semaphore_wait(pltpu.get_barrier_semaphore(), self.hailed)

    def hail(self, axes, everyone=False):
        barrier = pltpu.get_barrier_semaphore()
        if everyone:
            moves = self.moves(axes)
        else:
            moves = [{a: r} for a in axes for r in range(1, self.size[a])]
        for move in moves:
            pl.semaphore_signal(
                barrier,
                inc=1,
                device_id={a: self.at(a, r) for a, r in move.items()},
                device_id_type=pl.DeviceIdType.MESH,
            )
        self.hailed = len(moves)

    def send(self, src, dst, move):
        n, self.used = self.used, self.used + 1
        c = pltpu.make_async_remote_copy(
            src_ref=src,
            dst_ref=dst,
            send_sem=self.sends.at[n],
            recv_sem=self.recvs.at[n],
            device_id={a: self.at(a, r) for a, r in move.items()},
            device_id_type=pl.DeviceIdType.MESH,
        )
        c.start()
        self.open.append(c)
        return c

    def finish(self, copies=None):
        copies = list(self.open if copies is None else copies)
        for c in copies:
            c.wait_send()
        self.open = [c for c in self.open if not any(c is d for d in copies)]


class Gather:
    def __init__(self, links, src, dst, route, local):
        self.links, self.src, self.dst = links, src, dst
        self.route, self.local, self.waits, self.stage = list(route), local, [], 0
        self.sent = []

    def step(self):
        links = self.links
        for c in self.waits:
            c.wait_recv()
        self.waits = []
        if self.stage == len(self.route):
            return False
        if self.stage == 1 and self.local is not None:
            self.local.wait()
            self.local = None
        count = math.prod(links.size[a] for a in self.route[: self.stage])
        start = links.number(self.route[self.stage :][::-1], {}) * count
        here = self.dst.at[pl.ds(start, count)]
        block = self.src if self.stage == 0 else here
        there = self.dst.at[start] if self.stage == 0 else here
        axis = self.route[self.stage]
        for r in range(1, links.size[axis]):
            self.waits.append(links.send(block, there, {axis: r}))
        self.sent += self.waits
        self.stage += 1
        return True

    def close(self):
        if self.local is not None:
            self.local.wait()


class Reduce:
    def __init__(self, links, src, out, route, arrived, totals):
        self.links, self.now, self.out = links, src, out
        self.route, self.arrived, self.totals = list(route), arrived, totals
        self.waits, self.stage, self.done = [], 0, False

    def part(self, axis, step):
        count = self.now.shape[0] // self.links.size[axis]
        return pl.ds(self.links.at(axis, step) * count, count)

    def step(self):
        if self.done:
            return False
        if self.stage:
            axis = self.route[self.stage - 1]
            for c in self.waits:
                c.wait_recv()
            total = self.now[self.part(axis, 0)].astype(F32)
            for n in range(len(self.waits)):
                total = total + self.arrived[self.stage - 1][n].astype(F32)
            if self.stage == len(self.route):
                self.out[...] = total[0]
                self.done = True
                return False
            self.now = self.totals[self.stage - 1]
            self.now[...] = total.astype(self.now.dtype)
        axis = self.route[self.stage]
        self.waits = []
        for r in range(1, self.links.size[axis]):
            dst = self.arrived[self.stage].at[r - 1]
            self.waits.append(self.links.send(self.now.at[self.part(axis, r)], dst, {axis: r}))
        self.stage += 1
        return True


def start_scatters(links, jobs):
    copies = []
    for src, dst, axes, kind in jobs:
        me = links.number(axes, {})
        for move in links.moves(axes):
            block = src.at[links.number(axes, move)] if kind == "scatter" else src
            copies.append(links.send(block, dst.at[me], move))
    return copies


def run(jobs):
    jobs = list(jobs)
    while jobs:
        jobs = [j for j in jobs if j.step()]


def sizes_of(axes):
    return tuple(lax.axis_size(a) for a in axes)


def exchange_kernel(kinds, routes, *refs):
    count = len(kinds)
    srcs, dsts = refs[:count], refs[count : 2 * count]
    local_sem, send_sem, recv_sem = refs[2 * count :]
    links = Links(send_sem, recv_sem)
    local = []
    for i, route in enumerate(routes):
        me = links.number(route[::-1] if kinds[i] == "gather" else route, {})
        block = srcs[i].at[me] if kinds[i] == "scatter" else srcs[i]
        local.append(pltpu.make_async_copy(block, dsts[i].at[me], local_sem.at[i]))
        local[-1].start()
    everyone = any(k != "gather" for k in kinds)
    links.greet([a for a in ALL if any(a in x for x in routes)], everyone)
    gathers = [
        Gather(links, srcs[i], dsts[i], routes[i], local[i])
        for i in range(count)
        if kinds[i] == "gather"
    ]
    for j in gathers:
        j.step()
    copies = []
    for i in range(count):
        if kinds[i] != "gather":
            copies += start_scatters(links, [(srcs[i], dsts[i], routes[i], kinds[i])])
    run(gathers)
    for j in gathers:
        j.close()
    for c in copies:
        c.wait_recv()
    for i in range(count):
        if kinds[i] != "gather":
            local[i].wait()
    links.finish()


def natural(x, axes, route):
    back = route[::-1]
    x = x.reshape(sizes_of(back) + x.shape[1:])
    order = [back.index(a) for a in axes] + list(range(len(axes), x.ndim))
    return x.transpose(order).reshape((-1,) + x.shape[len(axes) :])


def for_route(x, axes, route):
    x = x.reshape(sizes_of(axes) + x.shape[1:])
    order = [axes.index(a) for a in route] + list(range(len(axes), x.ndim))
    return x.transpose(order).reshape((-1,) + x.shape[len(axes) :])


def exchange(items, ident):
    arrays, kinds, routes = zip(*items)
    shapes, copies = [], 0
    for x, kind, route in zip(arrays, kinds, routes):
        sizes = sizes_of(route)
        shape = x.shape if kind == "scatter" else (math.prod(sizes),) + x.shape
        shapes.append(jax.ShapeDtypeStruct(shape, x.dtype))
        copies += sum(sizes) - len(sizes) if kind == "gather" else math.prod(sizes) - 1
    n = len(arrays)
    return pl.pallas_call(
        functools.partial(exchange_kernel, kinds, routes),
        out_shape=shapes,
        in_specs=[pl.BlockSpec(memory_space=pl.ANY)] * n,
        out_specs=[pl.BlockSpec(memory_space=pl.ANY)] * n,
        scratch_shapes=[
            pltpu.SemaphoreType.DMA((n,)),
            pltpu.SemaphoreType.DMA((copies,)),
            pltpu.SemaphoreType.DMA((copies,)),
        ],
        compiler_params=pltpu.CompilerParams(collective_id=ident, has_side_effects=True),
    )(*arrays)


def reduce_buffers(shape, dtype, route):
    arrived, totals = [], []
    for i, axis in enumerate(route):
        rest = (math.prod(sizes_of(route[i + 1 :])),) + shape
        arrived.append(pltpu.VMEM((lax.axis_size(axis) - 1,) + rest, dtype))
        totals.append(pltpu.VMEM(rest, dtype))
    return arrived + totals[:-1]


def reduce_kernel(routes, other_axes, *refs):
    refs = list(refs)

    def take(n):
        got = refs[:n]
        del refs[:n]
        return got

    sums = len(routes)
    srcs, other_srcs = take(sums), take(len(other_axes))
    outs, other_dsts = take(sums), take(len(other_axes))
    buffers = [(take(len(r)), take(len(r) - 1)) for r in routes]
    local_sem, send_sem, recv_sem = refs
    links = Links(send_sem, recv_sem)
    local = []
    for i, axes in enumerate(other_axes):
        me = links.number(axes, {})
        local.append(
            pltpu.make_async_copy(other_srcs[i].at[me], other_dsts[i].at[me], local_sem.at[i])
        )
        local[-1].start()
    seen = [a for a in ALL if any(a in x for x in tuple(routes) + other_axes)]
    links.greet(seen, bool(other_axes))
    jobs = [
        Reduce(links, srcs[i], outs[i], routes[i], *buffers[i]) for i in range(sums)
    ]
    for j in jobs:
        j.step()
    copies = start_scatters(
        links, [(s, d, a, "scatter") for s, d, a in zip(other_srcs, other_dsts, other_axes)]
    )
    run(jobs)
    for c in copies:
        c.wait_recv()
    for c in local:
        c.wait()
    links.finish()


def reduce(arrays, routes, others, ident):
    outs = [jax.ShapeDtypeStruct(x.shape[1:], F32) for x in arrays]
    outs += [jax.ShapeDtypeStruct(x.shape, x.dtype) for x, _ in others]
    scratch = []
    for x, route in zip(arrays, routes):
        scratch += reduce_buffers(x.shape[1:], x.dtype, route)
    copies = sum(sum(sizes_of(r)) - len(r) for r in routes)
    copies += sum(math.prod(sizes_of(axes)) - 1 for _, axes in others)
    scratch += [
        pltpu.SemaphoreType.DMA((max(len(others), 1),)),
        pltpu.SemaphoreType.DMA((copies,)),
        pltpu.SemaphoreType.DMA((copies,)),
    ]
    vmem, hbm = pl.BlockSpec(memory_space=pltpu.VMEM), pl.BlockSpec(memory_space=pl.ANY)
    specs = [vmem] * len(arrays) + [hbm] * len(others)
    return pl.pallas_call(
        functools.partial(reduce_kernel, tuple(routes), tuple(axes for _, axes in others)),
        out_shape=outs,
        in_specs=specs,
        out_specs=specs,
        scratch_shapes=scratch,
        compiler_params=pltpu.CompilerParams(
            collective_id=ident, has_side_effects=True, vmem_limit_bytes=VMEM_LIMIT
        ),
    )(*arrays, *[x for x, _ in others])


def sum_everywhere(links, value, mine, slots):
    mine[...] = value
    moves = links.moves(ALL)
    waits = [links.send(mine, slots.at[n], move) for n, move in enumerate(moves)]
    for c in waits:
        c.wait_recv()
    return value + jnp.sum(slots[...], 0)


def all_sum_kernel(value, out, mine, slots, send_sem, recv_sem):
    links = Links(send_sem, recv_sem)
    links.greet(ALL, True)
    out[...] = sum_everywhere(links, value[...], mine, slots)
    links.finish()


def summed_call(body, arrays, ident):
    vmem = pl.BlockSpec(memory_space=pltpu.VMEM)
    copies = math.prod(sizes_of(ALL)) - 1
    return pl.pallas_call(
        body,
        out_shape=jax.ShapeDtypeStruct((8, LANES), F32),
        in_specs=[vmem] * len(arrays),
        out_specs=vmem,
        scratch_shapes=[
            pltpu.VMEM((8, LANES), F32),
            pltpu.VMEM((copies, 8, LANES), F32),
            pltpu.SemaphoreType.DMA((copies,)),
            pltpu.SemaphoreType.DMA((copies,)),
        ],
        compiler_params=pltpu.CompilerParams(
            collective_id=ident, has_side_effects=True, vmem_limit_bytes=VMEM_LIMIT
        ),
    )(*arrays)


def local_call(body, outs, arrays, scratch=(), **kw):
    return pl.pallas_call(
        body,
        out_shape=outs,
        scratch_shapes=list(scratch),
        compiler_params=pltpu.CompilerParams(vmem_limit_bytes=VMEM_LIMIT),
        **kw,
    )(*arrays)


def table_kernel(table, gains, w, cols_ref, scale_ref, center_ref, center_gain_ref, center):
    rows, width = table.shape
    gain = gains[0:1]
    for i in range(0, rows, 64):
        part = table[i : i + 64].astype(F32)
        part = part - jnp.mean(part, 1, keepdims=True)
        center[i : i + 64] = part
        center_ref[i : i + 64] = part.astype(BF)
        center_gain_ref[i : i + 64] = (part * gain).astype(BF)
    cols_ref[...] = dot(center_gain_ref[...], w[...]).T.astype(BF)
    first = FIRST_PLACE - 1
    places = center[first:rows]
    gram = dot(places, center[...], 1, 1, HIGH)
    own = jnp.sum(places * places, 1, keepdims=True)
    every = center[...]
    every = dot(jnp.ones((8, width), F32), every * every, 1, 1, HIGH)[0:1]
    scale = lax.rsqrt((2.0 * gram + own + every) / width + 1e-05)
    lane = lax.broadcasted_iota(jnp.int32, scale.shape, 1)
    scale = jnp.where(lane < FIRST_PLACE, scale, 0.0)
    high = scale.astype(BF)
    scale_ref[0 : rows - first] = high
    scale_ref[rows - first :] = (scale - high.astype(F32)).astype(BF)


def fill_hot(hot, code, place):
    rows, length = hot.shape
    for i in range(0, rows, 64):
        index = lax.broadcasted_iota(jnp.int32, (64, length), 0) + i
        hit = (index == code) | (index == place + FIRST_PLACE)
        hot[i : i + 64] = jnp.where(hit, 1.0, 0.0).astype(BF)


def attend_seq(s, heads, tokens, pos_col, seg_col, table, parts, scales, keep):
    att, q_ref, kv_ref, prob_ref, scale_ref, hot, bias = keep
    wide = att.shape[1]
    dim = wide // heads
    code, pos, seg, place = tokens
    fill_hot(hot, code, place)
    length = hot.shape[1]
    both = dot(scales[...], hot[...])
    half = both.shape[0] // 2
    both = both[:half] + both[half:]
    index = lax.broadcasted_iota(jnp.int32, both.shape, 0)
    scale = jnp.sum(jnp.where(index == place + 1, both, 0.0), 0, keepdims=True)
    scale_ref[s] = jnp.broadcast_to(scale, (8, length))
    q = dot(table[parts[0], :], hot[:, 0:LANES]) * scale[:, 0:LANES]
    q_low = q.astype(BF)
    q_ref[s] = q_low
    for i in range(2):
        part = dot(table[parts[1 + i], :], hot[...])
        kv_ref[s, i * wide : (i + 1) * wide] = (part * scale).astype(BF)
    seen = (pos <= pos_col) & (seg == seg_col)
    bias[...] = jnp.where(seen, 0.0, -1e30)
    factor = dim**-0.5
    for h in range(heads):
        part = slice(h * dim, (h + 1) * dim)
        query = (q_low[part].astype(F32) * factor).T.astype(BF)
        scores = dot(query, kv_ref[s, part]) + bias[...]
        expo = jnp.exp(scores - jnp.max(scores, 1, keepdims=True))
        probs = (expo * (1.0 / jnp.sum(expo, 1, keepdims=True))).astype(BF)
        prob_ref[s, h] = probs
        value = kv_ref[s, wide + h * dim : wide + (h + 1) * dim]
        att[s, part] = dot(value, probs, 1, 1).astype(BF)


def attend_back_seq(s, heads, width, code, place, keep, datt, d_table, pairs, grad, grad_q):
    att, q_ref, kv_ref, prob_ref, scale_ref, hot, bias = keep
    wide = att.shape[1]
    dim = wide // heads
    scale = scale_ref[s, 0:1]
    fill_hot(hot, code, place)
    length = hot.shape[1]
    factor = dim**-0.5
    kappa = jnp.zeros((1, length), F32)
    kappa_q = jnp.zeros((1, LANES), F32)
    for h in range(heads):
        part = slice(h * dim, (h + 1) * dim)
        part_v = slice(wide + h * dim, wide + (h + 1) * dim)
        key, value = kv_ref[s, part], kv_ref[s, part_v]
        query = q_ref[s, part]
        d_out = datt[s, part]
        d_rows = d_out.astype(F32).T.astype(BF)
        probs_low = prob_ref[s, h]
        probs = probs_low.astype(F32)
        d_prob = dot(d_rows, value)
        weighted = probs * d_prob
        d_score = (weighted - probs * jnp.sum(weighted, 1, keepdims=True)).astype(BF)
        dv = dot(d_out, probs_low)
        dk = dot(query, d_score) * factor
        dq = dot(key, d_score, 1, 1) * factor
        kappa += jnp.sum(dk * key.astype(F32) + dv * value.astype(F32), 0, keepdims=True)
        kappa_q += jnp.sum(dq * query.astype(F32), 0, keepdims=True)
        grad[part] = (dk * scale).astype(BF)
        grad[part_v] = (dv * scale).astype(BF)
        grad_q[part] = (dq * scale[:, 0:LANES]).astype(BF)
    d_table[0:wide] += dot(grad_q[...], hot[:, 0:LANES], 1, 1)
    d_table[wide:] += dot(grad[...], hot[...], 1, 1)
    kappa = jnp.concatenate([kappa[:, 0:LANES] + kappa_q, kappa[:, LANES:]], 1)
    weight = scale * scale * kappa * (1.0 / width)
    for i in range(0, hot.shape[0], 128):
        left = (hot[i : i + 128].astype(F32) * weight).astype(BF)
        pairs[i : i + 128] += dot(left, hot[...], 1, 1)


def norm_parts(v):
    center = v - jnp.mean(v, -1, keepdims=True)
    scale = lax.rsqrt(jnp.mean(center * center, -1, keepdims=True) + 1e-05)
    return center * scale, scale


def norm_back(unit, scale, gain, d_out):
    d_unit = d_out * gain
    inner = jnp.mean(d_unit * unit, -1, keepdims=True)
    d_in = scale * (d_unit - jnp.mean(d_unit, -1, keepdims=True) - unit * inner)
    return d_in, jnp.sum(d_out * unit, 0, keepdims=True)


GELU_SCALE = 0.7978845608028654
GELU_CUBE = 0.044715
HOP_ONE = ("bl", "kh", "kl")
HOP_TWO = ("kh", "bl", "kl")


def core_kernel(heads, parted, *refs):
    refs = list(refs)

    def take(n):
        got = refs[:n]
        del refs[:n]
        return got

    r = types.SimpleNamespace(heads=heads, parted=parted)
    r.chunks, r.near, r.hops = 2, "bc", (HOP_ONE, HOP_TWO)
    rows, cols, table_t, scales, r.table, r.gains, r.proj, r.head, own, up_own = take(10)
    down_a, down_b = take(2)
    r.d_table, r.pairs, r.up_out, r.down_out, r.proj_out, r.head_out = take(6)
    r.dy_out, r.small_out = take(2)
    r.keep = take(7)
    r.up, r.down, r.u, r.hid, r.low, r.wide_in = take(6)
    r.datt, r.grad, r.grad_q, r.d_up, r.d_down = take(5)
    take_middle(r, take)
    local_sem, send_sem, recv_sem = refs
    links = r.links = Links(send_sem, recv_sem)
    size, here = links.size, links.here
    seqs, width = r.keep[0].shape[0], r.table.shape[1]
    set_places(r)
    if not parted:
        r.up, r.down, r.d_up, r.d_down = up_own, down_a, r.up_out, r.down_out

    local, up_first, late = [], [], []

    def copy_here(src, dst):
        local.append(pltpu.make_async_copy(src, dst, local_sem.at[len(local)]))
        local[-1].start()

    def send_down(ref, part):
        half = r.ff_rows // 2
        for n in range(size["ba"]):
            start = (n * size["bc"] + here["bc"]) * r.ff_rows + part * half
            place = r.down.at[pl.ds(pl.multiple_of(start, 8), half)]
            copy_here(ref.at[n], place)
            waiting.append((ref.at[n], place))

    waiting = []
    if parted:
        for bl in range(2):
            copy_here(up_own.at[bl], r.up.at[r.up_at(here["ba"], bl, here["bc"])])
        for part, ref in enumerate((down_a, down_b)):
            send_down(ref, part)
    links.greet(ALL)
    if parted:
        for bl in range(2):
            for n in range(1, size["ba"]):
                place = r.up.at[r.up_at(here["ba"], bl, here["bc"])]
                up_first.append(links.send(up_own.at[bl], place, {"ba": n}))
        for src, place in waiting:
            late.append(links.send(src, place, {"bc": 1}))

    parts = [slice(i * r.wide, (i + 1) * r.wide) for i in range(3)]

    def forward(s, carry):
        tokens = [rows[s, i : i + 1] for i in range(4)]
        attend_seq(
            s, heads, tokens, cols[s, :, 0:1], cols[s, :, 1:2], table_t, parts, scales, r.keep
        )
        return carry

    lax.fori_loop(0, seqs, forward, 0)
    for c in local:
        c.wait()
    for c in up_first:
        c.wait_recv()
    for n in range(size["ba"] if parted else 0):
        for bl in range(2):
            place = r.up.at[r.up_at(n, bl, here["bc"])]
            late.append(links.send(place, place, {"bc": 1}))
    info = own[...]
    r.low_end, r.high_end, r.target, r.weight, r.kind, code, place = (
        info[:, i : i + 1] for i in range(7)
    )
    columns = lax.broadcasted_iota(jnp.int32, (r.own, r.table.shape[0]), 1).astype(F32)
    r.own_hot = jnp.where((columns == code) | (columns == place), 1.0, 0.0).astype(BF)

    def weights_here():
        for c in late:
            c.wait_recv()

    r.weights_here, r.tick, r.free_weights = weights_here, lambda: None, lambda: None
    r.proj_on = lambda: None

    def backward(s, carry):
        attend_back_seq(
            s,
            heads,
            width,
            rows[s, 0:1],
            rows[s, 3:4],
            r.keep,
            r.datt,
            r.d_table,
            r.pairs,
            r.grad,
            r.grad_q,
        )
        return carry

    r.backward = backward
    middle(r)
    links.finish()


def take_middle(r, take):
    r.up_got, r.up_sum, r.up_got2, r.down_got = take(4)
    r.blk_src, r.blk_buffers = take(2), [take(3), take(3)]
    r.low_parts, r.z_src = take(2), take(2)
    r.z_buffers, r.low_buffers = [take(5), take(5)], [take(5), take(5)]
    r.dz_parts, r.d_src, r.dy_parts, r.results = take(2), take(2), take(1), take(2)


def middle_scratch(na, own, width, ff_cols, chunks, hops):
    up_rows, ff_rows = width // (na * 2 * chunks), ff_cols // (na * 2)
    shapes = [
        (na, chunks, up_rows, ff_cols),
        (na, chunks, up_rows, ff_cols),
        (max(na - 1, 1), chunks, up_rows, ff_cols),
        (na, ff_rows, width),
    ]
    scratch = [pltpu.VMEM(x, BF) for x in shapes]
    block = (own, width // 2)
    four, eight = pltpu.VMEM((4,) + block, BF), pltpu.VMEM((8,) + block, BF)
    scratch += [four] * 2
    for _ in range(2):
        scratch += reduce_buffers(block, BF, ("kl", "kh"))
    scratch += [eight] * 4
    for _ in range(2):
        for hop in hops:
            scratch += reduce_buffers(block, BF, hop[::-1])
    scratch += [eight] * 4 + [pltpu.VMEM((4, own, width), BF)]
    return scratch + [pltpu.VMEM(block, F32)] * 2


def set_places(r):
    size = r.links.size
    r.seqs, r.wide = r.keep[0].shape[:2]
    r.width = r.table.shape[1]
    r.own = r.dy_out.shape[0]
    copies = size["ba"] * 2
    r.blocks, r.ff_rows = r.width // (copies * r.chunks), r.u.shape[1] // copies

    def up_at(ba, chunk, near):
        start = ((ba * r.chunks + chunk) * 2 + near) * r.blocks
        return pl.ds(pl.multiple_of(start, 8), r.blocks)

    def down_at(ba, near):
        return pl.ds(pl.multiple_of((ba * 2 + near) * r.ff_rows, 8), r.ff_rows)

    r.up_at, r.down_at = up_at, down_at


def middle(r):
    links, size, here, parted = r.links, r.links.size, r.links.here, r.parted
    att, proj, gains, results = r.keep[0], r.proj, r.gains, r.results
    seqs, width, own_rows, half = r.seqs, r.width, r.own, r.width // 2
    up, down, u_ref, hid, low, wide_in = r.up, r.down, r.u, r.hid, r.low, r.wide_in
    d_up, d_down, up_at, down_at = r.d_up, r.d_down, r.up_at, r.down_at

    def blk_index(k):
        return (k % 2) * 2 + k // 2

    for s in range(seqs):
        part = dot(att[s], proj[...], 0, 0).astype(BF)
        for j in range(LANES // own_rows):
            block = part[j * own_rows : (j + 1) * own_rows]
            at = blk_index(s * (LANES // own_rows) + j)
            r.blk_src[0][at], r.blk_src[1][at] = block[:, :half], block[:, half:]
    bufs = r.blk_buffers
    jobs = [
        Reduce(links, r.blk_src[i], results[i], ("kl", "kh"), bufs[i][:2], bufs[i][2:])
        for i in range(2)
    ]
    for j in jobs:
        j.step()
    x = dot(r.own_hot, r.table[...])
    r.tick()
    run(jobs)
    x2 = x + jnp.concatenate([results[0][...], results[1][...]], 1)
    unit_mid, scale_mid = norm_parts(x2)
    low_own = (unit_mid * gains[1:2]).astype(BF)

    def start_spread(value, parts):
        gathers = []
        for i, route in enumerate(r.hops):
            me = links.number(route[::-1], {})
            parts[i][me] = value[:, i * half : (i + 1) * half]
            gathers.append(Gather(links, parts[i].at[me], parts[i], route, None))
        for j in gathers:
            j.step()
        return gathers

    def swapped(j):
        kl, kh, bl = j // 4, j // 2 % 2, j % 2
        return (kl * 2 + bl) * 2 + kh

    def end_spread(gathers, parts, whole):
        run(gathers)
        for j in range(8):
            span = slice(j * own_rows, (j + 1) * own_rows)
            whole[span, 0:half] = parts[0][j]
            whole[span, half:] = parts[1][swapped(j)]

    def start_sum(parts, buffers):
        routes = [h[::-1] for h in r.hops]
        jobs = [
            Reduce(links, parts[i], results[i], routes[i], buffers[i][:3], buffers[i][3:])
            for i in range(2)
        ]
        for j in jobs:
            j.step()
        return jobs

    gathers = start_spread(low_own, r.low_parts)
    r.tick()
    end_spread(gathers, r.low_parts, low)
    r.weights_here()
    group = 8 * own_rows
    step = 2 * own_rows

    def hidden(i, carry):
        span = pl.ds(pl.multiple_of(i * step, step), step)
        u = dot(low[span, :], up[...])
        u_ref[span, :] = u
        t = jnp.tanh(GELU_SCALE * (u + GELU_CUBE * u * u * u))
        hid[span, :] = (0.5 * u * (1.0 + t)).astype(BF)
        return carry

    lax.fori_loop(0, group // step, hidden, 0)
    for i in range(group // step):
        part = dot(hid[i * step : (i + 1) * step], down[...]).astype(BF)
        for n in range(2):
            block = part[n * own_rows : (n + 1) * own_rows]
            j = 2 * i + n
            r.z_src[0][j], r.z_src[1][swapped(j)] = block[:, :half], block[:, half:]
    jobs = start_sum(r.z_src, r.z_buffers)
    r.tick()
    run(jobs)
    r.tick()
    x3 = x2 + jnp.concatenate([results[0][...], results[1][...]], 1)

    unit_last, scale_last = norm_parts(x3)
    c_low = (unit_last * gains[2:3]).astype(BF)
    logits = dot(c_low, r.head[...])
    lane = lax.broadcasted_iota(jnp.int32, logits.shape, 1).astype(F32)
    weight, kind = r.weight, r.kind
    masked = jnp.where((lane >= r.low_end) & (lane < r.high_end), logits, -1e30)
    top = jnp.max(masked, 1, keepdims=True)
    expo = jnp.exp(masked - top)
    expo_sum = jnp.sum(expo, 1, keepdims=True)
    hit = jnp.where(lane == r.target, 1.0, 0.0)
    picked = jnp.sum(hit * logits, 1, keepdims=True)
    row_loss = (jnp.log(expo_sum) + top - picked) * weight
    losses = [jnp.sum(jnp.where(kind == j, row_loss, 0.0)) for j in range(PICKS)]
    d_logits = (weight * (expo / expo_sum - hit)).astype(BF)
    dx3, gain_last = norm_back(unit_last, scale_last, gains[2:3], dot(d_logits, r.head[...], 1, 1))
    gathers = start_spread(dx3.astype(BF), r.dz_parts)
    r.head_out[...] = dot(c_low, d_logits, 0, 0).astype(BF)
    end_spread(gathers, r.dz_parts, wide_in)

    def hidden_back(i, carry):
        span = pl.ds(pl.multiple_of(i * step, step), step)
        d_hid = dot(wide_in[span, :], down[...], 1, 1)
        u = u_ref[span, :]
        t = jnp.tanh(GELU_SCALE * (u + GELU_CUBE * u * u * u))
        slope = GELU_SCALE * (1.0 + 3.0 * GELU_CUBE * u * u)
        u_ref[span, :] = d_hid * (0.5 * (1.0 + t) + 0.5 * u * (1.0 - t * t) * slope)
        return carry

    lax.fori_loop(0, group // step, hidden_back, 0)
    for i in range(group // step):
        du = u_ref[i * step : (i + 1) * step].astype(BF)
        part = dot(du, up[...], 1, 1).astype(BF)
        for n in range(2):
            block = part[n * own_rows : (n + 1) * own_rows]
            j = 2 * i + n
            r.d_src[0][j], r.d_src[1][swapped(j)] = block[:, :half], block[:, half:]
    jobs = start_sum(r.d_src, r.low_buffers)
    r.free_weights()
    du = u_ref[...].astype(BF)
    for i in range(0, width, LANES):
        d_up[i : i + LANES] = dot(low[:, i : i + LANES], du, 0, 0).astype(BF)
    sent_up, sent_down = [], []
    for n in range(size["ba"] if parted else 0):
        for chunk in range(r.chunks):
            part = d_up.at[up_at(n, chunk, links.at(r.near, 1))]
            sent_up.append(links.send(part, r.up_got.at[n, chunk], {r.near: 1}))
    for i in range(0, hid.shape[1], LANES):
        d_down[i : i + LANES] = dot(hid[:, i : i + LANES], wide_in[...], 0, 0).astype(BF)
    run(jobs)
    d_low = jnp.concatenate([results[0][...], results[1][...]], 1)
    d_mid, gain_mid = norm_back(unit_mid, scale_mid, gains[1:2], d_low)
    dy = (dx3 + d_mid).astype(BF)
    r.dy_out[...] = dy
    small_out = r.small_out
    small_out[...] = jnp.zeros_like(small_out)
    small_out[0:1] = gain_mid
    small_out[1:2] = gain_last
    lane = lax.broadcasted_iota(jnp.int32, (1, width), 1)
    for j in range(PICKS):
        small_out[2:3] += jnp.where(lane == j, losses[j], 0.0)
    me = links.number(("kl", "kh"), {})
    r.dy_parts[0][me] = dy
    run([Gather(links, r.dy_parts[0].at[me], r.dy_parts[0], ("kh", "kl"), None)])

    for s in range(seqs):
        first = r.dy_parts[0][blk_index(2 * s)]
        second = r.dy_parts[0][blk_index(2 * s + 1)]
        d_rows = jnp.concatenate([first, second], 0)
        r.datt[s] = dot(proj[...], d_rows, 1, 1).astype(BF)
        part = dot(att[s], d_rows)
        if s:
            part = part + r.proj_out[...]
        r.proj_out[...] = part
    r.d_table[...] = jnp.zeros_like(r.d_table)
    r.pairs[...] = jnp.zeros_like(r.pairs)
    r.proj_on()
    for c in sent_up:
        c.wait_recv()
    for n in range(size["ba"] if parted else 0):
        for chunk in range(r.chunks):
            mine = d_up[up_at(n, chunk, here[r.near]), :].astype(F32)
            r.up_sum[n, chunk] = (mine + r.up_got[n, chunk].astype(F32)).astype(BF)
    sent_up = []
    for n in range(1, size["ba"] if parted else 1):
        part = r.up_sum.at[links.at("ba", n)]
        sent_up.append(links.send(part, r.up_got2.at[n - 1], {"ba": n}))
    for n in range(size["ba"] if parted else 0):
        block = d_down.at[down_at(n, links.at(r.near, 1))]
        sent_down.append(links.send(block, r.down_got.at[n], {r.near: 1}))
    r.backward(0, 0)
    for s in range(1, seqs):
        r.backward(s, 0)
    for c in sent_down:
        c.wait_recv()
    for n in range(size["ba"] if parted else 0):
        mine = d_down[down_at(n, here[r.near]), :].astype(F32)
        r.down_out[n] = (mine + r.down_got[n].astype(F32)).astype(BF)
    if parted:
        total = r.up_sum[here["ba"]].astype(F32)
        for n, c in enumerate(sent_up):
            c.wait_recv()
            total = total + r.up_got2[n].astype(F32)
        r.up_out[...] = total.astype(BF)


def core(rows, cols, table_t, scales, table, gains, proj, head, own, up_own, down_a, down_b, heads, ident):
    seqs, _, length = rows.shape
    wide, width = proj.shape
    na = lax.axis_size("ba")
    ff_cols, own_rows = up_own.shape[-1], own.shape[0]
    up_rows, ff_rows = width // (na * 4), ff_cols // (na * 2)
    parted = up_own.ndim == 3
    group = 8 * own_rows
    outs = [
        ((3 * wide, TABLE), F32),
        ((TABLE, TABLE), F32),
        ((2, up_rows, ff_cols) if parted else (width, ff_cols), BF),
        ((na, ff_rows, width) if parted else (ff_cols, width), BF),
        ((wide, width), F32),
        ((width, 256), BF),
        ((own_rows, width), BF),
        ((8, width), F32),
    ]
    scratch = [
        ((seqs, wide, LANES), BF),
        ((seqs, wide, LANES), BF),
        ((seqs, 2 * wide, length), BF),
        ((seqs, heads, LANES, length), BF),
        ((seqs, 8, length), F32),
        ((TABLE, length), BF),
        ((LANES, length), F32),
        ((width, ff_cols), BF),
        ((ff_cols, width), BF),
        ((group, ff_cols), F32),
        ((group, ff_cols), BF),
        ((group, width), BF),
        ((group, width), BF),
        ((seqs, wide, LANES), BF),
        ((2 * wide, length), BF),
        ((wide, LANES), BF),
        ((width, ff_cols), BF),
        ((ff_cols, width), BF),
    ]
    scratch = [pltpu.VMEM(*x) for x in scratch]
    scratch += middle_scratch(na, own_rows, width, ff_cols, 2, (HOP_ONE, HOP_TWO))
    copies = 2 * (na - 1) + 4 * na + 4 + 4 * 6 + 2 + 4 * na + na
    scratch += [
        pltpu.SemaphoreType.DMA((2 + 2 * na,)),
        pltpu.SemaphoreType.DMA((copies,)),
        pltpu.SemaphoreType.DMA((copies,)),
    ]
    vmem = pl.BlockSpec(memory_space=pltpu.VMEM)
    return pl.pallas_call(
        functools.partial(core_kernel, heads, parted),
        out_shape=[jax.ShapeDtypeStruct(*x) for x in outs],
        in_specs=[vmem] * 12,
        out_specs=[vmem] * len(outs),
        scratch_shapes=scratch,
        compiler_params=pltpu.CompilerParams(
            collective_id=ident, has_side_effects=True, vmem_limit_bytes=62 * 2**20
        ),
    )(rows, cols, table_t, scales, table, gains, proj, head, own, up_own, down_a, down_b)


EARLY = ("ba", "bl", "kh", "bc", "kl")
TABLE_WAYS = (("ba", "bl", "bc"), ("ba", "bc", "bl"))
PROJ_WAY = ("ba", "bl", "bc")
TEAM = ("bl", "bc", "kl")
TEAM_HOPS = (("bl", "bc", "kl"), ("bc", "bl", "kl"))
EMBED_WAYS = (("ba", "bl", "bc", "kh", "kl"), EARLY)


def slots(axes, route):
    back, result = route[::-1], []
    for i in range(2 ** len(axes)):
        bits = {a: i >> (len(axes) - 1 - n) & 1 for n, a in enumerate(axes)}
        result.append(sum(bits[a] << (len(back) - 1 - n) for n, a in enumerate(back)))
    return result


def tile_column(kh, t):
    per = HEADS // 4
    t = jnp.minimum(t, 3 * per - 1) if not isinstance(t, int) else min(t, 3 * per - 1)
    return t // per * 2 * per + per * kh + t % per


def grow(x, rows):
    return jnp.concatenate([x, jnp.zeros((rows - x.shape[0],) + x.shape[1:], x.dtype)], 0)


def front_kernel(heads, steps, *refs):
    refs = list(refs)

    def take(n):
        got = refs[:n]
        del refs[:n]
        return got

    r = types.SimpleNamespace(heads=heads, parted=True, steps=steps)
    r.chunks, r.near, r.hops = 4, "kh", TEAM_HOPS
    embed, w_qkv, w_up, w_down, proj_in, tiny, head_in, info, lanes, units, places = take(11)
    r.d_table, r.pairs, r.up_out, r.down_out, proj_part, r.head_out = take(6)
    r.dy_out, r.small_out, r.table, w_own, r.gains, hot_out = take(6)
    r.keep = take(7)
    r.up, r.down, r.u, r.hid, r.low, r.wide_in = take(6)
    r.datt, r.grad, r.grad_q = take(3)
    r.d_up, r.d_down = r.up, r.down
    e_parts = take(2)
    tiny_got, w_low, w_got, info_got, up_src, up_got, proj_got, r.proj = take(8)
    head_got, r.head = take(2)
    t_parts = take(2)
    table_t, center, center_gain, scales, token_info, own_info = take(6)
    proj_new, r.proj_out = take(2)
    take_middle(r, take)
    local_sem, send_sem, recv_sem = refs
    links = r.links = Links(send_sem, recv_sem)
    size, here = links.size, links.here
    width = r.table.shape[1]
    half, rows = width // 2, w_qkv.shape[0]
    set_places(r)
    wide, seqs = r.wide, r.seqs
    padded = w_low.shape[0]
    table_rows = embed.shape[0]
    total, nb = 32, 8
    kl = here["kl"]
    b_here = links.number(BATCH, {})
    me = links.number(ALL, {})

    links.hail(ALL, True)
    low = embed[...].astype(BF)
    for i in range(2):
        slot = links.number(EMBED_WAYS[i][::-1], {})
        e_parts[i][slot] = low[:, i * half : (i + 1) * half]
    early = links.number(EARLY[::-1], {})
    tiny_got[early] = tiny[...]
    for i in range(0, w_low.shape[1], 640):
        w_low[:, i : i + 640] = grow(w_qkv[:, i : i + 640], padded).astype(BF)
    down_place = r.down.at[r.down_at(here["ba"], here["kh"])]
    down_place[...] = w_down[...].astype(BF)
    links.met()
    jobs = []
    for i in range(2):
        slot = links.number(EMBED_WAYS[i][::-1], {})
        jobs.append(Gather(links, e_parts[i].at[slot], e_parts[i], EMBED_WAYS[i], None))
    jobs.append(Gather(links, tiny_got.at[early], tiny_got, EARLY, None))
    for j in jobs:
        j.step()

    def columns_of(move):
        at = {a: links.at(a, move.get(a, 0)) for a in ALL}
        t = at["kl"] * nb + (at["ba"] * 2 + at["bl"]) * 2 + at["bc"]
        return pl.ds(pl.multiple_of(tile_column(at["kh"], t) * LANES, LANES), LANES)

    w_sent = []
    for move in links.moves(ALL):
        w_sent.append(links.send(w_low.at[:, columns_of(move)], w_got.at[me], move))
    own_tile = pltpu.make_async_copy(w_low.at[:, columns_of({})], w_got.at[me], local_sem.at[0])
    own_tile.start()
    blk_here = links.number(BLK, {})
    info_got[blk_here] = info[...]
    info_sent = start_scatters(links, [(info_got.at[blk_here], info_got, BLK, "direct")])

    down_first = [links.send(down_place, down_place, {"ba": 1})]
    late = []

    for g in range(8):
        pieces = []
        for c in range(4):
            i = ((c // 2 * 4 + g // 2) * 2 + c % 2) * 2 + g % 2
            pieces.append(w_up[:, i * r.ff_rows : (i + 1) * r.ff_rows])
        up_src[g] = grow(jnp.concatenate(pieces, 1), padded).astype(BF)
    for j in jobs:
        j.step()
    member = links.number(TEAM, {})
    up_sent = start_scatters(links, [(up_src, up_got, TEAM, "scatter")])
    up_got[member] = up_src[member]
    proj_slot = links.number(PROJ_WAY[::-1], {})
    proj_got[proj_slot] = proj_in[...]
    head_got[early] = head_in[...]
    run(jobs)
    for c in up_sent:
        c.wait_recv()
    up_first, up_places = [], []
    for c in range(4):
        parts = [up_got[c * 2 + n].astype(F32)[:rows] for n in range(2)]
        place = r.up.at[r.up_at(here["ba"], c, here["kh"])]
        place[...] = jnp.concatenate(parts, 0).astype(BF)
        up_places.append(place)

    where = [slots(ALL, way) for way in EMBED_WAYS]
    for i in range(total):
        span = slice(i * table_rows, (i + 1) * table_rows)
        r.table[span, 0:half] = e_parts[0][where[0][i]]
        r.table[span, half:] = e_parts[1][where[1][i]]
    flat = tiny_got[...].reshape(total * 16, LANES)
    row = lax.broadcasted_iota(jnp.int32, (total * 16, width), 0)
    local_row = lax.broadcasted_iota(jnp.int32, (LANES, width), 0)
    r.gains[...] = jnp.zeros_like(r.gains)

    def gain_row(j):
        pick = jnp.where(row == units[0:1] + j, 1.0, 0.0).astype(BF)
        spread = dot(flat, pick, 0, 0)
        r.gains[j : j + 1] = jnp.sum(
            jnp.where(local_row == units[1:2], spread, 0.0), 0, keepdims=True
        )

    gain_row(0)
    for i in range(0, TABLE, 64):
        part = r.table[i : i + 64].astype(F32)
        part = part - jnp.mean(part, 1, keepdims=True)
        center[i : i + 64] = part
        center_gain[i : i + 64] = (part * r.gains[0:1]).astype(BF)
    own_tile.wait()
    for c in w_sent:
        c.wait_recv()
    for i in range(0, total, 2):
        pair = [w_got[i + n].astype(F32)[:rows] for n in range(2)]
        w_own[i * rows : (i + 2) * rows] = jnp.concatenate(pair, 0).astype(BF)
    tile = dot(center_gain[...], w_own[...]).T.astype(BF)
    tables = []
    for i in range(2):
        slot = links.number(TABLE_WAYS[i][::-1], {})
        mine = t_parts[i].at[kl]
        mine[slot] = tile[i * LANES // 2 : (i + 1) * LANES // 2]
        tables.append(Gather(links, mine.at[slot], mine, TABLE_WAYS[i], None))
        tables[i].step()

    late.append(links.send(down_place, down_place, {"kh": 1}))
    for place in up_places:
        up_first.append(links.send(place, place, {"ba": 1}))
        late.append(links.send(place, place, {"kh": 1}))
    proj_job = Gather(links, proj_got.at[proj_slot], proj_got, PROJ_WAY, None)
    proj_job.step()
    head_job = Gather(links, head_got.at[early], head_got, EARLY, None)

    first = FIRST_PLACE - 1
    n_places = TABLE - first
    spots = center[first:TABLE]
    gram = dot(spots, center[...], 1, 1, HIGH)
    own_square = jnp.sum(spots * spots, 1, keepdims=True)
    every = center[...]
    every = dot(jnp.ones((8, width), F32), every * every, 1, 1, HIGH)[0:1]
    scale = lax.rsqrt((2.0 * gram + own_square + every) / width + 1e-05)
    lane = lax.broadcasted_iota(jnp.int32, scale.shape, 1)
    scale = jnp.where(lane < FIRST_PLACE, scale, 0.0)
    high = scale.astype(BF)
    scales[0:n_places] = high
    scales[n_places:] = (scale - high.astype(F32)).astype(BF)
    for j in tables:
        j.step()
    for c in down_first:
        c.wait_recv()
    place = r.down.at[r.down_at(links.at("ba", 1), here["kh"])]
    late.append(links.send(place, place, {"kh": 1}))

    for c in info_sent:
        c.wait_recv()
    fields = info_got[...].reshape(4 * info.shape[0], LANES)
    length = lanes.shape[1]
    lane_time, lane_place, lane_pos = (lanes[i : i + 1] for i in range(3))
    sub = lax.broadcasted_iota(jnp.int32, (LANES, length), 0).astype(F32)
    for s in range(seqs):
        pick = jnp.where(places[0 : fields.shape[0], s : s + 1] == lane_time, 1.0, 0.0)
        by_lane = dot(fields, pick, 0, 0, HIGH)
        code = jnp.sum(jnp.where(sub == lane_place, by_lane, 0.0), 0, keepdims=True)
        code = code + jnp.where(lane_place == OBS, float(PATCH), 0.0)
        code = code + jnp.where(lane_place == OBS + 1, float(PATCH + RET_BINS), 0.0)
        code = code + jnp.where(lane_place == OBS + 2, float(PATCH + RET_BINS + ACTIONS), 0.0)
        token_info[s, 0:1] = jnp.where(lane_place < 0.0, -1.0, code)
        token_info[s, 1:2] = by_lane[OBS + 4 : OBS + 5]
        own_info[s] = dot(pick[:, 0:LANES], fields, 0, 0, HIGH)
        for j in tables:
            if j.stage < 3:
                j.step()
    run(tables)
    other = []
    for i in range(2):
        mine = t_parts[i].at[kl]
        other.append(links.send(mine, mine, {"kl": 1}))
    proj_job.step()
    gain_row(1)
    gain_row(2)
    for c in other:
        c.wait_recv()
    for i in range(2):
        order = slots(BATCH, TABLE_WAYS[i])
        for n in range(2):
            for b in range(nb):
                start = (n * nb + b) * LANES + i * LANES // 2
                table_t[start : start + LANES // 2] = t_parts[i][n, order[b]]

    parts = [
        pl.ds(pl.multiple_of(i * 2 * wide + kl * wide, 64), wide) for i in range(3)
    ]
    query_pos = places[0:LANES, 2:3]

    def forward(s, carry):
        code = token_info[s, 0:1].astype(jnp.int32)
        tokens = (code, lane_pos, token_info[s, 1:2], lane_place.astype(jnp.int32))
        seg_col = own_info[s, :, OBS + 4 : OBS + 5]
        attend_seq(s, heads, tokens, query_pos, seg_col, table_t, parts, scales, r.keep)
        return carry

    for c in up_first:
        c.wait_recv()
    for chunk in range(4):
        place = r.up.at[r.up_at(links.at("ba", 1), chunk, here["kh"])]
        late.append(links.send(place, place, {"kh": 1}))
    head_job.step()
    forward(0, 0)
    proj_job.step()
    head_job.step()
    forward(1, 0)
    run([proj_job])
    order = slots(BATCH, PROJ_WAY)
    for b in range(0, nb, 2):
        pair = [proj_got[order[b + n]].astype(F32)[:rows] for n in range(2)]
        r.proj[b * rows : (b + 2) * rows] = jnp.concatenate(pair, 0).astype(BF)
    head_job.step()

    own = r.own
    mine = own_info[here["kh"], pl.ds(pl.multiple_of(kl * own, 8), own), :]
    slot = lax.broadcasted_iota(jnp.int32, (own, 1), 0) + kl * own
    steps = r.steps
    kind = jnp.where(slot >= 3 * steps, 3.0, jnp.where(slot >= 2 * steps, 2.0, jnp.where(slot >= steps, 1.0, 0.0)))

    def by_kind(*options):
        value = options[3]
        for j in range(3):
            value = jnp.where(kind == j, options[j], value)
        return value

    ret, act, rew = (mine[:, OBS + i : OBS + i + 1] for i in range(3))
    code = by_kind(
        mine[:, OBS - 1 : OBS], ret + PATCH, act + (PATCH + RET_BINS), mine[:, 0:1]
    )
    place = by_kind(OBS - 1.0, float(OBS), OBS + 1.0, 0.0) + FIRST_PLACE
    r.kind = kind
    r.low_end = by_kind(0.0, float(RET_BINS), float(RET_BINS + ACTIONS), 0.0)
    r.high_end = by_kind(
        float(RET_BINS), float(RET_BINS + ACTIONS), float(HEAD_COLS), float(RET_BINS)
    )
    r.target = by_kind(ret, act + RET_BINS, rew + (RET_BINS + ACTIONS), 0.0 * ret)
    counts = jnp.sum(tiny_got[...].astype(F32), 0)[3:4]
    per_game = 1.0 / (GAMES * jnp.maximum(counts, 1.0))
    lane = lax.broadcasted_iota(jnp.int32, (own, LANES), 1).astype(F32)
    game = jnp.where(lane == mine[:, OBS + 3 : OBS + 4], per_game, 0.0)
    r.weight = jnp.where(kind < 3.0, jnp.sum(game, 1, keepdims=True), 0.0)
    columns = lax.broadcasted_iota(jnp.int32, (own, TABLE), 1).astype(F32)
    r.own_hot = jnp.where((columns == code) | (columns == place), 1.0, 0.0).astype(BF)
    hot_out[...] = r.own_hot

    def tick():
        if head_job.stage < len(head_job.route):
            head_job.step()

    def weights_here():
        run([head_job])
        order = slots(ALL, EARLY)
        for i in range(0, total, 2):
            pair = [head_got[order[i + n]].astype(F32)[:rows] for n in range(2)]
            r.head[i * rows : (i + 2) * rows] = jnp.concatenate(pair, 0).astype(BF)
        for c in late:
            c.wait_recv()

    def free_weights():
        links.finish(late + down_first + up_first)

    r.tick, r.weights_here, r.free_weights = tick, weights_here, free_weights
    proj_sent = []

    def proj_on():
        links.finish(proj_job.sent)
        place = slots_for(BATCH, PROJ_BACK)
        for b in range(nb):
            block = grow(r.proj_out[b * rows : (b + 1) * rows], padded)
            proj_got[place[b]] = block.astype(BF)
        there = proj_got.at[pl.ds(links.at("bc", 1) * 4, 4)]
        proj_sent.append(links.send(there, proj_new, {"bc": 1}))

    r.proj_on = proj_on

    def backward(s, carry):
        attend_back_seq(
            s,
            heads,
            width,
            token_info[s, 0:1].astype(jnp.int32),
            lane_place.astype(jnp.int32),
            r.keep,
            r.datt,
            r.d_table,
            r.pairs,
            r.grad,
            r.grad_q,
        )
        return carry

    r.backward = backward
    middle(r)
    proj_sent[0].wait_recv()
    mine = proj_got[pl.ds(here["bc"] * 4, 4)].astype(F32)
    proj_part[...] = (mine + proj_new[...].astype(F32)).astype(BF)
    links.finish()


def front(embed, w_qkv, w_up, w_down, proj_rows, tiny, head, info, steps, ident):
    rows, width = w_qkv.shape[0], embed.shape[1]
    ff_rows = w_down.shape[0]
    ff_cols, na, seqs, padded = 4 * ff_rows, 2, 2, proj_rows.shape[0]
    wide, heads = width // 4, HEADS // 4
    own = seqs * LANES // 4
    group = 8 * own
    length = up_to(TSTEP * steps, LANES)
    tail = length - TSTEP * steps
    place_of = np.repeat(np.array(PLACES), steps)
    time_of = np.tile(np.arange(steps), TSTEP)
    lanes = np.zeros((8, length), np.float32)
    lanes[0] = np.pad(time_of, (0, tail), constant_values=-5)
    lanes[1] = np.pad(place_of, (0, tail), constant_values=-1000)
    lanes[2] = np.pad(time_of * TSTEP + place_of, (0, tail), constant_values=1 << 20)
    units = np.zeros((8, width), np.int32)
    units[0] = np.array(slots(ALL, EARLY))[np.arange(width) // rows] * 16
    units[1] = np.arange(width) % rows
    count = info.shape[0]
    at = np.arange(4 * count)
    place, local = at % count, steps // 4
    places = np.full((max(4 * count, LANES), 8), -9, np.float32)
    for s in range(seqs):
        fits = place // local == s
        places[: 4 * count, s] = np.where(fits, at // count * local + place % local, -9)
    places[:LANES, 2] = lanes[2, :LANES]
    outs = [
        ((3 * wide, TABLE), F32),
        ((TABLE, TABLE), F32),
        ((4, width // 16, ff_cols), BF),
        ((na, ff_rows, width), BF),
        ((4, padded, width), BF),
        ((width, 256), BF),
        ((own, width), BF),
        ((8, width), F32),
        ((TABLE, width), BF),
        ((width, LANES), BF),
        ((8, width), F32),
        ((own, TABLE), BF),
    ]
    n_places = TABLE - FIRST_PLACE + 1
    scratch = [
        ((seqs, wide, LANES), BF),
        ((seqs, wide, LANES), BF),
        ((seqs, 2 * wide, length), BF),
        ((seqs, heads, LANES, length), BF),
        ((seqs, 8, length), F32),
        ((TABLE, length), BF),
        ((LANES, length), F32),
        ((width, ff_cols), BF),
        ((ff_cols, width), BF),
        ((group, ff_cols), F32),
        ((group, ff_cols), BF),
        ((group, width), BF),
        ((group, width), BF),
        ((seqs, wide, LANES), BF),
        ((2 * wide, length), BF),
        ((wide, LANES), BF),
        ((32, TABLE // 32, width // 2), BF),
        ((32, TABLE // 32, width // 2), BF),
        ((32, 16, LANES), BF),
        ((padded, 3 * width), BF),
        ((32, padded, LANES), BF),
        ((4, count, LANES), F32),
        ((8, padded, ff_cols), BF),
        ((8, padded, ff_cols), BF),
        ((8, padded, width), BF),
        ((wide, width), BF),
        ((32, padded, 256), BF),
        ((width, 256), BF),
        ((2, 8, LANES // 2, TABLE), BF),
        ((2, 8, LANES // 2, TABLE), BF),
        ((16 * LANES, TABLE), BF),
        ((TABLE, width), F32),
        ((TABLE, width), BF),
        ((2 * n_places, TABLE), BF),
        ((seqs, 8, length), F32),
        ((seqs, LANES, LANES), F32),
    ]
    scratch = [pltpu.VMEM(*x) for x in scratch]
    scratch += [pltpu.VMEM((4, padded, width), BF), pltpu.VMEM((wide, width), F32)]
    scratch += middle_scratch(na, own, width, ff_cols, 4, TEAM_HOPS)
    copies = 15 + 31 + 3 + 7 + 6 + 2 + 1 + 3 + 5 + 4 + 10 + 4 + 24 + 2 + 10 + 4 + 1
    scratch += [
        pltpu.SemaphoreType.DMA((1,)),
        pltpu.SemaphoreType.DMA((copies,)),
        pltpu.SemaphoreType.DMA((copies,)),
    ]
    vmem = pl.BlockSpec(memory_space=pltpu.VMEM)
    arrays = (embed, w_qkv, w_up, w_down, proj_rows, tiny, head, info)
    arrays += (jnp.asarray(lanes), jnp.asarray(units), jnp.asarray(places))
    return pl.pallas_call(
        functools.partial(front_kernel, heads, steps),
        out_shape=[jax.ShapeDtypeStruct(*x) for x in outs],
        in_specs=[vmem] * len(arrays),
        out_specs=[vmem] * len(outs),
        scratch_shapes=scratch,
        compiler_params=pltpu.CompilerParams(
            collective_id=ident, has_side_effects=True, vmem_limit_bytes=63 * 2**20
        ),
    )(*arrays)


def over_rows(ref, body):
    rows, cols = ref.shape
    wide = 640 if cols % 640 == 0 else cols

    def piece(part, acc):
        for i in range(0, cols, wide):
            acc = acc + body(part, slice(i, i + wide))
        return acc

    start = jnp.zeros((8, LANES), F32)
    if rows % 8:
        return piece(slice(0, rows), start)

    def step(i, acc):
        return piece(pl.ds(pl.multiple_of(i * 8, 8), 8), acc)

    return lax.fori_loop(0, rows // 8, step, start)


def fold(v):
    rows, cols = v.shape
    if rows == 8 and cols % LANES == 0:
        total = v[:, 0:LANES]
        for i in range(LANES, cols, LANES):
            total = total + v[:, i : i + LANES]
        return total
    lane = lax.broadcasted_iota(jnp.int32, (8, LANES), 1)
    row = lax.broadcasted_iota(jnp.int32, (8, LANES), 0)
    return jnp.where((lane == 0) & (row == 0), jnp.sum(v), 0.0)


def lane_sums(values, offset):
    lane = lax.broadcasted_iota(jnp.int32, (8, LANES), 1)
    block = jnp.zeros((8, LANES), F32)
    for i, v in enumerate(values):
        block = jnp.where(lane == i + offset, v, block)
    return block


def sum_squares(ref):
    def add(part, cols):
        v = ref[part, cols]
        return fold(v * v)

    return over_rows(ref, add)


def group_sums(refs):
    sums = [jnp.sum(sum_squares(r)) for r in refs[:6]]
    square = refs[6][...] * refs[6][...]
    return sums + [jnp.sum(square[i : i + 1]) for i in range(3)]


def squares_kernel(*refs):
    grads, masters = refs[:7], refs[7:14]
    losses, out, mine, slots, send_sem, recv_sem = refs[14:]
    links = Links(send_sem, recv_sem)
    block = lane_sums(group_sums(grads), 0) + lane_sums(group_sums(masters), 9)
    links.greet(ALL, True)
    out[...] = sum_everywhere(links, block + losses[...], mine, slots)
    links.finish()


TILE_WAYS = (("kl", "bc", "bl", "ba"), ("kl", "bl", "bc", "ba"))
PROJ_BACK = ("bc", "bl", "ba")
BACK_WAYS = (("kl", "kh", "bc", "bl", "ba"), ("kl", "bc", "kh", "bl", "ba"))
MISC_BACK = BACK_WAYS[1]


def slots_for(axes, route):
    return slots(axes, route[::-1])


def back_kernel(*refs):
    refs = list(refs)

    def take(n):
        got = refs[:n]
        del refs[:n]
        return got

    d_table, pairs, up_in, down_in, proj_in, head_in, dy, small, table, w_own = take(10)
    gains, own_hot, units, losses = take(4)
    masters = take(7)
    grads, sums = take(7), take(1)[0]
    t_src, e_src, t_out, e_out = take(2), take(2), take(2), take(2)
    misc_src, gain_src, proj_out, misc_out, gain_out = take(5)
    center, center_gain, base, dw_src, dw_got, up_src, up_got = take(7)
    t_bufs = [take(7), take(7)]
    e_bufs = [take(9), take(9)]
    proj_bufs, misc_bufs, gain_bufs, down_bufs = take(3), take(9), take(9), take(1)
    mine, slots_got, local_sem, send_sem, recv_sem = refs
    links = Links(send_sem, recv_sem)
    size, here = links.size, links.here
    width = table.shape[1]
    half, rows, padded = width // 2, grads[1].shape[0], dw_src.shape[1]
    wide, total, nb = width // 4, 32, 8
    me = links.number(ALL, {})

    links.hail(ALL, True)
    for ref in t_src:
        ref[...] = jnp.zeros_like(ref)
    order = [slots_for(("kl",) + BATCH, way) for way in TILE_WAYS]
    for v in range(2):

        @pl.when(here["kl"] == v)
        def _(v=v):
            for p in range(3):
                for n in range(wide // 64):
                    unit = (p * 2 + v) * (wide // 64) + n
                    start = p * wide + n * 64
                    value = d_table[start : start + 64].astype(BF)
                    t_src[unit % 2][order[unit % 2][unit // 2]] = value

    links.met()

    def reduction(src, out, way, bufs):
        n = len(way)
        return Reduce(links, src, out, way, bufs[:n], bufs[n:])

    tiles = [reduction(t_src[i], t_out[i], TILE_WAYS[i], t_bufs[i]) for i in range(2)]
    for j in tiles:
        j.step()
    for c in range(4):
        for n in range(2):
            part = up_in[c].astype(F32)[n * rows : (n + 1) * rows]
            up_src[c * 2 + n] = grow(part, padded).astype(BF)
    up_sent = start_scatters(links, [(up_src, up_got, TEAM, "scatter")])
    member = links.number(TEAM, {})
    up_got[member] = up_src[member]
    proj_job = reduction(proj_in, proj_out, PROJ_BACK[1:], proj_bufs)
    proj_job.step()
    down_job = reduction(down_in, grads[4], ("ba",), down_bufs)
    down_job.step()

    owner = lax.broadcasted_iota(jnp.int32, (total, width), 0)
    inner = lax.broadcasted_iota(jnp.int32, (LANES, width), 0)
    inner = jnp.where(inner == units[1:2], 1.0, 0.0)

    def by_owner(row):
        return dot(jnp.where(owner == units[0:1], row, 0.0), inner, 1, 1, HIGH)

    mid, last = by_owner(small[0:1]), by_owner(small[1:2])
    sub = lax.broadcasted_iota(jnp.int32, (padded - rows, 256), 0)
    place = slots_for(ALL, MISC_BACK)
    for i in range(total):
        first, second = (
            jnp.concatenate([v[i : i + 1], v[i : i + 1]], 1) for v in (mid, last)
        )
        tail = jnp.where(sub == 0, first, jnp.where(sub == 1, second, 0.0))
        if i % 2 == 0:
            pair = head_in[i * rows : (i + 2) * rows].astype(F32)
        block = pair[i % 2 * rows : (i % 2 + 1) * rows]
        misc_src[place[i]] = jnp.concatenate([block, tail], 0).astype(BF)
    misc_job = reduction(misc_src, misc_out, MISC_BACK, misc_bufs)
    misc_job.step()
    for j in tiles:
        j.step()

    for i in range(0, TABLE, 64):
        part = table[i : i + 64].astype(F32)
        part = part - jnp.mean(part, 1, keepdims=True)
        center[i : i + 64] = part
        center_gain[i : i + 64] = (part * gains[0:1]).astype(BF)
    for j in tiles:
        j.step()
    proj_job.step()
    for i in range(0, TABLE, LANES):
        low = center[...].astype(BF)
        part = dot(own_hot[:, i : i + LANES], dy[...], 0, 0)
        base[i : i + LANES] = part - dot(pairs[i : i + LANES].astype(BF), low)
    for j in tiles:
        j.step()
    proj_job.step()
    run(tiles)
    d_tile = jnp.concatenate([t_out[0][...], t_out[1][...]], 0).astype(BF)
    d_w = dot(center_gain[...], d_tile, 0, 1)
    for i in range(total):
        dw_src[i] = grow(d_w[i * rows : (i + 1) * rows], padded).astype(BF)

    def tile_of(move):
        at = {a: links.at(a, move.get(a, 0)) for a in ALL}
        t = at["kl"] * nb + (at["ba"] * 2 + at["bl"]) * 2 + at["bc"]
        return pl.ds(pl.multiple_of((at["kh"] * 16 + t) * LANES, LANES), LANES)

    spot = dw_got.at[:, tile_of({})]
    dw_sent = []
    for move in links.moves(ALL):
        dw_sent.append(links.send(dw_src.at[links.number(ALL, move)], spot, move))
    own_tile = pltpu.make_async_copy(dw_src.at[me], spot, local_sem.at[0])
    own_tile.start()
    order = [slots_for(ALL, way) for way in BACK_WAYS]
    gain = jnp.zeros((1, width), F32)
    for i in range(0, TABLE, LANES):
        d_norm = dot(d_tile[:, i : i + LANES], w_own[...], 0, 1)
        gain += jnp.sum(center[i : i + LANES] * d_norm, 0, keepdims=True)
        scaled = d_norm * gains[0:1]
        value = base[i : i + LANES] + scaled - jnp.mean(scaled, 1, keepdims=True)
        value = value.astype(BF)
        for n in range(0, LANES, 16):
            block = (i + n) // 16
            for side in range(2):
                part = value[n : n + 16, side * half : (side + 1) * half]
                e_src[side][order[side][block]] = part
    embeds = [reduction(e_src[i], e_out[i], BACK_WAYS[i], e_bufs[i]) for i in range(2)]
    for j in embeds:
        j.step()
    run([proj_job])

    home = 8 * links.number(BLK, {}) + links.number(BATCH, {})
    stays = home == me
    count = links.used
    links.used += 1
    left, there = home, {}
    for axis in ALL[::-1]:
        there[axis] = lax.rem(left, 2)
        left = left // 2

    def proj_copy():
        return pltpu.make_async_remote_copy(
            src_ref=proj_out.at[0:rows],
            dst_ref=grads[2],
            send_sem=send_sem.at[count],
            recv_sem=recv_sem.at[count],
            device_id=there,
            device_id_type=pl.DeviceIdType.MESH,
        )

    @pl.when(jnp.logical_not(stays))
    def _():
        proj_copy().start()

    @pl.when(stays)
    def _():
        grads[2][...] = proj_out[0:rows]

    gain = by_owner(gain)
    sub = lax.broadcasted_iota(jnp.int32, (16, LANES), 0)
    place = slots_for(ALL, MISC_BACK)
    for i in range(total):
        gain_src[place[i]] = jnp.where(sub == 0, gain[i : i + 1], 0.0).astype(BF)
    gain_job = reduction(gain_src, gain_out, MISC_BACK, gain_bufs)
    gain_job.step()

    misc_job.step()
    block = lane_sums(group_sums(masters), 9)

    def advance():
        for j in embeds + [gain_job, misc_job]:
            if j.stage < len(j.route):
                j.step()

    advance()
    for c in up_sent:
        c.wait_recv()
    ff = grads[3].shape[1] // total
    for j in range(8):
        pieces = []
        for n in range(4):
            member, c = j % 4 * 2 + n % 2, j // 4 * 2 + n // 2
            pieces.append(up_got[member].astype(F32)[:rows, c * ff : (c + 1) * ff])
        grads[3][:, j * 4 * ff : (j + 1) * 4 * ff] = jnp.concatenate(pieces, 1)
    advance()
    own_tile.wait()
    for c in dw_sent:
        c.wait_recv()
    per = HEADS // 4
    for c in range(6 * per):
        t = c % (2 * per) // per * 16 + c // (2 * per) * per + c % per
        value = dw_got[:, t * LANES : (t + 1) * LANES].astype(F32)[:rows]
        grads[1][:, c * LANES : (c + 1) * LANES] = value

    @pl.when(jnp.logical_not(stays))
    def _():
        proj_copy().wait_recv()
        proj_copy().wait_send()

    advance()
    early = [jnp.sum(sum_squares(grads[i])) for i in (1, 2, 3)]
    run(embeds + [gain_job, misc_job])
    run([down_job])
    for side in range(2):
        grads[0][:, side * half : (side + 1) * half] = e_out[side][...]
    n_head = grads[5].shape[1]
    grads[5][...] = misc_out[0:rows, 0:n_head]
    grads[6][0:1] = gain_out[0:1, 0:rows]
    grads[6][1:3] = misc_out[rows : rows + 2, 0:rows]
    late = group_sums([grads[0]] * 4 + [grads[4], grads[5], grads[6]])
    late[1:4] = early
    block = block + lane_sums(late, 0)
    sums[...] = sum_everywhere(links, block + losses[...], mine, slots_got)
    links.finish()


def back(got, masters, loss_tile, ident):
    rows, width = masters[1].shape[0], masters[0].shape[1]
    padded, table_rows, half = up_to(rows, 16), masters[0].shape[0], width // 2
    ff_cols = got[2].shape[2]
    units = np.zeros((8, width), np.int32)
    units[0], units[1] = np.arange(width) // rows, np.arange(width) % rows
    f32_tile = (8, LANES)
    outs = [(w.shape, F32) for w in masters] + [(f32_tile, F32)]
    t_block, e_block = (LANES // 2, TABLE), (table_rows, half)
    scratch = [((16,) + t_block, BF)] * 2 + [((32,) + e_block, BF)] * 2
    scratch += [(t_block, F32)] * 2 + [(e_block, F32)] * 2
    scratch += [
        ((32, padded, 256), BF),
        ((32, 16, LANES), BF),
        ((padded, width), F32),
        ((padded, 256), F32),
        ((16, LANES), F32),
        ((TABLE, width), F32),
        ((TABLE, width), BF),
        ((TABLE, width), F32),
        ((32, padded, LANES), BF),
        ((padded, 32 * LANES), BF),
        ((8, padded, ff_cols), BF),
        ((8, padded, ff_cols), BF),
    ]
    scratch = [pltpu.VMEM(*x) for x in scratch]
    for way in TILE_WAYS:
        scratch += reduce_buffers(t_block, BF, way)
    for way in BACK_WAYS:
        scratch += reduce_buffers(e_block, BF, way)
    scratch += reduce_buffers((padded, width), BF, PROJ_BACK[1:])
    scratch += reduce_buffers((padded, 256), BF, MISC_BACK)
    scratch += reduce_buffers((16, LANES), BF, MISC_BACK)
    scratch += reduce_buffers(got[3].shape[1:], BF, ("ba",))
    copies = 8 + 10 + 3 + 5 + 5 + 1 + 7 + 31 + 1 + 31
    scratch += [
        pltpu.VMEM(f32_tile, F32),
        pltpu.VMEM((31,) + f32_tile, F32),
        pltpu.SemaphoreType.DMA((1,)),
        pltpu.SemaphoreType.DMA((copies,)),
        pltpu.SemaphoreType.DMA((copies,)),
    ]
    vmem = pl.BlockSpec(memory_space=pltpu.VMEM)
    arrays = tuple(got) + (jnp.asarray(units), loss_tile) + tuple(masters)
    result = pl.pallas_call(
        back_kernel,
        out_shape=[jax.ShapeDtypeStruct(*x) for x in outs],
        in_specs=[vmem] * len(arrays),
        out_specs=[vmem] * len(outs),
        scratch_shapes=scratch,
        compiler_params=pltpu.CompilerParams(
            collective_id=ident, has_side_effects=True, vmem_limit_bytes=63 * 2**20
        ),
    )(*arrays)
    return tuple(result[:7]), result[7]


def at_first(body):
    pl.when(pl.program_id(0) == 0)(body)


def moments_kernel(*refs):
    sums = refs[0]
    grads, masters, firsts, seconds = (refs[1 + 7 * i : 8 + 7 * i] for i in range(4))
    means, squares, updates = (refs[29 + 7 * i : 36 + 7 * i] for i in range(3))
    out = refs[50]
    total = sums[...]
    lane = lax.broadcasted_iota(jnp.int32, (8, LANES), 1)
    norm = jnp.sqrt(jnp.sum(jnp.where(lane < 9, total, 0.0)[0:1], 1, keepdims=True))
    factor = jnp.minimum(1.0, 0.05 / norm)

    def one(i):
        def step(part, cols):
            g = factor * grads[i][part, cols]
            mean = 0.9 * firsts[i][part, cols] + 0.1 * g
            square = 0.99 * seconds[i][part, cols] + 0.01 * g * g
            update = (mean * (1.0 / (1.0 - 0.9**STEP))) / (
                jnp.sqrt(square * (1.0 / (1.0 - 0.99**STEP))) + 1e-08
            ) + 0.01 * masters[i][part, cols]
            means[i][part, cols] = mean
            squares[i][part, cols] = square
            updates[i][part, cols] = update
            return fold(update * update)

        return over_rows(grads[i], step)

    @at_first
    def _():
        table = one(0)
        one(6)
        gains = updates[6][...] * updates[6][...]
        values = [jnp.sum(table)] + [0.0] * 5 + [jnp.sum(gains[j : j + 1]) for j in range(3)]
        out[...] = lane_sums(values, 0)

    out[...] += lane_sums([jnp.sum(one(i)) for i in range(1, 6)], 1)


def weights_kernel(*refs):
    update_sums, sums = refs[:2]
    masters, updates = refs[2:9], refs[9:16]
    news, copies = refs[16:23], refs[23:29]
    norms_ref, loss_ref, norm_ref = refs[29:]
    update_norm = jnp.sqrt(update_sums[0:1, 0:9])
    weight_norm = jnp.sqrt(sums[0:1, 9:18])
    ratio = weight_norm / update_norm

    def one(i):
        def step(part, cols):
            new = masters[i][part, cols] - 0.3 * ratio[0:1, i : i + 1] * updates[i][part, cols]
            news[i][part, cols] = new
            copies[i][part, cols] = new.astype(BF)
            return jnp.zeros((8, LANES), F32)

        over_rows(masters[i], step)

    @at_first
    def _():
        norms_ref[0:1] = weight_norm
        norms_ref[1:2] = update_norm
        loss_ref[...] = sums[0:1, 18 : 18 + PICKS]
        lane = lax.broadcasted_iota(jnp.int32, (1, LANES), 1)
        grad_sq = jnp.where(lane < 9, sums[0:1], 0.0)
        norm_ref[...] = jnp.sqrt(jnp.sum(grad_sq, 1, keepdims=True))
        one(0)
        for j in range(3):
            row = slice(j, j + 1)
            news[6][row] = masters[6][row] - 0.3 * ratio[0:1, 6 + j : 7 + j] * updates[6][row]

    for i in range(1, 6):
        one(i)


def by_rows(body, heads, groups, outs, tails):
    shapes = [x.shape for x in groups[0]]
    parts = 5 if all(shapes[i][0] % 80 == 0 or shapes[i][0] == 40 for i in range(1, 6)) else 1

    def spec(i, shape):
        if i in (0, 6):
            return pl.BlockSpec(shape, lambda n: (0, 0))
        return pl.BlockSpec((shape[0] // parts, shape[1]), lambda n: (n, 0))

    def whole(x):
        return pl.BlockSpec(x.shape, lambda n: (0,) * len(x.shape))

    in_specs = [whole(x) for x in heads]
    in_specs += [spec(i, s) for _ in groups for i, s in enumerate(shapes)]
    out_specs = [spec(i, x.shape) for group in outs for i, x in enumerate(group)]
    out_specs += [whole(x) for x in tails]
    return local_call(
        body,
        [x for group in outs for x in group] + tails,
        list(heads) + [x for group in groups for x in group],
        grid=(parts,),
        in_specs=in_specs,
        out_specs=out_specs,
    )


def layer_norm(v, gain):
    center = v - jnp.mean(v, -1, keepdims=True)
    return center * lax.rsqrt(jnp.mean(center * center, -1, keepdims=True) + 1e-05) * gain


def gradients(obs_tokens, returns, actions, rewards, game_ids, segments, masters):
    table, w_qkv, w_proj, w_up, w_down, w_head, gains = masters
    na, nk = lax.axis_size("ba"), 4
    nb, members = na * 4, 2 * nk
    total = nb * nk
    bl = lax.axis_index("bl")
    k = lax.axis_index("kh") * 2 + lax.axis_index("kl")
    g = bl * nk + k
    seqs, steps_here = obs_tokens.shape[:2]
    width = table.shape[1]
    rows, table_rows = w_qkv.shape[0], table.shape[0]
    steps = steps_here * nk
    heads = HEADS // nk
    wide = width // nk
    cols = 3 * wide // nb
    ff_rows = w_down.shape[0]
    padded_rows = up_to(rows, 16)
    padded_table = up_to(table_rows, 16)
    half = width // 2

    info = jnp.pad(obs_tokens, ((0, 0), (0, 0), (0, LANES - OBS)))
    for i, v in enumerate((returns, actions, rewards, game_ids, segments)):
        info = info + jnp.where(jnp.arange(LANES) == OBS + i, v[..., None], 0)
    info = info.reshape(seqs * steps_here, LANES)
    info = pad_to(info, up_to(seqs * steps_here, 8), LANES)
    counts_here = jnp.sum((game_ids[..., None] == jnp.arange(GAMES)).astype(F32), (0, 1))
    to_heads = [(i, i % nb * nk + i // nb) for i in range(total)]
    proj_rows = pad_to(lax.ppermute(w_proj.astype(BF), ALL, to_heads), padded_rows, width)
    if total == 32 and table_rows == 16 and rows == 40 and seqs == 2 and ff_rows == 160:
        tiny = jnp.pad(gains, ((0, 13), (0, LANES - rows)))
        tiny = tiny + jnp.pad(counts_here[None], ((3, 12), (0, LANES - GAMES)))
        tiny = tiny.astype(BF)
        got = front(
            table,
            w_qkv,
            w_up,
            w_down,
            proj_rows,
            tiny,
            pad_to(w_head.astype(BF), padded_rows, 256),
            info.astype(F32),
            steps,
            0,
        )
        losses = jnp.pad(got[7][2:3, :PICKS], ((0, 7), (18, LANES - 18 - PICKS)))
        return back(got, masters, losses, 1)
    table_bf = pad_to(table.astype(BF), padded_table, width)
    small = jnp.concatenate(
        [
            pad_to(w_head.astype(BF), rows, 256),
            pad_to(gains.astype(BF), 3, 256),
            pad_to(counts_here.astype(BF)[None], 1, 256),
            jnp.zeros((padded_rows - rows - 4, 256), BF),
        ]
    )
    qkv_blocks = w_qkv.astype(BF).reshape(rows, 3, nk, wide).transpose(2, 0, 1, 3)
    qkv_blocks = qkv_blocks.reshape(nk, rows, nb, cols).transpose(2, 0, 1, 3)
    qkv_blocks = pad_to(qkv_blocks.reshape(total, rows, cols), padded_rows, LANES)
    ff_cols = na * 2 * ff_rows
    up_blocks = w_up.astype(BF).reshape(rows, na, 2, 2, nk, ff_rows).transpose(2, 4, 0, 1, 3, 5)
    up_blocks = pad_to(up_blocks.reshape(members, rows, ff_cols), padded_rows, ff_cols)
    parted = ff_rows % 32 == 0 and nk * rows % 16 == 0
    down_low = w_down.astype(BF)
    one_way = ("ba", "bl", "bc", "kh", "kl")
    other_way = ("ba", "bl", "kh", "bc", "kl")
    items = [
        (table_bf[:, :half], "gather", one_way),
        (table_bf[:, half:], "gather", other_way),
        (small, "gather", other_way),
        (qkv_blocks, "scatter", ALL),
        (info, "direct", BLK),
        (up_blocks, "scatter", GROUP),
    ]
    if parted:
        items.append((down_low[: ff_rows // 2], "gather", ("ba",)))
    got = exchange(items, 0)
    table_left, table_right, small_all, qkv_mine, info_here, up_mine = got[:6]
    if parted:
        up_mine = up_mine[:, :rows].reshape(2, nk * rows, ff_cols)
        down_first = got[6]
    else:
        up_mine = lax.all_gather(up_mine[:, :rows], COPIES, axis=0, tiled=False)
        up_mine = up_mine.reshape(na, 2, 2, nk, rows, ff_cols).transpose(0, 2, 1, 3, 4, 5)
        up_mine = up_mine.reshape(width, ff_cols)
        down_first = lax.all_gather(down_low, COPIES, axis=0, tiled=True)

    table_all = jnp.concatenate(
        [
            natural(table_left, ALL, one_way)[:, :table_rows],
            natural(table_right, ALL, other_way)[:, :table_rows],
        ],
        2,
    ).reshape(TABLE, width)
    small_all = natural(small_all, ALL, other_way)
    gain = small_all[:, rows : rows + 3, :rows].transpose(1, 0, 2).reshape(3, width).astype(F32)
    w_mine = qkv_mine[:, :rows].reshape(width, LANES)
    scale_rows = TABLE - FIRST_PLACE + 1
    cols_mine, scale_table, center_bf, center_gain = local_call(
        table_kernel,
        [
            jax.ShapeDtypeStruct((LANES, TABLE), BF),
            jax.ShapeDtypeStruct((2 * scale_rows, TABLE), BF),
            jax.ShapeDtypeStruct((TABLE, width), BF),
            jax.ShapeDtypeStruct((TABLE, width), BF),
        ],
        (table_all, pad_to(gain, 8, width), w_mine),
        [pltpu.VMEM((TABLE, width), F32)],
    )
    table_ways = (("ba", "bl", "bc"), ("bc", "bl", "ba"))
    items = [
        (cols_mine[: LANES // 2], "gather", table_ways[0]),
        (cols_mine[LANES // 2 :], "gather", table_ways[1]),
        (proj_rows, "gather", ("ba", "bc", "bl")),
    ]
    if parted:
        items.append((down_low[ff_rows // 2 :], "gather", ("ba",)))
    got = exchange(items, 1)
    down_second = got[3] if parted else jnp.zeros((16, LANES), BF)
    qkv_table = jnp.concatenate(
        [natural(got[0], BATCH, table_ways[0]), natural(got[1], BATCH, table_ways[1])], 1
    )
    qkv_table = qkv_table[:, :cols].reshape(3 * wide, TABLE)
    proj_here = natural(got[2], BATCH, ("ba", "bc", "bl"))[:, :rows].reshape(wide, width)

    info_here = info_here[:, : seqs * steps_here].reshape(nk, seqs, steps_here, LANES)
    info_here = info_here.transpose(1, 0, 2, 3).reshape(seqs, steps, LANES)
    length = up_to(TSTEP * steps, LANES)
    place_of = np.repeat(np.array(PLACES), steps)
    time_of = np.tile(np.arange(steps), TSTEP)
    tail = length - TSTEP * steps
    pos = np.pad(time_of * TSTEP + place_of, (0, tail), constant_values=1 << 20)
    place_of = np.pad(place_of, (0, tail), constant_values=-1000)
    starts = np.array([0] * OBS + [PATCH, PATCH + RET_BINS, PATCH + RET_BINS + ACTIONS])
    codes = info_here[..., :TSTEP] + starts.astype(np.int32)
    codes = jnp.concatenate(
        [codes[..., OBS - 1 : OBS + 2], codes[..., : OBS - 1], codes[..., OBS + 2 :]], -1
    )
    codes = codes.transpose(0, 2, 1).reshape(seqs, TSTEP * steps)
    codes = jnp.pad(codes, ((0, 0), (0, tail)), constant_values=-1)
    seg = jnp.tile(info_here[..., OBS + 4], (1, TSTEP))
    seg = jnp.pad(seg, ((0, 0), (0, tail)), constant_values=-1)
    zero = jnp.zeros((seqs, length), jnp.int32)
    token_rows = jnp.stack(
        [codes, zero + jnp.asarray(pos, jnp.int32), seg, zero + jnp.asarray(place_of, jnp.int32)]
        + [zero] * 4,
        1,
    )
    token_cols = jnp.stack([zero[:, :LANES] + pos[:LANES].astype(np.int32), seg[:, :LANES]], -1)
    token_cols = jnp.pad(token_cols, ((0, 0), (0, 0), (0, LANES - 2)))

    own = seqs * LANES // nk
    slots = lax.rem(k, nk // seqs) * own + jnp.arange(own)
    seq_own = k * own // LANES
    codes_own = lax.dynamic_slice(codes, (seq_own, lax.rem(k, nk // seqs) * own), (1, own))[0]
    place_own = jnp.asarray(place_of[:LANES], jnp.int32)
    place_own = lax.dynamic_slice(place_own, (lax.rem(k, nk // seqs) * own,), (own,))
    kind = slots // steps
    info_seq = lax.dynamic_index_in_dim(info_here, seq_own, 0, False)
    info_own = info_seq.at[lax.rem(slots, steps)].get(mode="promise_in_bounds")
    counts = jnp.sum(small_all[:, rows + 3, :GAMES].astype(F32), 0)
    per_game = 1.0 / (GAMES * jnp.maximum(counts, 1.0))
    game_own = (info_own[:, OBS + 3, None] == jnp.arange(GAMES)).astype(F32)
    weight = jnp.where(kind < PICKS, jnp.sum(game_own * per_game, -1), 0.0)
    low_end = jnp.where(kind == 0, 0, jnp.where(kind == 1, RET_BINS, RET_BINS + ACTIONS))
    high_end = jnp.where(kind == 0, RET_BINS, jnp.where(kind == 1, RET_BINS + ACTIONS, HEAD_COLS))
    target = low_end + jnp.where(
        kind == 0,
        info_own[:, OBS],
        jnp.where(kind == 1, info_own[:, OBS + 1], info_own[:, OBS + 2]),
    )
    own_info = [low_end, high_end, target, weight, kind, codes_own, place_own + FIRST_PLACE]
    own_info = pad_to(jnp.stack([v.astype(F32) for v in own_info], 1), own, LANES)
    head_full = small_all[:, :rows].reshape(width, 256)
    d_table, pairs, sum_up, sum_down, d_proj, d_head, dy_own, d_small = core(
        token_rows,
        token_cols,
        qkv_table,
        scale_table,
        table_all,
        pad_to(gain, 8, width),
        proj_here,
        head_full,
        own_info,
        up_mine,
        down_first,
        down_second,
        heads,
        2,
    )
    d_gain_mid, d_gain_last = d_small[0], d_small[1]
    losses = [d_small[2, j] for j in range(PICKS)]
    columns = jnp.arange(TABLE)
    own_hot = (codes_own[:, None] == columns) | (place_own[:, None] + FIRST_PLACE == columns)
    own_hot = own_hot.astype(BF)
    if not parted:
        sum_up = sum_up.reshape(na, 2, 2, nk, rows, ff_cols).transpose(0, 2, 1, 3, 4, 5)
        sum_up = sum_up.reshape(width, ff_cols)
        sum_up = lax.psum_scatter(sum_up, COPIES, scatter_dimension=0, tiled=True)
        sum_down = lax.psum_scatter(sum_down, COPIES, scatter_dimension=0, tiled=True)

    d_table = pad_to(d_table.astype(BF).reshape(nb, cols, TABLE), LANES, TABLE)
    d_proj = pad_to(d_proj.astype(BF).reshape(nb, rows, width), padded_rows, width)
    proj_route = ("bl", "bc", "ba")
    table_routes = (("bc", "bl", "ba"), ("bl", "bc", "ba"))
    left, right, sum_proj = reduce(
        [
            for_route(d_table[..., : TABLE // 2], BATCH, table_routes[0]),
            for_route(d_table[..., TABLE // 2 :], BATCH, table_routes[1]),
            for_route(d_proj, BATCH, proj_route),
        ],
        table_routes + (proj_route,),
        [],
        3,
    )
    sum_proj = lax.ppermute(sum_proj[:rows], ALL, [(j, i) for i, j in to_heads])
    d_table_mine = jnp.concatenate([left, right], 1).astype(BF)
    d_w = dot(center_gain, d_table_mine, 0, 1)
    d_norm = dot(d_table_mine, w_mine, 0, 1)
    d_gain_first = jnp.sum(center_bf.astype(F32) * d_norm, 0)
    d_scaled = d_norm * gain[0]
    d_embed = (
        d_scaled
        - jnp.mean(d_scaled, 1, keepdims=True)
        - dot(pairs.astype(BF), center_bf)
        + dot(own_hot, dy_own, 0, 0)
    )
    d_gains = jnp.stack([d_gain_first, d_gain_mid, d_gain_last]).astype(BF)
    d_misc = jnp.concatenate(
        [
            d_head.reshape(total, rows, 256),
            pad_to(d_gains.reshape(3, total, rows).transpose(1, 0, 2), 3, 256),
            jnp.zeros((total, padded_rows - rows - 3, 256), BF),
        ],
        1,
    )
    d_w = pad_to(d_w.astype(BF).reshape(total, rows, LANES), padded_rows, LANES)
    d_embed = pad_to(d_embed.astype(BF).reshape(total, table_rows, width), padded_table, width)
    sum_up = pad_to(sum_up.reshape(members, rows, -1), padded_rows, ff_cols)
    one_way = ("kl", "kh", "bc", "bl", "ba")
    other_way = ("kl", "bc", "kh", "bl", "ba")
    arrays = [
        for_route(d_embed[..., :half], ALL, one_way),
        for_route(d_embed[..., half:], ALL, other_way),
        for_route(d_misc, ALL, other_way),
    ]
    routes = (one_way, other_way, other_way)
    if parted:
        arrays.append(sum_down)
        routes += (("ba",),)
    got = reduce(arrays, routes, [(d_w, ALL), (sum_up, GROUP)], 4)
    d_left, d_right, d_misc = got[:3]
    d_ws, ups = got[-2:]
    if parted:
        sum_down = got[3]
    d_embed = jnp.concatenate([d_left, d_right], 1)
    d_ws = d_ws[:, :rows, :cols].reshape(nb, nk, rows, cols).transpose(2, 1, 0, 3)
    d_ws = d_ws.reshape(rows, nk, 3, wide).transpose(0, 2, 1, 3).reshape(rows, 3 * width)
    ups = ups[:, :rows].reshape(2, nk, rows, na, 2, ff_rows).transpose(2, 3, 0, 4, 1, 5)
    ups = ups.reshape(rows, nb * nk * ff_rows)
    grads = (
        d_embed[:table_rows],
        d_ws.astype(F32),
        sum_proj,
        ups.astype(F32),
        sum_down.astype(F32),
        d_misc[:rows, :HEAD_COLS],
        d_misc[rows : rows + 3, :rows],
    )
    loss_tile = jnp.zeros((8, LANES), F32).at[:, 18:21].set(jnp.stack(losses))
    return grads, summed_call(squares_kernel, grads + masters + (loss_tile,), 5)


def shards(*args):
    masters, firsts, seconds = args[6:13], args[13:20], args[20:27]
    grads, sums = gradients(*args[:6], masters)
    like = [jax.ShapeDtypeStruct(w.shape, F32) for w in masters]
    low = [jax.ShapeDtypeStruct(w.shape, BF) for w in masters[:6]]
    tile = jax.ShapeDtypeStruct((8, LANES), F32)
    result = by_rows(
        moments_kernel, (sums,), (grads, masters, firsts, seconds), [like] * 3, [tile]
    )
    means, squares, updates = result[:7], result[7:14], result[14:21]
    update_sums = summed_call(all_sum_kernel, (result[21],), 6)
    last = [jax.ShapeDtypeStruct(x, F32) for x in ((2, 9), (1, PICKS), (1, 1))]
    result = by_rows(
        weights_kernel, (update_sums, sums), (masters, updates), [like, low], last
    )
    news, copies, norms = result[:7], result[7:13], result[13]
    loss_terms, grad_norm = result[14].reshape(PICKS), result[15].reshape(())
    return tuple(news) + tuple(means) + tuple(squares) + tuple(copies) + (
        grad_norm,
        loss_terms,
        norms,
    )


def solution(mesh):
    nb, nk = mesh.shape["batch"], mesh.shape["blk"]
    split = Mesh(mesh.devices.reshape(nb // 4, 2, 2, nk // 2, 2), ALL)
    rows, gains = P(ALL, None), P(None, ALL)
    weights = (rows,) * 6 + (gains,)
    in_specs = (P(BATCH, BLK, None),) + (P(BATCH, BLK),) * 5 + weights * 3
    out_specs = weights * 3 + (rows,) * 6 + (P(), P(), P())
    return jax.shard_map(
        shards, mesh=split, in_specs=in_specs, out_specs=out_specs, check_vma=False
    )
```

```python
import functools
import math
import types

import jax
import jax.numpy as jnp
import numpy as np
from jax import lax
from jax.experimental import pallas as pl
from jax.experimental.pallas import tpu as pltpu
from jax.sharding import Mesh
from jax.sharding import PartitionSpec as P

HEADS = 20
RET_BINS = 120
ACTIONS = 18
GAMES = 41
TSTEP = 39
OBS = 36
PATCH = 331
STEP = 10
HEAD_COLS = 142
TABLE = 512
PICKS = 3
LANES = 128
FIRST_PLACE = PATCH + HEAD_COLS
BF = jnp.bfloat16
F32 = jnp.float32
HIGH = lax.Precision.HIGHEST
BLK = ("kh", "kl")
GROUP = ("bl", "kh", "kl")
BATCH = ("ba", "bl", "bc")
COPIES = ("ba", "bc")
ALL = ("ba", "bl", "bc", "kh", "kl")
VMEM_LIMIT = 56 * 2**20
PLACES = list(range(OBS - 1, OBS + 2)) + [p for p in range(TSTEP) if not OBS - 1 <= p < OBS + 2]


def up_to(n, m):
    return -(-n // m) * m


def pad_to(x, rows, cols):
    if x.shape[-2:] == (rows, cols):
        return x
    widths = [(0, 0)] * (x.ndim - 2) + [(0, rows - x.shape[-2]), (0, cols - x.shape[-1])]
    return jnp.pad(x, widths)


def dot(left, right, ca=1, cb=0, precision=None):
    return lax.dot_general(
        left,
        right,
        (((ca,), (cb,)), ((), ())),
        precision=precision,
        preferred_element_type=F32,
    )


class Links:
    def __init__(self, sends, recvs):
        self.sends, self.recvs, self.open, self.used = sends, recvs, [], 0
        self.size = {a: lax.axis_size(a) for a in ALL}
        self.here = {a: lax.axis_index(a) for a in ALL}

    def at(self, axis, step):
        return lax.rem(self.here[axis] + step, self.size[axis])

    def number(self, axes, steps):
        n = 0
        for a in axes:
            n = n * self.size[a] + self.at(a, steps.get(a, 0))
        return n

    def moves(self, axes):
        result = [{}]
        for a in axes:
            result = [dict(m, **{a: r}) for m in result for r in range(self.size[a])]
        return [{a: r for a, r in m.items() if r} for m in result if any(m.values())]

    def greet(self, axes, everyone=False):
        self.hail(axes, everyone)
        self.met()

    def met(self):
        pl.semaphore_wait(pltpu.get_barrier_semaphore(), self.hailed)

    def hail(self, axes, everyone=False):
        barrier = pltpu.get_barrier_semaphore()
        if everyone:
            moves = self.moves(axes)
        else:
            moves = [{a: r} for a in axes for r in range(1, self.size[a])]
        for move in moves:
            pl.semaphore_signal(
                barrier,
                inc=1,
                device_id={a: self.at(a, r) for a, r in move.items()},
                device_id_type=pl.DeviceIdType.MESH,
            )
        self.hailed = len(moves)

    def send(self, src, dst, move):
        n, self.used = self.used, self.used + 1
        c = pltpu.make_async_remote_copy(
            src_ref=src,
            dst_ref=dst,
            send_sem=self.sends.at[n],
            recv_sem=self.recvs.at[n],
            device_id={a: self.at(a, r) for a, r in move.items()},
            device_id_type=pl.DeviceIdType.MESH,
        )
        c.start()
        self.open.append(c)
        return c

    def finish(self, copies=None):
        copies = list(self.open if copies is None else copies)
        for c in copies:
            c.wait_send()
        self.open = [c for c in self.open if not any(c is d for d in copies)]


class Gather:
    def __init__(self, links, src, dst, route, local):
        self.links, self.src, self.dst = links, src, dst
        self.route, self.local, self.waits, self.stage = list(route), local, [], 0
        self.sent = []

    def step(self):
        links = self.links
        for c in self.waits:
            c.wait_recv()
        self.waits = []
        if self.stage == len(self.route):
            return False
        if self.stage == 1 and self.local is not None:
            self.local.wait()
            self.local = None
        count = math.prod(links.size[a] for a in self.route[: self.stage])
        start = links.number(self.route[self.stage :][::-1], {}) * count
        here = self.dst.at[pl.ds(start, count)]
        block = self.src if self.stage == 0 else here
        there = self.dst.at[start] if self.stage == 0 else here
        axis = self.route[self.stage]
        for r in range(1, links.size[axis]):
            self.waits.append(links.send(block, there, {axis: r}))
        self.sent += self.waits
        self.stage += 1
        return True

    def close(self):
        if self.local is not None:
            self.local.wait()


class Reduce:
    def __init__(self, links, src, out, route, arrived, totals):
        self.links, self.now, self.out = links, src, out
        self.route, self.arrived, self.totals = list(route), arrived, totals
        self.waits, self.stage, self.done = [], 0, False

    def part(self, axis, step):
        count = self.now.shape[0] // self.links.size[axis]
        return pl.ds(self.links.at(axis, step) * count, count)

    def step(self):
        if self.done:
            return False
        if self.stage:
            axis = self.route[self.stage - 1]
            for c in self.waits:
                c.wait_recv()
            total = self.now[self.part(axis, 0)].astype(F32)
            for n in range(len(self.waits)):
                total = total + self.arrived[self.stage - 1][n].astype(F32)
            if self.stage == len(self.route):
                self.out[...] = total[0]
                self.done = True
                return False
            self.now = self.totals[self.stage - 1]
            self.now[...] = total.astype(self.now.dtype)
        axis = self.route[self.stage]
        self.waits = []
        for r in range(1, self.links.size[axis]):
            dst = self.arrived[self.stage].at[r - 1]
            self.waits.append(self.links.send(self.now.at[self.part(axis, r)], dst, {axis: r}))
        self.stage += 1
        return True


def start_scatters(links, jobs):
    copies = []
    for src, dst, axes, kind in jobs:
        me = links.number(axes, {})
        for move in links.moves(axes):
            block = src.at[links.number(axes, move)] if kind == "scatter" else src
            copies.append(links.send(block, dst.at[me], move))
    return copies


def run(jobs):
    jobs = list(jobs)
    while jobs:
        jobs = [j for j in jobs if j.step()]


def sizes_of(axes):
    return tuple(lax.axis_size(a) for a in axes)


def exchange_kernel(kinds, routes, *refs):
    count = len(kinds)
    srcs, dsts = refs[:count], refs[count : 2 * count]
    local_sem, send_sem, recv_sem = refs[2 * count :]
    links = Links(send_sem, recv_sem)
    local = []
    for i, route in enumerate(routes):
        me = links.number(route[::-1] if kinds[i] == "gather" else route, {})
        block = srcs[i].at[me] if kinds[i] == "scatter" else srcs[i]
        local.append(pltpu.make_async_copy(block, dsts[i].at[me], local_sem.at[i]))
        local[-1].start()
    everyone = any(k != "gather" for k in kinds)
    links.greet([a for a in ALL if any(a in x for x in routes)], everyone)
    gathers = [
        Gather(links, srcs[i], dsts[i], routes[i], local[i])
        for i in range(count)
        if kinds[i] == "gather"
    ]
    for j in gathers:
        j.step()
    copies = []
    for i in range(count):
        if kinds[i] != "gather":
            copies += start_scatters(links, [(srcs[i], dsts[i], routes[i], kinds[i])])
    run(gathers)
    for j in gathers:
        j.close()
    for c in copies:
        c.wait_recv()
    for i in range(count):
        if kinds[i] != "gather":
            local[i].wait()
    links.finish()


def natural(x, axes, route):
    back = route[::-1]
    x = x.reshape(sizes_of(back) + x.shape[1:])
    order = [back.index(a) for a in axes] + list(range(len(axes), x.ndim))
    return x.transpose(order).reshape((-1,) + x.shape[len(axes) :])


def for_route(x, axes, route):
    x = x.reshape(sizes_of(axes) + x.shape[1:])
    order = [axes.index(a) for a in route] + list(range(len(axes), x.ndim))
    return x.transpose(order).reshape((-1,) + x.shape[len(axes) :])


def exchange(items, ident):
    arrays, kinds, routes = zip(*items)
    shapes, copies = [], 0
    for x, kind, route in zip(arrays, kinds, routes):
        sizes = sizes_of(route)
        shape = x.shape if kind == "scatter" else (math.prod(sizes),) + x.shape
        shapes.append(jax.ShapeDtypeStruct(shape, x.dtype))
        copies += sum(sizes) - len(sizes) if kind == "gather" else math.prod(sizes) - 1
    n = len(arrays)
    return pl.pallas_call(
        functools.partial(exchange_kernel, kinds, routes),
        out_shape=shapes,
        in_specs=[pl.BlockSpec(memory_space=pl.ANY)] * n,
        out_specs=[pl.BlockSpec(memory_space=pl.ANY)] * n,
        scratch_shapes=[
            pltpu.SemaphoreType.DMA((n,)),
            pltpu.SemaphoreType.DMA((copies,)),
            pltpu.SemaphoreType.DMA((copies,)),
        ],
        compiler_params=pltpu.CompilerParams(collective_id=ident, has_side_effects=True),
    )(*arrays)


def reduce_buffers(shape, dtype, route):
    arrived, totals = [], []
    for i, axis in enumerate(route):
        rest = (math.prod(sizes_of(route[i + 1 :])),) + shape
        arrived.append(pltpu.VMEM((lax.axis_size(axis) - 1,) + rest, dtype))
        totals.append(pltpu.VMEM(rest, dtype))
    return arrived + totals[:-1]


def reduce_kernel(routes, other_axes, *refs):
    refs = list(refs)

    def take(n):
        got = refs[:n]
        del refs[:n]
        return got

    sums = len(routes)
    srcs, other_srcs = take(sums), take(len(other_axes))
    outs, other_dsts = take(sums), take(len(other_axes))
    buffers = [(take(len(r)), take(len(r) - 1)) for r in routes]
    local_sem, send_sem, recv_sem = refs
    links = Links(send_sem, recv_sem)
    local = []
    for i, axes in enumerate(other_axes):
        me = links.number(axes, {})
        local.append(
            pltpu.make_async_copy(other_srcs[i].at[me], other_dsts[i].at[me], local_sem.at[i])
        )
        local[-1].start()
    seen = [a for a in ALL if any(a in x for x in tuple(routes) + other_axes)]
    links.greet(seen, bool(other_axes))
    jobs = [
        Reduce(links, srcs[i], outs[i], routes[i], *buffers[i]) for i in range(sums)
    ]
    for j in jobs:
        j.step()
    copies = start_scatters(
        links, [(s, d, a, "scatter") for s, d, a in zip(other_srcs, other_dsts, other_axes)]
    )
    run(jobs)
    for c in copies:
        c.wait_recv()
    for c in local:
        c.wait()
    links.finish()


def reduce(arrays, routes, others, ident):
    outs = [jax.ShapeDtypeStruct(x.shape[1:], F32) for x in arrays]
    outs += [jax.ShapeDtypeStruct(x.shape, x.dtype) for x, _ in others]
    scratch = []
    for x, route in zip(arrays, routes):
        scratch += reduce_buffers(x.shape[1:], x.dtype, route)
    copies = sum(sum(sizes_of(r)) - len(r) for r in routes)
    copies += sum(math.prod(sizes_of(axes)) - 1 for _, axes in others)
    scratch += [
        pltpu.SemaphoreType.DMA((max(len(others), 1),)),
        pltpu.SemaphoreType.DMA((copies,)),
        pltpu.SemaphoreType.DMA((copies,)),
    ]
    vmem, hbm = pl.BlockSpec(memory_space=pltpu.VMEM), pl.BlockSpec(memory_space=pl.ANY)
    specs = [vmem] * len(arrays) + [hbm] * len(others)
    return pl.pallas_call(
        functools.partial(reduce_kernel, tuple(routes), tuple(axes for _, axes in others)),
        out_shape=outs,
        in_specs=specs,
        out_specs=specs,
        scratch_shapes=scratch,
        compiler_params=pltpu.CompilerParams(
            collective_id=ident, has_side_effects=True, vmem_limit_bytes=VMEM_LIMIT
        ),
    )(*arrays, *[x for x, _ in others])


def sum_everywhere(links, value, mine, slots):
    mine[...] = value
    moves = links.moves(ALL)
    waits = [links.send(mine, slots.at[n], move) for n, move in enumerate(moves)]
    for c in waits:
        c.wait_recv()
    return value + jnp.sum(slots[...], 0)


def all_sum_kernel(value, out, mine, slots, send_sem, recv_sem):
    links = Links(send_sem, recv_sem)
    links.greet(ALL, True)
    out[...] = sum_everywhere(links, value[...], mine, slots)
    links.finish()


def summed_call(body, arrays, ident):
    vmem = pl.BlockSpec(memory_space=pltpu.VMEM)
    copies = math.prod(sizes_of(ALL)) - 1
    return pl.pallas_call(
        body,
        out_shape=jax.ShapeDtypeStruct((8, LANES), F32),
        in_specs=[vmem] * len(arrays),
        out_specs=vmem,
        scratch_shapes=[
            pltpu.VMEM((8, LANES), F32),
            pltpu.VMEM((copies, 8, LANES), F32),
            pltpu.SemaphoreType.DMA((copies,)),
            pltpu.SemaphoreType.DMA((copies,)),
        ],
        compiler_params=pltpu.CompilerParams(
            collective_id=ident, has_side_effects=True, vmem_limit_bytes=VMEM_LIMIT
        ),
    )(*arrays)


def local_call(body, outs, arrays, scratch=(), **kw):
    return pl.pallas_call(
        body,
        out_shape=outs,
        scratch_shapes=list(scratch),
        compiler_params=pltpu.CompilerParams(vmem_limit_bytes=VMEM_LIMIT),
        **kw,
    )(*arrays)


def table_kernel(table, gains, w, cols_ref, scale_ref, center_ref, center_gain_ref, center):
    rows, width = table.shape
    gain = gains[0:1]
    for i in range(0, rows, 64):
        part = table[i : i + 64].astype(F32)
        part = part - jnp.mean(part, 1, keepdims=True)
        center[i : i + 64] = part
        center_ref[i : i + 64] = part.astype(BF)
        center_gain_ref[i : i + 64] = (part * gain).astype(BF)
    cols_ref[...] = dot(center_gain_ref[...], w[...]).T.astype(BF)
    first = FIRST_PLACE - 1
    places = center[first:rows]
    gram = dot(places, center[...], 1, 1, HIGH)
    own = jnp.sum(places * places, 1, keepdims=True)
    every = center[...]
    every = dot(jnp.ones((8, width), F32), every * every, 1, 1, HIGH)[0:1]
    scale = lax.rsqrt((2.0 * gram + own + every) / width + 1e-05)
    lane = lax.broadcasted_iota(jnp.int32, scale.shape, 1)
    scale = jnp.where(lane < FIRST_PLACE, scale, 0.0)
    high = scale.astype(BF)
    scale_ref[0 : rows - first] = high
    scale_ref[rows - first :] = (scale - high.astype(F32)).astype(BF)


def fill_hot(hot, code, place):
    rows, length = hot.shape
    for i in range(0, rows, 64):
        index = lax.broadcasted_iota(jnp.int32, (64, length), 0) + i
        hit = (index == code) | (index == place + FIRST_PLACE)
        hot[i : i + 64] = jnp.where(hit, 1.0, 0.0).astype(BF)


def attend_seq(s, heads, tokens, pos_col, seg_col, table, parts, scales, keep):
    att, q_ref, kv_ref, prob_ref, scale_ref, hot, bias = keep
    wide = att.shape[1]
    dim = wide // heads
    code, pos, seg, place = tokens
    fill_hot(hot, code, place)
    length = hot.shape[1]
    both = dot(scales[...], hot[...])
    half = both.shape[0] // 2
    both = both[:half] + both[half:]
    index = lax.broadcasted_iota(jnp.int32, both.shape, 0)
    scale = jnp.sum(jnp.where(index == place + 1, both, 0.0), 0, keepdims=True)
    scale_ref[s] = jnp.broadcast_to(scale, (8, length))
    q = dot(table[parts[0], :], hot[:, 0:LANES]) * scale[:, 0:LANES]
    q_low = q.astype(BF)
    q_ref[s] = q_low
    for i in range(2):
        part = dot(table[parts[1 + i], :], hot[...])
        kv_ref[s, i * wide : (i + 1) * wide] = (part * scale).astype(BF)
    seen = (pos <= pos_col) & (seg == seg_col)
    bias[...] = jnp.where(seen, 0.0, -1e30)
    factor = dim**-0.5
    for h in range(heads):
        part = slice(h * dim, (h + 1) * dim)
        query = (q_low[part].astype(F32) * factor).T.astype(BF)
        scores = dot(query, kv_ref[s, part]) + bias[...]
        expo = jnp.exp(scores - jnp.max(scores, 1, keepdims=True))
        probs = (expo * (1.0 / jnp.sum(expo, 1, keepdims=True))).astype(BF)
        prob_ref[s, h] = probs
        value = kv_ref[s, wide + h * dim : wide + (h + 1) * dim]
        att[s, part] = dot(value, probs, 1, 1).astype(BF)


def attend_back_seq(s, heads, width, code, place, keep, datt, d_table, pairs, grad, grad_q):
    att, q_ref, kv_ref, prob_ref, scale_ref, hot, bias = keep
    wide = att.shape[1]
    dim = wide // heads
    scale = scale_ref[s, 0:1]
    fill_hot(hot, code, place)
    length = hot.shape[1]
    factor = dim**-0.5
    kappa = jnp.zeros((1, length), F32)
    kappa_q = jnp.zeros((1, LANES), F32)
    for h in range(heads):
        part = slice(h * dim, (h + 1) * dim)
        part_v = slice(wide + h * dim, wide + (h + 1) * dim)
        key, value = kv_ref[s, part], kv_ref[s, part_v]
        query = q_ref[s, part]
        d_out = datt[s, part]
        d_rows = d_out.astype(F32).T.astype(BF)
        probs_low = prob_ref[s, h]
        probs = probs_low.astype(F32)
        d_prob = dot(d_rows, value)
        weighted = probs * d_prob
        d_score = (weighted - probs * jnp.sum(weighted, 1, keepdims=True)).astype(BF)
        dv = dot(d_out, probs_low)
        dk = dot(query, d_score) * factor
        dq = dot(key, d_score, 1, 1) * factor
        kappa += jnp.sum(dk * key.astype(F32) + dv * value.astype(F32), 0, keepdims=True)
        kappa_q += jnp.sum(dq * query.astype(F32), 0, keepdims=True)
        grad[part] = (dk * scale).astype(BF)
        grad[part_v] = (dv * scale).astype(BF)
        grad_q[part] = (dq * scale[:, 0:LANES]).astype(BF)
    d_table[0:wide] += dot(grad_q[...], hot[:, 0:LANES], 1, 1)
    d_table[wide:] += dot(grad[...], hot[...], 1, 1)
    kappa = jnp.concatenate([kappa[:, 0:LANES] + kappa_q, kappa[:, LANES:]], 1)
    weight = scale * scale * kappa * (1.0 / width)
    for i in range(0, hot.shape[0], 128):
        left = (hot[i : i + 128].astype(F32) * weight).astype(BF)
        pairs[i : i + 128] += dot(left, hot[...], 1, 1)


def norm_parts(v):
    center = v - jnp.mean(v, -1, keepdims=True)
    scale = lax.rsqrt(jnp.mean(center * center, -1, keepdims=True) + 1e-05)
    return center * scale, scale


def norm_back(unit, scale, gain, d_out):
    d_unit = d_out * gain
    inner = jnp.mean(d_unit * unit, -1, keepdims=True)
    d_in = scale * (d_unit - jnp.mean(d_unit, -1, keepdims=True) - unit * inner)
    return d_in, jnp.sum(d_out * unit, 0, keepdims=True)


GELU_SCALE = 0.7978845608028654
GELU_CUBE = 0.044715
HOP_ONE = ("bl", "kh", "kl")
HOP_TWO = ("kh", "bl", "kl")


def core_kernel(heads, parted, *refs):
    refs = list(refs)

    def take(n):
        got = refs[:n]
        del refs[:n]
        return got

    r = types.SimpleNamespace(heads=heads, parted=parted)
    r.chunks, r.near, r.hops = 2, "bc", (HOP_ONE, HOP_TWO)
    rows, cols, table_t, scales, r.table, r.gains, r.proj, r.head, own, up_own = take(10)
    down_a, down_b = take(2)
    r.d_table, r.pairs, r.up_out, r.down_out, r.proj_out, r.head_out = take(6)
    r.dy_out, r.small_out = take(2)
    r.keep = take(7)
    r.up, r.down, r.u, r.hid, r.low, r.wide_in = take(6)
    r.datt, r.grad, r.grad_q, r.d_up, r.d_down = take(5)
    take_middle(r, take)
    local_sem, send_sem, recv_sem = refs
    links = r.links = Links(send_sem, recv_sem)
    size, here = links.size, links.here
    seqs, width = r.keep[0].shape[0], r.table.shape[1]
    set_places(r)
    if not parted:
        r.up, r.down, r.d_up, r.d_down = up_own, down_a, r.up_out, r.down_out

    local, up_first, late = [], [], []

    def copy_here(src, dst):
        local.append(pltpu.make_async_copy(src, dst, local_sem.at[len(local)]))
        local[-1].start()

    def send_down(ref, part):
        half = r.ff_rows // 2
        for n in range(size["ba"]):
            start = (n * size["bc"] + here["bc"]) * r.ff_rows + part * half
            place = r.down.at[pl.ds(pl.multiple_of(start, 8), half)]
            copy_here(ref.at[n], place)
            waiting.append((ref.at[n], place))

    waiting = []
    if parted:
        for bl in range(2):
            copy_here(up_own.at[bl], r.up.at[r.up_at(here["ba"], bl, here["bc"])])
        for part, ref in enumerate((down_a, down_b)):
            send_down(ref, part)
    links.greet(ALL)
    if parted:
        for bl in range(2):
            for n in range(1, size["ba"]):
                place = r.up.at[r.up_at(here["ba"], bl, here["bc"])]
                up_first.append(links.send(up_own.at[bl], place, {"ba": n}))
        for src, place in waiting:
            late.append(links.send(src, place, {"bc": 1}))

    parts = [slice(i * r.wide, (i + 1) * r.wide) for i in range(3)]

    def forward(s, carry):
        tokens = [rows[s, i : i + 1] for i in range(4)]
        attend_seq(
            s, heads, tokens, cols[s, :, 0:1], cols[s, :, 1:2], table_t, parts, scales, r.keep
        )
        return carry

    lax.fori_loop(0, seqs, forward, 0)
    for c in local:
        c.wait()
    for c in up_first:
        c.wait_recv()
    for n in range(size["ba"] if parted else 0):
        for bl in range(2):
            place = r.up.at[r.up_at(n, bl, here["bc"])]
            late.append(links.send(place, place, {"bc": 1}))
    info = own[...]
    r.low_end, r.high_end, r.target, r.weight, r.kind, code, place = (
        info[:, i : i + 1] for i in range(7)
    )
    columns = lax.broadcasted_iota(jnp.int32, (r.own, r.table.shape[0]), 1).astype(F32)
    r.own_hot = jnp.where((columns == code) | (columns == place), 1.0, 0.0).astype(BF)

    def weights_here():
        for c in late:
            c.wait_recv()

    r.weights_here, r.tick, r.free_weights = weights_here, lambda: None, lambda: None
    r.proj_on = lambda: None

    def backward(s, carry):
        attend_back_seq(
            s,
            heads,
            width,
            rows[s, 0:1],
            rows[s, 3:4],
            r.keep,
            r.datt,
            r.d_table,
            r.pairs,
            r.grad,
            r.grad_q,
        )
        return carry

    r.backward = backward
    middle(r)
    links.finish()


def take_middle(r, take):
    r.up_got, r.up_sum, r.up_got2, r.down_got = take(4)
    r.blk_src, r.blk_buffers = take(2), [take(3), take(3)]
    r.low_parts, r.z_src = take(2), take(2)
    r.z_buffers, r.low_buffers = [take(5), take(5)], [take(5), take(5)]
    r.dz_parts, r.d_src, r.dy_parts, r.results = take(2), take(2), take(1), take(2)


def middle_scratch(na, own, width, ff_cols, chunks, hops):
    up_rows, ff_rows = width // (na * 2 * chunks), ff_cols // (na * 2)
    shapes = [
        (na, chunks, up_rows, ff_cols),
        (na, chunks, up_rows, ff_cols),
        (max(na - 1, 1), chunks, up_rows, ff_cols),
        (na, ff_rows, width),
    ]
    scratch = [pltpu.VMEM(x, BF) for x in shapes]
    block = (own, width // 2)
    four, eight = pltpu.VMEM((4,) + block, BF), pltpu.VMEM((8,) + block, BF)
    scratch += [four] * 2
    for _ in range(2):
        scratch += reduce_buffers(block, BF, ("kl", "kh"))
    scratch += [eight] * 4
    for _ in range(2):
        for hop in hops:
            scratch += reduce_buffers(block, BF, hop[::-1])
    scratch += [eight] * 4 + [pltpu.VMEM((4, own, width), BF)]
    return scratch + [pltpu.VMEM(block, F32)] * 2


def set_places(r):
    size = r.links.size
    r.seqs, r.wide = r.keep[0].shape[:2]
    r.width = r.table.shape[1]
    r.own = r.dy_out.shape[0]
    copies = size["ba"] * 2
    r.blocks, r.ff_rows = r.width // (copies * r.chunks), r.u.shape[1] // copies

    def up_at(ba, chunk, near):
        start = ((ba * r.chunks + chunk) * 2 + near) * r.blocks
        return pl.ds(pl.multiple_of(start, 8), r.blocks)

    def down_at(ba, near):
        return pl.ds(pl.multiple_of((ba * 2 + near) * r.ff_rows, 8), r.ff_rows)

    r.up_at, r.down_at = up_at, down_at


def middle(r):
    links, size, here, parted = r.links, r.links.size, r.links.here, r.parted
    att, proj, gains, results = r.keep[0], r.proj, r.gains, r.results
    seqs, width, own_rows, half = r.seqs, r.width, r.own, r.width // 2
    up, down, u_ref, hid, low, wide_in = r.up, r.down, r.u, r.hid, r.low, r.wide_in
    d_up, d_down, up_at, down_at = r.d_up, r.d_down, r.up_at, r.down_at

    def blk_index(k):
        return (k % 2) * 2 + k // 2

    for s in range(seqs):
        part = dot(att[s], proj[...], 0, 0).astype(BF)
        for j in range(LANES // own_rows):
            block = part[j * own_rows : (j + 1) * own_rows]
            at = blk_index(s * (LANES // own_rows) + j)
            r.blk_src[0][at], r.blk_src[1][at] = block[:, :half], block[:, half:]
    bufs = r.blk_buffers
    jobs = [
        Reduce(links, r.blk_src[i], results[i], ("kl", "kh"), bufs[i][:2], bufs[i][2:])
        for i in range(2)
    ]
    for j in jobs:
        j.step()
    x = dot(r.own_hot, r.table[...])
    r.tick()
    run(jobs)
    x2 = x + jnp.concatenate([results[0][...], results[1][...]], 1)
    unit_mid, scale_mid = norm_parts(x2)
    low_own = (unit_mid * gains[1:2]).astype(BF)

    def start_spread(value, parts):
        gathers = []
        for i, route in enumerate(r.hops):
            me = links.number(route[::-1], {})
            parts[i][me] = value[:, i * half : (i + 1) * half]
            gathers.append(Gather(links, parts[i].at[me], parts[i], route, None))
        for j in gathers:
            j.step()
        return gathers

    def swapped(j):
        kl, kh, bl = j // 4, j // 2 % 2, j % 2
        return (kl * 2 + bl) * 2 + kh

    def end_spread(gathers, parts, whole):
        run(gathers)
        for j in range(8):
            span = slice(j * own_rows, (j + 1) * own_rows)
            whole[span, 0:half] = parts[0][j]
            whole[span, half:] = parts[1][swapped(j)]

    def start_sum(parts, buffers):
        routes = [h[::-1] for h in r.hops]
        jobs = [
            Reduce(links, parts[i], results[i], routes[i], buffers[i][:3], buffers[i][3:])
            for i in range(2)
        ]
        for j in jobs:
            j.step()
        return jobs

    gathers = start_spread(low_own, r.low_parts)
    r.tick()
    end_spread(gathers, r.low_parts, low)
    r.weights_here()
    group = 8 * own_rows
    step = 2 * own_rows

    def hidden(i, carry):
        span = pl.ds(pl.multiple_of(i * step, step), step)
        u = dot(low[span, :], up[...])
        u_ref[span, :] = u
        t = jnp.tanh(GELU_SCALE * (u + GELU_CUBE * u * u * u))
        hid[span, :] = (0.5 * u * (1.0 + t)).astype(BF)
        return carry

    lax.fori_loop(0, group // step, hidden, 0)
    for i in range(group // step):
        part = dot(hid[i * step : (i + 1) * step], down[...]).astype(BF)
        for n in range(2):
            block = part[n * own_rows : (n + 1) * own_rows]
            j = 2 * i + n
            r.z_src[0][j], r.z_src[1][swapped(j)] = block[:, :half], block[:, half:]
    jobs = start_sum(r.z_src, r.z_buffers)
    r.tick()
    run(jobs)
    r.tick()
    x3 = x2 + jnp.concatenate([results[0][...], results[1][...]], 1)

    unit_last, scale_last = norm_parts(x3)
    c_low = (unit_last * gains[2:3]).astype(BF)
    logits = dot(c_low, r.head[...])
    lane = lax.broadcasted_iota(jnp.int32, logits.shape, 1).astype(F32)
    weight, kind = r.weight, r.kind
    masked = jnp.where((lane >= r.low_end) & (lane < r.high_end), logits, -1e30)
    top = jnp.max(masked, 1, keepdims=True)
    expo = jnp.exp(masked - top)
    expo_sum = jnp.sum(expo, 1, keepdims=True)
    hit = jnp.where(lane == r.target, 1.0, 0.0)
    picked = jnp.sum(hit * logits, 1, keepdims=True)
    row_loss = (jnp.log(expo_sum) + top - picked) * weight
    losses = [jnp.sum(jnp.where(kind == j, row_loss, 0.0)) for j in range(PICKS)]
    d_logits = (weight * (expo / expo_sum - hit)).astype(BF)
    dx3, gain_last = norm_back(unit_last, scale_last, gains[2:3], dot(d_logits, r.head[...], 1, 1))
    gathers = start_spread(dx3.astype(BF), r.dz_parts)
    r.head_out[...] = dot(c_low, d_logits, 0, 0).astype(BF)
    end_spread(gathers, r.dz_parts, wide_in)

    def hidden_back(i, carry):
        span = pl.ds(pl.multiple_of(i * step, step), step)
        d_hid = dot(wide_in[span, :], down[...], 1, 1)
        u = u_ref[span, :]
        t = jnp.tanh(GELU_SCALE * (u + GELU_CUBE * u * u * u))
        slope = GELU_SCALE * (1.0 + 3.0 * GELU_CUBE * u * u)
        u_ref[span, :] = d_hid * (0.5 * (1.0 + t) + 0.5 * u * (1.0 - t * t) * slope)
        return carry

    lax.fori_loop(0, group // step, hidden_back, 0)
    for i in range(group // step):
        du = u_ref[i * step : (i + 1) * step].astype(BF)
        part = dot(du, up[...], 1, 1).astype(BF)
        for n in range(2):
            block = part[n * own_rows : (n + 1) * own_rows]
            j = 2 * i + n
            r.d_src[0][j], r.d_src[1][swapped(j)] = block[:, :half], block[:, half:]
    jobs = start_sum(r.d_src, r.low_buffers)
    r.free_weights()
    du = u_ref[...].astype(BF)
    for i in range(0, width, LANES):
        d_up[i : i + LANES] = dot(low[:, i : i + LANES], du, 0, 0).astype(BF)
    sent_up, sent_down = [], []
    for n in range(size["ba"] if parted else 0):
        for chunk in range(r.chunks):
            part = d_up.at[up_at(n, chunk, links.at(r.near, 1))]
            sent_up.append(links.send(part, r.up_got.at[n, chunk], {r.near: 1}))
    for i in range(0, hid.shape[1], LANES):
        d_down[i : i + LANES] = dot(hid[:, i : i + LANES], wide_in[...], 0, 0).astype(BF)
    run(jobs)
    d_low = jnp.concatenate([results[0][...], results[1][...]], 1)
    d_mid, gain_mid = norm_back(unit_mid, scale_mid, gains[1:2], d_low)
    dy = (dx3 + d_mid).astype(BF)
    r.dy_out[...] = dy
    small_out = r.small_out
    small_out[...] = jnp.zeros_like(small_out)
    small_out[0:1] = gain_mid
    small_out[1:2] = gain_last
    lane = lax.broadcasted_iota(jnp.int32, (1, width), 1)
    for j in range(PICKS):
        small_out[2:3] += jnp.where(lane == j, losses[j], 0.0)
    me = links.number(("kl", "kh"), {})
    r.dy_parts[0][me] = dy
    run([Gather(links, r.dy_parts[0].at[me], r.dy_parts[0], ("kh", "kl"), None)])

    for s in range(seqs):
        first = r.dy_parts[0][blk_index(2 * s)]
        second = r.dy_parts[0][blk_index(2 * s + 1)]
        d_rows = jnp.concatenate([first, second], 0)
        r.datt[s] = dot(proj[...], d_rows, 1, 1).astype(BF)
        part = dot(att[s], d_rows)
        if s:
            part = part + r.proj_out[...]
        r.proj_out[...] = part
    r.d_table[...] = jnp.zeros_like(r.d_table)
    r.pairs[...] = jnp.zeros_like(r.pairs)
    r.proj_on()
    for c in sent_up:
        c.wait_recv()
    for n in range(size["ba"] if parted else 0):
        for chunk in range(r.chunks):
            mine = d_up[up_at(n, chunk, here[r.near]), :].astype(F32)
            r.up_sum[n, chunk] = (mine + r.up_got[n, chunk].astype(F32)).astype(BF)
    sent_up = []
    for n in range(1, size["ba"] if parted else 1):
        part = r.up_sum.at[links.at("ba", n)]
        sent_up.append(links.send(part, r.up_got2.at[n - 1], {"ba": n}))
    for n in range(size["ba"] if parted else 0):
        block = d_down.at[down_at(n, links.at(r.near, 1))]
        sent_down.append(links.send(block, r.down_got.at[n], {r.near: 1}))
    r.backward(0, 0)
    for s in range(1, seqs):
        r.backward(s, 0)
    for c in sent_down:
        c.wait_recv()
    for n in range(size["ba"] if parted else 0):
        mine = d_down[down_at(n, here[r.near]), :].astype(F32)
        r.down_out[n] = (mine + r.down_got[n].astype(F32)).astype(BF)
    if parted:
        total = r.up_sum[here["ba"]].astype(F32)
        for n, c in enumerate(sent_up):
            c.wait_recv()
            total = total + r.up_got2[n].astype(F32)
        r.up_out[...] = total.astype(BF)


def core(rows, cols, table_t, scales, table, gains, proj, head, own, up_own, down_a, down_b, heads, ident):
    seqs, _, length = rows.shape
    wide, width = proj.shape
    na = lax.axis_size("ba")
    ff_cols, own_rows = up_own.shape[-1], own.shape[0]
    up_rows, ff_rows = width // (na * 4), ff_cols // (na * 2)
    parted = up_own.ndim == 3
    group = 8 * own_rows
    outs = [
        ((3 * wide, TABLE), F32),
        ((TABLE, TABLE), F32),
        ((2, up_rows, ff_cols) if parted else (width, ff_cols), BF),
        ((na, ff_rows, width) if parted else (ff_cols, width), BF),
        ((wide, width), F32),
        ((width, 256), BF),
        ((own_rows, width), BF),
        ((8, width), F32),
    ]
    scratch = [
        ((seqs, wide, LANES), BF),
        ((seqs, wide, LANES), BF),
        ((seqs, 2 * wide, length), BF),
        ((seqs, heads, LANES, length), BF),
        ((seqs, 8, length), F32),
        ((TABLE, length), BF),
        ((LANES, length), F32),
        ((width, ff_cols), BF),
        ((ff_cols, width), BF),
        ((group, ff_cols), F32),
        ((group, ff_cols), BF),
        ((group, width), BF),
        ((group, width), BF),
        ((seqs, wide, LANES), BF),
        ((2 * wide, length), BF),
        ((wide, LANES), BF),
        ((width, ff_cols), BF),
        ((ff_cols, width), BF),
    ]
    scratch = [pltpu.VMEM(*x) for x in scratch]
    scratch += middle_scratch(na, own_rows, width, ff_cols, 2, (HOP_ONE, HOP_TWO))
    copies = 2 * (na - 1) + 4 * na + 4 + 4 * 6 + 2 + 4 * na + na
    scratch += [
        pltpu.SemaphoreType.DMA((2 + 2 * na,)),
        pltpu.SemaphoreType.DMA((copies,)),
        pltpu.SemaphoreType.DMA((copies,)),
    ]
    vmem = pl.BlockSpec(memory_space=pltpu.VMEM)
    return pl.pallas_call(
        functools.partial(core_kernel, heads, parted),
        out_shape=[jax.ShapeDtypeStruct(*x) for x in outs],
        in_specs=[vmem] * 12,
        out_specs=[vmem] * len(outs),
        scratch_shapes=scratch,
        compiler_params=pltpu.CompilerParams(
            collective_id=ident, has_side_effects=True, vmem_limit_bytes=62 * 2**20
        ),
    )(rows, cols, table_t, scales, table, gains, proj, head, own, up_own, down_a, down_b)


EARLY = ("ba", "bl", "kh", "bc", "kl")
TABLE_WAYS = (("ba", "bl", "bc"), ("ba", "bc", "bl"))
PROJ_WAY = ("ba", "bl", "bc")
TEAM = ("bl", "bc", "kl")
TEAM_HOPS = (("bl", "bc", "kl"), ("bc", "bl", "kl"))
EMBED_WAYS = (("ba", "bl", "bc", "kh", "kl"), EARLY)


def slots(axes, route):
    back, result = route[::-1], []
    for i in range(2 ** len(axes)):
        bits = {a: i >> (len(axes) - 1 - n) & 1 for n, a in enumerate(axes)}
        result.append(sum(bits[a] << (len(back) - 1 - n) for n, a in enumerate(back)))
    return result


def tile_column(kh, t):
    per = HEADS // 4
    t = jnp.minimum(t, 3 * per - 1) if not isinstance(t, int) else min(t, 3 * per - 1)
    return t // per * 2 * per + per * kh + t % per


def grow(x, rows):
    return jnp.concatenate([x, jnp.zeros((rows - x.shape[0],) + x.shape[1:], x.dtype)], 0)


def front_kernel(heads, steps, *refs):
    refs = list(refs)

    def take(n):
        got = refs[:n]
        del refs[:n]
        return got

    r = types.SimpleNamespace(heads=heads, parted=True, steps=steps)
    r.chunks, r.near, r.hops = 4, "kh", TEAM_HOPS
    embed, w_qkv, w_up, w_down, proj_in, tiny, head_in, info, lanes, units, places = take(11)
    r.d_table, r.pairs, r.up_out, r.down_out, proj_part, r.head_out = take(6)
    r.dy_out, r.small_out, r.table, w_own, r.gains, hot_out = take(6)
    r.keep = take(7)
    r.up, r.down, r.u, r.hid, r.low, r.wide_in = take(6)
    r.datt, r.grad, r.grad_q = take(3)
    r.d_up, r.d_down = r.up, r.down
    e_parts = take(2)
    tiny_got, w_low, w_got, info_got, up_src, up_got, proj_got, r.proj = take(8)
    head_got, r.head = take(2)
    t_parts = take(2)
    table_t, center, center_gain, scales, token_info, own_info = take(6)
    proj_new, r.proj_out = take(2)
    take_middle(r, take)
    local_sem, send_sem, recv_sem = refs
    links = r.links = Links(send_sem, recv_sem)
    size, here = links.size, links.here
    width = r.table.shape[1]
    half, rows = width // 2, w_qkv.shape[0]
    set_places(r)
    wide, seqs = r.wide, r.seqs
    padded = w_low.shape[0]
    table_rows = embed.shape[0]
    total, nb = 32, 8
    kl = here["kl"]
    b_here = links.number(BATCH, {})
    me = links.number(ALL, {})

    links.hail(ALL, True)
    low = embed[...].astype(BF)
    for i in range(2):
        slot = links.number(EMBED_WAYS[i][::-1], {})
        e_parts[i][slot] = low[:, i * half : (i + 1) * half]
    early = links.number(EARLY[::-1], {})
    tiny_got[early] = tiny[...]
    for i in range(0, w_low.shape[1], 640):
        w_low[:, i : i + 640] = grow(w_qkv[:, i : i + 640], padded).astype(BF)
    down_place = r.down.at[r.down_at(here["ba"], here["kh"])]
    down_place[...] = w_down[...].astype(BF)
    links.met()
    jobs = []
    for i in range(2):
        slot = links.number(EMBED_WAYS[i][::-1], {})
        jobs.append(Gather(links, e_parts[i].at[slot], e_parts[i], EMBED_WAYS[i], None))
    jobs.append(Gather(links, tiny_got.at[early], tiny_got, EARLY, None))
    for j in jobs:
        j.step()

    def columns_of(move):
        at = {a: links.at(a, move.get(a, 0)) for a in ALL}
        t = at["kl"] * nb + (at["ba"] * 2 + at["bl"]) * 2 + at["bc"]
        return pl.ds(pl.multiple_of(tile_column(at["kh"], t) * LANES, LANES), LANES)

    w_sent = []
    for move in links.moves(ALL):
        w_sent.append(links.send(w_low.at[:, columns_of(move)], w_got.at[me], move))
    own_tile = pltpu.make_async_copy(w_low.at[:, columns_of({})], w_got.at[me], local_sem.at[0])
    own_tile.start()
    blk_here = links.number(BLK, {})
    info_got[blk_here] = info[...]
    info_sent = start_scatters(links, [(info_got.at[blk_here], info_got, BLK, "direct")])

    down_first = [links.send(down_place, down_place, {"ba": 1})]
    late = []

    for g in range(8):
        pieces = []
        for c in range(4):
            i = ((c // 2 * 4 + g // 2) * 2 + c % 2) * 2 + g % 2
            pieces.append(w_up[:, i * r.ff_rows : (i + 1) * r.ff_rows])
        up_src[g] = grow(jnp.concatenate(pieces, 1), padded).astype(BF)
    for j in jobs:
        j.step()
    member = links.number(TEAM, {})
    up_sent = start_scatters(links, [(up_src, up_got, TEAM, "scatter")])
    up_got[member] = up_src[member]
    proj_slot = links.number(PROJ_WAY[::-1], {})
    proj_got[proj_slot] = proj_in[...]
    head_got[early] = head_in[...]
    run(jobs)
    for c in up_sent:
        c.wait_recv()
    up_first, up_places = [], []
    for c in range(4):
        parts = [up_got[c * 2 + n].astype(F32)[:rows] for n in range(2)]
        place = r.up.at[r.up_at(here["ba"], c, here["kh"])]
        place[...] = jnp.concatenate(parts, 0).astype(BF)
        up_places.append(place)

    where = [slots(ALL, way) for way in EMBED_WAYS]
    for i in range(total):
        span = slice(i * table_rows, (i + 1) * table_rows)
        r.table[span, 0:half] = e_parts[0][where[0][i]]
        r.table[span, half:] = e_parts[1][where[1][i]]
    flat = tiny_got[...].reshape(total * 16, LANES)
    row = lax.broadcasted_iota(jnp.int32, (total * 16, width), 0)
    local_row = lax.broadcasted_iota(jnp.int32, (LANES, width), 0)
    r.gains[...] = jnp.zeros_like(r.gains)

    def gain_row(j):
        pick = jnp.where(row == units[0:1] + j, 1.0, 0.0).astype(BF)
        spread = dot(flat, pick, 0, 0)
        r.gains[j : j + 1] = jnp.sum(
            jnp.where(local_row == units[1:2], spread, 0.0), 0, keepdims=True
        )

    gain_row(0)
    for i in range(0, TABLE, 64):
        part = r.table[i : i + 64].astype(F32)
        part = part - jnp.mean(part, 1, keepdims=True)
        center[i : i + 64] = part
        center_gain[i : i + 64] = (part * r.gains[0:1]).astype(BF)
    own_tile.wait()
    for c in w_sent:
        c.wait_recv()
    for i in range(0, total, 2):
        pair = [w_got[i + n].astype(F32)[:rows] for n in range(2)]
        w_own[i * rows : (i + 2) * rows] = jnp.concatenate(pair, 0).astype(BF)
    tile = dot(center_gain[...], w_own[...]).T.astype(BF)
    tables = []
    for i in range(2):
        slot = links.number(TABLE_WAYS[i][::-1], {})
        mine = t_parts[i].at[kl]
        mine[slot] = tile[i * LANES // 2 : (i + 1) * LANES // 2]
        tables.append(Gather(links, mine.at[slot], mine, TABLE_WAYS[i], None))
        tables[i].step()

    late.append(links.send(down_place, down_place, {"kh": 1}))
    for place in up_places:
        up_first.append(links.send(place, place, {"ba": 1}))
        late.append(links.send(place, place, {"kh": 1}))
    proj_job = Gather(links, proj_got.at[proj_slot], proj_got, PROJ_WAY, None)
    proj_job.step()
    head_job = Gather(links, head_got.at[early], head_got, EARLY, None)

    first = FIRST_PLACE - 1
    n_places = TABLE - first
    spots = center[first:TABLE]
    gram = dot(spots, center[...], 1, 1, HIGH)
    own_square = jnp.sum(spots * spots, 1, keepdims=True)
    every = center[...]
    every = dot(jnp.ones((8, width), F32), every * every, 1, 1, HIGH)[0:1]
    scale = lax.rsqrt((2.0 * gram + own_square + every) / width + 1e-05)
    lane = lax.broadcasted_iota(jnp.int32, scale.shape, 1)
    scale = jnp.where(lane < FIRST_PLACE, scale, 0.0)
    high = scale.astype(BF)
    scales[0:n_places] = high
    scales[n_places:] = (scale - high.astype(F32)).astype(BF)
    for j in tables:
        j.step()
    for c in down_first:
        c.wait_recv()
    place = r.down.at[r.down_at(links.at("ba", 1), here["kh"])]
    late.append(links.send(place, place, {"kh": 1}))

    for c in info_sent:
        c.wait_recv()
    fields = info_got[...].reshape(4 * info.shape[0], LANES)
    length = lanes.shape[1]
    lane_time, lane_place, lane_pos = (lanes[i : i + 1] for i in range(3))
    sub = lax.broadcasted_iota(jnp.int32, (LANES, length), 0).astype(F32)
    for s in range(seqs):
        pick = jnp.where(places[0 : fields.shape[0], s : s + 1] == lane_time, 1.0, 0.0)
        by_lane = dot(fields, pick, 0, 0, HIGH)
        code = jnp.sum(jnp.where(sub == lane_place, by_lane, 0.0), 0, keepdims=True)
        code = code + jnp.where(lane_place == OBS, float(PATCH), 0.0)
        code = code + jnp.where(lane_place == OBS + 1, float(PATCH + RET_BINS), 0.0)
        code = code + jnp.where(lane_place == OBS + 2, float(PATCH + RET_BINS + ACTIONS), 0.0)
        token_info[s, 0:1] = jnp.where(lane_place < 0.0, -1.0, code)
        token_info[s, 1:2] = by_lane[OBS + 4 : OBS + 5]
        own_info[s] = dot(pick[:, 0:LANES], fields, 0, 0, HIGH)
        for j in tables:
            if j.stage < 3:
                j.step()
    run(tables)
    other = []
    for i in range(2):
        mine = t_parts[i].at[kl]
        other.append(links.send(mine, mine, {"kl": 1}))
    proj_job.step()
    gain_row(1)
    gain_row(2)
    for c in other:
        c.wait_recv()
    for i in range(2):
        order = slots(BATCH, TABLE_WAYS[i])
        for n in range(2):
            for b in range(nb):
                start = (n * nb + b) * LANES + i * LANES // 2
                table_t[start : start + LANES // 2] = t_parts[i][n, order[b]]

    parts = [
        pl.ds(pl.multiple_of(i * 2 * wide + kl * wide, 64), wide) for i in range(3)
    ]
    query_pos = places[0:LANES, 2:3]

    def forward(s, carry):
        code = token_info[s, 0:1].astype(jnp.int32)
        tokens = (code, lane_pos, token_info[s, 1:2], lane_place.astype(jnp.int32))
        seg_col = own_info[s, :, OBS + 4 : OBS + 5]
        attend_seq(s, heads, tokens, query_pos, seg_col, table_t, parts, scales, r.keep)
        return carry

    for c in up_first:
        c.wait_recv()
    for chunk in range(4):
        place = r.up.at[r.up_at(links.at("ba", 1), chunk, here["kh"])]
        late.append(links.send(place, place, {"kh": 1}))
    head_job.step()
    forward(0, 0)
    proj_job.step()
    head_job.step()
    forward(1, 0)
    run([proj_job])
    order = slots(BATCH, PROJ_WAY)
    for b in range(0, nb, 2):
        pair = [proj_got[order[b + n]].astype(F32)[:rows] for n in range(2)]
        r.proj[b * rows : (b + 2) * rows] = jnp.concatenate(pair, 0).astype(BF)
    head_job.step()

    own = r.own
    mine = own_info[here["kh"], pl.ds(pl.multiple_of(kl * own, 8), own), :]
    slot = lax.broadcasted_iota(jnp.int32, (own, 1), 0) + kl * own
    steps = r.steps
    kind = jnp.where(slot >= 3 * steps, 3.0, jnp.where(slot >= 2 * steps, 2.0, jnp.where(slot >= steps, 1.0, 0.0)))

    def by_kind(*options):
        value = options[3]
        for j in range(3):
            value = jnp.where(kind == j, options[j], value)
        return value

    ret, act, rew = (mine[:, OBS + i : OBS + i + 1] for i in range(3))
    code = by_kind(
        mine[:, OBS - 1 : OBS], ret + PATCH, act + (PATCH + RET_BINS), mine[:, 0:1]
    )
    place = by_kind(OBS - 1.0, float(OBS), OBS + 1.0, 0.0) + FIRST_PLACE
    r.kind = kind
    r.low_end = by_kind(0.0, float(RET_BINS), float(RET_BINS + ACTIONS), 0.0)
    r.high_end = by_kind(
        float(RET_BINS), float(RET_BINS + ACTIONS), float(HEAD_COLS), float(RET_BINS)
    )
    r.target = by_kind(ret, act + RET_BINS, rew + (RET_BINS + ACTIONS), 0.0 * ret)
    counts = jnp.sum(tiny_got[...].astype(F32), 0)[3:4]
    per_game = 1.0 / (GAMES * jnp.maximum(counts, 1.0))
    lane = lax.broadcasted_iota(jnp.int32, (own, LANES), 1).astype(F32)
    game = jnp.where(lane == mine[:, OBS + 3 : OBS + 4], per_game, 0.0)
    r.weight = jnp.where(kind < 3.0, jnp.sum(game, 1, keepdims=True), 0.0)
    columns = lax.broadcasted_iota(jnp.int32, (own, TABLE), 1).astype(F32)
    r.own_hot = jnp.where((columns == code) | (columns == place), 1.0, 0.0).astype(BF)
    hot_out[...] = r.own_hot

    def tick():
        if head_job.stage < len(head_job.route):
            head_job.step()

    def weights_here():
        run([head_job])
        order = slots(ALL, EARLY)
        for i in range(0, total, 2):
            pair = [head_got[order[i + n]].astype(F32)[:rows] for n in range(2)]
            r.head[i * rows : (i + 2) * rows] = jnp.concatenate(pair, 0).astype(BF)
        for c in late:
            c.wait_recv()

    def free_weights():
        links.finish(late + down_first + up_first)

    r.tick, r.weights_here, r.free_weights = tick, weights_here, free_weights
    proj_sent = []

    def proj_on():
        links.finish(proj_job.sent)
        place = slots_for(BATCH, PROJ_BACK)
        for b in range(nb):
            block = grow(r.proj_out[b * rows : (b + 1) * rows], padded)
            proj_got[place[b]] = block.astype(BF)
        there = proj_got.at[pl.ds(links.at("bc", 1) * 4, 4)]
        proj_sent.append(links.send(there, proj_new, {"bc": 1}))

    r.proj_on = proj_on

    def backward(s, carry):
        attend_back_seq(
            s,
            heads,
            width,
            token_info[s, 0:1].astype(jnp.int32),
            lane_place.astype(jnp.int32),
            r.keep,
            r.datt,
            r.d_table,
            r.pairs,
            r.grad,
            r.grad_q,
        )
        return carry

    r.backward = backward
    middle(r)
    proj_sent[0].wait_recv()
    mine = proj_got[pl.ds(here["bc"] * 4, 4)].astype(F32)
    proj_part[...] = (mine + proj_new[...].astype(F32)).astype(BF)
    links.finish()


def front(embed, w_qkv, w_up, w_down, proj_rows, tiny, head, info, steps, ident):
    rows, width = w_qkv.shape[0], embed.shape[1]
    ff_rows = w_down.shape[0]
    ff_cols, na, seqs, padded = 4 * ff_rows, 2, 2, proj_rows.shape[0]
    wide, heads = width // 4, HEADS // 4
    own = seqs * LANES // 4
    group = 8 * own
    length = up_to(TSTEP * steps, LANES)
    tail = length - TSTEP * steps
    place_of = np.repeat(np.array(PLACES), steps)
    time_of = np.tile(np.arange(steps), TSTEP)
    lanes = np.zeros((8, length), np.float32)
    lanes[0] = np.pad(time_of, (0, tail), constant_values=-5)
    lanes[1] = np.pad(place_of, (0, tail), constant_values=-1000)
    lanes[2] = np.pad(time_of * TSTEP + place_of, (0, tail), constant_values=1 << 20)
    units = np.zeros((8, width), np.int32)
    units[0] = np.array(slots(ALL, EARLY))[np.arange(width) // rows] * 16
    units[1] = np.arange(width) % rows
    count = info.shape[0]
    at = np.arange(4 * count)
    place, local = at % count, steps // 4
    places = np.full((max(4 * count, LANES), 8), -9, np.float32)
    for s in range(seqs):
        fits = place // local == s
        places[: 4 * count, s] = np.where(fits, at // count * local + place % local, -9)
    places[:LANES, 2] = lanes[2, :LANES]
    outs = [
        ((3 * wide, TABLE), F32),
        ((TABLE, TABLE), F32),
        ((4, width // 16, ff_cols), BF),
        ((na, ff_rows, width), BF),
        ((4, padded, width), BF),
        ((width, 256), BF),
        ((own, width), BF),
        ((8, width), F32),
        ((TABLE, width), BF),
        ((width, LANES), BF),
        ((8, width), F32),
        ((own, TABLE), BF),
    ]
    n_places = TABLE - FIRST_PLACE + 1
    scratch = [
        ((seqs, wide, LANES), BF),
        ((seqs, wide, LANES), BF),
        ((seqs, 2 * wide, length), BF),
        ((seqs, heads, LANES, length), BF),
        ((seqs, 8, length), F32),
        ((TABLE, length), BF),
        ((LANES, length), F32),
        ((width, ff_cols), BF),
        ((ff_cols, width), BF),
        ((group, ff_cols), F32),
        ((group, ff_cols), BF),
        ((group, width), BF),
        ((group, width), BF),
        ((seqs, wide, LANES), BF),
        ((2 * wide, length), BF),
        ((wide, LANES), BF),
        ((32, TABLE // 32, width // 2), BF),
        ((32, TABLE // 32, width // 2), BF),
        ((32, 16, LANES), BF),
        ((padded, 3 * width), BF),
        ((32, padded, LANES), BF),
        ((4, count, LANES), F32),
        ((8, padded, ff_cols), BF),
        ((8, padded, ff_cols), BF),
        ((8, padded, width), BF),
        ((wide, width), BF),
        ((32, padded, 256), BF),
        ((width, 256), BF),
        ((2, 8, LANES // 2, TABLE), BF),
        ((2, 8, LANES // 2, TABLE), BF),
        ((16 * LANES, TABLE), BF),
        ((TABLE, width), F32),
        ((TABLE, width), BF),
        ((2 * n_places, TABLE), BF),
        ((seqs, 8, length), F32),
        ((seqs, LANES, LANES), F32),
    ]
    scratch = [pltpu.VMEM(*x) for x in scratch]
    scratch += [pltpu.VMEM((4, padded, width), BF), pltpu.VMEM((wide, width), F32)]
    scratch += middle_scratch(na, own, width, ff_cols, 4, TEAM_HOPS)
    copies = 15 + 31 + 3 + 7 + 6 + 2 + 1 + 3 + 5 + 4 + 10 + 4 + 24 + 2 + 10 + 4 + 1
    scratch += [
        pltpu.SemaphoreType.DMA((1,)),
        pltpu.SemaphoreType.DMA((copies,)),
        pltpu.SemaphoreType.DMA((copies,)),
    ]
    vmem = pl.BlockSpec(memory_space=pltpu.VMEM)
    arrays = (embed, w_qkv, w_up, w_down, proj_rows, tiny, head, info)
    arrays += (jnp.asarray(lanes), jnp.asarray(units), jnp.asarray(places))
    return pl.pallas_call(
        functools.partial(front_kernel, heads, steps),
        out_shape=[jax.ShapeDtypeStruct(*x) for x in outs],
        in_specs=[vmem] * len(arrays),
        out_specs=[vmem] * len(outs),
        scratch_shapes=scratch,
        compiler_params=pltpu.CompilerParams(
            collective_id=ident, has_side_effects=True, vmem_limit_bytes=63 * 2**20
        ),
    )(*arrays)


def over_rows(ref, body):
    rows, cols = ref.shape
    wide = 640 if cols % 640 == 0 else cols

    def piece(part, acc):
        for i in range(0, cols, wide):
            acc = acc + body(part, slice(i, i + wide))
        return acc

    start = jnp.zeros((8, LANES), F32)
    if rows % 8:
        return piece(slice(0, rows), start)

    def step(i, acc):
        return piece(pl.ds(pl.multiple_of(i * 8, 8), 8), acc)

    return lax.fori_loop(0, rows // 8, step, start)


def fold(v):
    rows, cols = v.shape
    if rows == 8 and cols % LANES == 0:
        total = v[:, 0:LANES]
        for i in range(LANES, cols, LANES):
            total = total + v[:, i : i + LANES]
        return total
    lane = lax.broadcasted_iota(jnp.int32, (8, LANES), 1)
    row = lax.broadcasted_iota(jnp.int32, (8, LANES), 0)
    return jnp.where((lane == 0) & (row == 0), jnp.sum(v), 0.0)


def lane_sums(values, offset):
    lane = lax.broadcasted_iota(jnp.int32, (8, LANES), 1)
    block = jnp.zeros((8, LANES), F32)
    for i, v in enumerate(values):
        block = jnp.where(lane == i + offset, v, block)
    return block


def sum_squares(ref):
    def add(part, cols):
        v = ref[part, cols]
        return fold(v * v)

    return over_rows(ref, add)


def group_sums(refs):
    sums = [jnp.sum(sum_squares(r)) for r in refs[:6]]
    square = refs[6][...] * refs[6][...]
    return sums + [jnp.sum(square[i : i + 1]) for i in range(3)]


def squares_kernel(*refs):
    grads, masters = refs[:7], refs[7:14]
    losses, out, mine, slots, send_sem, recv_sem = refs[14:]
    links = Links(send_sem, recv_sem)
    block = lane_sums(group_sums(grads), 0) + lane_sums(group_sums(masters), 9)
    links.greet(ALL, True)
    out[...] = sum_everywhere(links, block + losses[...], mine, slots)
    links.finish()


TILE_WAYS = (("kl", "bc", "bl", "ba"), ("kl", "bl", "bc", "ba"))
PROJ_BACK = ("bc", "bl", "ba")
BACK_WAYS = (("kl", "kh", "bc", "bl", "ba"), ("kl", "bc", "kh", "bl", "ba"))
MISC_BACK = BACK_WAYS[1]


def slots_for(axes, route):
    return slots(axes, route[::-1])


def back_kernel(*refs):
    refs = list(refs)

    def take(n):
        got = refs[:n]
        del refs[:n]
        return got

    d_table, pairs, up_in, down_in, proj_in, head_in, dy, small, table, w_own = take(10)
    gains, own_hot, units, losses = take(4)
    masters = take(7)
    grads, sums = take(7), take(1)[0]
    t_src, e_src, t_out, e_out = take(2), take(2), take(2), take(2)
    misc_src, gain_src, proj_out, misc_out, gain_out = take(5)
    center, center_gain, base, dw_src, dw_got, up_src, up_got = take(7)
    t_bufs = [take(7), take(7)]
    e_bufs = [take(9), take(9)]
    proj_bufs, misc_bufs, gain_bufs, down_bufs = take(3), take(9), take(9), take(1)
    mine, slots_got, local_sem, send_sem, recv_sem = refs
    links = Links(send_sem, recv_sem)
    size, here = links.size, links.here
    width = table.shape[1]
    half, rows, padded = width // 2, grads[1].shape[0], dw_src.shape[1]
    wide, total, nb = width // 4, 32, 8
    me = links.number(ALL, {})

    links.hail(ALL, True)
    for ref in t_src:
        ref[...] = jnp.zeros_like(ref)
    order = [slots_for(("kl",) + BATCH, way) for way in TILE_WAYS]
    for v in range(2):

        @pl.when(here["kl"] == v)
        def _(v=v):
            for p in range(3):
                for n in range(wide // 64):
                    unit = (p * 2 + v) * (wide // 64) + n
                    start = p * wide + n * 64
                    value = d_table[start : start + 64].astype(BF)
                    t_src[unit % 2][order[unit % 2][unit // 2]] = value

    links.met()

    def reduction(src, out, way, bufs):
        n = len(way)
        return Reduce(links, src, out, way, bufs[:n], bufs[n:])

    tiles = [reduction(t_src[i], t_out[i], TILE_WAYS[i], t_bufs[i]) for i in range(2)]
    for j in tiles:
        j.step()
    for c in range(4):
        for n in range(2):
            part = up_in[c].astype(F32)[n * rows : (n + 1) * rows]
            up_src[c * 2 + n] = grow(part, padded).astype(BF)
    up_sent = start_scatters(links, [(up_src, up_got, TEAM, "scatter")])
    member = links.number(TEAM, {})
    up_got[member] = up_src[member]
    proj_job = reduction(proj_in, proj_out, PROJ_BACK[1:], proj_bufs)
    proj_job.step()
    down_job = reduction(down_in, grads[4], ("ba",), down_bufs)
    down_job.step()

    owner = lax.broadcasted_iota(jnp.int32, (total, width), 0)
    inner = lax.broadcasted_iota(jnp.int32, (LANES, width), 0)
    inner = jnp.where(inner == units[1:2], 1.0, 0.0)

    def by_owner(row):
        return dot(jnp.where(owner == units[0:1], row, 0.0), inner, 1, 1, HIGH)

    mid, last = by_owner(small[0:1]), by_owner(small[1:2])
    sub = lax.broadcasted_iota(jnp.int32, (padded - rows, 256), 0)
    place = slots_for(ALL, MISC_BACK)
    for i in range(total):
        first, second = (
            jnp.concatenate([v[i : i + 1], v[i : i + 1]], 1) for v in (mid, last)
        )
        tail = jnp.where(sub == 0, first, jnp.where(sub == 1, second, 0.0))
        if i % 2 == 0:
            pair = head_in[i * rows : (i + 2) * rows].astype(F32)
        block = pair[i % 2 * rows : (i % 2 + 1) * rows]
        misc_src[place[i]] = jnp.concatenate([block, tail], 0).astype(BF)
    misc_job = reduction(misc_src, misc_out, MISC_BACK, misc_bufs)
    misc_job.step()
    for j in tiles:
        j.step()

    for i in range(0, TABLE, 64):
        part = table[i : i + 64].astype(F32)
        part = part - jnp.mean(part, 1, keepdims=True)
        center[i : i + 64] = part
        center_gain[i : i + 64] = (part * gains[0:1]).astype(BF)
    for j in tiles:
        j.step()
    proj_job.step()
    for i in range(0, TABLE, LANES):
        low = center[...].astype(BF)
        part = dot(own_hot[:, i : i + LANES], dy[...], 0, 0)
        base[i : i + LANES] = part - dot(pairs[i : i + LANES].astype(BF), low)
    for j in tiles:
        j.step()
    proj_job.step()
    run(tiles)
    d_tile = jnp.concatenate([t_out[0][...], t_out[1][...]], 0).astype(BF)
    order = [slots_for(ALL, way) for way in BACK_WAYS]
    gain = jnp.zeros((1, width), F32)
    for i in range(0, TABLE, LANES):
        d_norm = dot(d_tile[:, i : i + LANES], w_own[...], 0, 1)
        gain += jnp.sum(center[i : i + LANES] * d_norm, 0, keepdims=True)
        scaled = d_norm * gains[0:1]
        value = base[i : i + LANES] + scaled - jnp.mean(scaled, 1, keepdims=True)
        value = value.astype(BF)
        for n in range(0, LANES, 16):
            block = (i + n) // 16
            for side in range(2):
                part = value[n : n + 16, side * half : (side + 1) * half]
                e_src[side][order[side][block]] = part
    embeds = [reduction(e_src[i], e_out[i], BACK_WAYS[i], e_bufs[i]) for i in range(2)]
    for j in embeds:
        j.step()
    d_w = dot(center_gain[...], d_tile, 0, 1)
    for i in range(total):
        dw_src[i] = grow(d_w[i * rows : (i + 1) * rows], padded).astype(BF)

    def tile_of(move):
        at = {a: links.at(a, move.get(a, 0)) for a in ALL}
        t = at["kl"] * nb + (at["ba"] * 2 + at["bl"]) * 2 + at["bc"]
        return pl.ds(pl.multiple_of((at["kh"] * 16 + t) * LANES, LANES), LANES)

    spot = dw_got.at[:, tile_of({})]
    dw_sent = []
    for move in links.moves(ALL):
        dw_sent.append(links.send(dw_src.at[links.number(ALL, move)], spot, move))
    own_tile = pltpu.make_async_copy(dw_src.at[me], spot, local_sem.at[0])
    own_tile.start()
    run([proj_job])

    home = 8 * links.number(BLK, {}) + links.number(BATCH, {})
    stays = home == me
    count = links.used
    links.used += 1
    left, there = home, {}
    for axis in ALL[::-1]:
        there[axis] = lax.rem(left, 2)
        left = left // 2

    def proj_copy():
        return pltpu.make_async_remote_copy(
            src_ref=proj_out.at[0:rows],
            dst_ref=grads[2],
            send_sem=send_sem.at[count],
            recv_sem=recv_sem.at[count],
            device_id=there,
            device_id_type=pl.DeviceIdType.MESH,
        )

    @pl.when(jnp.logical_not(stays))
    def _():
        proj_copy().start()

    @pl.when(stays)
    def _():
        grads[2][...] = proj_out[0:rows]

    gain = by_owner(gain)
    sub = lax.broadcasted_iota(jnp.int32, (16, LANES), 0)
    place = slots_for(ALL, MISC_BACK)
    for i in range(total):
        gain_src[place[i]] = jnp.where(sub == 0, gain[i : i + 1], 0.0).astype(BF)
    gain_job = reduction(gain_src, gain_out, MISC_BACK, gain_bufs)
    gain_job.step()

    misc_job.step()
    block = lane_sums(group_sums(masters), 9)

    def advance():
        for j in embeds + [gain_job, misc_job]:
            if j.stage < len(j.route):
                j.step()

    advance()
    for c in up_sent:
        c.wait_recv()
    ff = grads[3].shape[1] // total
    for j in range(8):
        pieces = []
        for n in range(4):
            member, c = j % 4 * 2 + n % 2, j // 4 * 2 + n // 2
            pieces.append(up_got[member].astype(F32)[:rows, c * ff : (c + 1) * ff])
        grads[3][:, j * 4 * ff : (j + 1) * 4 * ff] = jnp.concatenate(pieces, 1)
    advance()
    own_tile.wait()
    for c in dw_sent:
        c.wait_recv()
    per = HEADS // 4
    for c in range(6 * per):
        t = c % (2 * per) // per * 16 + c // (2 * per) * per + c % per
        value = dw_got[:, t * LANES : (t + 1) * LANES].astype(F32)[:rows]
        grads[1][:, c * LANES : (c + 1) * LANES] = value

    @pl.when(jnp.logical_not(stays))
    def _():
        proj_copy().wait_recv()
        proj_copy().wait_send()

    advance()
    early = [jnp.sum(sum_squares(grads[i])) for i in (1, 2, 3)]
    run(embeds + [gain_job, misc_job])
    run([down_job])
    for side in range(2):
        grads[0][:, side * half : (side + 1) * half] = e_out[side][...]
    n_head = grads[5].shape[1]
    grads[5][...] = misc_out[0:rows, 0:n_head]
    grads[6][0:1] = gain_out[0:1, 0:rows]
    grads[6][1:3] = misc_out[rows : rows + 2, 0:rows]
    late = group_sums([grads[0]] * 4 + [grads[4], grads[5], grads[6]])
    late[1:4] = early
    block = block + lane_sums(late, 0)
    sums[...] = sum_everywhere(links, block + losses[...], mine, slots_got)
    links.finish()


def back(got, masters, loss_tile, ident):
    rows, width = masters[1].shape[0], masters[0].shape[1]
    padded, table_rows, half = up_to(rows, 16), masters[0].shape[0], width // 2
    ff_cols = got[2].shape[2]
    units = np.zeros((8, width), np.int32)
    units[0], units[1] = np.arange(width) // rows, np.arange(width) % rows
    f32_tile = (8, LANES)
    outs = [(w.shape, F32) for w in masters] + [(f32_tile, F32)]
    t_block, e_block = (LANES // 2, TABLE), (table_rows, half)
    scratch = [((16,) + t_block, BF)] * 2 + [((32,) + e_block, BF)] * 2
    scratch += [(t_block, F32)] * 2 + [(e_block, F32)] * 2
    scratch += [
        ((32, padded, 256), BF),
        ((32, 16, LANES), BF),
        ((padded, width), F32),
        ((padded, 256), F32),
        ((16, LANES), F32),
        ((TABLE, width), F32),
        ((TABLE, width), BF),
        ((TABLE, width), F32),
        ((32, padded, LANES), BF),
        ((padded, 32 * LANES), BF),
        ((8, padded, ff_cols), BF),
        ((8, padded, ff_cols), BF),
    ]
    scratch = [pltpu.VMEM(*x) for x in scratch]
    for way in TILE_WAYS:
        scratch += reduce_buffers(t_block, BF, way)
    for way in BACK_WAYS:
        scratch += reduce_buffers(e_block, BF, way)
    scratch += reduce_buffers((padded, width), BF, PROJ_BACK[1:])
    scratch += reduce_buffers((padded, 256), BF, MISC_BACK)
    scratch += reduce_buffers((16, LANES), BF, MISC_BACK)
    scratch += reduce_buffers(got[3].shape[1:], BF, ("ba",))
    copies = 8 + 10 + 3 + 5 + 5 + 1 + 7 + 31 + 1 + 31
    scratch += [
        pltpu.VMEM(f32_tile, F32),
        pltpu.VMEM((31,) + f32_tile, F32),
        pltpu.SemaphoreType.DMA((1,)),
        pltpu.SemaphoreType.DMA((copies,)),
        pltpu.SemaphoreType.DMA((copies,)),
    ]
    vmem = pl.BlockSpec(memory_space=pltpu.VMEM)
    arrays = tuple(got) + (jnp.asarray(units), loss_tile) + tuple(masters)
    result = pl.pallas_call(
        back_kernel,
        out_shape=[jax.ShapeDtypeStruct(*x) for x in outs],
        in_specs=[vmem] * len(arrays),
        out_specs=[vmem] * len(outs),
        scratch_shapes=scratch,
        compiler_params=pltpu.CompilerParams(
            collective_id=ident, has_side_effects=True, vmem_limit_bytes=63 * 2**20
        ),
    )(*arrays)
    return tuple(result[:7]), result[7]


def at_first(body):
    pl.when(pl.program_id(0) == 0)(body)


def moments_kernel(*refs):
    sums = refs[0]
    grads, masters, firsts, seconds = (refs[1 + 7 * i : 8 + 7 * i] for i in range(4))
    means, squares, updates = (refs[29 + 7 * i : 36 + 7 * i] for i in range(3))
    out = refs[50]
    total = sums[...]
    lane = lax.broadcasted_iota(jnp.int32, (8, LANES), 1)
    norm = jnp.sqrt(jnp.sum(jnp.where(lane < 9, total, 0.0)[0:1], 1, keepdims=True))
    factor = jnp.minimum(1.0, 0.05 / norm)

    def one(i):
        def step(part, cols):
            g = factor * grads[i][part, cols]
            mean = 0.9 * firsts[i][part, cols] + 0.1 * g
            square = 0.99 * seconds[i][part, cols] + 0.01 * g * g
            update = (mean * (1.0 / (1.0 - 0.9**STEP))) / (
                jnp.sqrt(square * (1.0 / (1.0 - 0.99**STEP))) + 1e-08
            ) + 0.01 * masters[i][part, cols]
            means[i][part, cols] = mean
            squares[i][part, cols] = square
            updates[i][part, cols] = update
            return fold(update * update)

        return over_rows(grads[i], step)

    @at_first
    def _():
        table = one(0)
        one(6)
        gains = updates[6][...] * updates[6][...]
        values = [jnp.sum(table)] + [0.0] * 5 + [jnp.sum(gains[j : j + 1]) for j in range(3)]
        out[...] = lane_sums(values, 0)

    out[...] += lane_sums([jnp.sum(one(i)) for i in range(1, 6)], 1)


def weights_kernel(*refs):
    update_sums, sums = refs[:2]
    masters, updates = refs[2:9], refs[9:16]
    news, copies = refs[16:23], refs[23:29]
    norms_ref, loss_ref, norm_ref = refs[29:]
    update_norm = jnp.sqrt(update_sums[0:1, 0:9])
    weight_norm = jnp.sqrt(sums[0:1, 9:18])
    ratio = weight_norm / update_norm

    def one(i):
        def step(part, cols):
            new = masters[i][part, cols] - 0.3 * ratio[0:1, i : i + 1] * updates[i][part, cols]
            news[i][part, cols] = new
            copies[i][part, cols] = new.astype(BF)
            return jnp.zeros((8, LANES), F32)

        over_rows(masters[i], step)

    @at_first
    def _():
        norms_ref[0:1] = weight_norm
        norms_ref[1:2] = update_norm
        loss_ref[...] = sums[0:1, 18 : 18 + PICKS]
        lane = lax.broadcasted_iota(jnp.int32, (1, LANES), 1)
        grad_sq = jnp.where(lane < 9, sums[0:1], 0.0)
        norm_ref[...] = jnp.sqrt(jnp.sum(grad_sq, 1, keepdims=True))
        one(0)
        for j in range(3):
            row = slice(j, j + 1)
            news[6][row] = masters[6][row] - 0.3 * ratio[0:1, 6 + j : 7 + j] * updates[6][row]

    for i in range(1, 6):
        one(i)


def by_rows(body, heads, groups, outs, tails):
    shapes = [x.shape for x in groups[0]]
    parts = 5 if all(shapes[i][0] % 80 == 0 or shapes[i][0] == 40 for i in range(1, 6)) else 1

    def spec(i, shape):
        if i in (0, 6):
            return pl.BlockSpec(shape, lambda n: (0, 0))
        return pl.BlockSpec((shape[0] // parts, shape[1]), lambda n: (n, 0))

    def whole(x):
        return pl.BlockSpec(x.shape, lambda n: (0,) * len(x.shape))

    in_specs = [whole(x) for x in heads]
    in_specs += [spec(i, s) for _ in groups for i, s in enumerate(shapes)]
    out_specs = [spec(i, x.shape) for group in outs for i, x in enumerate(group)]
    out_specs += [whole(x) for x in tails]
    return local_call(
        body,
        [x for group in outs for x in group] + tails,
        list(heads) + [x for group in groups for x in group],
        grid=(parts,),
        in_specs=in_specs,
        out_specs=out_specs,
    )


def layer_norm(v, gain):
    center = v - jnp.mean(v, -1, keepdims=True)
    return center * lax.rsqrt(jnp.mean(center * center, -1, keepdims=True) + 1e-05) * gain


def gradients(obs_tokens, returns, actions, rewards, game_ids, segments, masters):
    table, w_qkv, w_proj, w_up, w_down, w_head, gains = masters
    na, nk = lax.axis_size("ba"), 4
    nb, members = na * 4, 2 * nk
    total = nb * nk
    bl = lax.axis_index("bl")
    k = lax.axis_index("kh") * 2 + lax.axis_index("kl")
    g = bl * nk + k
    seqs, steps_here = obs_tokens.shape[:2]
    width = table.shape[1]
    rows, table_rows = w_qkv.shape[0], table.shape[0]
    steps = steps_here * nk
    heads = HEADS // nk
    wide = width // nk
    cols = 3 * wide // nb
    ff_rows = w_down.shape[0]
    padded_rows = up_to(rows, 16)
    padded_table = up_to(table_rows, 16)
    half = width // 2

    info = jnp.pad(obs_tokens, ((0, 0), (0, 0), (0, LANES - OBS)))
    for i, v in enumerate((returns, actions, rewards, game_ids, segments)):
        info = info + jnp.where(jnp.arange(LANES) == OBS + i, v[..., None], 0)
    info = info.reshape(seqs * steps_here, LANES)
    info = pad_to(info, up_to(seqs * steps_here, 8), LANES)
    counts_here = jnp.sum((game_ids[..., None] == jnp.arange(GAMES)).astype(F32), (0, 1))
    to_heads = [(i, i % nb * nk + i // nb) for i in range(total)]
    proj_rows = pad_to(lax.ppermute(w_proj.astype(BF), ALL, to_heads), padded_rows, width)
    if total == 32 and table_rows == 16 and rows == 40 and seqs == 2 and ff_rows == 160:
        tiny = jnp.pad(gains, ((0, 13), (0, LANES - rows)))
        tiny = tiny + jnp.pad(counts_here[None], ((3, 12), (0, LANES - GAMES)))
        tiny = tiny.astype(BF)
        got = front(
            table,
            w_qkv,
            w_up,
            w_down,
            proj_rows,
            tiny,
            pad_to(w_head.astype(BF), padded_rows, 256),
            info.astype(F32),
            steps,
            0,
        )
        losses = jnp.pad(got[7][2:3, :PICKS], ((0, 7), (18, LANES - 18 - PICKS)))
        return back(got, masters, losses, 1)
    table_bf = pad_to(table.astype(BF), padded_table, width)
    small = jnp.concatenate(
        [
            pad_to(w_head.astype(BF), rows, 256),
            pad_to(gains.astype(BF), 3, 256),
            pad_to(counts_here.astype(BF)[None], 1, 256),
            jnp.zeros((padded_rows - rows - 4, 256), BF),
        ]
    )
    qkv_blocks = w_qkv.astype(BF).reshape(rows, 3, nk, wide).transpose(2, 0, 1, 3)
    qkv_blocks = qkv_blocks.reshape(nk, rows, nb, cols).transpose(2, 0, 1, 3)
    qkv_blocks = pad_to(qkv_blocks.reshape(total, rows, cols), padded_rows, LANES)
    ff_cols = na * 2 * ff_rows
    up_blocks = w_up.astype(BF).reshape(rows, na, 2, 2, nk, ff_rows).transpose(2, 4, 0, 1, 3, 5)
    up_blocks = pad_to(up_blocks.reshape(members, rows, ff_cols), padded_rows, ff_cols)
    parted = ff_rows % 32 == 0 and nk * rows % 16 == 0
    down_low = w_down.astype(BF)
    one_way = ("ba", "bl", "bc", "kh", "kl")
    other_way = ("ba", "bl", "kh", "bc", "kl")
    items = [
        (table_bf[:, :half], "gather", one_way),
        (table_bf[:, half:], "gather", other_way),
        (small, "gather", other_way),
        (qkv_blocks, "scatter", ALL),
        (info, "direct", BLK),
        (up_blocks, "scatter", GROUP),
    ]
    if parted:
        items.append((down_low[: ff_rows // 2], "gather", ("ba",)))
    got = exchange(items, 0)
    table_left, table_right, small_all, qkv_mine, info_here, up_mine = got[:6]
    if parted:
        up_mine = up_mine[:, :rows].reshape(2, nk * rows, ff_cols)
        down_first = got[6]
    else:
        up_mine = lax.all_gather(up_mine[:, :rows], COPIES, axis=0, tiled=False)
        up_mine = up_mine.reshape(na, 2, 2, nk, rows, ff_cols).transpose(0, 2, 1, 3, 4, 5)
        up_mine = up_mine.reshape(width, ff_cols)
        down_first = lax.all_gather(down_low, COPIES, axis=0, tiled=True)

    table_all = jnp.concatenate(
        [
            natural(table_left, ALL, one_way)[:, :table_rows],
            natural(table_right, ALL, other_way)[:, :table_rows],
        ],
        2,
    ).reshape(TABLE, width)
    small_all = natural(small_all, ALL, other_way)
    gain = small_all[:, rows : rows + 3, :rows].transpose(1, 0, 2).reshape(3, width).astype(F32)
    w_mine = qkv_mine[:, :rows].reshape(width, LANES)
    scale_rows = TABLE - FIRST_PLACE + 1
    cols_mine, scale_table, center_bf, center_gain = local_call(
        table_kernel,
        [
            jax.ShapeDtypeStruct((LANES, TABLE), BF),
            jax.ShapeDtypeStruct((2 * scale_rows, TABLE), BF),
            jax.ShapeDtypeStruct((TABLE, width), BF),
            jax.ShapeDtypeStruct((TABLE, width), BF),
        ],
        (table_all, pad_to(gain, 8, width), w_mine),
        [pltpu.VMEM((TABLE, width), F32)],
    )
    table_ways = (("ba", "bl", "bc"), ("bc", "bl", "ba"))
    items = [
        (cols_mine[: LANES // 2], "gather", table_ways[0]),
        (cols_mine[LANES // 2 :], "gather", table_ways[1]),
        (proj_rows, "gather", ("ba", "bc", "bl")),
    ]
    if parted:
        items.append((down_low[ff_rows // 2 :], "gather", ("ba",)))
    got = exchange(items, 1)
    down_second = got[3] if parted else jnp.zeros((16, LANES), BF)
    qkv_table = jnp.concatenate(
        [natural(got[0], BATCH, table_ways[0]), natural(got[1], BATCH, table_ways[1])], 1
    )
    qkv_table = qkv_table[:, :cols].reshape(3 * wide, TABLE)
    proj_here = natural(got[2], BATCH, ("ba", "bc", "bl"))[:, :rows].reshape(wide, width)

    info_here = info_here[:, : seqs * steps_here].reshape(nk, seqs, steps_here, LANES)
    info_here = info_here.transpose(1, 0, 2, 3).reshape(seqs, steps, LANES)
    length = up_to(TSTEP * steps, LANES)
    place_of = np.repeat(np.array(PLACES), steps)
    time_of = np.tile(np.arange(steps), TSTEP)
    tail = length - TSTEP * steps
    pos = np.pad(time_of * TSTEP + place_of, (0, tail), constant_values=1 << 20)
    place_of = np.pad(place_of, (0, tail), constant_values=-1000)
    starts = np.array([0] * OBS + [PATCH, PATCH + RET_BINS, PATCH + RET_BINS + ACTIONS])
    codes = info_here[..., :TSTEP] + starts.astype(np.int32)
    codes = jnp.concatenate(
        [codes[..., OBS - 1 : OBS + 2], codes[..., : OBS - 1], codes[..., OBS + 2 :]], -1
    )
    codes = codes.transpose(0, 2, 1).reshape(seqs, TSTEP * steps)
    codes = jnp.pad(codes, ((0, 0), (0, tail)), constant_values=-1)
    seg = jnp.tile(info_here[..., OBS + 4], (1, TSTEP))
    seg = jnp.pad(seg, ((0, 0), (0, tail)), constant_values=-1)
    zero = jnp.zeros((seqs, length), jnp.int32)
    token_rows = jnp.stack(
        [codes, zero + jnp.asarray(pos, jnp.int32), seg, zero + jnp.asarray(place_of, jnp.int32)]
        + [zero] * 4,
        1,
    )
    token_cols = jnp.stack([zero[:, :LANES] + pos[:LANES].astype(np.int32), seg[:, :LANES]], -1)
    token_cols = jnp.pad(token_cols, ((0, 0), (0, 0), (0, LANES - 2)))

    own = seqs * LANES // nk
    slots = lax.rem(k, nk // seqs) * own + jnp.arange(own)
    seq_own = k * own // LANES
    codes_own = lax.dynamic_slice(codes, (seq_own, lax.rem(k, nk // seqs) * own), (1, own))[0]
    place_own = jnp.asarray(place_of[:LANES], jnp.int32)
    place_own = lax.dynamic_slice(place_own, (lax.rem(k, nk // seqs) * own,), (own,))
    kind = slots // steps
    info_seq = lax.dynamic_index_in_dim(info_here, seq_own, 0, False)
    info_own = info_seq.at[lax.rem(slots, steps)].get(mode="promise_in_bounds")
    counts = jnp.sum(small_all[:, rows + 3, :GAMES].astype(F32), 0)
    per_game = 1.0 / (GAMES * jnp.maximum(counts, 1.0))
    game_own = (info_own[:, OBS + 3, None] == jnp.arange(GAMES)).astype(F32)
    weight = jnp.where(kind < PICKS, jnp.sum(game_own * per_game, -1), 0.0)
    low_end = jnp.where(kind == 0, 0, jnp.where(kind == 1, RET_BINS, RET_BINS + ACTIONS))
    high_end = jnp.where(kind == 0, RET_BINS, jnp.where(kind == 1, RET_BINS + ACTIONS, HEAD_COLS))
    target = low_end + jnp.where(
        kind == 0,
        info_own[:, OBS],
        jnp.where(kind == 1, info_own[:, OBS + 1], info_own[:, OBS + 2]),
    )
    own_info = [low_end, high_end, target, weight, kind, codes_own, place_own + FIRST_PLACE]
    own_info = pad_to(jnp.stack([v.astype(F32) for v in own_info], 1), own, LANES)
    head_full = small_all[:, :rows].reshape(width, 256)
    d_table, pairs, sum_up, sum_down, d_proj, d_head, dy_own, d_small = core(
        token_rows,
        token_cols,
        qkv_table,
        scale_table,
        table_all,
        pad_to(gain, 8, width),
        proj_here,
        head_full,
        own_info,
        up_mine,
        down_first,
        down_second,
        heads,
        2,
    )
    d_gain_mid, d_gain_last = d_small[0], d_small[1]
    losses = [d_small[2, j] for j in range(PICKS)]
    columns = jnp.arange(TABLE)
    own_hot = (codes_own[:, None] == columns) | (place_own[:, None] + FIRST_PLACE == columns)
    own_hot = own_hot.astype(BF)
    if not parted:
        sum_up = sum_up.reshape(na, 2, 2, nk, rows, ff_cols).transpose(0, 2, 1, 3, 4, 5)
        sum_up = sum_up.reshape(width, ff_cols)
        sum_up = lax.psum_scatter(sum_up, COPIES, scatter_dimension=0, tiled=True)
        sum_down = lax.psum_scatter(sum_down, COPIES, scatter_dimension=0, tiled=True)

    d_table = pad_to(d_table.astype(BF).reshape(nb, cols, TABLE), LANES, TABLE)
    d_proj = pad_to(d_proj.astype(BF).reshape(nb, rows, width), padded_rows, width)
    proj_route = ("bl", "bc", "ba")
    table_routes = (("bc", "bl", "ba"), ("bl", "bc", "ba"))
    left, right, sum_proj = reduce(
        [
            for_route(d_table[..., : TABLE // 2], BATCH, table_routes[0]),
            for_route(d_table[..., TABLE // 2 :], BATCH, table_routes[1]),
            for_route(d_proj, BATCH, proj_route),
        ],
        table_routes + (proj_route,),
        [],
        3,
    )
    sum_proj = lax.ppermute(sum_proj[:rows], ALL, [(j, i) for i, j in to_heads])
    d_table_mine = jnp.concatenate([left, right], 1).astype(BF)
    d_w = dot(center_gain, d_table_mine, 0, 1)
    d_norm = dot(d_table_mine, w_mine, 0, 1)
    d_gain_first = jnp.sum(center_bf.astype(F32) * d_norm, 0)
    d_scaled = d_norm * gain[0]
    d_embed = (
        d_scaled
        - jnp.mean(d_scaled, 1, keepdims=True)
        - dot(pairs.astype(BF), center_bf)
        + dot(own_hot, dy_own, 0, 0)
    )
    d_gains = jnp.stack([d_gain_first, d_gain_mid, d_gain_last]).astype(BF)
    d_misc = jnp.concatenate(
        [
            d_head.reshape(total, rows, 256),
            pad_to(d_gains.reshape(3, total, rows).transpose(1, 0, 2), 3, 256),
            jnp.zeros((total, padded_rows - rows - 3, 256), BF),
        ],
        1,
    )
    d_w = pad_to(d_w.astype(BF).reshape(total, rows, LANES), padded_rows, LANES)
    d_embed = pad_to(d_embed.astype(BF).reshape(total, table_rows, width), padded_table, width)
    sum_up = pad_to(sum_up.reshape(members, rows, -1), padded_rows, ff_cols)
    one_way = ("kl", "kh", "bc", "bl", "ba")
    other_way = ("kl", "bc", "kh", "bl", "ba")
    arrays = [
        for_route(d_embed[..., :half], ALL, one_way),
        for_route(d_embed[..., half:], ALL, other_way),
        for_route(d_misc, ALL, other_way),
    ]
    routes = (one_way, other_way, other_way)
    if parted:
        arrays.append(sum_down)
        routes += (("ba",),)
    got = reduce(arrays, routes, [(d_w, ALL), (sum_up, GROUP)], 4)
    d_left, d_right, d_misc = got[:3]
    d_ws, ups = got[-2:]
    if parted:
        sum_down = got[3]
    d_embed = jnp.concatenate([d_left, d_right], 1)
    d_ws = d_ws[:, :rows, :cols].reshape(nb, nk, rows, cols).transpose(2, 1, 0, 3)
    d_ws = d_ws.reshape(rows, nk, 3, wide).transpose(0, 2, 1, 3).reshape(rows, 3 * width)
    ups = ups[:, :rows].reshape(2, nk, rows, na, 2, ff_rows).transpose(2, 3, 0, 4, 1, 5)
    ups = ups.reshape(rows, nb * nk * ff_rows)
    grads = (
        d_embed[:table_rows],
        d_ws.astype(F32),
        sum_proj,
        ups.astype(F32),
        sum_down.astype(F32),
        d_misc[:rows, :HEAD_COLS],
        d_misc[rows : rows + 3, :rows],
    )
    loss_tile = jnp.zeros((8, LANES), F32).at[:, 18:21].set(jnp.stack(losses))
    return grads, summed_call(squares_kernel, grads + masters + (loss_tile,), 5)


def shards(*args):
    masters, firsts, seconds = args[6:13], args[13:20], args[20:27]
    grads, sums = gradients(*args[:6], masters)
    like = [jax.ShapeDtypeStruct(w.shape, F32) for w in masters]
    low = [jax.ShapeDtypeStruct(w.shape, BF) for w in masters[:6]]
    tile = jax.ShapeDtypeStruct((8, LANES), F32)
    result = by_rows(
        moments_kernel, (sums,), (grads, masters, firsts, seconds), [like] * 3, [tile]
    )
    means, squares, updates = result[:7], result[7:14], result[14:21]
    update_sums = summed_call(all_sum_kernel, (result[21],), 6)
    last = [jax.ShapeDtypeStruct(x, F32) for x in ((2, 9), (1, PICKS), (1, 1))]
    result = by_rows(
        weights_kernel, (update_sums, sums), (masters, updates), [like, low], last
    )
    news, copies, norms = result[:7], result[7:13], result[13]
    loss_terms, grad_norm = result[14].reshape(PICKS), result[15].reshape(())
    return tuple(news) + tuple(means) + tuple(squares) + tuple(copies) + (
        grad_norm,
        loss_terms,
        norms,
    )


def solution(mesh):
    nb, nk = mesh.shape["batch"], mesh.shape["blk"]
    split = Mesh(mesh.devices.reshape(nb // 4, 2, 2, nk // 2, 2), ALL)
    rows, gains = P(ALL, None), P(None, ALL)
    weights = (rows,) * 6 + (gains,)
    in_specs = (P(BATCH, BLK, None),) + (P(BATCH, BLK),) * 5 + weights * 3
    out_specs = weights * 3 + (rows,) * 6 + (P(), P(), P())
    return jax.shard_map(
        shards, mesh=split, in_specs=in_specs, out_specs=out_specs, check_vma=False
    )
```
